32 devices in a mesh: dp: 4 (over y, x), vocab: 8 (over z, core).
Axes of the slice: x: 2, y: 2, z: 4, core: 2. Of those that a mesh axis runs over, the one named last changes fastest.
Arguments:
- master_tiles: float32 [2816, 64, 64], P(('dp', 'vocab')), may hold values from -0.25 to 0.25
- mom1_tiles: float32 [2816, 64, 64], P(('dp', 'vocab')), may hold values from -5.722046e-06 to 5.722046e-06
- mom2_tiles: float32 [2816, 64, 64], P(('dp', 'vocab')), may hold values from 3.7079958e-13 to 5.9327933e-12
- stat_left: float32 [2816, 64, 64], P(('dp', 'vocab')), as said below
- stat_right: float32 [2816, 64, 64], P(('dp', 'vocab')), as said below
- basis_left: float32 [2816, 64, 64], P(('dp', 'vocab')), as said below
- basis_right: float32 [2816, 64, 64], P(('dp', 'vocab')), as said below
- table_master: float32 [32768, 512], P('vocab')
- table_mom1: float32 [32768, 512], P('vocab'), may hold values from -5.722046e-06 to 5.722046e-06
- table_mom2: float32 [32768, 512], P('vocab'), may hold values from 3.7079958e-13 to 5.9327933e-12
- gains: float32 [11, 512], replicated, may hold values from 0.5 to 1.5
- gain_mom1: float32 [11, 512], replicated, may hold values from -2.2888184e-05 to 2.2888184e-05
- gain_mom2: float32 [11, 512], replicated, may hold values from 5.9327933e-12 to 9.5348465e-11
- source_ids: int32 [2, 32, 1024], P(None, ('dp', 'vocab')), may hold values from 0 to 32767
- target_ids: int32 [2, 32, 256], P(None, ('dp', 'vocab')), may hold values from 0 to 32767
- source_len: int32 [2, 32], P(None, ('dp', 'vocab')), may hold values from 1 to 1024, as said below
- target_len: int32 [2, 32], P(None, ('dp', 'vocab')), may hold values from 1 to 256, as said below
- loss_place: int32 [2, 32, 16], P(None, ('dp', 'vocab')), may hold values from 0 to 255
- exit_layer: int32 [2, 32, 16], P(None, ('dp', 'vocab')), may hold values from 0 to 1
- slot_list: int32 [2816], replicated, may hold values from 0 to 2815, each once
Outputs:
- loss_sum: float32 [], replicated
- loss_count: float32 [], replicated
- grad_norm: float32 [], replicated
- master_new: float32 [2816, 64, 64], P(('dp', 'vocab'))
- master_low: bfloat16 [2816, 64, 64], P(('dp', 'vocab'))
- mom1_new: float32 [2816, 64, 64], P(('dp', 'vocab'))
- mom2_new: float32 [2816, 64, 64], P(('dp', 'vocab'))
- stat_left_new: float32 [2816, 64, 64], P(('dp', 'vocab'))
- stat_right_new: float32 [2816, 64, 64], P(('dp', 'vocab'))
- basis_left_new: float32 [2816, 64, 64], P(('dp', 'vocab'))
- basis_right_new: float32 [2816, 64, 64], P(('dp', 'vocab'))
- table_new: float32 [32768, 512], P('vocab')
- table_low: bfloat16 [32768, 512], P('vocab')
- table_mom1_new: float32 [32768, 512], P('vocab')
- table_mom2_new: float32 [32768, 512], P('vocab')
- gains_new: float32 [11, 512], replicated
- gain_mom1_new: float32 [11, 512], replicated
- gain_mom2_new: float32 [11, 512], replicated
The draws below stay inside these ranges and needn't reach their ends.
Inputs may be any that keep to these rules, and one draw needn't show every extreme that they name: `stat_left`: each block is symmetric positive definite. `stat_right`: each block is symmetric positive definite. `basis_left`: each block is orthogonal. `basis_right`: each block is orthogonal. `source_len`: some sequence has source length 1024. `target_len`: some sequence has target length 256.
All inputs are finite; a program needn't handle non-finite values.
Results may differ from the reference program's by a relative error of at most 0.0056.
Values may be sent and summed in bfloat16 or wider, within the bound.
No kernel may reach another device: no remote copies, remote signals or barrier semaphores. Data moves between devices by JAX's collectives and lax.ppermute only.
A program may use at most 768 MiB of HBM per device.

```python
import math
import jax
import jax.numpy as jnp
from jax import lax

D = 512
HEADS = 8
HEAD_DIM = 64
FF = 2048
VOCAB = 32768
ENC = 1
DEC = 2
MICRO = 2
SEQ_DEV = 1
SRC = 1024
TGT = 256
LOSS_POS = 16
PB = 64
STEP = 10
MATS = 11
GAINS = 11
TILES = 2816
SEQS = 32
N_DP = 4
N_VOCAB = 8


def rising_lengths(jitter, longest):
    device_at = jnp.arange(SEQS, dtype=jnp.int32) // SEQ_DEV
    numer = device_at // N_VOCAB * max(N_VOCAB - 1, 1) + device_at % N_VOCAB * max(N_DP - 1, 1)
    denom = max(N_DP - 1, 1) * max(N_VOCAB - 1, 1)
    base_len = longest // 4 + 3 * longest * numer // (8 * denom)
    lengths = jnp.clip(base_len[None, :] + jitter, 1, longest)
    return lengths.at[0, SEQS - 1].set(longest)


def draw_source_len(key, part):
    key = jax.random.fold_in(key, 21)
    jitter = jax.random.randint(key, (MICRO, SEQS), -(SRC // 8), SRC // 8 + 1)
    return rising_lengths(jitter, SRC)


def draw_target_len(key, part):
    key = jax.random.fold_in(key, 22)
    jitter = jax.random.randint(key, (MICRO, SEQS), -(TGT // 8), TGT // 8 + 1)
    return rising_lengths(jitter, TGT)


def assemble_stat(diagonal, noise):
    eye_mat = jnp.eye(PB, dtype=jnp.float32)
    symmetric = (noise + jnp.swapaxes(noise, 1, 2)) * 0.70710678
    scale_by = 0.0001 * PB / (MATS * D * FF + VOCAB * D + GAINS * D)
    return (symmetric * (1.0 - eye_mat) + eye_mat * diagonal[:, :, None]) * scale_by


def draw_stat_left(key, part):
    key = jax.random.fold_in(key, 31)
    diag_key, noise_key = jax.random.split(key)
    diagonal = jax.random.uniform(diag_key, (TILES, PB), minval=2.0, maxval=8.0)
    noise = jax.random.normal(noise_key, (TILES, PB, PB)) * 0.08
    return assemble_stat(diagonal, noise)


def draw_stat_right(key, part):
    key = jax.random.fold_in(key, 32)
    diag_key, noise_key = jax.random.split(key)
    diagonal = jax.random.uniform(diag_key, (TILES, PB), minval=2.0, maxval=8.0)
    noise = jax.random.normal(noise_key, (TILES, PB, PB)) * 0.08
    return assemble_stat(diagonal, noise)


def reflections(vectors):
    basis = jnp.broadcast_to(jnp.eye(PB, dtype=jnp.float32), (TILES, PB, PB))
    for reflect_no in range(4):
        direction = vectors[reflect_no] * lax.rsqrt(jnp.sum(vectors[reflect_no] ** 2, axis=1, keepdims=True))
        image = jnp.einsum('tij,tj->ti', basis, direction, precision=lax.Precision.HIGHEST)
        basis = basis - 2.0 * image[:, :, None] * direction[:, None, :]
    return basis


def draw_basis_left(key, part):
    key = jax.random.fold_in(key, 41)
    return reflections(jax.random.normal(key, (4, TILES, PB)))


def draw_basis_right(key, part):
    key = jax.random.fold_in(key, 42)
    return reflections(jax.random.normal(key, (4, TILES, PB)))


def draw_table_master(key, part):
    key = jax.random.fold_in(key, 51)
    row_at = jnp.arange(VOCAB, dtype=jnp.float32)[:, None] / (VOCAB - 1)
    values = jax.random.normal(key, (VOCAB, D)) * (1.0 + 2.0 * row_at)
    return values / D ** 0.5


def place_ends(entries, rng, least, high):
    longest = entries.shape.index(max(entries.shape))
    spots = []
    for shift in (0, 1):
        where = [jax.random.randint(jax.random.fold_in(rng, axis), (), 0, length) for axis, length in enumerate(entries.shape)]
        where[longest] = (where[longest] + shift) % entries.shape[longest]
        spots.append(tuple(where))
    return entries.at[spots[0]].set(least).at[spots[1]].set(high)


def levels(rng, dims, cuts, low, largest):
    gain, own = 1.0, jax.random.fold_in(rng, 6)
    for dim, parts in cuts:
        steps = jnp.exp(jax.random.uniform(jax.random.fold_in(own, dim), (parts,), jnp.float32, low / len(cuts), largest / len(cuts)))
        gain = gain * jnp.repeat(steps, dims[dim] // parts).reshape([-1 if axis == dim else 1 for axis in range(len(dims))])
    return gain


def centred(own_key, shape, deviation, bound, cuts=(), kind=jnp.bfloat16):
    array = jax.random.normal(own_key, shape, jnp.float32) * deviation
    if len(cuts) > 0:
        array = levels(own_key, shape, cuts, -0.22, 0.18) * array
    return jnp.clip(array, min=-bound, max=bound).astype(kind)


def setup_inputs(seed: int = 0) -> dict:
    keys = jax.random.split(jax.random.key(seed), 21)
    master_tiles = centred(keys[0], (TILES, PB, PB), D ** -0.5, 0.25, ((0, 32),), jnp.float32)
    mom1_tiles = centred(keys[1], (TILES, PB, PB), (0.0022 / (MATS * D * FF + VOCAB * D + GAINS * D) ** 0.5), 5.7220458984375e-06, ((0, 32),), jnp.float32)
    mom2_tiles = jnp.clip(jnp.exp(math.log(5.93279331911889e-12) - 2.7725887 * jax.random.uniform(keys[2], (TILES, PB, PB), jnp.float32) ** levels(keys[2], (TILES, PB, PB), ((0, 32),), -0.2, 0.2)), 3.707995824449306e-13, 5.93279331911889e-12)
    stat_left = draw_stat_left(jax.random.fold_in(keys[20], 71), 0)
    stat_right = draw_stat_right(jax.random.fold_in(keys[20], 71), 0)
    basis_left = draw_basis_left(jax.random.fold_in(keys[20], 71), 0)
    basis_right = draw_basis_right(jax.random.fold_in(keys[20], 71), 0)
    table_master = draw_table_master(jax.random.fold_in(keys[20], 71), 0)
    table_mom1 = centred(keys[8], (VOCAB, D), (0.0022 / (MATS * D * FF + VOCAB * D + GAINS * D) ** 0.5), 5.7220458984375e-06, ((0, 8),), jnp.float32)
    table_mom2 = jnp.clip(jnp.exp(math.log(5.93279331911889e-12) - 2.7725887 * jax.random.uniform(keys[9], (VOCAB, D), jnp.float32) ** levels(keys[9], (VOCAB, D), ((0, 8),), -0.2, 0.2)), 3.707995824449306e-13, 5.93279331911889e-12)
    gains = jnp.clip(1.0 + 0.1 * jax.random.normal(keys[10], (GAINS, D), jnp.float32), 0.5, 1.5)
    gain_mom1 = centred(keys[11], (GAINS, D), (0.0088 / (MATS * D * FF + VOCAB * D + GAINS * D) ** 0.5), 2.288818359375e-05, (), jnp.float32)
    gain_mom2 = jnp.clip(jnp.exp(jax.random.uniform(keys[12], (GAINS, D), jnp.float32, math.log(5.93279331911889e-12), math.log(9.534846523440166e-11))), 5.93279331911889e-12, 9.534846523440166e-11)
    source_ids = place_ends(jax.random.randint(keys[13], (MICRO, SEQS, SRC), 0, VOCAB), jax.random.fold_in(keys[13], 1), 0, VOCAB - 1).astype(jnp.int32)
    target_ids = place_ends(jax.random.randint(keys[14], (MICRO, SEQS, TGT), 0, VOCAB), jax.random.fold_in(keys[14], 1), 0, VOCAB - 1).astype(jnp.int32)
    source_len = draw_source_len(jax.random.fold_in(keys[20], 71), 0)
    target_len = draw_target_len(jax.random.fold_in(keys[20], 71), 0)
    loss_place = place_ends(jax.random.randint(keys[17], (MICRO, SEQS, LOSS_POS), 0, TGT), jax.random.fold_in(keys[17], 1), 0, TGT - 1).astype(jnp.int32)
    exit_layer = place_ends(jax.random.randint(keys[18], (MICRO, SEQS, LOSS_POS), 0, DEC), jax.random.fold_in(keys[18], 1), 0, DEC - 1).astype(jnp.int32)
    slot_list = jax.random.permutation(keys[19], TILES).astype(jnp.int32)
    return {"master_tiles": master_tiles, "mom1_tiles": mom1_tiles, "mom2_tiles": mom2_tiles, "stat_left": stat_left, "stat_right": stat_right, "basis_left": basis_left, "basis_right": basis_right, "table_master": table_master, "table_mom1": table_mom1, "table_mom2": table_mom2, "gains": gains, "gain_mom1": gain_mom1, "gain_mom2": gain_mom2, "source_ids": source_ids, "target_ids": target_ids, "source_len": source_len, "target_len": target_len, "loss_place": loss_place, "exit_layer": exit_layer, "slot_list": slot_list}


HIGHEST = lax.Precision.HIGHEST
NORM_EPS = 1e-06
CLIP_AT = 0.02
RATE_MATRIX = 0.1
RATE_VECTOR = 0.8
BETA_FIRST = 0.9
BETA_SECOND = 0.95
BETA_STAT = 0.95
ADAM_EPS = 1e-08
DECAY = 0.01

@jax.custom_vjp
def low(v):
    return lax.optimization_barrier(v.astype(jnp.bfloat16)).astype(jnp.float32)

@jax.custom_vjp
def low_back(v):
    return v

def low_keep(v):
    return (low(v), None)

def low_pass(kept, grad):
    return (grad,)

def back_keep(v):
    return (v, None)

def back_low(kept, grad):
    return (low(grad),)
low.defvjp(low_keep, low_pass)
low_back.defvjp(back_keep, back_low)

def rms_norm(stream, gain_row):
    return stream * lax.rsqrt(lax.optimization_barrier(jnp.mean(stream * stream, axis=-1, keepdims=True)) + NORM_EPS) * gain_row

def waves(length, columns):
    place_at = jnp.arange(length).astype(jnp.float32)[:, None]
    rate_at = jnp.exp(jnp.arange(columns // 2).astype(jnp.float32) * (-2.0 * math.log(10000.0) / columns))
    angle = place_at * rate_at[None, :]
    return jnp.concatenate([jnp.sin(angle), jnp.cos(angle)], axis=1)

def matmul(left_op, right_op):
    return jnp.dot(left_op, right_op, precision=HIGHEST)

def attend(query_in, keys_in, values_in, valid_len, causal):
    row_count = query_in.shape[0]
    block_rows = min(512, row_count)
    key_count = keys_in.shape[0]
    query_heads = query_in.reshape(row_count // block_rows, block_rows, HEADS, HEAD_DIM)
    key_heads = keys_in.reshape(key_count, HEADS, HEAD_DIM)
    value_heads = values_in.reshape(key_count, HEADS, HEAD_DIM)
    key_at = jnp.arange(key_count)
    starts = jnp.arange(row_count // block_rows) * block_rows

    def one_block(pair_in):
        piece_q, start_at = pair_in
        scores = low_back(jnp.einsum('qhd,khd->hqk', piece_q, key_heads, precision=HIGHEST) * HEAD_DIM ** (-0.5))
        allowed = jnp.broadcast_to(key_at[None, :] < valid_len, (block_rows, key_count))
        if causal:
            allowed = allowed & (key_at[None, :] <= start_at + jnp.arange(block_rows)[:, None])
        scores = jnp.where(allowed[None], scores, -1000000000.0)
        summit = lax.optimization_barrier(jnp.max(scores, axis=-1, keepdims=True))
        expo_val = jnp.exp(scores - summit)
        probs_f = expo_val / lax.optimization_barrier(jnp.sum(expo_val, axis=-1, keepdims=True))
        return jnp.einsum('hqk,khd->qhd', low(probs_f), value_heads, precision=HIGHEST)
    mixed_out = lax.map(jax.checkpoint(one_block), (query_heads, starts))
    return mixed_out.reshape(row_count, HEADS * HEAD_DIM)

def self_block(stream, gain_row, weight, valid_len, causal):
    normed = low(rms_norm(stream, gain_row))
    joint_qkv = low_back(low(matmul(normed, weight[:, :3 * D])))
    mixed_out = low_back(low(attend(joint_qkv[:, :D], joint_qkv[:, D:2 * D], joint_qkv[:, 2 * D:], valid_len, causal)))
    return stream + low_back(matmul(mixed_out, weight[:, 3 * D:]))

def cross_block(stream, gain_row, weight, memory, valid_len):
    normed = low(rms_norm(stream, gain_row))
    query_in = low_back(low(matmul(normed, weight[:, :D])))
    pair_kv = low_back(low(matmul(memory, weight[:, D:3 * D])))
    mixed_out = low_back(low(attend(query_in, pair_kv[:, :D], pair_kv[:, D:], valid_len, False)))
    return stream + low_back(matmul(mixed_out, weight[:, 3 * D:]))

def ffn_block(stream, gain_row, w_in, w_out):
    normed = low(rms_norm(stream, gain_row))
    hidden = low_back(matmul(normed, w_in))
    active = low(jax.nn.gelu(hidden, approximate=True))
    return stream + low_back(jnp.dot(active, w_out.T, precision=HIGHEST))

def sequence_loss(weights, table, gain_set, source, target, source_len, target_len, place_at, fraction):
    stream = table[source] * math.sqrt(D) + waves(SRC, D)
    for layer_no in range(ENC):
        stream = self_block(stream, gain_set[2 * layer_no], weights[layer_no], source_len, False)
        stream = ffn_block(stream, gain_set[2 * layer_no + 1], weights[ENC + 2 * DEC + layer_no], weights[2 * ENC + 3 * DEC + layer_no])
    memory = low(rms_norm(stream, gain_set[2 * ENC]))
    shifted = jnp.concatenate([jnp.zeros((1,), jnp.int32), target[:-1]])
    decoded = table[shifted] * math.sqrt(D) + waves(TGT, D)
    counted = (place_at < target_len).astype(jnp.float32)
    labels = target[place_at]
    total = jnp.zeros((), jnp.float32)
    for layer_no in range(DEC):
        base_at = 2 * ENC + 1 + 3 * layer_no
        decoded = self_block(decoded, gain_set[base_at], weights[ENC + layer_no], target_len, True)
        decoded = cross_block(decoded, gain_set[base_at + 1], weights[ENC + DEC + layer_no], memory, source_len)
        decoded = ffn_block(decoded, gain_set[base_at + 2], weights[2 * ENC + 2 * DEC + layer_no], weights[3 * ENC + 3 * DEC + layer_no])
        row_set = low(rms_norm(decoded[place_at], gain_set[2 * ENC + 1 + 3 * DEC + layer_no]))
        logits = low_back(jnp.dot(row_set, table.T, precision=HIGHEST))
        summit = lax.optimization_barrier(jnp.max(logits, axis=1, keepdims=True))
        spread = jnp.log(lax.optimization_barrier(jnp.sum(jnp.exp(logits - summit), axis=1))) + summit[:, 0]
        picked = jnp.take_along_axis(logits, labels[:, None], axis=1)[:, 0]
        total = total + fraction[layer_no] * jnp.sum(counted * (spread - picked))
    return total

def untile(tiles):
    split = tiles.reshape(MATS, D // PB, FF // PB, PB, PB)
    return split.transpose(0, 1, 3, 2, 4).reshape(MATS, D, FF)

def turn_in(left_basis, tiles, right_basis):
    half = jnp.einsum('tki,tkl->til', left_basis, tiles, precision=HIGHEST)
    return jnp.einsum('til,tlj->tij', half, right_basis, precision=HIGHEST)

def turn_out(left_basis, tiles, right_basis):
    half = jnp.einsum('tik,tkl->til', left_basis, tiles, precision=HIGHEST)
    return jnp.einsum('til,tjl->tij', half, right_basis, precision=HIGHEST)

def solve_lower(lower_tri, right_side):
    return jax.scipy.linalg.solve_triangular(lower_tri, right_side, lower=True)

def renew_basis(statistic, basis):
    moved = jnp.einsum('tij,tjk->tik', statistic, basis, precision=HIGHEST)
    gram = jnp.einsum('tki,tkj->tij', moved, moved, precision=HIGHEST)
    lower_tri = jnp.linalg.cholesky(gram)
    solved = jax.vmap(solve_lower)(lower_tri, jnp.swapaxes(moved, 1, 2))
    return jnp.swapaxes(solved, 1, 2)

def soap_update(master, grad_tiles, first_mom, second_mom, left_stat, right_stat, left_basis, right_basis):
    first_new = BETA_FIRST * first_mom + (1 - BETA_FIRST) * grad_tiles
    grad_turned = turn_in(left_basis, grad_tiles, right_basis)
    first_turned = turn_in(left_basis, first_new, right_basis)
    second_new = BETA_SECOND * second_mom + (1 - BETA_SECOND) * grad_turned * grad_turned
    direction = first_turned / (1 - BETA_FIRST ** STEP) / (jnp.sqrt(second_new / (1 - BETA_SECOND ** STEP)) + ADAM_EPS)
    master_new = master - RATE_MATRIX * (turn_out(left_basis, direction, right_basis) + DECAY * master)
    left_new = BETA_STAT * left_stat + (1 - BETA_STAT) * jnp.einsum('tik,tjk->tij', grad_tiles, grad_tiles, precision=HIGHEST)
    right_new = BETA_STAT * right_stat + (1 - BETA_STAT) * jnp.einsum('tki,tkj->tij', grad_tiles, grad_tiles, precision=HIGHEST)
    return (master_new, first_new, second_new, left_new, right_new, renew_basis(left_new, left_basis), renew_basis(right_new, right_basis))

def adamw_update(master, grad_now, first_mom, second_mom, rate, decay_by):
    first_new = BETA_FIRST * first_mom + (1 - BETA_FIRST) * grad_now
    second_new = BETA_SECOND * second_mom + (1 - BETA_SECOND) * grad_now * grad_now
    direction = first_new / (1 - BETA_FIRST ** STEP) / (jnp.sqrt(second_new / (1 - BETA_SECOND ** STEP)) + ADAM_EPS)
    return (master - rate * (direction + decay_by * master), first_new, second_new)

def reference(master_tiles, mom1_tiles, mom2_tiles, stat_left, stat_right, basis_left, basis_right, table_master, table_mom1, table_mom2, gains, gain_mom1, gain_mom2, source_ids, target_ids, source_len, target_len, loss_place, exit_layer, slot_list):
    counted = loss_place < target_len[:, :, None]
    count_all = jnp.sum(counted.astype(jnp.float32))
    reach = jnp.stack([jnp.sum((counted & (exit_layer >= layer_no)).astype(jnp.float32)) for layer_no in range(DEC)])
    fraction = reach / jnp.sum(reach)
    items = (source_ids.reshape(-1, SRC), target_ids.reshape(-1, TGT), source_len.reshape(-1), target_len.reshape(-1), loss_place.reshape(-1, LOSS_POS))

    def objective(tiles, table, gain_set):
        weights = low(untile(jnp.zeros_like(tiles).at[slot_list].set(tiles)))
        table_used = low(table)

        def one_step(carry, item):
            return (carry + jax.checkpoint(sequence_loss)(weights, table_used, gain_set, *item, fraction), None)
        total, _ = lax.scan(one_step, jnp.zeros((), jnp.float32), items)
        return (total / count_all, total)
    _, pull_back, total = jax.vjp(objective, master_tiles, table_master, gains, has_aux=True)
    grad_tiles, grad_table, grad_gain = pull_back(jnp.ones((), jnp.float32))
    grad_norm = jnp.sqrt(jnp.sum(grad_tiles * grad_tiles) + jnp.sum(grad_table * grad_table) + jnp.sum(grad_gain * grad_gain))
    factor = jnp.minimum(1.0, CLIP_AT / grad_norm)
    master_new, mom1_new, mom2_new, left_new, right_new, bleft_new, bright_new = soap_update(master_tiles, grad_tiles * factor, mom1_tiles, mom2_tiles, stat_left, stat_right, basis_left, basis_right)
    table_new, table_m, table_v = adamw_update(table_master, grad_table * factor, table_mom1, table_mom2, RATE_MATRIX, DECAY)
    gains_new, gains_m, gains_v = adamw_update(gains, grad_gain * factor, gain_mom1, gain_mom2, RATE_VECTOR, 0.0)
    return (total, count_all, grad_norm, master_new, master_new.astype(jnp.bfloat16), mom1_new, mom2_new, left_new, right_new, bleft_new, bright_new, table_new, table_new.astype(jnp.bfloat16), table_m, table_v, gains_new, gains_m, gains_v)
```

```python
import math

import jax
import jax.numpy as jnp
from jax import lax
from jax.experimental import pallas as pl
from jax.experimental.pallas import tpu as pltpu
from jax.sharding import PartitionSpec as P

D = 512
HEADS = 8
HEAD_DIM = 64
FF = 2048
ENC = 1
DEC = 2
MICRO = 2
LOSS_POS = 16
PB = 64
STEP = 10
MATS = 11
GAINS = 11


HIGHEST = lax.Precision.HIGHEST
NORM_EPS = 1e-06
CLIP_AT = 0.02
RATE_MATRIX = 0.1
RATE_VECTOR = 0.8
BETA_FIRST = 0.9
BETA_SECOND = 0.95
BETA_STAT = 0.95
ADAM_EPS = 1e-08
DECAY = 0.01


def rms_norm(stream, gain_row):
    return (
        stream * lax.rsqrt(jnp.mean(stream * stream, axis=-1, keepdims=True) + NORM_EPS) * gain_row
    )


def waves(length, columns):
    place_at = jnp.arange(length).astype(jnp.float32)[:, None]
    rate_at = jnp.exp(
        jnp.arange(columns // 2).astype(jnp.float32) * (-2.0 * math.log(10000.0) / columns)
    )
    angle = place_at * rate_at[None, :]
    return jnp.concatenate([jnp.sin(angle), jnp.cos(angle)], axis=1)


def linear(left_op, right_op):
    return jnp.dot(left_op, right_op, preferred_element_type=jnp.float32)


def linear_tr(left_op, right_op):
    return lax.dot_general(
        left_op, right_op, (((1,), (1,)), ((), ())), preferred_element_type=jnp.float32
    )


def outer_sum(left_op, right_op):
    return lax.dot_general(
        left_op, right_op, (((0,), (0,)), ((), ())), preferred_element_type=jnp.float32
    )


def split_heads(matrix):
    return matrix.reshape(matrix.shape[0], HEADS, HEAD_DIM)


def block_scores(piece_q, key_heads, valid_len, causal, start_at):
    block_rows, key_count = (piece_q.shape[0], key_heads.shape[0])
    scores = jnp.einsum(
        "qhd,khd->hqk", piece_q, key_heads, preferred_element_type=jnp.float32
    ) * HEAD_DIM ** (-0.5)
    key_at = jnp.arange(key_count)
    allowed = jnp.broadcast_to(key_at[None, :] < valid_len, (block_rows, key_count))
    if causal:
        allowed = allowed & (key_at[None, :] <= start_at + jnp.arange(block_rows)[:, None])
    return jnp.where(allowed[None], scores, -1000000000.0)


def attend_forward(query_in, keys_in, values_in, valid_len, causal):
    row_count = query_in.shape[0]
    block_rows = min(512, row_count)
    key_heads, value_heads = (split_heads(keys_in), split_heads(values_in))
    outputs, stats_kept = ([], [])
    for start_at in range(0, row_count, block_rows):
        scores = block_scores(
            split_heads(query_in[start_at : start_at + block_rows]),
            key_heads,
            valid_len,
            causal,
            start_at,
        )
        summit = jnp.max(scores, axis=-1, keepdims=True)
        expo_val = jnp.exp(scores - summit)
        totals = jnp.sum(expo_val, axis=-1, keepdims=True)
        probs_low = (expo_val / totals).astype(jnp.bfloat16)
        mixed_out = jnp.einsum(
            "hqk,khd->qhd", probs_low, value_heads, preferred_element_type=jnp.float32
        )
        outputs.append(mixed_out.reshape(block_rows, -1))
        stats_kept.append(summit + jnp.log(totals))
    return (jnp.concatenate(outputs, 0).astype(jnp.bfloat16), stats_kept)


def attend_backward(query_in, keys_in, values_in, valid_len, causal, stats_kept, grad_out):
    row_count = query_in.shape[0]
    block_rows = min(512, row_count)
    key_heads, value_heads = (split_heads(keys_in), split_heads(values_in))
    grad_keys = jnp.zeros(key_heads.shape, jnp.float32)
    grad_values = jnp.zeros(value_heads.shape, jnp.float32)
    grad_query = []
    for block_no, start_at in enumerate(range(0, row_count, block_rows)):
        piece_q = split_heads(query_in[start_at : start_at + block_rows])
        upstream = split_heads(grad_out[start_at : start_at + block_rows])
        probs_f = jnp.exp(
            block_scores(piece_q, key_heads, valid_len, causal, start_at) - stats_kept[block_no]
        )
        grad_probs = jnp.einsum(
            "qhd,khd->hqk", upstream, value_heads, preferred_element_type=jnp.float32
        )
        inner_sum = jnp.sum(probs_f * grad_probs, axis=-1, keepdims=True)
        grad_scores = (probs_f * (grad_probs - inner_sum)).astype(jnp.bfloat16)
        grad_query.append(
            (
                jnp.einsum(
                    "hqk,khd->qhd", grad_scores, key_heads, preferred_element_type=jnp.float32
                )
                * HEAD_DIM ** (-0.5)
            ).reshape(block_rows, -1)
        )
        grad_keys = grad_keys + jnp.einsum(
            "hqk,qhd->khd", grad_scores, piece_q, preferred_element_type=jnp.float32
        ) * HEAD_DIM ** (-0.5)
        grad_values = grad_values + jnp.einsum(
            "hqk,qhd->khd",
            probs_f.astype(jnp.bfloat16),
            upstream,
            preferred_element_type=jnp.float32,
        )
    key_count = keys_in.shape[0]
    return (
        jnp.concatenate(grad_query, 0),
        grad_keys.reshape(key_count, -1),
        grad_values.reshape(key_count, -1),
    )


def norm_backward(stream, gain_row, grad_normed):
    _, pull_back = jax.vjp(rms_norm, stream, gain_row)
    return pull_back(grad_normed)


def by_sequence(matrix):
    return jnp.split(matrix, MICRO, axis=0)


def attend_all(query_in, keys_in, values_in, valid_len, causal):
    outs, stats = ([], [])
    for seq_no, (piece_q, piece_k, piece_v) in enumerate(
        zip(by_sequence(query_in), by_sequence(keys_in), by_sequence(values_in))
    ):
        out, kept = attend_forward(piece_q, piece_k, piece_v, valid_len[seq_no], causal)
        outs.append(out)
        stats.append(kept)
    return (jnp.concatenate(outs, 0), stats)


def attend_all_backward(query_in, keys_in, values_in, valid_len, causal, stats, mixed_out, grad_out):
    parts = []
    for seq_no, pieces in enumerate(
        zip(
            by_sequence(query_in), by_sequence(keys_in), by_sequence(values_in),
            by_sequence(grad_out),
        )
    ):
        piece_q, piece_k, piece_v, upstream = pieces
        parts.append(
            attend_backward(
                piece_q, piece_k, piece_v, valid_len[seq_no], causal, stats[seq_no], upstream
            )
        )
    return tuple(
        jnp.concatenate([part[item] for part in parts], 0).astype(jnp.bfloat16)
        for item in range(3)
    )


def self_forward(stream, gain_row, weight, valid_len, causal):
    normed = rms_norm(stream, gain_row).astype(jnp.bfloat16)
    joint_qkv = linear(normed, weight[:, : 3 * D]).astype(jnp.bfloat16)
    mixed_out, stats_kept = attend_all(
        joint_qkv[:, :D], joint_qkv[:, D : 2 * D], joint_qkv[:, 2 * D :], valid_len, causal
    )
    return (
        stream + linear(mixed_out, weight[:, 3 * D :]),
        (stream, normed, joint_qkv, mixed_out, stats_kept),
    )


def self_backward(grad_stream, kept_block, gain_row, weight, valid_len, causal):
    stream, normed, joint_qkv, mixed_out, stats_kept = kept_block
    grad_low = grad_stream.astype(jnp.bfloat16)
    grad_out_w = outer_sum(mixed_out, grad_low)
    grad_mixed = linear_tr(grad_low, weight[:, 3 * D :]).astype(jnp.bfloat16)
    grad_q, grad_k, grad_v = attend_all_backward(
        joint_qkv[:, :D],
        joint_qkv[:, D : 2 * D],
        joint_qkv[:, 2 * D :],
        valid_len,
        causal,
        stats_kept,
        mixed_out,
        grad_mixed,
    )
    grad_joint = jnp.concatenate([grad_q, grad_k, grad_v], 1)
    grad_x, grad_gain = norm_backward(stream, gain_row, linear_tr(grad_joint, weight[:, : 3 * D]))
    return (
        grad_stream + grad_x,
        grad_gain,
        jnp.concatenate([outer_sum(normed, grad_joint), grad_out_w], 1).astype(jnp.bfloat16),
    )


def cross_forward(stream, gain_row, weight, memory, valid_len):
    normed = rms_norm(stream, gain_row).astype(jnp.bfloat16)
    query_in = linear(normed, weight[:, :D]).astype(jnp.bfloat16)
    pair_kv = linear(memory, weight[:, D : 3 * D]).astype(jnp.bfloat16)
    mixed_out, stats_kept = attend_all(query_in, pair_kv[:, :D], pair_kv[:, D:], valid_len, False)
    return (
        stream + linear(mixed_out, weight[:, 3 * D :]),
        (stream, normed, query_in, pair_kv, mixed_out, stats_kept),
    )


def cross_backward(grad_stream, kept_block, gain_row, weight, memory, valid_len):
    stream, normed, query_in, pair_kv, mixed_out, stats_kept = kept_block
    grad_low = grad_stream.astype(jnp.bfloat16)
    grad_out_w = outer_sum(mixed_out, grad_low)
    grad_mixed = linear_tr(grad_low, weight[:, 3 * D :]).astype(jnp.bfloat16)
    grad_query, grad_k, grad_v = attend_all_backward(
        query_in, pair_kv[:, :D], pair_kv[:, D:], valid_len, False, stats_kept, mixed_out, grad_mixed
    )
    grad_pair = jnp.concatenate([grad_k, grad_v], 1)
    grad_weight = jnp.concatenate(
        [outer_sum(normed, grad_query), outer_sum(memory, grad_pair), grad_out_w], 1
    ).astype(jnp.bfloat16)
    grad_x, grad_gain = norm_backward(stream, gain_row, linear_tr(grad_query, weight[:, :D]))
    return (
        grad_stream + grad_x,
        grad_gain,
        grad_weight,
        linear_tr(grad_pair, weight[:, D : 3 * D]),
    )


def gelu_tanh(hidden):
    return jax.nn.gelu(hidden, approximate=True)


def ffn_forward(stream, gain_row, w_in, w_out):
    normed = rms_norm(stream, gain_row).astype(jnp.bfloat16)
    hidden = linear(normed, w_in)
    active = gelu_tanh(hidden).astype(jnp.bfloat16)
    return (stream + linear_tr(active, w_out), (stream, normed, hidden, active))


def ffn_backward(grad_stream, kept_block, gain_row, w_in, w_out):
    stream, normed, hidden, active = kept_block
    grad_low = grad_stream.astype(jnp.bfloat16)
    grad_out_w = outer_sum(grad_low, active).astype(jnp.bfloat16)
    _, pull_back = jax.vjp(gelu_tanh, hidden)
    grad_hidden = pull_back(linear(grad_low, w_out))[0].astype(jnp.bfloat16)
    grad_x, grad_gain = norm_backward(stream, gain_row, linear_tr(grad_hidden, w_in))
    return (
        grad_stream + grad_x,
        grad_gain,
        outer_sum(normed, grad_hidden).astype(jnp.bfloat16),
        grad_out_w,
    )


def forward_all(weights, gain_set, source_rows, target_rows, source_len, target_len, place_rows):
    stream = source_rows
    enc_kept = []
    for layer_no in range(ENC):
        stream, kept_self = self_forward(
            stream, gain_set[2 * layer_no], weights[layer_no], source_len, False
        )
        stream, kept_ffn = ffn_forward(
            stream,
            gain_set[2 * layer_no + 1],
            weights[ENC + 2 * DEC + layer_no],
            weights[2 * ENC + 3 * DEC + layer_no],
        )
        enc_kept.append((kept_self, kept_ffn))
    memory = rms_norm(stream, gain_set[2 * ENC]).astype(jnp.bfloat16)
    decoded = target_rows
    dec_kept, exit_in, exit_rows = ([], [], [])
    for layer_no in range(DEC):
        base_at = 2 * ENC + 1 + 3 * layer_no
        decoded, kept_self = self_forward(
            decoded, gain_set[base_at], weights[ENC + layer_no], target_len, True
        )
        decoded, kept_cross = cross_forward(
            decoded, gain_set[base_at + 1], weights[ENC + DEC + layer_no], memory, source_len
        )
        decoded, kept_ffn = ffn_forward(
            decoded,
            gain_set[base_at + 2],
            weights[2 * ENC + 2 * DEC + layer_no],
            weights[3 * ENC + 3 * DEC + layer_no],
        )
        dec_kept.append((kept_self, kept_cross, kept_ffn))
        picked_rows = decoded[place_rows]
        exit_in.append(picked_rows)
        exit_rows.append(
            rms_norm(picked_rows, gain_set[2 * ENC + 1 + 3 * DEC + layer_no]).astype(jnp.bfloat16)
        )
    kept = (source_len, target_len, place_rows, enc_kept, stream, memory, dec_kept, exit_in)
    return (kept, jnp.concatenate(exit_rows, 0))


def backward_all(weights, gain_set, kept, exit_grads, matrix_store, gain_store):
    source_len, target_len, place_rows, enc_kept, stream, memory, dec_kept, exit_in = kept
    exit_each = jnp.split(exit_grads, DEC, axis=0)
    grad_decoded = jnp.zeros(dec_kept[0][0][0].shape, jnp.float32)
    grad_memory = jnp.zeros(memory.shape, jnp.float32)
    for layer_no in reversed(range(DEC)):
        base_at = 2 * ENC + 1 + 3 * layer_no
        exit_at = 2 * ENC + 1 + 3 * DEC + layer_no
        grad_rows, gain_store[exit_at] = norm_backward(
            exit_in[layer_no], gain_set[exit_at], exit_each[layer_no]
        )
        grad_decoded = grad_decoded.at[place_rows].add(grad_rows)
        kept_self, kept_cross, kept_ffn = dec_kept[layer_no]
        in_at, out_at = (2 * ENC + 2 * DEC + layer_no, 3 * ENC + 3 * DEC + layer_no)
        grad_decoded, gain_store[base_at + 2], matrix_store[in_at], matrix_store[out_at] = (
            ffn_backward(
                grad_decoded, kept_ffn, gain_set[base_at + 2], weights[in_at], weights[out_at]
            )
        )
        cross_at = ENC + DEC + layer_no
        grad_decoded, gain_store[base_at + 1], matrix_store[cross_at], grad_mem = cross_backward(
            grad_decoded, kept_cross, gain_set[base_at + 1], weights[cross_at], memory, source_len
        )
        grad_memory = grad_memory + grad_mem
        grad_decoded, gain_store[base_at], matrix_store[ENC + layer_no] = self_backward(
            grad_decoded, kept_self, gain_set[base_at], weights[ENC + layer_no], target_len, True
        )
    grad_stream, gain_store[2 * ENC] = norm_backward(stream, gain_set[2 * ENC], grad_memory)
    for layer_no in reversed(range(ENC)):
        kept_self, kept_ffn = enc_kept[layer_no]
        in_at, out_at = (ENC + 2 * DEC + layer_no, 2 * ENC + 3 * DEC + layer_no)
        grad_stream, gain_store[2 * layer_no + 1], matrix_store[in_at], matrix_store[out_at] = (
            ffn_backward(
                grad_stream, kept_ffn, gain_set[2 * layer_no + 1], weights[in_at], weights[out_at]
            )
        )
        grad_stream, gain_store[2 * layer_no], matrix_store[layer_no] = self_backward(
            grad_stream, kept_self, gain_set[2 * layer_no], weights[layer_no], source_len, False
        )
    return (grad_stream, grad_decoded)


def fold_blocks(tiles):
    return jnp.concatenate([tiles[:, : PB // 2], tiles[:, PB // 2 :]], axis=2)


def unfold_blocks(folded):
    return jnp.concatenate([folded[:, :, :PB], folded[:, :, PB:]], axis=1)


def swap_halves(value):
    return jnp.concatenate([value[:, PB:], value[:, :PB]], axis=1)


def lay_matrices(folded_all, slot_of):
    half = PB // 2
    row_blocks, pairs = (D // PB, FF // (2 * PB))

    def kernel(slot_ref, folded_ref, out_ref):
        first = pl.program_id(0) * row_blocks * 2 * pairs + pl.program_id(1) * 2 * pairs
        left_half = lax.broadcasted_iota(jnp.int32, (half, 2 * PB), 1) < PB
        for pair_no in range(pairs):
            even = folded_ref[slot_ref[first + 2 * pair_no]].astype(jnp.float32)
            odd = folded_ref[slot_ref[first + 2 * pair_no + 1]].astype(jnp.float32)
            even_turned = pltpu.roll(even, PB, 1)
            odd_turned = pltpu.roll(odd, PB, 1)
            columns = slice(2 * PB * pair_no, 2 * PB * (pair_no + 1))
            out_ref[0, :half, columns] = jnp.where(left_half, even, odd_turned).astype(jnp.bfloat16)
            out_ref[0, half:, columns] = jnp.where(left_half, even_turned, odd).astype(jnp.bfloat16)

    return pl.pallas_call(
        kernel,
        out_shape=jax.ShapeDtypeStruct((MATS, D, FF), jnp.bfloat16),
        grid_spec=pltpu.PrefetchScalarGridSpec(
            num_scalar_prefetch=1,
            grid=(MATS, row_blocks),
            in_specs=[pl.BlockSpec(memory_space=pltpu.VMEM)],
            out_specs=pl.BlockSpec((1, PB, FF), lambda mat_no, row_no, slots: (mat_no, row_no, 0)),
        ),
        compiler_params=pltpu.CompilerParams(vmem_limit_bytes=40 * 2**20),
    )(slot_of, folded_all)


def fold_gradients(matrices, slot_of):
    half = PB // 2
    row_blocks, pairs = (D // PB, FF // (2 * PB))
    count = MATS * row_blocks * 2 * pairs

    def kernel(slot_ref, *refs):
        sources, out_ref, held, arrived = (refs[:MATS], refs[MATS], refs[MATS + 1], refs[MATS + 2])
        left_half = lax.broadcasted_iota(jnp.int32, (half, 2 * PB), 1) < PB

        def fetch(mat_no):
            return pltpu.make_async_copy(
                sources[mat_no], held.at[mat_no % 2], arrived.at[mat_no % 2]
            )

        fetch(0).start()
        for mat_no in range(MATS):
            if mat_no + 1 < MATS:
                fetch(mat_no + 1).start()
            fetch(mat_no).wait()

            def one_row(row_no, carry, mat_no=mat_no):
                first = (mat_no * row_blocks + row_no) * 2 * pairs
                row_at = pl.multiple_of(row_no * PB, PB)
                for pair_no in range(pairs):
                    columns = slice(2 * PB * pair_no, 2 * PB * (pair_no + 1))
                    upper = held[mat_no % 2, pl.ds(row_at, half), columns].astype(jnp.float32)
                    lower = held[mat_no % 2, pl.ds(row_at + half, half), columns].astype(jnp.float32)
                    even = jnp.where(left_half, upper, pltpu.roll(lower, PB, 1))
                    odd = jnp.where(left_half, pltpu.roll(upper, PB, 1), lower)
                    out_ref[slot_ref[first + 2 * pair_no]] = even.astype(jnp.bfloat16)
                    out_ref[slot_ref[first + 2 * pair_no + 1]] = odd.astype(jnp.bfloat16)
                return carry

            lax.fori_loop(0, row_blocks, one_row, 0)

    return pl.pallas_call(
        kernel,
        out_shape=jax.ShapeDtypeStruct((count, half, 2 * PB), jnp.bfloat16),
        grid_spec=pltpu.PrefetchScalarGridSpec(
            num_scalar_prefetch=1,
            grid=(1,),
            in_specs=[pl.BlockSpec(memory_space=pl.ANY)] * MATS,
            out_specs=pl.BlockSpec(memory_space=pltpu.VMEM),
            scratch_shapes=[
                pltpu.VMEM((2, D, FF), jnp.bfloat16),
                pltpu.SemaphoreType.DMA((2,)),
            ],
        ),
        compiler_params=pltpu.CompilerParams(vmem_limit_bytes=40 * 2**20),
    )(slot_of, *matrices)


def take_rows(source, index_at, kind):
    count, width, block = (index_at.shape[0], source.shape[1], 128)
    whole = -(-count // block) * block
    index_at = jnp.pad(index_at, (0, whole - count))

    def kernel(index_ref, source_ref, out_ref, held_ref):
        first = pl.program_id(0) * block

        def copy_eight(group, carry):
            base = pl.multiple_of(group * 8, 8)
            for row_no in range(8):
                held_ref[pl.ds(base + row_no, 1), :] = source_ref[
                    pl.ds(index_ref[first + base + row_no], 1), :
                ]
            return carry

        lax.fori_loop(0, block // 8, copy_eight, 0)
        out_ref[...] = held_ref[...].astype(kind)

    taken = pl.pallas_call(
        kernel,
        out_shape=jax.ShapeDtypeStruct((whole, width), kind),
        grid_spec=pltpu.PrefetchScalarGridSpec(
            num_scalar_prefetch=1,
            grid=(whole // block,),
            in_specs=[pl.BlockSpec(memory_space=pltpu.VMEM)],
            out_specs=pl.BlockSpec((block, width), lambda step, index: (step, 0)),
            scratch_shapes=[pltpu.VMEM((block, width), jnp.float32)],
        ),
        compiler_params=pltpu.CompilerParams(vmem_limit_bytes=40 * 2**20),
    )(index_at, source)
    return taken[:count]


def add_rows(rows, index_at, total):
    count, width, block = (rows.shape[0], rows.shape[1], 512)
    whole = -(-count // block) * block
    index_at = jnp.pad(index_at, (0, whole - count), constant_values=-1)[None, :]
    rows = jnp.pad(rows, ((0, whole - count), (0, 0)))
    height = total.shape[0]

    def kernel(index_ref, rows_ref, total_ref, out_ref):
        @pl.when(pl.program_id(0) == 0)
        def _():
            out_ref[...] = total_ref[...]

        hits = lax.broadcasted_iota(jnp.int32, (height, block), 0) == index_ref[...]
        out_ref[...] += jnp.dot(
            hits.astype(jnp.float32).astype(jnp.bfloat16),
            rows_ref[...],
            preferred_element_type=jnp.float32,
        )

    return pl.pallas_call(
        kernel,
        out_shape=jax.ShapeDtypeStruct(total.shape, jnp.float32),
        grid=(whole // block,),
        in_specs=[
            pl.BlockSpec((1, block), lambda step: (0, step)),
            pl.BlockSpec((block, width), lambda step: (step, 0)),
            pl.BlockSpec((height, width), lambda step: (0, 0)),
        ],
        out_specs=pl.BlockSpec((height, width), lambda step: (0, 0)),
        compiler_params=pltpu.CompilerParams(vmem_limit_bytes=40 * 2**20),
    )(index_at, rows, total)


def count_before(mask):
    size, width = (mask.shape[-1], 128)
    parts = mask.reshape(*mask.shape[:-1], size // width, width).astype(jnp.bfloat16)
    earlier = (jnp.arange(width)[:, None] < jnp.arange(width)[None, :]).astype(jnp.bfloat16)
    inside = jnp.einsum("...pw,wk->...pk", parts, earlier, preferred_element_type=jnp.float32)
    totals = jnp.sum(parts.astype(jnp.float32), axis=-1)
    ahead = jnp.cumsum(totals, axis=-1) - totals
    return (inside + ahead[..., None]).reshape(mask.shape).astype(jnp.int32)


def room(count, peers):
    mean = count / peers
    return min(count, -(-int(mean + 5.0 * math.sqrt(mean)) // 16) * 16)


def listed(mask, rank, values, size, empty):
    spot = jnp.arange(size)[:, None]
    chosen = mask[..., None, :] & (rank[..., None, :] == spot)
    return jnp.sum(jnp.where(chosen, values[..., None, :] - empty, 0), axis=-1) + empty


def rounds_needed(owner_all, peers, size):
    held = jnp.sum((owner_all[:, None, :] == jnp.arange(peers)[:, None]).astype(jnp.int32), axis=2)
    return (jnp.max(held) + size - 1) // size


def fetch_rows(table_part, tokens_all, peers_here, peer_me):
    peers, rows_each = (peers_here.shape[0], table_part.shape[0])
    count = tokens_all.shape[1]
    size = room(count, peers)
    asked = peers_here // rows_each == peer_me
    asked_rank = count_before(asked)
    own_tokens = lax.dynamic_index_in_dim(peers_here, peer_me, 0, keepdims=False)
    own_owner = own_tokens // rows_each
    own_mask = own_owner[None, :] == jnp.arange(peers)[:, None]
    own_rank = jnp.sum(jnp.where(own_mask, count_before(own_mask), 0), axis=0)

    def one_round(round_no):
        wanted = listed(
            asked, asked_rank - round_no * size, peers_here - peer_me * rows_each, size, 0
        )
        rows = take_rows(table_part, wanted.reshape(-1), jnp.bfloat16)
        arrived = lax.all_to_all(rows, "vocab", 0, 0, tiled=True)
        rank_now = own_rank - round_no * size
        now = (rank_now >= 0) & (rank_now < size)
        found = take_rows(
            arrived.astype(jnp.float32), jnp.where(now, own_owner * size + rank_now, 0), jnp.float32
        )
        return (now, found)

    def again(round_no, rows):
        now, found = one_round(round_no)
        return jnp.where(now[:, None], found, rows)

    rounds = rounds_needed(tokens_all // rows_each, peers, size)
    return lax.fori_loop(1, rounds, again, one_round(0)[1])


def return_rows(grad_rows, tokens_all, rows_each, dp_size, total):
    peers, count = tokens_all.shape
    along = peers // dp_size
    quarter = rows_each // dp_size
    me = lax.axis_index("dp") * along + lax.axis_index("vocab")
    size = room(count, peers)
    owner_all = (tokens_all % rows_each) // quarter * along + tokens_all // rows_each
    arriving = owner_all == me
    arriving_rank = count_before(arriving)
    own_owner = lax.dynamic_index_in_dim(owner_all, me, 0, keepdims=False)
    leaving = own_owner[None, :] == jnp.arange(peers)[:, None]
    leaving_rank = count_before(leaving)
    place = jnp.broadcast_to(jnp.arange(count)[None, :], leaving.shape)

    def one_round(round_no, so_far):
        chosen = listed(leaving, leaving_rank - round_no * size, place, size, 0)
        rows = take_rows(grad_rows, chosen.reshape(-1), jnp.bfloat16)
        arrived = lax.all_to_all(rows, ("dp", "vocab"), 0, 0, tiled=True)
        where = listed(
            arriving, arriving_rank - round_no * size, tokens_all % quarter, size, -1
        )
        return add_rows(arrived, where.reshape(-1), so_far)

    rounds = rounds_needed(owner_all, peers, size)
    return lax.fori_loop(1, rounds, one_round, one_round(0, total))


def turn_in(left_basis, tiles, right_basis):
    half = jnp.einsum("tki,tkl->til", left_basis, tiles, precision=HIGHEST)
    return jnp.einsum("til,tlj->tij", half, right_basis, precision=HIGHEST)


def turn_out(left_basis, tiles, right_basis):
    half = jnp.einsum("tik,tkl->til", left_basis, tiles, precision=HIGHEST)
    return jnp.einsum("til,tjl->tij", half, right_basis, precision=HIGHEST)


def orthonormal(columns):
    lanes, group = (128, 4)

    def kernel(in_ref, out_ref):
        out_ref[...] = in_ref[...]

        def one_column(column_no, carry):
            pivot = out_ref[column_no]
            pivot = pivot / jnp.sqrt(jnp.sum(pivot * pivot, axis=0, keepdims=True))
            out_ref[column_no] = pivot

            def one_group(group_no, inner):
                first = group_no * group
                held = [out_ref[first + item] for item in range(group)]
                for item in range(group):
                    share = jnp.sum(pivot * held[item], axis=0, keepdims=True)
                    share = jnp.where(first + item > column_no, share, 0.0)
                    held[item] = held[item] - share * pivot
                for item in range(group):
                    out_ref[first + item] = held[item]
                return inner

            return lax.fori_loop((column_no + 1) // group, PB // group, one_group, carry)

        lax.fori_loop(0, PB, one_column, 0)

    spec = pl.BlockSpec((PB, PB, lanes), lambda step: (0, 0, step))
    return pl.pallas_call(
        kernel,
        out_shape=jax.ShapeDtypeStruct(columns.shape, jnp.float32),
        grid=(columns.shape[2] // lanes,),
        in_specs=[spec],
        out_specs=spec,
        compiler_params=pltpu.CompilerParams(vmem_limit_bytes=40 * 2**20),
    )(columns)


def renew_bases(left_stat, right_stat, left_basis, right_basis):
    moved = jnp.concatenate(
        [
            jnp.einsum("tij,tjk->tik", left_stat, left_basis, precision=HIGHEST),
            jnp.einsum("tij,tjk->tik", right_stat, right_basis, precision=HIGHEST),
        ],
        0,
    )
    count = moved.shape[0]
    whole = -(-count // 128) * 128
    columns = jnp.pad(jnp.transpose(moved, (2, 1, 0)), ((0, 0), (0, 0), (0, whole - count)))
    renewed = jnp.transpose(orthonormal(columns)[:, :, :count], (2, 1, 0))
    return (renewed[: count // 2], renewed[count // 2 :])


def soap_update(
    master, grad_tiles, first_mom, second_mom, left_stat, right_stat, left_basis, right_basis
):
    first_new = BETA_FIRST * first_mom + (1 - BETA_FIRST) * grad_tiles
    grad_turned = turn_in(left_basis, grad_tiles, right_basis)
    first_turned = turn_in(left_basis, first_new, right_basis)
    second_new = BETA_SECOND * second_mom + (1 - BETA_SECOND) * grad_turned * grad_turned
    direction = (
        first_turned
        / (1 - BETA_FIRST**STEP)
        / (jnp.sqrt(second_new / (1 - BETA_SECOND**STEP)) + ADAM_EPS)
    )
    master_new = master - RATE_MATRIX * (
        turn_out(left_basis, direction, right_basis) + DECAY * master
    )
    left_new = BETA_STAT * left_stat + (1 - BETA_STAT) * jnp.einsum(
        "tik,tjk->tij", grad_tiles, grad_tiles, precision=HIGHEST
    )
    right_new = BETA_STAT * right_stat + (1 - BETA_STAT) * jnp.einsum(
        "tki,tkj->tij", grad_tiles, grad_tiles, precision=HIGHEST
    )
    return (
        master_new,
        first_new,
        second_new,
        left_new,
        right_new,
        *renew_bases(left_new, right_new, left_basis, right_basis),
    )


def adamw_update(master, grad_now, first_mom, second_mom, rate, decay_by):
    first_new = BETA_FIRST * first_mom + (1 - BETA_FIRST) * grad_now
    second_new = BETA_SECOND * second_mom + (1 - BETA_SECOND) * grad_now * grad_now
    direction = (
        first_new
        / (1 - BETA_FIRST**STEP)
        / (jnp.sqrt(second_new / (1 - BETA_SECOND**STEP)) + ADAM_EPS)
    )
    return (master - rate * (direction + decay_by * master), first_new, second_new)


def per_device(
    master_tiles,
    mom1_tiles,
    mom2_tiles,
    stat_left,
    stat_right,
    basis_left,
    basis_right,
    table_master,
    table_mom1,
    table_mom2,
    gains,
    gain_mom1,
    gain_mom2,
    source_ids,
    target_ids,
    source_len,
    target_len,
    loss_place,
    exit_layer,
    slot_list,
):
    dp_size, along = (lax.axis_size("dp"), lax.axis_size("vocab"))
    dp_me, peer_me = (lax.axis_index("dp"), lax.axis_index("vocab"))
    devices = dp_size * along
    rows_each = table_master.shape[0]
    quarter = rows_each // dp_size
    source_len, target_len = (source_len[:, 0], target_len[:, 0])

    shifted = jnp.pad(target_ids[:, 0, :-1], ((0, 0), (1, 0)))
    tokens = jnp.concatenate([source_ids.reshape(-1), shifted.reshape(-1)])
    places = loss_place[:, 0]
    counted = places < target_len[:, None]
    reach = [
        jnp.sum((counted & (exit_layer[:, 0] >= layer_no)).astype(jnp.int32))
        for layer_no in range(DEC)
    ]
    labels = jnp.take_along_axis(target_ids[:, 0], places, axis=1).reshape(-1)
    row_count = MICRO * LOSS_POS
    own_facts = jnp.concatenate(
        [tokens, labels, counted.reshape(-1).astype(jnp.int32), jnp.stack(reach)]
    )
    fact_count = own_facts.shape[0]
    own_facts = jnp.pad(own_facts, (0, -fact_count % 128))
    facts = lax.all_gather(own_facts, ("dp", "vocab"), axis=0, tiled=False)
    tokens_all = facts[:, : tokens.shape[0]]
    after = facts[:, tokens.shape[0] :]
    labels_all = after[:, :row_count]
    counted_all = after[:, row_count : 2 * row_count].astype(jnp.float32)
    reach_all = jnp.sum(after[:, 2 * row_count : 2 * row_count + DEC].astype(jnp.float32), axis=0)
    count_all = jnp.sum(counted_all)
    fraction = reach_all / jnp.sum(reach_all)

    every_tile = lax.all_gather(
        fold_blocks(master_tiles).astype(jnp.bfloat16), ("dp", "vocab"), axis=0, tiled=True
    )
    slot_at = jnp.arange(slot_list.shape[0])
    slot_of = jnp.sum(
        jnp.where(slot_list[None, :] == slot_at[:, None], slot_at[None, :], 0), axis=1
    )
    peers_here = lax.dynamic_slice_in_dim(tokens_all, dp_me * along, along, 0)
    embedded = fetch_rows(table_master, tokens_all, peers_here, peer_me) * math.sqrt(D)
    src_count, tgt_count = (source_ids.shape[2], target_ids.shape[2])
    wave_set = waves(src_count, D)
    source_rows = embedded[: MICRO * src_count] + jnp.tile(wave_set, (MICRO, 1))
    target_rows = embedded[MICRO * src_count :] + jnp.tile(wave_set[:tgt_count], (MICRO, 1))
    weights = lay_matrices(every_tile, slot_of)

    place_rows = (places + jnp.arange(MICRO)[:, None] * tgt_count).reshape(-1)
    kept, exit_rows = forward_all(
        weights, gains, source_rows, target_rows, source_len, target_len, place_rows
    )

    table_low_part = table_master.astype(jnp.bfloat16)
    exit_count = DEC * row_count
    exit_all = lax.all_gather(exit_rows, ("dp", "vocab"), axis=0, tiled=True)
    label_rows = jnp.tile(labels_all, (1, DEC)).reshape(-1)
    weight_rows = (
        jnp.repeat(fraction, row_count)[None, :] * jnp.tile(counted_all, (1, DEC))
    ).reshape(-1)
    group_rows = along * exit_count
    group_at = dp_me * group_rows
    exit_here = lax.dynamic_slice_in_dim(exit_all, group_at, group_rows, 0)
    label_here = lax.dynamic_slice_in_dim(label_rows, group_at, group_rows, 0)
    weight_here = lax.dynamic_slice_in_dim(weight_rows, group_at, group_rows, 0)
    logits = linear_tr(exit_here, table_low_part)
    hit_here = label_here[:, None] - peer_me * rows_each == jnp.arange(rows_each)[None, :]
    summit = jnp.max(logits, axis=1)
    spread_part = jnp.sum(jnp.exp(logits - summit[:, None]), axis=1)
    picked_part = jnp.sum(jnp.where(hit_here, logits, 0.0), axis=1)
    stats = lax.all_gather(
        jnp.stack([summit, spread_part, picked_part]), ("dp", "vocab"), axis=0, tiled=False
    ).reshape(dp_size, along, 3, group_rows)
    summit_all = jnp.max(stats[:, :, 0], axis=1)
    total_all = jnp.sum(stats[:, :, 1] * jnp.exp(stats[:, :, 0] - summit_all[:, None]), axis=1)
    spread_all = summit_all + jnp.log(total_all)
    picked_all = jnp.sum(stats[:, :, 2], axis=1)
    loss_sum = jnp.sum(weight_rows * (spread_all - picked_all).reshape(-1))
    spread_here = lax.dynamic_index_in_dim(spread_all, dp_me, 0, keepdims=False)

    def logit_grads(logit_set, spread, weight_set, hits):
        return (
            (weight_set / count_all)[:, None]
            * (jnp.exp(logit_set - spread[:, None]) - hits.astype(jnp.float32))
        ).astype(jnp.bfloat16)

    grads_here = logit_grads(logits, spread_here, weight_here, hit_here)
    grad_parts = linear(grads_here, table_low_part).astype(jnp.bfloat16)
    grad_parts = lax.all_to_all(grad_parts, "vocab", 0, 0, tiled=True)
    exit_grads = jnp.sum(
        grad_parts.reshape(along, exit_count, D).astype(jnp.float32), axis=0
    )

    matrix_store = [None] * MATS
    gain_store = [None] * GAINS
    grad_source, grad_target = backward_all(
        weights, gains, kept, exit_grads, matrix_store, gain_store
    )

    first_row = peer_me * rows_each + dp_me * quarter
    table_quarter = lax.dynamic_slice_in_dim(table_low_part, dp_me * quarter, quarter, 0)
    hit_quarter = label_rows[:, None] - first_row == jnp.arange(quarter)[None, :]
    grads_quarter = logit_grads(
        linear_tr(exit_all, table_quarter), spread_all.reshape(-1), weight_rows, hit_quarter
    )
    grad_quarter = outer_sum(grads_quarter, exit_all)
    grad_rows = jnp.concatenate([grad_source, grad_target], 0) * math.sqrt(D)
    grad_quarter = return_rows(grad_rows, tokens_all, rows_each, dp_size, grad_quarter)

    owned_grad = unfold_blocks(
        lax.psum_scatter(
            lax.psum_scatter(
                fold_gradients(matrix_store, slot_of), "dp", scatter_dimension=0, tiled=True
            ),
            "vocab",
            scatter_dimension=0,
            tiled=True,
        ).astype(jnp.float32)
    )
    squares = jnp.sum(owned_grad * owned_grad) + jnp.sum(grad_quarter * grad_quarter)
    gain_total, square_total = lax.psum((jnp.stack(gain_store), squares), ("dp", "vocab"))
    grad_norm = jnp.sqrt(square_total + jnp.sum(gain_total * gain_total))
    factor = jnp.minimum(1.0, CLIP_AT / grad_norm)
    table_grad = lax.all_gather(
        grad_quarter.astype(jnp.bfloat16), "dp", axis=0, tiled=True
    ).astype(jnp.float32)
    master_new, mom1_new, mom2_new, left_new, right_new, bleft_new, bright_new = soap_update(
        master_tiles,
        owned_grad * factor,
        mom1_tiles,
        mom2_tiles,
        stat_left,
        stat_right,
        basis_left,
        basis_right,
    )
    table_new, table_m, table_v = adamw_update(
        table_master, table_grad * factor, table_mom1, table_mom2, RATE_MATRIX, DECAY
    )
    gains_new, gains_m, gains_v = adamw_update(
        gains, gain_total * factor, gain_mom1, gain_mom2, RATE_VECTOR, 0.0
    )
    return (
        loss_sum,
        count_all,
        grad_norm,
        master_new,
        master_new.astype(jnp.bfloat16),
        mom1_new,
        mom2_new,
        left_new,
        right_new,
        bleft_new,
        bright_new,
        table_new,
        table_new.astype(jnp.bfloat16),
        table_m,
        table_v,
        gains_new,
        gains_m,
        gains_v,
    )


def solution(mesh):
    placed = (
        P(("dp", "vocab"), None, None),
        P(("dp", "vocab"), None, None),
        P(("dp", "vocab"), None, None),
        P(("dp", "vocab"), None, None),
        P(("dp", "vocab"), None, None),
        P(("dp", "vocab"), None, None),
        P(("dp", "vocab"), None, None),
        P("vocab", None),
        P("vocab", None),
        P("vocab", None),
        P(),
        P(),
        P(),
        P(None, ("dp", "vocab"), None),
        P(None, ("dp", "vocab"), None),
        P(None, ("dp", "vocab")),
        P(None, ("dp", "vocab")),
        P(None, ("dp", "vocab"), None),
        P(None, ("dp", "vocab"), None),
        P(),
    )
    return jax.shard_map(
        per_device,
        mesh=mesh,
        in_specs=placed,
        out_specs=(
            P(),
            P(),
            P(),
            P(("dp", "vocab"), None, None),
            P(("dp", "vocab"), None, None),
            P(("dp", "vocab"), None, None),
            P(("dp", "vocab"), None, None),
            P(("dp", "vocab"), None, None),
            P(("dp", "vocab"), None, None),
            P(("dp", "vocab"), None, None),
            P(("dp", "vocab"), None, None),
            P("vocab", None),
            P("vocab", None),
            P("vocab", None),
            P("vocab", None),
            P(),
            P(),
            P(),
        ),
        check_vma=False,
    )
```

```python
import math

import jax
import jax.numpy as jnp
from jax import lax
from jax.experimental import pallas as pl
from jax.experimental.pallas import tpu as pltpu
from jax.sharding import PartitionSpec as P

D = 512
HEADS = 8
HEAD_DIM = 64
FF = 2048
ENC = 1
DEC = 2
MICRO = 2
LOSS_POS = 16
PB = 64
STEP = 10
MATS = 11
GAINS = 11


HIGH = lax.Precision.HIGH
NORM_EPS = 1e-06
CLIP_AT = 0.02
RATE_MATRIX = 0.1
RATE_VECTOR = 0.8
BETA_FIRST = 0.9
BETA_SECOND = 0.95
BETA_STAT = 0.95
ADAM_EPS = 1e-08
DECAY = 0.01


def rms_norm(stream, gain_row):
    return (
        stream * lax.rsqrt(jnp.mean(stream * stream, axis=-1, keepdims=True) + NORM_EPS) * gain_row
    )


def waves(length, columns):
    place_at = jnp.arange(length).astype(jnp.float32)[:, None]
    rate_at = jnp.exp(
        jnp.arange(columns // 2).astype(jnp.float32) * (-2.0 * math.log(10000.0) / columns)
    )
    angle = place_at * rate_at[None, :]
    return jnp.concatenate([jnp.sin(angle), jnp.cos(angle)], axis=1)


def linear(left_op, right_op):
    return jnp.dot(left_op, right_op, preferred_element_type=jnp.float32)


def linear_tr(left_op, right_op):
    return lax.dot_general(
        left_op, right_op, (((1,), (1,)), ((), ())), preferred_element_type=jnp.float32
    )


def outer_sum(left_op, right_op):
    return lax.dot_general(
        left_op, right_op, (((0,), (0,)), ((), ())), preferred_element_type=jnp.float32
    )


def split_heads(matrix):
    return matrix.reshape(matrix.shape[0], HEADS, HEAD_DIM)


NEVER=-1000000000.0
PAIR=2*HEAD_DIM
def kept_scores(query, keys, valid_len, causal, start_at):
    scores = lax.dot_general(query, keys, (((1,), (1,)), ((), ())), preferred_element_type=jnp.float32)
    key_at = lax.broadcasted_iota(jnp.int32, scores.shape if causal else (1, scores.shape[1]), 1)
    allowed = key_at < valid_len
    if causal:
        allowed = allowed & (key_at <= start_at + lax.broadcasted_iota(jnp.int32, scores.shape, 0))
    return jnp.where(allowed, scores, NEVER)

def head_masks(value):
    first = lax.broadcasted_iota(jnp.int32, value.shape, 1) < HEAD_DIM
    zero = jnp.zeros_like(value)
    return (jnp.where(first, value, zero), jnp.where(first, zero, value))

def attend_forward(query_in, query_at, keys_in, key_at, value_at, valid_len, causal):
    rows, keys = (query_in.shape[0] // MICRO, keys_in.shape[0] // MICRO)
    block = min(256, rows)
    steps = rows // block
    scale = HEAD_DIM ** (-0.5)

    def kernel(len_ref, query_ref, key_ref, value_ref, out_ref, stat_ref):
        start_at = pl.program_id(2) * block
        length = len_ref[pl.program_id(0)]
        queries = head_masks((query_ref[...].astype(jnp.float32) * scale).astype(jnp.bfloat16))
        values = head_masks(value_ref[...])
        total = jnp.zeros((block, PAIR), jnp.float32)
        stats = []
        for head in range(2):
            scores = kept_scores(queries[head], key_ref[...], length, causal, start_at)
            summit = jnp.max(scores, axis=1, keepdims=True)
            expo = jnp.exp(scores - summit)
            sums = jnp.sum(expo, axis=1, keepdims=True)
            probs = (expo * (1.0 / sums)).astype(jnp.bfloat16)
            total += jnp.dot(probs, values[head], preferred_element_type=jnp.float32)
            stats.append(summit + jnp.log(sums))
        out_ref[...] = total.astype(jnp.bfloat16)
        first = lax.broadcasted_iota(jnp.int32, (block, PAIR), 1) < HEAD_DIM
        stat_ref[...] = jnp.where(first, stats[0], stats[1])

    out_spec = pl.BlockSpec((block, PAIR), lambda seq, pair, step, lens: (seq * steps + step, pair))
    return pl.pallas_call(
        kernel,
        out_shape=(
            jax.ShapeDtypeStruct((MICRO * rows, D), jnp.bfloat16),
            jax.ShapeDtypeStruct((MICRO * rows, D), jnp.float32),
        ),
        grid_spec=pltpu.PrefetchScalarGridSpec(
            num_scalar_prefetch=1,
            grid=(MICRO, D // PAIR, steps),
            in_specs=[
                pl.BlockSpec((block, PAIR), lambda seq, pair, step, lens: (seq * steps + step, query_at + pair)),
                pl.BlockSpec((keys, PAIR), lambda seq, pair, step, lens: (seq, key_at + pair)),
                pl.BlockSpec((keys, PAIR), lambda seq, pair, step, lens: (seq, value_at + pair)),
            ],
            out_specs=(out_spec, out_spec),
        ),
        compiler_params=pltpu.CompilerParams(vmem_limit_bytes=40 * 2**20),
        cost_estimate=pl.CostEstimate(flops=4*MICRO*rows*keys*D, bytes_accessed=MICRO*(rows+keys)*D*8, transcendentals=MICRO*HEADS*rows*keys),
    )(valid_len, query_in, keys_in, keys_in)

def attend_backward(query_in, query_at, keys_in, key_at, value_at, valid_len, causal, stats, grad_out, first=0, seqs=MICRO, begun=()):
    rows, keys = (query_in.shape[0] // MICRO, keys_in.shape[0] // MICRO)
    block = min(512, rows)
    steps = rows // block
    scale = HEAD_DIM ** (-0.5)

    def kernel(len_ref, query_ref, key_ref, value_ref, stat_ref, up_ref, *refs):
        dq_ref, dk_ref, dv_ref, key_sum, value_sum = refs[len(begun) :]
        step = pl.program_id(2)
        start_at = step * block
        length = len_ref[first + pl.program_id(0)]
        queries = head_masks((query_ref[...].astype(jnp.float32) * scale).astype(jnp.bfloat16))
        upstream = head_masks(up_ref[...])
        keys_each = head_masks(key_ref[...])
        grad_query = jnp.zeros((block, PAIR), jnp.float32)
        grad_key = jnp.zeros((keys, PAIR), jnp.float32)
        grad_value = jnp.zeros((keys, PAIR), jnp.float32)
        over_rows = (((0,), (0,)), ((), ()))
        for head in range(2):
            scores = kept_scores(queries[head], key_ref[...], length, causal, start_at)
            probs = jnp.exp(scores - stat_ref[:, head * HEAD_DIM : head * HEAD_DIM + 1])
            grad_probs = lax.dot_general(upstream[head], value_ref[...], (((1,), (1,)), ((), ())), preferred_element_type=jnp.float32)
            inner = jnp.sum(probs * grad_probs, axis=1, keepdims=True)
            grad_scores = (probs * (grad_probs - inner)).astype(jnp.bfloat16)
            grad_query += jnp.dot(grad_scores, keys_each[head], preferred_element_type=jnp.float32)
            grad_key += lax.dot_general(grad_scores, queries[head], over_rows, preferred_element_type=jnp.float32)
            grad_value += lax.dot_general(probs.astype(jnp.bfloat16), upstream[head], over_rows, preferred_element_type=jnp.float32)
        dq_ref[...] = (grad_query * scale).astype(jnp.bfloat16)
        if steps == 1:
            dk_ref[...] = grad_key.astype(jnp.bfloat16)
            dv_ref[...] = grad_value.astype(jnp.bfloat16)
        else:
            @pl.when(step == 0)
            def _():
                key_sum[...] = grad_key
                value_sum[...] = grad_value

            @pl.when(step > 0)
            def _():
                key_sum[...] += grad_key
                value_sum[...] += grad_value

            @pl.when(step == steps - 1)
            def _():
                dk_ref[...] = key_sum[...].astype(jnp.bfloat16)
                dv_ref[...] = value_sum[...].astype(jnp.bfloat16)

    def row_spec(at, begin):
        return pl.BlockSpec(
            (block, PAIR),
            lambda seq, pair, step, lens: ((begin + seq) * steps + step, at + pair),
        )

    def key_spec(at, begin):
        return pl.BlockSpec((keys, PAIR), lambda seq, pair, step, lens: (begin + seq, at + pair))

    return pl.pallas_call(
        kernel,
        out_shape=(
            jax.ShapeDtypeStruct((MICRO * rows, D), jnp.bfloat16),
            jax.ShapeDtypeStruct((MICRO * keys, D), jnp.bfloat16),
            jax.ShapeDtypeStruct((MICRO * keys, D), jnp.bfloat16),
        ),
        grid_spec=pltpu.PrefetchScalarGridSpec(
            num_scalar_prefetch=1,
            grid=(seqs, D // PAIR, steps),
            in_specs=[
                row_spec(query_at, first),
                key_spec(key_at, first),
                key_spec(value_at, first),
                row_spec(0, first),
                row_spec(0, first),
            ]
            + [pl.BlockSpec(memory_space=pl.ANY)] * len(begun),
            out_specs=(row_spec(0, first), key_spec(0, first), key_spec(0, first)),
            scratch_shapes=[pltpu.VMEM((keys, PAIR), jnp.float32)] * 2,
        ),
        input_output_aliases={6 + item: item for item in range(len(begun))},
        compiler_params=pltpu.CompilerParams(vmem_limit_bytes=40 * 2**20),
        cost_estimate=pl.CostEstimate(flops=10*seqs*rows*keys*D, bytes_accessed=seqs*(rows+keys)*D*16, transcendentals=seqs*HEADS*rows*keys),
    )(valid_len, query_in, keys_in, keys_in, stats, grad_out, *begun)


def norm_backward(stream, gain_row, grad_normed):
    _, pull_back = jax.vjp(rms_norm, stream, gain_row)
    return pull_back(grad_normed)


def self_forward(stream, gain_row, weight, valid_len, causal):
    normed = rms_norm(stream, gain_row).astype(jnp.bfloat16)
    joint_qkv = linear(normed, weight[:, : 3 * D]).astype(jnp.bfloat16)
    pairs = D // PAIR
    mixed_out, stats_kept = attend_forward(
        joint_qkv, 0, joint_qkv, pairs, 2 * pairs, valid_len, causal
    )
    return (
        stream + linear(mixed_out, weight[:, 3 * D :]),
        (stream, normed, joint_qkv, mixed_out, stats_kept),
    )


def self_backward(grad_stream, kept_block, gain_row, weight, valid_len, causal, between=None):
    stream, normed, joint_qkv, mixed_out, stats_kept = kept_block
    grad_low = grad_stream.astype(jnp.bfloat16)
    grad_out_w = outer_sum(mixed_out, grad_low)
    grad_mixed = linear_tr(grad_low, weight[:, 3 * D :]).astype(jnp.bfloat16)
    pairs = D // PAIR
    stages = 1 if between is None else MICRO
    grads = ()
    for stage in range(stages):
        if stage > 0:
            grad_mixed = between(grad_mixed)
        grads = attend_backward(
            joint_qkv,
            0,
            joint_qkv,
            pairs,
            2 * pairs,
            valid_len,
            causal,
            stats_kept,
            grad_mixed,
            stage * MICRO // stages,
            MICRO // stages,
            tuple(grads),
        )
    grad_joint = jnp.concatenate(grads, 1)
    if between is not None:
        grad_joint = between(grad_joint)
    grad_x, grad_gain = norm_backward(stream, gain_row, linear_tr(grad_joint, weight[:, : 3 * D]))
    return (
        grad_stream + grad_x,
        grad_gain,
        jnp.concatenate([outer_sum(normed, grad_joint), grad_out_w], 1).astype(jnp.bfloat16),
    )


def cross_forward(stream, gain_row, weight, memory, valid_len):
    normed = rms_norm(stream, gain_row).astype(jnp.bfloat16)
    query_in = linear(normed, weight[:, :D]).astype(jnp.bfloat16)
    pair_kv = linear(memory, weight[:, D : 3 * D]).astype(jnp.bfloat16)
    mixed_out, stats_kept = attend_forward(
        query_in, 0, pair_kv, 0, D // PAIR, valid_len, False
    )
    return (
        stream + linear(mixed_out, weight[:, 3 * D :]),
        (stream, normed, query_in, pair_kv, mixed_out, stats_kept),
    )


def cross_backward(grad_stream, kept_block, gain_row, weight, memory, valid_len):
    stream, normed, query_in, pair_kv, mixed_out, stats_kept = kept_block
    grad_low = grad_stream.astype(jnp.bfloat16)
    grad_out_w = outer_sum(mixed_out, grad_low)
    grad_mixed = linear_tr(grad_low, weight[:, 3 * D :]).astype(jnp.bfloat16)
    grad_query, grad_k, grad_v = attend_backward(
        query_in, 0, pair_kv, 0, D // PAIR, valid_len, False, stats_kept, grad_mixed
    )
    grad_pair = jnp.concatenate([grad_k, grad_v], 1)
    grad_weight = jnp.concatenate(
        [outer_sum(normed, grad_query), outer_sum(memory, grad_pair), grad_out_w], 1
    ).astype(jnp.bfloat16)
    grad_x, grad_gain = norm_backward(stream, gain_row, linear_tr(grad_query, weight[:, :D]))
    return (
        grad_stream + grad_x,
        grad_gain,
        grad_weight,
        linear_tr(grad_pair, weight[:, D : 3 * D]),
    )


def gelu_tanh(hidden):
    return jax.nn.gelu(hidden, approximate=True)


def ffn_forward(stream, gain_row, w_in, w_out):
    normed = rms_norm(stream, gain_row).astype(jnp.bfloat16)
    hidden = linear(normed, w_in)
    active = gelu_tanh(hidden).astype(jnp.bfloat16)
    return (stream + linear_tr(active, w_out), (stream, normed, hidden, active))


def ffn_backward(grad_stream, kept_block, gain_row, w_in, w_out):
    stream, normed, hidden, active = kept_block
    grad_low = grad_stream.astype(jnp.bfloat16)
    grad_out_w = outer_sum(grad_low, active).astype(jnp.bfloat16)
    _, pull_back = jax.vjp(gelu_tanh, hidden)
    grad_hidden = pull_back(linear(grad_low, w_out))[0].astype(jnp.bfloat16)
    grad_x, grad_gain = norm_backward(stream, gain_row, linear_tr(grad_hidden, w_in))
    return (
        grad_stream + grad_x,
        grad_gain,
        outer_sum(normed, grad_hidden).astype(jnp.bfloat16),
        grad_out_w,
    )


def forward_all(
    weights,
    gain_set,
    source_rows,
    source_len,
    target_len,
    place_rows,
    lay_decoder,
):
    stream = source_rows
    enc_kept = []
    for layer_no in range(ENC):
        stream, kept_self = self_forward(
            stream, gain_set[2 * layer_no], weights[layer_no], source_len, False
        )
        stream, kept_ffn = ffn_forward(
            stream,
            gain_set[2 * layer_no + 1],
            weights[ENC + 2 * DEC + layer_no],
            weights[2 * ENC + 3 * DEC + layer_no],
        )
        enc_kept.append((kept_self, kept_ffn))
    memory, decoded = lay_decoder(rms_norm(stream, gain_set[2 * ENC]).astype(jnp.bfloat16))
    dec_kept, exit_in, exit_rows = ([], [], [])
    for layer_no in range(DEC):
        base_at = 2 * ENC + 1 + 3 * layer_no
        decoded, kept_self = self_forward(
            decoded, gain_set[base_at], weights[ENC + layer_no], target_len, True
        )
        decoded, kept_cross = cross_forward(
            decoded, gain_set[base_at + 1], weights[ENC + DEC + layer_no], memory, source_len
        )
        decoded, kept_ffn = ffn_forward(
            decoded,
            gain_set[base_at + 2],
            weights[2 * ENC + 2 * DEC + layer_no],
            weights[3 * ENC + 3 * DEC + layer_no],
        )
        dec_kept.append((kept_self, kept_cross, kept_ffn))
        picked_rows = decoded[place_rows]
        exit_in.append(picked_rows)
        exit_rows.append(
            rms_norm(picked_rows, gain_set[2 * ENC + 1 + 3 * DEC + layer_no]).astype(jnp.bfloat16)
        )
    kept = (source_len, target_len, place_rows, enc_kept, stream, memory, dec_kept, exit_in)
    return (kept, jnp.concatenate(exit_rows, 0))


def backward_all(
    weights, gain_set, kept, exit_grads, matrix_store, gain_store, before_last, between_last
):
    source_len, target_len, place_rows, enc_kept, stream, memory, dec_kept, exit_in = kept
    exit_each = jnp.split(exit_grads, DEC, axis=0)
    grad_decoded = jnp.zeros(dec_kept[0][0][0].shape, jnp.float32)
    grad_memory = jnp.zeros(memory.shape, jnp.float32)
    for layer_no in reversed(range(DEC)):
        base_at = 2 * ENC + 1 + 3 * layer_no
        exit_at = 2 * ENC + 1 + 3 * DEC + layer_no
        grad_rows, gain_store[exit_at] = norm_backward(
            exit_in[layer_no], gain_set[exit_at], exit_each[layer_no]
        )
        grad_decoded = grad_decoded.at[place_rows].add(grad_rows)
        kept_self, kept_cross, kept_ffn = dec_kept[layer_no]
        in_at, out_at = (2 * ENC + 2 * DEC + layer_no, 3 * ENC + 3 * DEC + layer_no)
        grad_decoded, gain_store[base_at + 2], matrix_store[in_at], matrix_store[out_at] = (
            ffn_backward(
                grad_decoded, kept_ffn, gain_set[base_at + 2], weights[in_at], weights[out_at]
            )
        )
        cross_at = ENC + DEC + layer_no
        grad_decoded, gain_store[base_at + 1], matrix_store[cross_at], grad_mem = cross_backward(
            grad_decoded, kept_cross, gain_set[base_at + 1], weights[cross_at], memory, source_len
        )
        grad_memory = grad_memory + grad_mem
        grad_decoded, gain_store[base_at], matrix_store[ENC + layer_no] = self_backward(
            grad_decoded, kept_self, gain_set[base_at], weights[ENC + layer_no], target_len, True
        )
    grad_stream, gain_store[2 * ENC] = norm_backward(stream, gain_set[2 * ENC], grad_memory)
    for layer_no in reversed(range(ENC)):
        kept_self, kept_ffn = enc_kept[layer_no]
        in_at, out_at = (ENC + 2 * DEC + layer_no, 2 * ENC + 3 * DEC + layer_no)
        grad_stream, gain_store[2 * layer_no + 1], matrix_store[in_at], matrix_store[out_at] = (
            ffn_backward(
                grad_stream, kept_ffn, gain_set[2 * layer_no + 1], weights[in_at], weights[out_at]
            )
        )
        if layer_no == 0:
            grad_stream = before_last(grad_stream)
        grad_stream, gain_store[2 * layer_no], matrix_store[layer_no] = self_backward(
            grad_stream,
            kept_self,
            gain_set[2 * layer_no],
            weights[layer_no],
            source_len,
            False,
            between_last if layer_no == 0 else None,
        )
    return (grad_stream, grad_decoded)


def fold_ranked(tiles, rank_of):
    count, half = (tiles.shape[0], PB // 2)

    def kernel(rank_ref, tile_ref, out_ref):
        def one_block(tile_no, carry):
            value = tile_ref[tile_no]
            folded = jnp.concatenate([value[:half], value[half:]], axis=1)
            out_ref[rank_ref[tile_no]] = folded.astype(jnp.bfloat16)
            return carry

        lax.fori_loop(0, count, one_block, 0)

    return pl.pallas_call(
        kernel,
        out_shape=jax.ShapeDtypeStruct((count, half, 2 * PB), jnp.bfloat16),
        grid_spec=pltpu.PrefetchScalarGridSpec(
            num_scalar_prefetch=1,
            grid=(1,),
            in_specs=[pl.BlockSpec(memory_space=pltpu.VMEM)],
            out_specs=pl.BlockSpec(memory_space=pltpu.VMEM),
        ),
        compiler_params=pltpu.CompilerParams(vmem_limit_bytes=40 * 2**20),
    )(rank_of, tiles)


def unfold_ranked(folded, rank_of):
    count, half = (folded.shape[0], PB // 2)

    def kernel(rank_ref, folded_ref, out_ref):
        def one_block(tile_no, carry):
            value = folded_ref[rank_ref[tile_no]]
            out_ref[tile_no, :half] = value[:, :PB]
            out_ref[tile_no, half:] = value[:, PB:]
            return carry

        lax.fori_loop(0, count, one_block, 0)

    return pl.pallas_call(
        kernel,
        out_shape=jax.ShapeDtypeStruct((count, PB, PB), jnp.float32),
        grid_spec=pltpu.PrefetchScalarGridSpec(
            num_scalar_prefetch=1,
            grid=(1,),
            in_specs=[pl.BlockSpec(memory_space=pltpu.VMEM)],
            out_specs=pl.BlockSpec(memory_space=pltpu.VMEM),
        ),
        compiler_params=pltpu.CompilerParams(vmem_limit_bytes=40 * 2**20),
    )(rank_of, folded)


def is_encoder(mat_no):
    return (
        mat_no < ENC
        or ENC + 2 * DEC <= mat_no < 2 * ENC + 2 * DEC
        or 2 * ENC + 3 * DEC <= mat_no < 3 * ENC + 3 * DEC
    )


def is_last(mat_no):
    return mat_no == 0


def rank_blocks(slot_list, devices, is_first):
    blocks_each = D // PB * (FF // PB)
    mats = slot_list // blocks_each
    early = jnp.zeros(mats.shape, jnp.bool_)
    for mat_no in range(MATS):
        if is_first(mat_no):
            early = early | (mats == mat_no)
    early = early.reshape(devices, -1).astype(jnp.int32)
    early_count = jnp.sum(early, axis=1)
    ahead = jnp.cumsum(early, axis=1) - early
    later = early_count[:, None] + jnp.arange(early.shape[1])[None, :] - ahead
    return (jnp.where(early == 1, ahead, later), early_count)


def room_for(per_device, chosen):
    share = sum(chosen(mat_no) for mat_no in range(MATS)) / MATS
    mean = per_device * share
    return min(per_device - 1, -(-int(mean + 5.0 * math.sqrt(mean * (1 - share))) // 4) * 4)


def by_block(slot_list, values):
    width, base = (64, 128)
    height = -(-slot_list.shape[0] // width)
    rows = (slot_list[:, None] // width == jnp.arange(height)[None, :]).astype(jnp.bfloat16)
    lanes = (slot_list[:, None] % width == jnp.arange(width)[None, :]).astype(jnp.bfloat16)
    found = []
    for value in values:
        high, low = (
            outer_sum(rows * (part.astype(jnp.bfloat16))[:, None], lanes)
            for part in (value // base, value % base)
        )
        found.append((high * base + low).astype(jnp.int32).reshape(-1)[: slot_list.shape[0]])
    return found


def lay_matrices(buffers, place_of, mats):
    half = PB // 2
    row_blocks, pairs = (D // PB, FF // (2 * PB))
    sizes = [buffer.shape[0] for buffer in buffers]
    starts = [sum(sizes[:item]) for item in range(len(sizes))]
    count = len(mats)

    def kernel(place_ref, *refs):
        sources, outs = (refs[: len(sizes)], refs[len(sizes) : len(sizes) + count])
        folded_ref, made, arrived, left = refs[len(sizes) + count :]
        left_half = lax.broadcasted_iota(jnp.int32, (half, 2 * PB), 1) < PB
        fetches = [
            pltpu.make_async_copy(
                source, folded_ref.at[pl.ds(start, size)], arrived.at[item]
            )
            for item, (source, start, size) in enumerate(zip(sources, starts, sizes))
        ]
        for fetch in fetches:
            fetch.start()
        for fetch in fetches:
            fetch.wait()

        def send(item):
            return pltpu.make_async_copy(made.at[item % 2], outs[item], left.at[item % 2])

        for item, mat_no in enumerate(mats):
            if item >= 2:
                send(item - 2).wait()

            def one_row(row_no, carry, item=item, mat_no=mat_no):
                first = (mat_no * row_blocks + row_no) * 2 * pairs
                row_at = pl.multiple_of(row_no * PB, PB)
                for pair_no in range(pairs):
                    even = folded_ref[place_ref[first + 2 * pair_no]].astype(jnp.float32)
                    odd = folded_ref[place_ref[first + 2 * pair_no + 1]].astype(jnp.float32)
                    columns = slice(2 * PB * pair_no, 2 * PB * (pair_no + 1))
                    upper = jnp.where(left_half, even, pltpu.roll(odd, PB, 1))
                    lower = jnp.where(left_half, pltpu.roll(even, PB, 1), odd)
                    made[item % 2, pl.ds(row_at, half), columns] = upper.astype(jnp.bfloat16)
                    made[item % 2, pl.ds(row_at + half, half), columns] = lower.astype(jnp.bfloat16)
                return carry

            lax.fori_loop(0, row_blocks, one_row, 0)
            send(item).start()
        for item in range(max(count - 2, 0), count):
            send(item).wait()

    return pl.pallas_call(
        kernel,
        out_shape=[jax.ShapeDtypeStruct((D, FF), jnp.bfloat16)] * count,
        grid_spec=pltpu.PrefetchScalarGridSpec(
            num_scalar_prefetch=1,
            grid=(1,),
            in_specs=[pl.BlockSpec(memory_space=pl.ANY)] * len(sizes),
            out_specs=[pl.BlockSpec(memory_space=pl.ANY)] * count,
            scratch_shapes=[
                pltpu.VMEM((sum(sizes), half, 2 * PB), jnp.bfloat16),
                pltpu.VMEM((2, D, FF), jnp.bfloat16),
                pltpu.SemaphoreType.DMA((len(sizes),)),
                pltpu.SemaphoreType.DMA((2,)),
            ],
        ),
        compiler_params=pltpu.CompilerParams(vmem_limit_bytes=40 * 2**20),
    )(place_of, *buffers)


def fold_gradients(matrices, mats, place_of, sizes, begun=None):
    half = PB // 2
    row_blocks, pairs = (D // PB, FF // (2 * PB))
    count = len(mats)
    whole = sum(sizes)
    given = 0 if begun is None else 1
    skipped = 0 if begun is None else whole - begun.shape[0]
    kept = whole - skipped

    def kernel(place_ref, *refs):
        sources, old = (refs[:count], refs[count : count + given])
        outs = refs[count + given : -5]
        folded_ref, held, arrived, left, old_sem = refs[-5:]
        left_half = lax.broadcasted_iota(jnp.int32, (half, 2 * PB), 1) < PB

        def fetch(item):
            return pltpu.make_async_copy(sources[item], held.at[item % 2], arrived.at[item % 2])

        fetch(0).start()
        if given:
            before = pltpu.make_async_copy(
                old[0], folded_ref.at[pl.ds(0, kept)], old_sem.at[0]
            )
            before.start()
            before.wait()
        for item, mat_no in enumerate(mats):
            if item + 1 < count:
                fetch(item + 1).start()
            fetch(item).wait()

            def place(block, carry=None):
                spot = place_ref[block] - skipped
                return jnp.where(spot < 0, kept, spot) if given else spot

            def one_row(row_no, carry, item=item, mat_no=mat_no):
                first = (mat_no * row_blocks + row_no) * 2 * pairs
                row_at = pl.multiple_of(row_no * PB, PB)
                for pair_no in range(pairs):
                    columns = slice(2 * PB * pair_no, 2 * PB * (pair_no + 1))
                    upper = held[item % 2, pl.ds(row_at, half), columns].astype(jnp.float32)
                    lower = held[item % 2, pl.ds(row_at + half, half), columns].astype(jnp.float32)
                    even = jnp.where(left_half, upper, pltpu.roll(lower, PB, 1))
                    odd = jnp.where(left_half, pltpu.roll(upper, PB, 1), lower)
                    folded_ref[place(first + 2 * pair_no)] = even.astype(jnp.bfloat16)
                    folded_ref[place(first + 2 * pair_no + 1)] = odd.astype(jnp.bfloat16)
                return carry

            lax.fori_loop(0, row_blocks, one_row, 0)
        begin = 0
        sends = []
        for item, out in enumerate(outs):
            size = out.shape[0]
            sends.append(
                pltpu.make_async_copy(folded_ref.at[pl.ds(begin, size)], out, left.at[item])
            )
            begin += size
        for send in sends:
            send.start()
        for send in sends:
            send.wait()

    shapes = [kept] if given else list(sizes)
    return pl.pallas_call(
        kernel,
        out_shape=[jax.ShapeDtypeStruct((size, half, 2 * PB), jnp.bfloat16) for size in shapes],
        grid_spec=pltpu.PrefetchScalarGridSpec(
            num_scalar_prefetch=1,
            grid=(1,),
            in_specs=[pl.BlockSpec(memory_space=pl.ANY)] * (count + given),
            out_specs=[pl.BlockSpec(memory_space=pl.ANY)] * len(shapes),
            scratch_shapes=[
                pltpu.VMEM((kept + given, half, 2 * PB), jnp.bfloat16),
                pltpu.VMEM((2, D, FF), jnp.bfloat16),
                pltpu.SemaphoreType.DMA((2,)),
                pltpu.SemaphoreType.DMA((2,)),
                pltpu.SemaphoreType.DMA((1,)),
            ],
        ),
        compiler_params=pltpu.CompilerParams(vmem_limit_bytes=40 * 2**20),
    )(place_of, *[matrices[mat_no] for mat_no in mats], *([begun] if given else []))


def exchange_plan(dp_size, along, per_device):
    low, high = (along.bit_length() - 1, dp_size.bit_length() - 1)
    base = [low + bit for bit in range(high)] + list(range(1, low))
    third = per_device // 3
    sizes = [per_device - 2 * third, third, third]
    return [(size, base[turn:] + base[:turn]) for turn, size in enumerate(sizes)]


def places_for(ranks, plan, devices):
    per_device = sum(size for size, _ in plan)
    owner = jnp.arange(devices)[:, None]
    place = jnp.zeros_like(ranks)
    begin = 0
    for size, order in plan:
        spot = jnp.zeros_like(owner)
        for bit in order:
            spot = spot * 2 + owner // 2**bit % 2
        here = begin * (devices // 2) + spot * size + ranks - begin
        place = jnp.where((ranks >= begin) & (ranks < begin + size), here, place)
        begin += size
    return place + owner % 2 * (devices // 2 * per_device)


def halve(value, bit, devices):
    me = lax.axis_index("dp") * lax.axis_size("vocab") + lax.axis_index("vocab")

    mine = me // 2**bit % 2
    value = value.reshape(2, value.shape[0] // 2, *value.shape[1:])
    sent = lax.dynamic_index_in_dim(value, 1 - mine, 0, keepdims=False)
    kept = lax.dynamic_index_in_dim(value, mine, 0, keepdims=False)
    pairs = [(index, index ^ 2**bit) for index in range(devices)]
    arrived = lax.ppermute(sent, ("dp", "vocab"), pairs)
    return kept.astype(jnp.float32) + arrived.astype(jnp.float32)


def first_exchange(folded, devices):
    return halve(folded, 0, devices).astype(jnp.bfloat16)


def split_parts(total, plan, devices):
    parts, begin = ([], 0)
    for size, _ in plan:
        count = size * (devices // 2)
        parts.append(total[begin : begin + count])
        begin += count
    return parts


def one_exchange(parts, plan, round_no, devices):
    return [
        halve(part.astype(jnp.bfloat16), order[round_no], devices)
        for part, (_, order) in zip(parts, plan)
    ]


def other_exchanges(parts, plan, devices, done=0):
    for round_no in range(done, len(plan[0][1])):
        parts = one_exchange(parts, plan, round_no, devices)
    return jnp.concatenate(parts, 0)


def take_rows(source, index_at, kind):
    count, width, block = (index_at.shape[0], source.shape[1], 128)
    whole = -(-count // block) * block
    index_at = jnp.pad(index_at, (0, whole - count))

    def kernel(index_ref, source_ref, out_ref, held_ref):
        first = pl.program_id(0) * block

        def copy_eight(group, carry):
            base = pl.multiple_of(group * 8, 8)
            for row_no in range(8):
                held_ref[pl.ds(base + row_no, 1), :] = source_ref[
                    pl.ds(index_ref[first + base + row_no], 1), :
                ]
            return carry

        lax.fori_loop(0, block // 8, copy_eight, 0)
        out_ref[...] = held_ref[...].astype(kind)

    taken = pl.pallas_call(
        kernel,
        out_shape=jax.ShapeDtypeStruct((whole, width), kind),
        grid_spec=pltpu.PrefetchScalarGridSpec(
            num_scalar_prefetch=1,
            grid=(whole // block,),
            in_specs=[pl.BlockSpec(memory_space=pltpu.VMEM)],
            out_specs=pl.BlockSpec((block, width), lambda step, index: (step, 0)),
            scratch_shapes=[pltpu.VMEM((block, width), jnp.float32)],
        ),
        compiler_params=pltpu.CompilerParams(vmem_limit_bytes=40 * 2**20),
    )(index_at, source)
    return taken[:count]


def add_rows(rows, index_at, total):
    count, width, block = (rows.shape[0], rows.shape[1], 512)
    whole = -(-count // block) * block
    index_at = jnp.pad(index_at, (0, whole - count), constant_values=-1)[None, :]
    rows = jnp.pad(rows, ((0, whole - count), (0, 0)))
    height = total.shape[0]

    def kernel(index_ref, rows_ref, total_ref, out_ref):
        @pl.when(pl.program_id(0) == 0)
        def _():
            out_ref[...] = total_ref[...]

        hits = lax.broadcasted_iota(jnp.int32, (height, block), 0) == index_ref[...]
        out_ref[...] += jnp.dot(
            hits.astype(jnp.float32).astype(jnp.bfloat16),
            rows_ref[...],
            preferred_element_type=jnp.float32,
        )

    return pl.pallas_call(
        kernel,
        out_shape=jax.ShapeDtypeStruct(total.shape, jnp.float32),
        grid=(whole // block,),
        in_specs=[
            pl.BlockSpec((1, block), lambda step: (0, step)),
            pl.BlockSpec((block, width), lambda step: (step, 0)),
            pl.BlockSpec((height, width), lambda step: (0, 0)),
        ],
        out_specs=pl.BlockSpec((height, width), lambda step: (0, 0)),
        compiler_params=pltpu.CompilerParams(vmem_limit_bytes=40 * 2**20),
    )(index_at, rows, total)


def spread(value, axes, peers):
    return lax.all_to_all(
        jnp.broadcast_to(value[None], (peers, *value.shape)), axes, 0, 0, tiled=True
    )


def count_before(mask):
    size, width = (mask.shape[-1], 128)
    parts = mask.reshape(*mask.shape[:-1], size // width, width).astype(jnp.bfloat16)
    earlier = (jnp.arange(width)[:, None] < jnp.arange(width)[None, :]).astype(jnp.bfloat16)
    inside = jnp.einsum("...pw,wk->...pk", parts, earlier, preferred_element_type=jnp.float32)
    totals = jnp.sum(parts.astype(jnp.float32), axis=-1)
    ahead = jnp.cumsum(totals, axis=-1) - totals
    return (inside + ahead[..., None]).reshape(mask.shape).astype(jnp.int32)


def room(count, peers):
    mean = count / peers
    return min(count, -(-int(mean + 5.0 * math.sqrt(mean)) // 16) * 16)


def listed(mask, rank, values, size):
    width, base = (16, 128)
    rows = mask[..., None] & (rank[..., None] // width == jnp.arange(size // width))
    lanes = (rank[..., None] % width == jnp.arange(width)).astype(jnp.bfloat16)
    values = values + 1
    high, low = (
        jnp.einsum(
            "...th,...tl->...hl",
            jnp.where(rows, part[..., None].astype(jnp.bfloat16), 0),
            lanes,
            preferred_element_type=jnp.float32,
        )
        for part in (values // base, values % base)
    )
    return (high * base + low).astype(jnp.int32).reshape(*mask.shape[:-1], size) - 1


def rounds_needed(owner_all, peers, size):
    held = jnp.sum((owner_all[:, None, :] == jnp.arange(peers)[:, None]).astype(jnp.int32), axis=2)
    return (jnp.max(held) + size - 1) // size


def fetch_plan(table_part, tokens_all, peers_here, peer_me):
    peers, rows_each = (peers_here.shape[0], table_part.shape[0])
    count = tokens_all.shape[1]
    size = room(count, peers)
    asked = peers_here // rows_each == peer_me
    asked_rank = count_before(asked)
    own_tokens = lax.dynamic_index_in_dim(peers_here, peer_me, 0, keepdims=False)
    own_owner = own_tokens // rows_each
    own_mask = own_owner[None, :] == jnp.arange(peers)[:, None]
    own_rank = jnp.sum(jnp.where(own_mask, count_before(own_mask), 0), axis=0)

    def to_send(round_no):
        wanted = listed(
            asked, asked_rank - round_no * size, peers_here % rows_each, size
        )
        return take_rows(table_part, jnp.maximum(wanted.reshape(-1), 0), jnp.bfloat16)

    def found_in(arrived, round_no):
        rank_now = own_rank - round_no * size
        now = (rank_now >= 0) & (rank_now < size)
        found = take_rows(
            arrived.astype(jnp.float32), jnp.where(now, own_owner * size + rank_now, 0), jnp.float32
        )
        return (now, found)

    def again(round_no, rows):
        now, found = found_in(swap_rows(to_send(round_no)), round_no)
        return jnp.where(now[:, None], found, rows)

    rounds = rounds_needed(tokens_all // rows_each, peers, size)

    def finish(arrived):
        return lax.fori_loop(1, rounds, again, found_in(arrived, 0)[1])

    return (to_send(0), finish)


def swap_rows(rows):
    return lax.all_to_all(rows, "vocab", 0, 0, tiled=True)


def return_plan(tokens_all, rows_each, dp_size):
    peers, count = tokens_all.shape
    along = peers // dp_size
    quarter = rows_each // dp_size
    me = lax.axis_index("dp") * along + lax.axis_index("vocab")
    size = room(count, peers)
    owner_all = (tokens_all % rows_each) // quarter * along + tokens_all // rows_each
    arriving = owner_all == me
    arriving_rank = count_before(arriving)
    own_owner = lax.dynamic_index_in_dim(owner_all, me, 0, keepdims=False)
    leaving = own_owner[None, :] == jnp.arange(peers)[:, None]
    leaving_rank = count_before(leaving)
    place = jnp.broadcast_to(jnp.arange(count)[None, :], leaving.shape)

    def lists(round_no):
        return (
            jnp.maximum(
                listed(leaving, leaving_rank - round_no * size, place, size).reshape(-1), 0
            ),
            listed(
                arriving, arriving_rank - round_no * size, tokens_all % quarter, size
            ).reshape(-1),
        )

    return (lists, rounds_needed(owner_all, peers, size))


def return_rows(grad_rows, lists, first_lists, rounds, total, ready):
    def swap_all(rows):
        return lax.all_to_all(rows, ("dp", "vocab"), 0, 0, tiled=True)

    def again(round_no, so_far):
        chosen, where = lists(round_no)
        return add_rows(swap_all(take_rows(grad_rows, chosen, jnp.bfloat16)), where, so_far)

    arrived = swap_all(ready(take_rows(grad_rows, first_lists[0], jnp.bfloat16)))
    return lax.fori_loop(1, rounds, again, add_rows(arrived, first_lists[1], total))


def turn_in(left_basis, tiles, right_basis):
    half = jnp.einsum("tki,tkl->til", left_basis, tiles, precision=HIGH)
    return jnp.einsum("til,tlj->tij", half, right_basis, precision=HIGH)


def turn_out(left_basis, tiles, right_basis):
    half = jnp.einsum("tik,tkl->til", left_basis, tiles, precision=HIGH)
    return jnp.einsum("til,tjl->tij", half, right_basis, precision=HIGH)


def orthonormal(columns):
    lanes, group = (128, 4)

    def kernel(in_ref, out_ref):
        out_ref[...] = in_ref[...]

        def one_column(column_no, carry):
            pivot = out_ref[column_no]
            pivot = pivot / jnp.sqrt(jnp.sum(pivot * pivot, axis=0, keepdims=True))
            out_ref[column_no] = pivot

            def one_group(group_no, inner):
                first = group_no * group
                held = [out_ref[first + item] for item in range(group)]
                for item in range(group):
                    share = jnp.sum(pivot * held[item], axis=0, keepdims=True)
                    share = jnp.where(first + item > column_no, share, 0.0)
                    held[item] = held[item] - share * pivot
                for item in range(group):
                    out_ref[first + item] = held[item]
                return inner

            return lax.fori_loop((column_no + 1) // group, PB // group, one_group, carry)

        lax.fori_loop(0, PB, one_column, 0)

    spec = pl.BlockSpec((PB, PB, lanes), lambda step: (0, 0, step))
    return pl.pallas_call(
        kernel,
        out_shape=jax.ShapeDtypeStruct(columns.shape, jnp.float32),
        grid=(columns.shape[2] // lanes,),
        in_specs=[spec],
        out_specs=spec,
        compiler_params=pltpu.CompilerParams(vmem_limit_bytes=40 * 2**20),
    )(columns)


def renew_bases(left_stat, right_stat, left_basis, right_basis):
    moved = jnp.concatenate(
        [
            jnp.einsum("tij,tjk->tik", left_stat, left_basis, precision=HIGH),
            jnp.einsum("tij,tjk->tik", right_stat, right_basis, precision=HIGH),
        ],
        0,
    )
    count = moved.shape[0]
    whole = -(-count // 128) * 128
    columns = jnp.pad(jnp.transpose(moved, (2, 1, 0)), ((0, 0), (0, 0), (0, whole - count)))
    renewed = jnp.transpose(orthonormal(columns)[:, :, :count], (2, 1, 0))
    return (renewed[: count // 2], renewed[count // 2 :])


def soap_update(
    master,
    grad_tiles,
    first_mom,
    first_turned,
    second_mom,
    left_stat,
    right_stat,
    left_basis,
    right_basis,
    factor,
):
    first_new = BETA_FIRST * first_mom + (1 - BETA_FIRST) * (factor * grad_tiles)
    grad_turned = factor * turn_in(left_basis, grad_tiles, right_basis)
    first_turned = BETA_FIRST * first_turned + (1 - BETA_FIRST) * grad_turned
    second_new = BETA_SECOND * second_mom + (1 - BETA_SECOND) * grad_turned * grad_turned
    direction = (
        first_turned
        / (1 - BETA_FIRST**STEP)
        / (jnp.sqrt(second_new / (1 - BETA_SECOND**STEP)) + ADAM_EPS)
    )
    master_new = master - RATE_MATRIX * (
        turn_out(left_basis, direction, right_basis) + DECAY * master
    )
    left_new = BETA_STAT * left_stat + (1 - BETA_STAT) * (
        factor
        * (factor * jnp.einsum("tik,tjk->tij", grad_tiles, grad_tiles, precision=HIGH))
    )
    right_new = BETA_STAT * right_stat + (1 - BETA_STAT) * (
        factor
        * (factor * jnp.einsum("tki,tkj->tij", grad_tiles, grad_tiles, precision=HIGH))
    )
    return (
        master_new,
        first_new,
        second_new,
        left_new,
        right_new,
        *renew_bases(left_new, right_new, left_basis, right_basis),
    )


def adamw_update(master, grad_now, first_mom, second_mom, rate, decay_by):
    first_new = BETA_FIRST * first_mom + (1 - BETA_FIRST) * grad_now
    second_new = BETA_SECOND * second_mom + (1 - BETA_SECOND) * grad_now * grad_now
    direction = (
        first_new
        / (1 - BETA_FIRST**STEP)
        / (jnp.sqrt(second_new / (1 - BETA_SECOND**STEP)) + ADAM_EPS)
    )
    return (master - rate * (direction + decay_by * master), first_new, second_new)


def per_device(
    master_tiles,
    mom1_tiles,
    mom2_tiles,
    stat_left,
    stat_right,
    basis_left,
    basis_right,
    table_master,
    table_mom1,
    table_mom2,
    gains,
    gain_mom1,
    gain_mom2,
    source_ids,
    target_ids,
    source_len,
    target_len,
    loss_place,
    exit_layer,
    slot_list,
):
    dp_size, along = (lax.axis_size("dp"), lax.axis_size("vocab"))
    dp_me, peer_me = (lax.axis_index("dp"), lax.axis_index("vocab"))
    devices = dp_size * along
    rows_each = table_master.shape[0]
    quarter = rows_each // dp_size
    source_len, target_len = (source_len[:, 0], target_len[:, 0])

    shifted = jnp.pad(target_ids[:, 0, :-1], ((0, 0), (1, 0)))
    tokens = jnp.concatenate([source_ids.reshape(-1), shifted.reshape(-1)])
    places = loss_place[:, 0]
    counted = places < target_len[:, None]
    reach = [
        jnp.sum((counted & (exit_layer[:, 0] >= layer_no)).astype(jnp.int32))
        for layer_no in range(DEC)
    ]
    labels = jnp.take_along_axis(target_ids[:, 0], places, axis=1).reshape(-1)
    row_count = MICRO * LOSS_POS
    own_facts = jnp.concatenate(
        [tokens, labels, counted.reshape(-1).astype(jnp.int32), jnp.stack(reach)]
    )
    fact_count = own_facts.shape[0]
    own_facts = jnp.pad(own_facts, (0, -fact_count % 128))
    facts = spread(own_facts, ("dp", "vocab"), devices)
    slots_later, facts = lax.optimization_barrier((slot_list, facts))
    tokens_all = facts[:, : tokens.shape[0]]
    after = facts[:, tokens.shape[0] :]
    labels_all = after[:, :row_count]
    counted_all = after[:, row_count : 2 * row_count].astype(jnp.float32)
    reach_all = jnp.sum(after[:, 2 * row_count : 2 * row_count + DEC].astype(jnp.float32), axis=0)
    count_all = jnp.sum(counted_all)
    fraction = reach_all / jnp.sum(reach_all)

    per_device = master_tiles.shape[0]
    me = dp_me * along + peer_me
    ranks, early_count = rank_blocks(slot_list, devices, is_encoder)
    first_size = room_for(per_device, is_encoder)
    second_size = per_device - first_size
    place_at = jnp.where(
        ranks < first_size,
        jnp.arange(devices)[:, None] * first_size + ranks,
        devices * first_size
        + jnp.arange(devices)[:, None] * second_size
        + ranks
        - first_size,
    )
    late_size = room_for(per_device, is_last)
    soon_size = per_device - late_size
    back_ranks, soon_count = rank_blocks(slots_later, devices, lambda mat_no: not is_last(mat_no))
    soon_plan = exchange_plan(dp_size, along, soon_size)
    late_plan = exchange_plan(dp_size, along, late_size)
    back_at = jnp.where(
        back_ranks < soon_size,
        places_for(back_ranks, soon_plan, devices),
        devices * soon_size + places_for(back_ranks - soon_size, late_plan, devices),
    )
    place_of, back_of = by_block(slots_later, [place_at.reshape(-1), back_at.reshape(-1)])
    own_folded = fold_ranked(
        master_tiles, lax.dynamic_index_in_dim(ranks, me, 0, keepdims=False)
    )
    src_count, tgt_count = (source_ids.shape[2], target_ids.shape[2])

    def planned(first, length):
        ids_all = tokens_all[:, first : first + MICRO * length]
        peers_here = lax.dynamic_slice_in_dim(ids_all, dp_me * along, along, 0)
        return fetch_plan(table_master, ids_all, peers_here, peer_me)

    source_sent, source_finish = planned(0, src_count)
    target_sent, target_finish = planned(MICRO * src_count, tgt_count)
    first_tiles = lax.all_gather(own_folded[:first_size], ("dp", "vocab"), axis=0, tiled=True)
    own_second, first_tiles, source_arrived = lax.optimization_barrier(
        (own_folded[first_size:], first_tiles, swap_rows(source_sent))
    )
    second_tiles = lax.all_gather(own_second, ("dp", "vocab"), axis=0, tiled=True)
    encoder_mats = [mat_no for mat_no in range(MATS) if is_encoder(mat_no)]
    decoder_mats = [mat_no for mat_no in range(MATS) if not is_encoder(mat_no)]

    def lay_with_all():
        others = lax.all_gather(own_second, ("dp", "vocab"), axis=0, tiled=True)
        return lay_matrices([first_tiles, others], place_of, encoder_mats)

    def lay_with_first():
        return lay_matrices([first_tiles], place_of, encoder_mats)

    encoder_set = lax.cond(
        jnp.max(early_count) > first_size, lay_with_all, lay_with_first
    )
    weights = [None] * MATS
    for mat_no, matrix in zip(encoder_mats, encoder_set):
        weights[mat_no] = matrix

    def lay_decoder(memory):
        held, tiles, arrived = lax.optimization_barrier((memory, second_tiles, target_arrived))
        decoder_set = lay_matrices([first_tiles, tiles], place_of, decoder_mats)
        for mat_no, matrix in zip(decoder_mats, decoder_set):
            weights[mat_no] = matrix
        return (held, with_waves(target_finish(arrived), tgt_count))

    wave_set = waves(src_count, D)

    def with_waves(rows, length):
        return rows * math.sqrt(D) + jnp.tile(wave_set[:length], (MICRO, 1))

    lists, rounds = return_plan(tokens_all, rows_each, dp_size)
    source_rows = with_waves(source_finish(source_arrived), src_count)
    first_turned = turn_in(basis_left, mom1_tiles, basis_right)
    source_rows, first_lists, first_turned, target_sent = lax.optimization_barrier(
        (source_rows, lists(0), first_turned, target_sent)
    )
    target_arrived = swap_rows(target_sent)

    place_rows = (places + jnp.arange(MICRO)[:, None] * tgt_count).reshape(-1)
    kept, exit_rows = forward_all(
        weights,
        gains,
        source_rows,
        source_len,
        target_len,
        place_rows,
        lay_decoder,
    )

    table_low_part = table_master.astype(jnp.bfloat16)
    exit_count = DEC * row_count
    exit_all = lax.all_gather(exit_rows, ("dp", "vocab"), axis=0, tiled=True)
    exit_here = spread(exit_rows, "vocab", along).reshape(-1, D)
    label_rows = jnp.tile(labels_all, (1, DEC)).reshape(-1)
    weight_rows = (
        jnp.repeat(fraction, row_count)[None, :] * jnp.tile(counted_all, (1, DEC))
    ).reshape(-1)
    group_rows = along * exit_count
    group_at = dp_me * group_rows
    label_here = lax.dynamic_slice_in_dim(label_rows, group_at, group_rows, 0)
    weight_here = lax.dynamic_slice_in_dim(weight_rows, group_at, group_rows, 0)
    logits = linear_tr(exit_here, table_low_part)
    hit_here = label_here[:, None] - peer_me * rows_each == jnp.arange(rows_each)[None, :]
    summit = jnp.max(logits, axis=1)
    spread_part = jnp.sum(jnp.exp(logits - summit[:, None]), axis=1)
    picked_part = jnp.sum(jnp.where(hit_here, logits, 0.0), axis=1)
    stats = spread(
        jnp.stack([summit, spread_part, picked_part]), ("dp", "vocab"), devices
    ).reshape(dp_size, along, 3, group_rows)
    summit_all = jnp.max(stats[:, :, 0], axis=1)
    total_all = jnp.sum(stats[:, :, 1] * jnp.exp(stats[:, :, 0] - summit_all[:, None]), axis=1)
    spread_all = summit_all + jnp.log(total_all)
    picked_all = jnp.sum(stats[:, :, 2], axis=1)
    loss_sum = jnp.sum(weight_rows * (spread_all - picked_all).reshape(-1))
    spread_here = lax.dynamic_index_in_dim(spread_all, dp_me, 0, keepdims=False)

    def logit_grads(logit_set, spread, weight_set, hits):
        return (
            (weight_set / count_all)[:, None]
            * (jnp.exp(logit_set - spread[:, None]) - hits.astype(jnp.float32))
        ).astype(jnp.bfloat16)

    grads_here = logit_grads(logits, spread_here, weight_here, hit_here)
    grad_parts = linear(grads_here, table_low_part).astype(jnp.bfloat16)
    grad_parts = lax.all_to_all(grad_parts, "vocab", 0, 0, tiled=True)
    exit_grads = jnp.sum(
        grad_parts.reshape(along, exit_count, D).astype(jnp.float32), axis=0
    )

    matrix_store = [None] * MATS
    gain_store = [None] * GAINS
    soon_mats = [mat_no for mat_no in range(MATS) if not is_last(mat_no)]
    late_mats = [mat_no for mat_no in range(MATS) if is_last(mat_no)]
    both = [devices * soon_size, devices * late_size]
    held = {}

    def before_last(grad_stream):
        blocks, held["begun"] = fold_gradients(matrix_store, soon_mats, back_of, both)
        grad_stream, blocks = lax.optimization_barrier((grad_stream, blocks))
        held["total"] = first_exchange(blocks, devices)
        return grad_stream

    def between_last(value):
        if "parts" not in held:
            value, total = lax.optimization_barrier((value, held["total"]))
            held["parts"], held["done"] = (split_parts(total, soon_plan, devices), 0)
        elif held["done"] < len(soon_plan[0][1]):
            parts = one_exchange(held["parts"], soon_plan, held["done"], devices)
            value, held["parts"] = lax.optimization_barrier((value, parts))
            held["done"] += 1
        return value

    grad_source, grad_target = backward_all(
        weights,
        gains,
        kept,
        exit_grads,
        matrix_store,
        gain_store,
        before_last,
        between_last,
    )

    first_row = peer_me * rows_each + dp_me * quarter
    table_quarter = lax.dynamic_slice_in_dim(table_low_part, dp_me * quarter, quarter, 0)
    hit_quarter = label_rows[:, None] - first_row == jnp.arange(quarter)[None, :]
    grads_quarter = logit_grads(
        linear_tr(exit_all, table_quarter), spread_all.reshape(-1), weight_rows, hit_quarter
    )
    grad_quarter = outer_sum(grads_quarter, exit_all)
    grad_source = between_last(grad_source)
    grad_rows = jnp.concatenate([grad_source, grad_target], 0) * math.sqrt(D)
    grad_rows = between_last(grad_rows)
    [late_blocks] = fold_gradients(matrix_store, late_mats, back_of, both, held["begun"])
    late_parts = split_parts(first_exchange(late_blocks, devices), late_plan, devices)
    late_parts = one_exchange(late_parts, late_plan, 0, devices)

    def ready(rows):
        rows = between_last(rows)
        rows, held["late"] = lax.optimization_barrier((rows, late_parts))
        return rows

    grad_quarter = return_rows(grad_rows, lists, first_lists, rounds, grad_quarter, ready)

    soon_sum = other_exchanges(held["parts"], soon_plan, devices, held["done"])
    late_sum = other_exchanges(held["late"], late_plan, devices, 1)

    def exchange_again():
        blocks, _ = fold_gradients(matrix_store, list(range(MATS)), back_of, both)
        parts = split_parts(first_exchange(blocks, devices), soon_plan, devices)
        return other_exchanges(parts, soon_plan, devices)

    soon_sum = lax.cond(
        jnp.min(soon_count) < soon_size, exchange_again, lambda: soon_sum
    )
    owned_grad = unfold_ranked(
        jnp.concatenate([soon_sum, late_sum], 0),
        lax.dynamic_index_in_dim(back_ranks, me, 0, keepdims=False),
    )
    squares = jnp.sum(owned_grad * owned_grad) + jnp.sum(grad_quarter * grad_quarter)
    square_total = jnp.sum(
        spread(jnp.full((1, 128), squares), ("dp", "vocab"), devices)[:, 0, 0]
    )
    share = -(-GAINS * D // (devices * 128)) * 128
    gain_flat = jnp.stack(gain_store).reshape(-1)
    gain_flat = jnp.pad(gain_flat, (0, devices * share - GAINS * D)).reshape(devices, share)
    gain_part = jnp.sum(lax.all_to_all(gain_flat, ("dp", "vocab"), 0, 0, tiled=True), axis=0)
    gain_total = spread(gain_part[None], ("dp", "vocab"), devices).reshape(-1)[: GAINS * D]
    gain_total = gain_total.reshape(GAINS, D)
    grad_norm = jnp.sqrt(square_total + jnp.sum(gain_total * gain_total))
    factor = jnp.minimum(1.0, CLIP_AT / grad_norm)
    table_grad = lax.all_gather(
        grad_quarter.astype(jnp.bfloat16), "dp", axis=0, tiled=True
    ).astype(jnp.float32)
    master_new, mom1_new, mom2_new, left_new, right_new, bleft_new, bright_new = soap_update(
        master_tiles,
        owned_grad,
        mom1_tiles,
        first_turned,
        mom2_tiles,
        stat_left,
        stat_right,
        basis_left,
        basis_right,
        factor,
    )
    table_new, table_m, table_v = adamw_update(
        table_master, table_grad * factor, table_mom1, table_mom2, RATE_MATRIX, DECAY
    )
    gains_new, gains_m, gains_v = adamw_update(
        gains, gain_total * factor, gain_mom1, gain_mom2, RATE_VECTOR, 0.0
    )
    return (
        loss_sum,
        count_all,
        grad_norm,
        master_new,
        master_new.astype(jnp.bfloat16),
        mom1_new,
        mom2_new,
        left_new,
        right_new,
        bleft_new,
        bright_new,
        table_new,
        table_new.astype(jnp.bfloat16),
        table_m,
        table_v,
        gains_new,
        gains_m,
        gains_v,
    )


def solution(mesh):
    placed = (
        P(("dp", "vocab"), None, None),
        P(("dp", "vocab"), None, None),
        P(("dp", "vocab"), None, None),
        P(("dp", "vocab"), None, None),
        P(("dp", "vocab"), None, None),
        P(("dp", "vocab"), None, None),
        P(("dp", "vocab"), None, None),
        P("vocab", None),
        P("vocab", None),
        P("vocab", None),
        P(),
        P(),
        P(),
        P(None, ("dp", "vocab"), None),
        P(None, ("dp", "vocab"), None),
        P(None, ("dp", "vocab")),
        P(None, ("dp", "vocab")),
        P(None, ("dp", "vocab"), None),
        P(None, ("dp", "vocab"), None),
        P(),
    )
    return jax.shard_map(
        per_device,
        mesh=mesh,
        in_specs=placed,
        out_specs=(
            P(),
            P(),
            P(),
            P(("dp", "vocab"), None, None),
            P(("dp", "vocab"), None, None),
            P(("dp", "vocab"), None, None),
            P(("dp", "vocab"), None, None),
            P(("dp", "vocab"), None, None),
            P(("dp", "vocab"), None, None),
            P(("dp", "vocab"), None, None),
            P(("dp", "vocab"), None, None),
            P("vocab", None),
            P("vocab", None),
            P("vocab", None),
            P("vocab", None),
            P(),
            P(),
            P(),
        ),
        check_vma=False,
    )
```

```python
import math

import jax
import jax.numpy as jnp
from jax import lax
from jax.experimental import pallas as pl
from jax.experimental.pallas import tpu as pltpu
from jax.sharding import PartitionSpec as P

D = 512
HEADS = 8
HEAD_DIM = 64
FF = 2048
ENC = 1
DEC = 2
MICRO = 2
LOSS_POS = 16
PB = 64
STEP = 10
MATS = 11
GAINS = 11


HIGH = lax.Precision.HIGH
NORM_EPS = 1e-06
CLIP_AT = 0.02
RATE_MATRIX = 0.1
RATE_VECTOR = 0.8
BETA_FIRST = 0.9
BETA_SECOND = 0.95
BETA_STAT = 0.95
ADAM_EPS = 1e-08
DECAY = 0.01


def rms_norm(stream, gain_row):
    return (
        stream * lax.rsqrt(jnp.mean(stream * stream, axis=-1, keepdims=True) + NORM_EPS) * gain_row
    )


def waves(length, columns):
    place_at = jnp.arange(length).astype(jnp.float32)[:, None]
    rate_at = jnp.exp(
        jnp.arange(columns // 2).astype(jnp.float32) * (-2.0 * math.log(10000.0) / columns)
    )
    angle = place_at * rate_at[None, :]
    return jnp.concatenate([jnp.sin(angle), jnp.cos(angle)], axis=1)


def linear(left_op, right_op):
    return jnp.dot(left_op, right_op, preferred_element_type=jnp.float32)


def linear_tr(left_op, right_op):
    return lax.dot_general(
        left_op, right_op, (((1,), (1,)), ((), ())), preferred_element_type=jnp.float32
    )


def outer_sum(left_op, right_op):
    return lax.dot_general(
        left_op, right_op, (((0,), (0,)), ((), ())), preferred_element_type=jnp.float32
    )


def split_heads(matrix):
    return matrix.reshape(matrix.shape[0], HEADS, HEAD_DIM)


NEVER=-1000000000.0
PAIR=2*HEAD_DIM
def kept_scores(query, keys, valid_len, causal, start_at):
    scores = lax.dot_general(query, keys, (((1,), (1,)), ((), ())), preferred_element_type=jnp.float32)
    key_at = lax.broadcasted_iota(jnp.int32, scores.shape if causal else (1, scores.shape[1]), 1)
    allowed = key_at < valid_len
    if causal:
        allowed = allowed & (key_at <= start_at + lax.broadcasted_iota(jnp.int32, scores.shape, 0))
    return jnp.where(allowed, scores, NEVER)

def head_masks(value):
    first = lax.broadcasted_iota(jnp.int32, value.shape, 1) < HEAD_DIM
    zero = jnp.zeros_like(value)
    return (jnp.where(first, value, zero), jnp.where(first, zero, value))

def attend_forward(query_in, query_at, keys_in, key_at, value_at, valid_len, causal):
    rows, keys = (query_in.shape[0] // MICRO, keys_in.shape[0] // MICRO)
    block = min(256, rows)
    steps = rows // block
    scale = HEAD_DIM ** (-0.5)

    def kernel(len_ref, query_ref, key_ref, value_ref, out_ref, stat_ref):
        start_at = pl.program_id(2) * block
        length = len_ref[pl.program_id(0)]
        queries = head_masks((query_ref[...].astype(jnp.float32) * scale).astype(jnp.bfloat16))
        values = head_masks(value_ref[...])
        total = jnp.zeros((block, PAIR), jnp.float32)
        stats = []
        for head in range(2):
            scores = kept_scores(queries[head], key_ref[...], length, causal, start_at)
            summit = jnp.max(scores, axis=1, keepdims=True)
            expo = jnp.exp(scores - summit)
            sums = jnp.sum(expo, axis=1, keepdims=True)
            probs = (expo * (1.0 / sums)).astype(jnp.bfloat16)
            total += jnp.dot(probs, values[head], preferred_element_type=jnp.float32)
            stats.append(summit + jnp.log(sums))
        out_ref[...] = total.astype(jnp.bfloat16)
        first = lax.broadcasted_iota(jnp.int32, (block, PAIR), 1) < HEAD_DIM
        stat_ref[...] = jnp.where(first, stats[0], stats[1])

    out_spec = pl.BlockSpec((block, PAIR), lambda seq, pair, step, lens: (seq * steps + step, pair))
    return pl.pallas_call(
        kernel,
        out_shape=(
            jax.ShapeDtypeStruct((MICRO * rows, D), jnp.bfloat16),
            jax.ShapeDtypeStruct((MICRO * rows, D), jnp.float32),
        ),
        grid_spec=pltpu.PrefetchScalarGridSpec(
            num_scalar_prefetch=1,
            grid=(MICRO, D // PAIR, steps),
            in_specs=[
                pl.BlockSpec((block, PAIR), lambda seq, pair, step, lens: (seq * steps + step, query_at + pair)),
                pl.BlockSpec((keys, PAIR), lambda seq, pair, step, lens: (seq, key_at + pair)),
                pl.BlockSpec((keys, PAIR), lambda seq, pair, step, lens: (seq, value_at + pair)),
            ],
            out_specs=(out_spec, out_spec),
        ),
        compiler_params=pltpu.CompilerParams(vmem_limit_bytes=40 * 2**20),
        cost_estimate=pl.CostEstimate(flops=4*MICRO*rows*keys*D, bytes_accessed=MICRO*(rows+keys)*D*8, transcendentals=MICRO*HEADS*rows*keys),
    )(valid_len, query_in, keys_in, keys_in)

def attend_backward(query_in, query_at, keys_in, key_at, value_at, valid_len, causal, stats, grad_out, first=0, seqs=MICRO, begun=()):
    rows, keys = (query_in.shape[0] // MICRO, keys_in.shape[0] // MICRO)
    block = min(512, rows)
    steps = rows // block
    scale = HEAD_DIM ** (-0.5)

    def kernel(len_ref, query_ref, key_ref, value_ref, stat_ref, up_ref, *refs):
        dq_ref, dk_ref, dv_ref, key_sum, value_sum = refs[len(begun) :]
        step = pl.program_id(2)
        start_at = step * block
        length = len_ref[first + pl.program_id(0)]
        queries = head_masks((query_ref[...].astype(jnp.float32) * scale).astype(jnp.bfloat16))
        upstream = head_masks(up_ref[...])
        keys_each = head_masks(key_ref[...])
        grad_query = jnp.zeros((block, PAIR), jnp.float32)
        grad_key = jnp.zeros((keys, PAIR), jnp.float32)
        grad_value = jnp.zeros((keys, PAIR), jnp.float32)
        over_rows = (((0,), (0,)), ((), ()))
        for head in range(2):
            scores = kept_scores(queries[head], key_ref[...], length, causal, start_at)
            probs = jnp.exp(scores - stat_ref[:, head * HEAD_DIM : head * HEAD_DIM + 1])
            grad_probs = lax.dot_general(upstream[head], value_ref[...], (((1,), (1,)), ((), ())), preferred_element_type=jnp.float32)
            inner = jnp.sum(probs * grad_probs, axis=1, keepdims=True)
            grad_scores = (probs * (grad_probs - inner)).astype(jnp.bfloat16)
            grad_query += jnp.dot(grad_scores, keys_each[head], preferred_element_type=jnp.float32)
            grad_key += lax.dot_general(grad_scores, queries[head], over_rows, preferred_element_type=jnp.float32)
            grad_value += lax.dot_general(probs.astype(jnp.bfloat16), upstream[head], over_rows, preferred_element_type=jnp.float32)
        dq_ref[...] = (grad_query * scale).astype(jnp.bfloat16)
        if steps == 1:
            dk_ref[...] = grad_key.astype(jnp.bfloat16)
            dv_ref[...] = grad_value.astype(jnp.bfloat16)
        else:
            @pl.when(step == 0)
            def _():
                key_sum[...] = grad_key
                value_sum[...] = grad_value

            @pl.when(step > 0)
            def _():
                key_sum[...] += grad_key
                value_sum[...] += grad_value

            @pl.when(step == steps - 1)
            def _():
                dk_ref[...] = key_sum[...].astype(jnp.bfloat16)
                dv_ref[...] = value_sum[...].astype(jnp.bfloat16)

    def row_spec(at, begin):
        return pl.BlockSpec(
            (block, PAIR),
            lambda seq, pair, step, lens: ((begin + seq) * steps + step, at + pair),
        )

    def key_spec(at, begin):
        return pl.BlockSpec((keys, PAIR), lambda seq, pair, step, lens: (begin + seq, at + pair))

    return pl.pallas_call(
        kernel,
        out_shape=(
            jax.ShapeDtypeStruct((MICRO * rows, D), jnp.bfloat16),
            jax.ShapeDtypeStruct((MICRO * keys, D), jnp.bfloat16),
            jax.ShapeDtypeStruct((MICRO * keys, D), jnp.bfloat16),
        ),
        grid_spec=pltpu.PrefetchScalarGridSpec(
            num_scalar_prefetch=1,
            grid=(seqs, D // PAIR, steps),
            in_specs=[
                row_spec(query_at, first),
                key_spec(key_at, first),
                key_spec(value_at, first),
                row_spec(0, first),
                row_spec(0, first),
            ]
            + [pl.BlockSpec(memory_space=pl.ANY)] * len(begun),
            out_specs=(row_spec(0, first), key_spec(0, first), key_spec(0, first)),
            scratch_shapes=[pltpu.VMEM((keys, PAIR), jnp.float32)] * 2,
        ),
        input_output_aliases={6 + item: item for item in range(len(begun))},
        compiler_params=pltpu.CompilerParams(vmem_limit_bytes=40 * 2**20),
        cost_estimate=pl.CostEstimate(flops=10*seqs*rows*keys*D, bytes_accessed=seqs*(rows+keys)*D*16, transcendentals=seqs*HEADS*rows*keys),
    )(valid_len, query_in, keys_in, keys_in, stats, grad_out, *begun)


def norm_backward(stream, gain_row, grad_normed):
    _, pull_back = jax.vjp(rms_norm, stream, gain_row)
    return pull_back(grad_normed)


def self_forward(stream, gain_row, weight, valid_len, causal):
    normed = rms_norm(stream, gain_row).astype(jnp.bfloat16)
    joint_qkv = linear(normed, weight[:, : 3 * D]).astype(jnp.bfloat16)
    pairs = D // PAIR
    mixed_out, stats_kept = attend_forward(
        joint_qkv, 0, joint_qkv, pairs, 2 * pairs, valid_len, causal
    )
    return (
        stream + linear(mixed_out, weight[:, 3 * D :]),
        (stream, normed, joint_qkv, mixed_out, stats_kept),
    )


def self_backward(grad_stream, kept_block, gain_row, weight, valid_len, causal, between=None):
    stream, normed, joint_qkv, mixed_out, stats_kept = kept_block
    grad_low = grad_stream.astype(jnp.bfloat16)
    grad_out_w = outer_sum(mixed_out, grad_low)
    grad_mixed = linear_tr(grad_low, weight[:, 3 * D :]).astype(jnp.bfloat16)
    pairs = D // PAIR
    stages = 1 if between is None else MICRO
    grads = ()
    for stage in range(stages):
        if stage > 0:
            grad_mixed = between(grad_mixed)
        grads = attend_backward(
            joint_qkv,
            0,
            joint_qkv,
            pairs,
            2 * pairs,
            valid_len,
            causal,
            stats_kept,
            grad_mixed,
            stage * MICRO // stages,
            MICRO // stages,
            tuple(grads),
        )
    grad_joint = jnp.concatenate(grads, 1)
    if between is not None:
        grad_joint = between(grad_joint)
    grad_x, grad_gain = norm_backward(stream, gain_row, linear_tr(grad_joint, weight[:, : 3 * D]))
    return (
        grad_stream + grad_x,
        grad_gain,
        jnp.concatenate([outer_sum(normed, grad_joint), grad_out_w], 1).astype(jnp.bfloat16),
    )


def cross_forward(stream, gain_row, weight, memory, valid_len):
    normed = rms_norm(stream, gain_row).astype(jnp.bfloat16)
    query_in = linear(normed, weight[:, :D]).astype(jnp.bfloat16)
    pair_kv = linear(memory, weight[:, D : 3 * D]).astype(jnp.bfloat16)
    mixed_out, stats_kept = attend_forward(
        query_in, 0, pair_kv, 0, D // PAIR, valid_len, False
    )
    return (
        stream + linear(mixed_out, weight[:, 3 * D :]),
        (stream, normed, query_in, pair_kv, mixed_out, stats_kept),
    )


def cross_backward(grad_stream, kept_block, gain_row, weight, memory, valid_len):
    stream, normed, query_in, pair_kv, mixed_out, stats_kept = kept_block
    grad_low = grad_stream.astype(jnp.bfloat16)
    grad_out_w = outer_sum(mixed_out, grad_low)
    grad_mixed = linear_tr(grad_low, weight[:, 3 * D :]).astype(jnp.bfloat16)
    grad_query, grad_k, grad_v = attend_backward(
        query_in, 0, pair_kv, 0, D // PAIR, valid_len, False, stats_kept, grad_mixed
    )
    grad_pair = jnp.concatenate([grad_k, grad_v], 1)
    grad_weight = jnp.concatenate(
        [outer_sum(normed, grad_query), outer_sum(memory, grad_pair), grad_out_w], 1
    ).astype(jnp.bfloat16)
    grad_x, grad_gain = norm_backward(stream, gain_row, linear_tr(grad_query, weight[:, :D]))
    return (
        grad_stream + grad_x,
        grad_gain,
        grad_weight,
        linear_tr(grad_pair, weight[:, D : 3 * D]),
    )


def gelu_tanh(hidden):
    return jax.nn.gelu(hidden, approximate=True)


def ffn_forward(stream, gain_row, w_in, w_out):
    normed = rms_norm(stream, gain_row).astype(jnp.bfloat16)
    hidden = linear(normed, w_in)
    active = gelu_tanh(hidden).astype(jnp.bfloat16)
    return (stream + linear_tr(active, w_out), (stream, normed, hidden, active))


def ffn_backward(grad_stream, kept_block, gain_row, w_in, w_out):
    stream, normed, hidden, active = kept_block
    grad_low = grad_stream.astype(jnp.bfloat16)
    grad_out_w = outer_sum(grad_low, active).astype(jnp.bfloat16)
    _, pull_back = jax.vjp(gelu_tanh, hidden)
    grad_hidden = pull_back(linear(grad_low, w_out))[0].astype(jnp.bfloat16)
    grad_x, grad_gain = norm_backward(stream, gain_row, linear_tr(grad_hidden, w_in))
    return (
        grad_stream + grad_x,
        grad_gain,
        outer_sum(normed, grad_hidden).astype(jnp.bfloat16),
        grad_out_w,
    )


def forward_all(
    weights,
    gain_set,
    source_rows,
    source_len,
    target_len,
    place_rows,
    lay_decoder,
):
    stream = source_rows
    enc_kept = []
    for layer_no in range(ENC):
        stream, kept_self = self_forward(
            stream, gain_set[2 * layer_no], weights[layer_no], source_len, False
        )
        stream, kept_ffn = ffn_forward(
            stream,
            gain_set[2 * layer_no + 1],
            weights[ENC + 2 * DEC + layer_no],
            weights[2 * ENC + 3 * DEC + layer_no],
        )
        enc_kept.append((kept_self, kept_ffn))
    memory, decoded = lay_decoder(rms_norm(stream, gain_set[2 * ENC]).astype(jnp.bfloat16))
    dec_kept, exit_in, exit_rows = ([], [], [])
    for layer_no in range(DEC):
        base_at = 2 * ENC + 1 + 3 * layer_no
        decoded, kept_self = self_forward(
            decoded, gain_set[base_at], weights[ENC + layer_no], target_len, True
        )
        decoded, kept_cross = cross_forward(
            decoded, gain_set[base_at + 1], weights[ENC + DEC + layer_no], memory, source_len
        )
        decoded, kept_ffn = ffn_forward(
            decoded,
            gain_set[base_at + 2],
            weights[2 * ENC + 2 * DEC + layer_no],
            weights[3 * ENC + 3 * DEC + layer_no],
        )
        dec_kept.append((kept_self, kept_cross, kept_ffn))
        picked_rows = decoded[place_rows]
        exit_in.append(picked_rows)
        exit_rows.append(
            rms_norm(picked_rows, gain_set[2 * ENC + 1 + 3 * DEC + layer_no]).astype(jnp.bfloat16)
        )
    kept = (source_len, target_len, place_rows, enc_kept, stream, memory, dec_kept, exit_in)
    return (kept, jnp.concatenate(exit_rows, 0))


def backward_all(
    weights, gain_set, kept, exit_grads, matrix_store, gain_store, before_last, between_last
):
    source_len, target_len, place_rows, enc_kept, stream, memory, dec_kept, exit_in = kept
    exit_each = jnp.split(exit_grads, DEC, axis=0)
    grad_decoded = jnp.zeros(dec_kept[0][0][0].shape, jnp.float32)
    grad_memory = jnp.zeros(memory.shape, jnp.float32)
    for layer_no in reversed(range(DEC)):
        base_at = 2 * ENC + 1 + 3 * layer_no
        exit_at = 2 * ENC + 1 + 3 * DEC + layer_no
        grad_rows, gain_store[exit_at] = norm_backward(
            exit_in[layer_no], gain_set[exit_at], exit_each[layer_no]
        )
        grad_decoded = grad_decoded.at[place_rows].add(grad_rows)
        kept_self, kept_cross, kept_ffn = dec_kept[layer_no]
        in_at, out_at = (2 * ENC + 2 * DEC + layer_no, 3 * ENC + 3 * DEC + layer_no)
        grad_decoded, gain_store[base_at + 2], matrix_store[in_at], matrix_store[out_at] = (
            ffn_backward(
                grad_decoded, kept_ffn, gain_set[base_at + 2], weights[in_at], weights[out_at]
            )
        )
        cross_at = ENC + DEC + layer_no
        grad_decoded, gain_store[base_at + 1], matrix_store[cross_at], grad_mem = cross_backward(
            grad_decoded, kept_cross, gain_set[base_at + 1], weights[cross_at], memory, source_len
        )
        grad_memory = grad_memory + grad_mem
        grad_decoded, gain_store[base_at], matrix_store[ENC + layer_no] = self_backward(
            grad_decoded, kept_self, gain_set[base_at], weights[ENC + layer_no], target_len, True
        )
    grad_stream, gain_store[2 * ENC] = norm_backward(stream, gain_set[2 * ENC], grad_memory)
    for layer_no in reversed(range(ENC)):
        kept_self, kept_ffn = enc_kept[layer_no]
        in_at, out_at = (ENC + 2 * DEC + layer_no, 2 * ENC + 3 * DEC + layer_no)
        grad_stream, gain_store[2 * layer_no + 1], matrix_store[in_at], matrix_store[out_at] = (
            ffn_backward(
                grad_stream, kept_ffn, gain_set[2 * layer_no + 1], weights[in_at], weights[out_at]
            )
        )
        if layer_no == 0:
            grad_stream = before_last(grad_stream)
        grad_stream, gain_store[2 * layer_no], matrix_store[layer_no] = self_backward(
            grad_stream,
            kept_self,
            gain_set[2 * layer_no],
            weights[layer_no],
            source_len,
            False,
            between_last if layer_no == 0 else None,
        )
    return (grad_stream, grad_decoded)


def fold_ranked(tiles, rank_of):
    count, half = (tiles.shape[0], PB // 2)

    def kernel(rank_ref, tile_ref, out_ref):
        def one_block(tile_no, carry):
            value = tile_ref[tile_no]
            folded = jnp.concatenate([value[:half], value[half:]], axis=1)
            out_ref[rank_ref[tile_no]] = folded.astype(jnp.bfloat16)
            return carry

        lax.fori_loop(0, count, one_block, 0)

    return pl.pallas_call(
        kernel,
        out_shape=jax.ShapeDtypeStruct((count, half, 2 * PB), jnp.bfloat16),
        grid_spec=pltpu.PrefetchScalarGridSpec(
            num_scalar_prefetch=1,
            grid=(1,),
            in_specs=[pl.BlockSpec(memory_space=pltpu.VMEM)],
            out_specs=pl.BlockSpec(memory_space=pltpu.VMEM),
        ),
        compiler_params=pltpu.CompilerParams(vmem_limit_bytes=40 * 2**20),
    )(rank_of, tiles)


def unfold_ranked(folded, rank_of):
    count, half = (folded.shape[0], PB // 2)

    def kernel(rank_ref, folded_ref, out_ref):
        def one_block(tile_no, carry):
            value = folded_ref[rank_ref[tile_no]]
            out_ref[tile_no, :half] = value[:, :PB]
            out_ref[tile_no, half:] = value[:, PB:]
            return carry

        lax.fori_loop(0, count, one_block, 0)

    return pl.pallas_call(
        kernel,
        out_shape=jax.ShapeDtypeStruct((count, PB, PB), jnp.float32),
        grid_spec=pltpu.PrefetchScalarGridSpec(
            num_scalar_prefetch=1,
            grid=(1,),
            in_specs=[pl.BlockSpec(memory_space=pltpu.VMEM)],
            out_specs=pl.BlockSpec(memory_space=pltpu.VMEM),
        ),
        compiler_params=pltpu.CompilerParams(vmem_limit_bytes=40 * 2**20),
    )(rank_of, folded)


def is_encoder(mat_no):
    return (
        mat_no < ENC
        or ENC + 2 * DEC <= mat_no < 2 * ENC + 2 * DEC
        or 2 * ENC + 3 * DEC <= mat_no < 3 * ENC + 3 * DEC
    )


def is_last(mat_no):
    return mat_no == 0


def rank_blocks(slot_list, devices, is_first):
    blocks_each = D // PB * (FF // PB)
    mats = slot_list // blocks_each
    early = jnp.zeros(mats.shape, jnp.bool_)
    for mat_no in range(MATS):
        if is_first(mat_no):
            early = early | (mats == mat_no)
    early = early.reshape(devices, -1).astype(jnp.int32)
    early_count = jnp.sum(early, axis=1)
    ahead = jnp.cumsum(early, axis=1) - early
    later = early_count[:, None] + jnp.arange(early.shape[1])[None, :] - ahead
    return (jnp.where(early == 1, ahead, later), early_count)


def room_for(per_device, chosen):
    share = sum(chosen(mat_no) for mat_no in range(MATS)) / MATS
    mean = per_device * share
    return min(per_device - 1, -(-int(mean + 4.2 * math.sqrt(mean * (1 - share))) // 4) * 4)


def by_block(slot_list, values):
    width, base = (64, 128)
    height = -(-slot_list.shape[0] // width)
    rows = (slot_list[:, None] // width == jnp.arange(height)[None, :]).astype(jnp.bfloat16)
    lanes = (slot_list[:, None] % width == jnp.arange(width)[None, :]).astype(jnp.bfloat16)
    found = []
    for value in values:
        high, low = (
            outer_sum(rows * (part.astype(jnp.bfloat16))[:, None], lanes)
            for part in (value // base, value % base)
        )
        found.append((high * base + low).astype(jnp.int32).reshape(-1)[: slot_list.shape[0]])
    return found


def lay_matrices(buffers, place_of, mats):
    half = PB // 2
    row_blocks, pairs = (D // PB, FF // (2 * PB))
    sizes = [buffer.shape[0] for buffer in buffers]
    starts = [sum(sizes[:item]) for item in range(len(sizes))]
    count = len(mats)

    def kernel(place_ref, *refs):
        sources, outs = (refs[: len(sizes)], refs[len(sizes) : len(sizes) + count])
        folded_ref, made, arrived, left = refs[len(sizes) + count :]
        left_half = lax.broadcasted_iota(jnp.int32, (half, 2 * PB), 1) < PB
        fetches = [
            pltpu.make_async_copy(
                source, folded_ref.at[pl.ds(start, size)], arrived.at[item]
            )
            for item, (source, start, size) in enumerate(zip(sources, starts, sizes))
        ]
        for fetch in fetches:
            fetch.start()
        for fetch in fetches:
            fetch.wait()

        def send(item):
            return pltpu.make_async_copy(made.at[item % 2], outs[item], left.at[item % 2])

        for item, mat_no in enumerate(mats):
            if item >= 2:
                send(item - 2).wait()

            def one_row(row_no, carry, item=item, mat_no=mat_no):
                first = (mat_no * row_blocks + row_no) * 2 * pairs
                row_at = pl.multiple_of(row_no * PB, PB)
                for pair_no in range(pairs):
                    even = folded_ref[place_ref[first + 2 * pair_no]].astype(jnp.float32)
                    odd = folded_ref[place_ref[first + 2 * pair_no + 1]].astype(jnp.float32)
                    columns = slice(2 * PB * pair_no, 2 * PB * (pair_no + 1))
                    upper = jnp.where(left_half, even, pltpu.roll(odd, PB, 1))
                    lower = jnp.where(left_half, pltpu.roll(even, PB, 1), odd)
                    made[item % 2, pl.ds(row_at, half), columns] = upper.astype(jnp.bfloat16)
                    made[item % 2, pl.ds(row_at + half, half), columns] = lower.astype(jnp.bfloat16)
                return carry

            lax.fori_loop(0, row_blocks, one_row, 0)
            send(item).start()
        for item in range(max(count - 2, 0), count):
            send(item).wait()

    return pl.pallas_call(
        kernel,
        out_shape=[jax.ShapeDtypeStruct((D, FF), jnp.bfloat16)] * count,
        grid_spec=pltpu.PrefetchScalarGridSpec(
            num_scalar_prefetch=1,
            grid=(1,),
            in_specs=[pl.BlockSpec(memory_space=pl.ANY)] * len(sizes),
            out_specs=[pl.BlockSpec(memory_space=pl.ANY)] * count,
            scratch_shapes=[
                pltpu.VMEM((sum(sizes), half, 2 * PB), jnp.bfloat16),
                pltpu.VMEM((2, D, FF), jnp.bfloat16),
                pltpu.SemaphoreType.DMA((len(sizes),)),
                pltpu.SemaphoreType.DMA((2,)),
            ],
        ),
        compiler_params=pltpu.CompilerParams(vmem_limit_bytes=40 * 2**20),
    )(place_of, *buffers)


def fold_gradients(matrices, mats, place_of, sizes, begun=None):
    half = PB // 2
    row_blocks, pairs = (D // PB, FF // (2 * PB))
    count = len(mats)
    whole = sum(sizes)
    given = 0 if begun is None else 1
    skipped = 0 if begun is None else whole - begun.shape[0]
    kept = whole - skipped

    def kernel(place_ref, *refs):
        sources, old = (refs[:count], refs[count : count + given])
        outs = refs[count + given : -5]
        folded_ref, held, arrived, left, old_sem = refs[-5:]
        left_half = lax.broadcasted_iota(jnp.int32, (half, 2 * PB), 1) < PB

        def fetch(item):
            return pltpu.make_async_copy(sources[item], held.at[item % 2], arrived.at[item % 2])

        fetch(0).start()
        if given:
            before = pltpu.make_async_copy(
                old[0], folded_ref.at[pl.ds(0, kept)], old_sem.at[0]
            )
            before.start()
            before.wait()
        for item, mat_no in enumerate(mats):
            if item + 1 < count:
                fetch(item + 1).start()
            fetch(item).wait()

            def place(block, carry=None):
                spot = place_ref[block] - skipped
                return jnp.where(spot < 0, kept, spot) if given else spot

            def one_row(row_no, carry, item=item, mat_no=mat_no):
                first = (mat_no * row_blocks + row_no) * 2 * pairs
                row_at = pl.multiple_of(row_no * PB, PB)
                for pair_no in range(pairs):
                    columns = slice(2 * PB * pair_no, 2 * PB * (pair_no + 1))
                    upper = held[item % 2, pl.ds(row_at, half), columns].astype(jnp.float32)
                    lower = held[item % 2, pl.ds(row_at + half, half), columns].astype(jnp.float32)
                    even = jnp.where(left_half, upper, pltpu.roll(lower, PB, 1))
                    odd = jnp.where(left_half, pltpu.roll(upper, PB, 1), lower)
                    folded_ref[place(first + 2 * pair_no)] = even.astype(jnp.bfloat16)
                    folded_ref[place(first + 2 * pair_no + 1)] = odd.astype(jnp.bfloat16)
                return carry

            lax.fori_loop(0, row_blocks, one_row, 0)
        begin = 0
        sends = []
        for item, out in enumerate(outs):
            size = out.shape[0]
            sends.append(
                pltpu.make_async_copy(folded_ref.at[pl.ds(begin, size)], out, left.at[item])
            )
            begin += size
        for send in sends:
            send.start()
        for send in sends:
            send.wait()

    shapes = [kept] if given else list(sizes)
    return pl.pallas_call(
        kernel,
        out_shape=[jax.ShapeDtypeStruct((size, half, 2 * PB), jnp.bfloat16) for size in shapes],
        grid_spec=pltpu.PrefetchScalarGridSpec(
            num_scalar_prefetch=1,
            grid=(1,),
            in_specs=[pl.BlockSpec(memory_space=pl.ANY)] * (count + given),
            out_specs=[pl.BlockSpec(memory_space=pl.ANY)] * len(shapes),
            scratch_shapes=[
                pltpu.VMEM((kept + given, half, 2 * PB), jnp.bfloat16),
                pltpu.VMEM((2, D, FF), jnp.bfloat16),
                pltpu.SemaphoreType.DMA((2,)),
                pltpu.SemaphoreType.DMA((2,)),
                pltpu.SemaphoreType.DMA((1,)),
            ],
        ),
        compiler_params=pltpu.CompilerParams(vmem_limit_bytes=40 * 2**20),
    )(place_of, *[matrices[mat_no] for mat_no in mats], *([begun] if given else []))


def exchange_plan(dp_size, along, per_device):
    low, high = (along.bit_length() - 1, dp_size.bit_length() - 1)
    base = [low + bit for bit in range(high)] + list(range(1, low))
    third = per_device // 3
    sizes = [per_device - 2 * third, third, third]
    return [(size, base[turn:] + base[:turn]) for turn, size in enumerate(sizes)]


def places_for(ranks, plan, devices):
    per_device = sum(size for size, _ in plan)
    owner = jnp.arange(devices)[:, None]
    place = jnp.zeros_like(ranks)
    begin = 0
    for size, order in plan:
        spot = jnp.zeros_like(owner)
        for bit in order:
            spot = spot * 2 + owner // 2**bit % 2
        here = begin * (devices // 2) + spot * size + ranks - begin
        place = jnp.where((ranks >= begin) & (ranks < begin + size), here, place)
        begin += size
    return place + owner % 2 * (devices // 2 * per_device)


def halve(value, bit, devices):
    me = lax.axis_index("dp") * lax.axis_size("vocab") + lax.axis_index("vocab")

    mine = me // 2**bit % 2
    value = value.reshape(2, value.shape[0] // 2, *value.shape[1:])
    sent = lax.dynamic_index_in_dim(value, 1 - mine, 0, keepdims=False)
    kept = lax.dynamic_index_in_dim(value, mine, 0, keepdims=False)
    pairs = [(index, index ^ 2**bit) for index in range(devices)]
    arrived = lax.ppermute(sent, ("dp", "vocab"), pairs)
    return kept.astype(jnp.float32) + arrived.astype(jnp.float32)


def first_exchange(folded, devices):
    return halve(folded, 0, devices).astype(jnp.bfloat16)


def split_parts(total, plan, devices):
    parts, begin = ([], 0)
    for size, _ in plan:
        count = size * (devices // 2)
        parts.append(total[begin : begin + count])
        begin += count
    return parts


def one_exchange(parts, plan, round_no, devices):
    return [
        halve(part.astype(jnp.bfloat16), order[round_no], devices)
        for part, (_, order) in zip(parts, plan)
    ]


def other_exchanges(parts, plan, devices, done=0):
    for round_no in range(done, len(plan[0][1])):
        parts = one_exchange(parts, plan, round_no, devices)
    return jnp.concatenate(parts, 0)


def take_rows(source, index_at, kind):
    count, width, block = (index_at.shape[0], source.shape[1], 128)
    whole = -(-count // block) * block
    index_at = jnp.pad(index_at, (0, whole - count))

    def kernel(index_ref, source_ref, out_ref, held_ref):
        first = pl.program_id(0) * block

        def copy_eight(group, carry):
            base = pl.multiple_of(group * 8, 8)
            for row_no in range(8):
                held_ref[pl.ds(base + row_no, 1), :] = source_ref[
                    pl.ds(index_ref[first + base + row_no], 1), :
                ]
            return carry

        lax.fori_loop(0, block // 8, copy_eight, 0)
        out_ref[...] = held_ref[...].astype(kind)

    taken = pl.pallas_call(
        kernel,
        out_shape=jax.ShapeDtypeStruct((whole, width), kind),
        grid_spec=pltpu.PrefetchScalarGridSpec(
            num_scalar_prefetch=1,
            grid=(whole // block,),
            in_specs=[pl.BlockSpec(memory_space=pltpu.VMEM)],
            out_specs=pl.BlockSpec((block, width), lambda step, index: (step, 0)),
            scratch_shapes=[pltpu.VMEM((block, width), jnp.float32)],
        ),
        compiler_params=pltpu.CompilerParams(vmem_limit_bytes=40 * 2**20),
    )(index_at, source)
    return taken[:count]


def add_rows(rows, index_at, total):
    count, width, block = (rows.shape[0], rows.shape[1], 512)
    whole = -(-count // block) * block
    index_at = jnp.pad(index_at, (0, whole - count), constant_values=-1)[None, :]
    rows = jnp.pad(rows, ((0, whole - count), (0, 0)))
    height = total.shape[0]

    def kernel(index_ref, rows_ref, total_ref, out_ref):
        @pl.when(pl.program_id(0) == 0)
        def _():
            out_ref[...] = total_ref[...]

        hits = lax.broadcasted_iota(jnp.int32, (height, block), 0) == index_ref[...]
        out_ref[...] += jnp.dot(
            hits.astype(jnp.float32).astype(jnp.bfloat16),
            rows_ref[...],
            preferred_element_type=jnp.float32,
        )

    return pl.pallas_call(
        kernel,
        out_shape=jax.ShapeDtypeStruct(total.shape, jnp.float32),
        grid=(whole // block,),
        in_specs=[
            pl.BlockSpec((1, block), lambda step: (0, step)),
            pl.BlockSpec((block, width), lambda step: (step, 0)),
            pl.BlockSpec((height, width), lambda step: (0, 0)),
        ],
        out_specs=pl.BlockSpec((height, width), lambda step: (0, 0)),
        compiler_params=pltpu.CompilerParams(vmem_limit_bytes=40 * 2**20),
    )(index_at, rows, total)


def spread(value, axes, peers):
    return lax.all_to_all(
        jnp.broadcast_to(value[None], (peers, *value.shape)), axes, 0, 0, tiled=True
    )


def count_before(mask):
    size, width = (mask.shape[-1], 128)
    parts = mask.reshape(*mask.shape[:-1], size // width, width).astype(jnp.bfloat16)
    earlier = (jnp.arange(width)[:, None] < jnp.arange(width)[None, :]).astype(jnp.bfloat16)
    inside = jnp.einsum("...pw,wk->...pk", parts, earlier, preferred_element_type=jnp.float32)
    totals = jnp.sum(parts.astype(jnp.float32), axis=-1)
    ahead = jnp.cumsum(totals, axis=-1) - totals
    return (inside + ahead[..., None]).reshape(mask.shape).astype(jnp.int32)


def room(count, peers):
    mean = count / peers
    return min(count, -(-int(mean + 5.0 * math.sqrt(mean)) // 16) * 16)


def listed(mask, rank, values, size):
    width, base = (16, 128)
    rows = mask[..., None] & (rank[..., None] // width == jnp.arange(size // width))
    lanes = (rank[..., None] % width == jnp.arange(width)).astype(jnp.bfloat16)
    values = values + 1
    high, low = (
        jnp.einsum(
            "...th,...tl->...hl",
            jnp.where(rows, part[..., None].astype(jnp.bfloat16), 0),
            lanes,
            preferred_element_type=jnp.float32,
        )
        for part in (values // base, values % base)
    )
    return (high * base + low).astype(jnp.int32).reshape(*mask.shape[:-1], size) - 1


def rounds_needed(owner_all, peers, size):
    held = jnp.sum((owner_all[:, None, :] == jnp.arange(peers)[:, None]).astype(jnp.int32), axis=2)
    return (jnp.max(held) + size - 1) // size


def fetch_plan(table_part, tokens_all, peers_here, peer_me):
    peers, rows_each = (peers_here.shape[0], table_part.shape[0])
    count = tokens_all.shape[1]
    size = room(count, peers)
    asked = peers_here // rows_each == peer_me
    asked_rank = count_before(asked)
    own_tokens = lax.dynamic_index_in_dim(peers_here, peer_me, 0, keepdims=False)
    own_owner = own_tokens // rows_each
    own_mask = own_owner[None, :] == jnp.arange(peers)[:, None]
    own_rank = jnp.sum(jnp.where(own_mask, count_before(own_mask), 0), axis=0)

    def to_send(round_no):
        wanted = listed(
            asked, asked_rank - round_no * size, peers_here % rows_each, size
        )
        return take_rows(table_part, jnp.maximum(wanted.reshape(-1), 0), jnp.bfloat16)

    def found_in(arrived, round_no):
        rank_now = own_rank - round_no * size
        now = (rank_now >= 0) & (rank_now < size)
        found = take_rows(
            arrived.astype(jnp.float32), jnp.where(now, own_owner * size + rank_now, 0), jnp.float32
        )
        return (now, found)

    def again(round_no, rows):
        now, found = found_in(swap_rows(to_send(round_no)), round_no)
        return jnp.where(now[:, None], found, rows)

    rounds = rounds_needed(tokens_all // rows_each, peers, size)

    def finish(arrived):
        return lax.fori_loop(1, rounds, again, found_in(arrived, 0)[1])

    return (to_send(0), finish)


def swap_rows(rows):
    return lax.all_to_all(rows, "vocab", 0, 0, tiled=True)


def return_plan(tokens_all, rows_each, dp_size):
    peers, count = tokens_all.shape
    along = peers // dp_size
    quarter = rows_each // dp_size
    me = lax.axis_index("dp") * along + lax.axis_index("vocab")
    size = room(count, peers)
    owner_all = (tokens_all % rows_each) // quarter * along + tokens_all // rows_each
    arriving = owner_all == me
    arriving_rank = count_before(arriving)
    own_owner = lax.dynamic_index_in_dim(owner_all, me, 0, keepdims=False)
    leaving = own_owner[None, :] == jnp.arange(peers)[:, None]
    leaving_rank = count_before(leaving)
    place = jnp.broadcast_to(jnp.arange(count)[None, :], leaving.shape)

    def lists(round_no):
        return (
            jnp.maximum(
                listed(leaving, leaving_rank - round_no * size, place, size).reshape(-1), 0
            ),
            listed(
                arriving, arriving_rank - round_no * size, tokens_all % quarter, size
            ).reshape(-1),
        )

    return (lists, rounds_needed(owner_all, peers, size))


def return_rows(grad_rows, lists, first_lists, rounds, total, ready, landed):
    def swap_all(rows):
        return lax.all_to_all(rows, ("dp", "vocab"), 0, 0, tiled=True)

    def again(round_no, so_far):
        chosen, where = lists(round_no)
        return add_rows(swap_all(take_rows(grad_rows, chosen, jnp.bfloat16)), where, so_far)

    arrived = landed(swap_all(ready(take_rows(grad_rows, first_lists[0], jnp.bfloat16))))
    return lax.fori_loop(1, rounds, again, add_rows(arrived, first_lists[1], total))


def turn_in(left_basis, tiles, right_basis):
    half = jnp.einsum("tki,tkl->til", left_basis, tiles, precision=HIGH)
    return jnp.einsum("til,tlj->tij", half, right_basis, precision=HIGH)


def turn_out(left_basis, tiles, right_basis):
    half = jnp.einsum("tik,tkl->til", left_basis, tiles, precision=HIGH)
    return jnp.einsum("til,tjl->tij", half, right_basis, precision=HIGH)


def orthonormal(columns):
    lanes, group = (128, 4)

    def kernel(in_ref, out_ref):
        out_ref[...] = in_ref[...]

        def one_column(column_no, carry):
            pivot = out_ref[column_no]
            pivot = pivot / jnp.sqrt(jnp.sum(pivot * pivot, axis=0, keepdims=True))
            out_ref[column_no] = pivot

            def one_group(group_no, inner):
                first = group_no * group
                held = [out_ref[first + item] for item in range(group)]
                for item in range(group):
                    share = jnp.sum(pivot * held[item], axis=0, keepdims=True)
                    share = jnp.where(first + item > column_no, share, 0.0)
                    held[item] = held[item] - share * pivot
                for item in range(group):
                    out_ref[first + item] = held[item]
                return inner

            return lax.fori_loop((column_no + 1) // group, PB // group, one_group, carry)

        lax.fori_loop(0, PB, one_column, 0)

    spec = pl.BlockSpec((PB, PB, lanes), lambda step: (0, 0, step))
    return pl.pallas_call(
        kernel,
        out_shape=jax.ShapeDtypeStruct(columns.shape, jnp.float32),
        grid=(columns.shape[2] // lanes,),
        in_specs=[spec],
        out_specs=spec,
        compiler_params=pltpu.CompilerParams(vmem_limit_bytes=40 * 2**20),
    )(columns)


def renew_bases(left_stat, right_stat, left_basis, right_basis):
    moved = jnp.concatenate(
        [
            jnp.einsum("tij,tjk->tik", left_stat, left_basis, precision=HIGH),
            jnp.einsum("tij,tjk->tik", right_stat, right_basis, precision=HIGH),
        ],
        0,
    )
    count = moved.shape[0]
    whole = -(-count // 128) * 128
    columns = jnp.pad(jnp.transpose(moved, (2, 1, 0)), ((0, 0), (0, 0), (0, whole - count)))
    renewed = jnp.transpose(orthonormal(columns)[:, :, :count], (2, 1, 0))
    return (renewed[: count // 2], renewed[count // 2 :])


def soap_update(
    master,
    grad_tiles,
    grad_turned,
    left_outer,
    right_outer,
    first_mom,
    first_turned,
    second_mom,
    left_stat,
    right_stat,
    left_basis,
    right_basis,
    factor,
):
    first_new = BETA_FIRST * first_mom + (1 - BETA_FIRST) * (factor * grad_tiles)
    grad_turned = factor * grad_turned
    first_turned = BETA_FIRST * first_turned + (1 - BETA_FIRST) * grad_turned
    second_new = BETA_SECOND * second_mom + (1 - BETA_SECOND) * grad_turned * grad_turned
    direction = (
        first_turned
        / (1 - BETA_FIRST**STEP)
        / (jnp.sqrt(second_new / (1 - BETA_SECOND**STEP)) + ADAM_EPS)
    )
    master_new = master - RATE_MATRIX * (
        turn_out(left_basis, direction, right_basis) + DECAY * master
    )
    left_new = BETA_STAT * left_stat + (1 - BETA_STAT) * (factor * (factor * left_outer))
    right_new = BETA_STAT * right_stat + (1 - BETA_STAT) * (factor * (factor * right_outer))
    return (
        master_new,
        first_new,
        second_new,
        left_new,
        right_new,
        *renew_bases(left_new, right_new, left_basis, right_basis),
    )


def adamw_update(master, grad_now, first_mom, second_mom, rate, decay_by):
    first_new = BETA_FIRST * first_mom + (1 - BETA_FIRST) * grad_now
    second_new = BETA_SECOND * second_mom + (1 - BETA_SECOND) * grad_now * grad_now
    direction = (
        first_new
        / (1 - BETA_FIRST**STEP)
        / (jnp.sqrt(second_new / (1 - BETA_SECOND**STEP)) + ADAM_EPS)
    )
    return (master - rate * (direction + decay_by * master), first_new, second_new)


def per_device(
    master_tiles,
    mom1_tiles,
    mom2_tiles,
    stat_left,
    stat_right,
    basis_left,
    basis_right,
    table_master,
    table_mom1,
    table_mom2,
    gains,
    gain_mom1,
    gain_mom2,
    source_ids,
    target_ids,
    source_len,
    target_len,
    loss_place,
    exit_layer,
    slot_list,
):
    dp_size, along = (lax.axis_size("dp"), lax.axis_size("vocab"))
    dp_me, peer_me = (lax.axis_index("dp"), lax.axis_index("vocab"))
    devices = dp_size * along
    rows_each = table_master.shape[0]
    quarter = rows_each // dp_size
    source_len, target_len = (source_len[:, 0], target_len[:, 0])

    shifted = jnp.pad(target_ids[:, 0, :-1], ((0, 0), (1, 0)))
    tokens = jnp.concatenate([source_ids.reshape(-1), shifted.reshape(-1)])
    places = loss_place[:, 0]
    counted = places < target_len[:, None]
    reach = [
        jnp.sum((counted & (exit_layer[:, 0] >= layer_no)).astype(jnp.int32))
        for layer_no in range(DEC)
    ]
    labels = jnp.take_along_axis(target_ids[:, 0], places, axis=1).reshape(-1)
    row_count = MICRO * LOSS_POS
    own_facts = jnp.concatenate(
        [tokens, labels, counted.reshape(-1).astype(jnp.int32), jnp.stack(reach)]
    )
    fact_count = own_facts.shape[0]
    own_facts = jnp.pad(own_facts, (0, -fact_count % 128))
    facts = spread(own_facts, ("dp", "vocab"), devices)
    slots_later, facts, mom1_later, left_later, right_later = lax.optimization_barrier(
        (slot_list, facts, mom1_tiles, basis_left, basis_right)
    )
    tokens_all = facts[:, : tokens.shape[0]]
    after = facts[:, tokens.shape[0] :]
    labels_all = after[:, :row_count]
    counted_all = after[:, row_count : 2 * row_count].astype(jnp.float32)
    reach_all = jnp.sum(after[:, 2 * row_count : 2 * row_count + DEC].astype(jnp.float32), axis=0)
    count_all = jnp.sum(counted_all)
    fraction = reach_all / jnp.sum(reach_all)

    per_device = master_tiles.shape[0]
    me = dp_me * along + peer_me
    ranks, early_count = rank_blocks(slot_list, devices, is_encoder)
    first_size = room_for(per_device, is_encoder)
    second_size = per_device - first_size
    place_at = jnp.where(
        ranks < first_size,
        jnp.arange(devices)[:, None] * first_size + ranks,
        devices * first_size
        + jnp.arange(devices)[:, None] * second_size
        + ranks
        - first_size,
    )
    late_size = room_for(per_device, is_last)
    soon_size = per_device - late_size
    back_ranks, soon_count = rank_blocks(slots_later, devices, lambda mat_no: not is_last(mat_no))
    soon_plan = exchange_plan(dp_size, along, soon_size)
    late_plan = exchange_plan(dp_size, along, late_size)
    back_at = jnp.where(
        back_ranks < soon_size,
        places_for(back_ranks, soon_plan, devices),
        devices * soon_size + places_for(back_ranks - soon_size, late_plan, devices),
    )
    place_of, back_of = by_block(slots_later, [place_at.reshape(-1), back_at.reshape(-1)])
    own_folded = fold_ranked(
        master_tiles, lax.dynamic_index_in_dim(ranks, me, 0, keepdims=False)
    )
    src_count, tgt_count = (source_ids.shape[2], target_ids.shape[2])

    def planned(first, length):
        ids_all = tokens_all[:, first : first + MICRO * length]
        peers_here = lax.dynamic_slice_in_dim(ids_all, dp_me * along, along, 0)
        return fetch_plan(table_master, ids_all, peers_here, peer_me)

    source_sent, source_finish = planned(0, src_count)
    target_sent, target_finish = planned(MICRO * src_count, tgt_count)
    first_tiles = lax.all_gather(own_folded[:first_size], ("dp", "vocab"), axis=0, tiled=True)
    own_second, first_tiles, source_arrived = lax.optimization_barrier(
        (own_folded[first_size:], first_tiles, swap_rows(source_sent))
    )
    second_tiles = lax.all_gather(own_second, ("dp", "vocab"), axis=0, tiled=True)
    encoder_mats = [mat_no for mat_no in range(MATS) if is_encoder(mat_no)]
    decoder_mats = [mat_no for mat_no in range(MATS) if not is_encoder(mat_no)]

    def lay_with_all():
        others = lax.all_gather(own_second, ("dp", "vocab"), axis=0, tiled=True)
        return lay_matrices([first_tiles, others], place_of, encoder_mats)

    def lay_with_first():
        return lay_matrices([first_tiles], place_of, encoder_mats)

    encoder_set = lax.cond(
        jnp.max(early_count) > first_size, lay_with_all, lay_with_first
    )
    weights = [None] * MATS
    for mat_no, matrix in zip(encoder_mats, encoder_set):
        weights[mat_no] = matrix

    def lay_decoder(memory):
        held, tiles, arrived = lax.optimization_barrier((memory, second_tiles, target_arrived))
        decoder_set = lay_matrices([first_tiles, tiles], place_of, decoder_mats)
        for mat_no, matrix in zip(decoder_mats, decoder_set):
            weights[mat_no] = matrix
        return (held, with_waves(target_finish(arrived), tgt_count))

    wave_set = waves(src_count, D)

    def with_waves(rows, length):
        return rows * math.sqrt(D) + jnp.tile(wave_set[:length], (MICRO, 1))

    lists, rounds = return_plan(tokens_all, rows_each, dp_size)
    source_rows = with_waves(source_finish(source_arrived), src_count)
    first_turned = turn_in(left_later, mom1_later, right_later)
    source_rows, first_lists, first_turned, target_sent = lax.optimization_barrier(
        (source_rows, lists(0), first_turned, target_sent)
    )
    target_arrived = swap_rows(target_sent)

    place_rows = (places + jnp.arange(MICRO)[:, None] * tgt_count).reshape(-1)
    kept, exit_rows = forward_all(
        weights,
        gains,
        source_rows,
        source_len,
        target_len,
        place_rows,
        lay_decoder,
    )

    table_low_part = table_master.astype(jnp.bfloat16)
    exit_count = DEC * row_count
    exit_all = lax.all_gather(exit_rows, ("dp", "vocab"), axis=0, tiled=True)
    exit_here = spread(exit_rows, "vocab", along).reshape(-1, D)
    label_rows = jnp.tile(labels_all, (1, DEC)).reshape(-1)
    weight_rows = (
        jnp.repeat(fraction, row_count)[None, :] * jnp.tile(counted_all, (1, DEC))
    ).reshape(-1)
    group_rows = along * exit_count
    group_at = dp_me * group_rows
    label_here = lax.dynamic_slice_in_dim(label_rows, group_at, group_rows, 0)
    weight_here = lax.dynamic_slice_in_dim(weight_rows, group_at, group_rows, 0)
    logits = linear_tr(exit_here, table_low_part)
    hit_here = label_here[:, None] - peer_me * rows_each == jnp.arange(rows_each)[None, :]
    summit = jnp.max(logits, axis=1)
    spread_part = jnp.sum(jnp.exp(logits - summit[:, None]), axis=1)
    picked_part = jnp.sum(jnp.where(hit_here, logits, 0.0), axis=1)
    stats = spread(
        jnp.stack([summit, spread_part, picked_part]), ("dp", "vocab"), devices
    ).reshape(dp_size, along, 3, group_rows)
    summit_all = jnp.max(stats[:, :, 0], axis=1)
    total_all = jnp.sum(stats[:, :, 1] * jnp.exp(stats[:, :, 0] - summit_all[:, None]), axis=1)
    spread_all = summit_all + jnp.log(total_all)
    picked_all = jnp.sum(stats[:, :, 2], axis=1)
    loss_sum = jnp.sum(weight_rows * (spread_all - picked_all).reshape(-1))
    spread_here = lax.dynamic_index_in_dim(spread_all, dp_me, 0, keepdims=False)

    def logit_grads(logit_set, spread, weight_set, hits):
        return (
            (weight_set / count_all)[:, None]
            * (jnp.exp(logit_set - spread[:, None]) - hits.astype(jnp.float32))
        ).astype(jnp.bfloat16)

    grads_here = logit_grads(logits, spread_here, weight_here, hit_here)
    grad_parts = linear(grads_here, table_low_part).astype(jnp.bfloat16)
    grad_parts = lax.all_to_all(grad_parts, "vocab", 0, 0, tiled=True)
    exit_grads = jnp.sum(
        grad_parts.reshape(along, exit_count, D).astype(jnp.float32), axis=0
    )

    matrix_store = [None] * MATS
    gain_store = [None] * GAINS
    first_row = peer_me * rows_each + dp_me * quarter
    table_quarter = lax.dynamic_slice_in_dim(table_low_part, dp_me * quarter, quarter, 0)
    hit_quarter = label_rows[:, None] - first_row == jnp.arange(quarter)[None, :]
    grads_quarter = logit_grads(
        linear_tr(exit_all, table_quarter), spread_all.reshape(-1), weight_rows, hit_quarter
    )
    grad_quarter = outer_sum(grads_quarter, exit_all)
    soon_mats = [mat_no for mat_no in range(MATS) if not is_last(mat_no)]
    late_mats = [mat_no for mat_no in range(MATS) if is_last(mat_no)]
    both = [devices * soon_size, devices * late_size]
    held = {}

    def before_last(grad_stream):
        blocks, held["begun"] = fold_gradients(matrix_store, soon_mats, back_of, both)
        grad_stream, blocks, held["quarter"] = lax.optimization_barrier(
            (grad_stream, blocks, grad_quarter)
        )
        held["total"] = first_exchange(blocks, devices)
        return grad_stream

    def between_last(value):
        if "parts" not in held:
            value, total = lax.optimization_barrier((value, held["total"]))
            held["parts"], held["done"] = (split_parts(total, soon_plan, devices), 0)
        elif held["done"] < len(soon_plan[0][1]):
            parts = one_exchange(held["parts"], soon_plan, held["done"], devices)
            value, held["parts"] = lax.optimization_barrier((value, parts))
            held["done"] += 1
        return value

    grad_source, grad_target = backward_all(
        weights,
        gains,
        kept,
        exit_grads,
        matrix_store,
        gain_store,
        before_last,
        between_last,
    )

    grad_source = between_last(grad_source)
    grad_rows = jnp.concatenate([grad_source, grad_target], 0) * math.sqrt(D)
    grad_rows = between_last(grad_rows)
    [late_blocks] = fold_gradients(matrix_store, late_mats, back_of, both, held["begun"])
    late_parts = split_parts(first_exchange(late_blocks, devices), late_plan, devices)
    late_parts = one_exchange(late_parts, late_plan, 0, devices)

    late_sum = other_exchanges(late_parts, late_plan, devices, 1)

    def exchange_again():
        blocks, _ = fold_gradients(matrix_store, list(range(MATS)), back_of, both)
        parts = split_parts(first_exchange(blocks, devices), soon_plan, devices)
        return other_exchanges(parts, soon_plan, devices)

    share = -(-GAINS * D // (devices * 128)) * 128
    gain_flat = jnp.stack(gain_store).reshape(-1)
    gain_flat = jnp.pad(gain_flat, (0, devices * share - GAINS * D)).reshape(devices, share)

    def ready(rows):
        sums = other_exchanges(held["parts"], soon_plan, devices, held["done"])
        rows, sums, late, held["gains"] = lax.optimization_barrier(
            (rows, sums, late_sum, gain_flat)
        )
        sums = lax.cond(jnp.min(soon_count) < soon_size, exchange_again, lambda: sums)
        owned_grad = unfold_ranked(
            jnp.concatenate([sums, late], 0),
            lax.dynamic_index_in_dim(back_ranks, me, 0, keepdims=False),
        )
        held["owned"] = (
            owned_grad,
            turn_in(basis_left, owned_grad, basis_right),
            jnp.einsum("tik,tjk->tij", owned_grad, owned_grad, precision=HIGH),
            jnp.einsum("tki,tkj->tij", owned_grad, owned_grad, precision=HIGH),
            jnp.sum(owned_grad * owned_grad),
        )
        return rows

    def landed(arrived):
        arrived, held["owned"] = lax.optimization_barrier((arrived, held["owned"]))
        return arrived

    grad_quarter = return_rows(
        grad_rows, lists, first_lists, rounds, held["quarter"], ready, landed
    )

    owned_grad, owned_turned, left_outer, right_outer, owned_squares = held["owned"]
    squares = owned_squares + jnp.sum(grad_quarter * grad_quarter)
    square_total = jnp.sum(
        spread(jnp.full((1, 128), squares), ("dp", "vocab"), devices)[:, 0, 0]
    )
    gain_part = jnp.sum(
        lax.all_to_all(held["gains"], ("dp", "vocab"), 0, 0, tiled=True), axis=0
    )
    gain_total = spread(gain_part[None], ("dp", "vocab"), devices).reshape(-1)[: GAINS * D]
    gain_total = gain_total.reshape(GAINS, D)
    grad_norm = jnp.sqrt(square_total + jnp.sum(gain_total * gain_total))
    factor = jnp.minimum(1.0, CLIP_AT / grad_norm)
    table_grad = lax.all_gather(
        grad_quarter.astype(jnp.bfloat16), "dp", axis=0, tiled=True
    ).astype(jnp.float32)
    master_new, mom1_new, mom2_new, left_new, right_new, bleft_new, bright_new = soap_update(
        master_tiles,
        owned_grad,
        owned_turned,
        left_outer,
        right_outer,
        mom1_tiles,
        first_turned,
        mom2_tiles,
        stat_left,
        stat_right,
        basis_left,
        basis_right,
        factor,
    )
    table_new, table_m, table_v = adamw_update(
        table_master, table_grad * factor, table_mom1, table_mom2, RATE_MATRIX, DECAY
    )
    gains_new, gains_m, gains_v = adamw_update(
        gains, gain_total * factor, gain_mom1, gain_mom2, RATE_VECTOR, 0.0
    )
    return (
        loss_sum,
        count_all,
        grad_norm,
        master_new,
        master_new.astype(jnp.bfloat16),
        mom1_new,
        mom2_new,
        left_new,
        right_new,
        bleft_new,
        bright_new,
        table_new,
        table_new.astype(jnp.bfloat16),
        table_m,
        table_v,
        gains_new,
        gains_m,
        gains_v,
    )


def solution(mesh):
    placed = (
        P(("dp", "vocab"), None, None),
        P(("dp", "vocab"), None, None),
        P(("dp", "vocab"), None, None),
        P(("dp", "vocab"), None, None),
        P(("dp", "vocab"), None, None),
        P(("dp", "vocab"), None, None),
        P(("dp", "vocab"), None, None),
        P("vocab", None),
        P("vocab", None),
        P("vocab", None),
        P(),
        P(),
        P(),
        P(None, ("dp", "vocab"), None),
        P(None, ("dp", "vocab"), None),
        P(None, ("dp", "vocab")),
        P(None, ("dp", "vocab")),
        P(None, ("dp", "vocab"), None),
        P(None, ("dp", "vocab"), None),
        P(),
    )
    return jax.shard_map(
        per_device,
        mesh=mesh,
        in_specs=placed,
        out_specs=(
            P(),
            P(),
            P(),
            P(("dp", "vocab"), None, None),
            P(("dp", "vocab"), None, None),
            P(("dp", "vocab"), None, None),
            P(("dp", "vocab"), None, None),
            P(("dp", "vocab"), None, None),
            P(("dp", "vocab"), None, None),
            P(("dp", "vocab"), None, None),
            P(("dp", "vocab"), None, None),
            P("vocab", None),
            P("vocab", None),
            P("vocab", None),
            P("vocab", None),
            P(),
            P(),
            P(),
        ),
        check_vma=False,
    )
```

```python
import math

import jax
import jax.numpy as jnp
from jax import lax
from jax.experimental import pallas as pl
from jax.experimental.pallas import tpu as pltpu
from jax.sharding import PartitionSpec as P

D = 512
HEADS = 8
HEAD_DIM = 64
FF = 2048
ENC = 1
DEC = 2
MICRO = 2
LOSS_POS = 16
PB = 64
STEP = 10
MATS = 11
GAINS = 11


HIGH = lax.Precision.HIGH
NORM_EPS = 1e-06
CLIP_AT = 0.02
RATE_MATRIX = 0.1
RATE_VECTOR = 0.8
BETA_FIRST = 0.9
BETA_SECOND = 0.95
BETA_STAT = 0.95
ADAM_EPS = 1e-08
DECAY = 0.01


def rms_norm(stream, gain_row):
    return (
        stream * lax.rsqrt(jnp.mean(stream * stream, axis=-1, keepdims=True) + NORM_EPS) * gain_row
    )


def waves(length, columns):
    place_at = jnp.arange(length).astype(jnp.float32)[:, None]
    rate_at = jnp.exp(
        jnp.arange(columns // 2).astype(jnp.float32) * (-2.0 * math.log(10000.0) / columns)
    )
    angle = place_at * rate_at[None, :]
    return jnp.concatenate([jnp.sin(angle), jnp.cos(angle)], axis=1)


def linear(left_op, right_op):
    return jnp.dot(left_op, right_op, preferred_element_type=jnp.float32)


def linear_tr(left_op, right_op):
    return lax.dot_general(
        left_op, right_op, (((1,), (1,)), ((), ())), preferred_element_type=jnp.float32
    )


def outer_sum(left_op, right_op):
    return lax.dot_general(
        left_op, right_op, (((0,), (0,)), ((), ())), preferred_element_type=jnp.float32
    )


def split_heads(matrix):
    return matrix.reshape(matrix.shape[0], HEADS, HEAD_DIM)


NEVER=-1000000000.0
PAIR=2*HEAD_DIM
def kept_scores(query, keys, valid_len, causal, start_at):
    scores = lax.dot_general(query, keys, (((1,), (1,)), ((), ())), preferred_element_type=jnp.float32)
    key_at = lax.broadcasted_iota(jnp.int32, scores.shape if causal else (1, scores.shape[1]), 1)
    allowed = key_at < valid_len
    if causal:
        allowed = allowed & (key_at <= start_at + lax.broadcasted_iota(jnp.int32, scores.shape, 0))
    return jnp.where(allowed, scores, NEVER)

def head_masks(value):
    first = lax.broadcasted_iota(jnp.int32, value.shape, 1) < HEAD_DIM
    zero = jnp.zeros_like(value)
    return (jnp.where(first, value, zero), jnp.where(first, zero, value))

def attend_forward(query_in, query_at, keys_in, key_at, value_at, valid_len, causal):
    rows, keys = (query_in.shape[0] // MICRO, keys_in.shape[0] // MICRO)
    block = min(256, rows)
    steps = rows // block
    scale = HEAD_DIM ** (-0.5)

    def kernel(len_ref, query_ref, key_ref, value_ref, out_ref, stat_ref):
        start_at = pl.program_id(2) * block
        length = len_ref[pl.program_id(0)]
        queries = head_masks((query_ref[...].astype(jnp.float32) * scale).astype(jnp.bfloat16))
        values = head_masks(value_ref[...])
        total = jnp.zeros((block, PAIR), jnp.float32)
        stats = []
        for head in range(2):
            scores = kept_scores(queries[head], key_ref[...], length, causal, start_at)
            summit = jnp.max(scores, axis=1, keepdims=True)
            expo = jnp.exp(scores - summit)
            sums = jnp.sum(expo, axis=1, keepdims=True)
            probs = (expo * (1.0 / sums)).astype(jnp.bfloat16)
            total += jnp.dot(probs, values[head], preferred_element_type=jnp.float32)
            stats.append(summit + jnp.log(sums))
        out_ref[...] = total.astype(jnp.bfloat16)
        first = lax.broadcasted_iota(jnp.int32, (block, PAIR), 1) < HEAD_DIM
        stat_ref[...] = jnp.where(first, stats[0], stats[1])

    out_spec = pl.BlockSpec((block, PAIR), lambda seq, pair, step, lens: (seq * steps + step, pair))
    return pl.pallas_call(
        kernel,
        out_shape=(
            jax.ShapeDtypeStruct((MICRO * rows, D), jnp.bfloat16),
            jax.ShapeDtypeStruct((MICRO * rows, D), jnp.float32),
        ),
        grid_spec=pltpu.PrefetchScalarGridSpec(
            num_scalar_prefetch=1,
            grid=(MICRO, D // PAIR, steps),
            in_specs=[
                pl.BlockSpec((block, PAIR), lambda seq, pair, step, lens: (seq * steps + step, query_at + pair)),
                pl.BlockSpec((keys, PAIR), lambda seq, pair, step, lens: (seq, key_at + pair)),
                pl.BlockSpec((keys, PAIR), lambda seq, pair, step, lens: (seq, value_at + pair)),
            ],
            out_specs=(out_spec, out_spec),
        ),
        compiler_params=pltpu.CompilerParams(vmem_limit_bytes=40 * 2**20),
        cost_estimate=pl.CostEstimate(flops=4*MICRO*rows*keys*D, bytes_accessed=MICRO*(rows+keys)*D*8, transcendentals=MICRO*HEADS*rows*keys),
    )(valid_len, query_in, keys_in, keys_in)

def attend_backward(query_in, query_at, keys_in, key_at, value_at, valid_len, causal, stats, grad_out, first=0, seqs=MICRO, begun=()):
    rows, keys = (query_in.shape[0] // MICRO, keys_in.shape[0] // MICRO)
    block = min(512, rows)
    steps = rows // block
    scale = HEAD_DIM ** (-0.5)

    def kernel(len_ref, query_ref, key_ref, value_ref, stat_ref, up_ref, *refs):
        dq_ref, dk_ref, dv_ref, key_sum, value_sum = refs[len(begun) :]
        step = pl.program_id(2)
        start_at = step * block
        length = len_ref[first + pl.program_id(0)]
        queries = head_masks((query_ref[...].astype(jnp.float32) * scale).astype(jnp.bfloat16))
        upstream = head_masks(up_ref[...])
        keys_each = head_masks(key_ref[...])
        grad_query = jnp.zeros((block, PAIR), jnp.float32)
        grad_key = jnp.zeros((keys, PAIR), jnp.float32)
        grad_value = jnp.zeros((keys, PAIR), jnp.float32)
        over_rows = (((0,), (0,)), ((), ()))
        for head in range(2):
            scores = kept_scores(queries[head], key_ref[...], length, causal, start_at)
            probs = jnp.exp(scores - stat_ref[:, head * HEAD_DIM : head * HEAD_DIM + 1])
            grad_probs = lax.dot_general(upstream[head], value_ref[...], (((1,), (1,)), ((), ())), preferred_element_type=jnp.float32)
            inner = jnp.sum(probs * grad_probs, axis=1, keepdims=True)
            grad_scores = (probs * (grad_probs - inner)).astype(jnp.bfloat16)
            grad_query += jnp.dot(grad_scores, keys_each[head], preferred_element_type=jnp.float32)
            grad_key += lax.dot_general(grad_scores, queries[head], over_rows, preferred_element_type=jnp.float32)
            grad_value += lax.dot_general(probs.astype(jnp.bfloat16), upstream[head], over_rows, preferred_element_type=jnp.float32)
        dq_ref[...] = (grad_query * scale).astype(jnp.bfloat16)
        if steps == 1:
            dk_ref[...] = grad_key.astype(jnp.bfloat16)
            dv_ref[...] = grad_value.astype(jnp.bfloat16)
        else:
            @pl.when(step == 0)
            def _():
                key_sum[...] = grad_key
                value_sum[...] = grad_value

            @pl.when(step > 0)
            def _():
                key_sum[...] += grad_key
                value_sum[...] += grad_value

            @pl.when(step == steps - 1)
            def _():
                dk_ref[...] = key_sum[...].astype(jnp.bfloat16)
                dv_ref[...] = value_sum[...].astype(jnp.bfloat16)

    def row_spec(at, begin):
        return pl.BlockSpec(
            (block, PAIR),
            lambda seq, pair, step, lens: ((begin + seq) * steps + step, at + pair),
        )

    def key_spec(at, begin):
        return pl.BlockSpec((keys, PAIR), lambda seq, pair, step, lens: (begin + seq, at + pair))

    return pl.pallas_call(
        kernel,
        out_shape=(
            jax.ShapeDtypeStruct((MICRO * rows, D), jnp.bfloat16),
            jax.ShapeDtypeStruct((MICRO * keys, D), jnp.bfloat16),
            jax.ShapeDtypeStruct((MICRO * keys, D), jnp.bfloat16),
        ),
        grid_spec=pltpu.PrefetchScalarGridSpec(
            num_scalar_prefetch=1,
            grid=(seqs, D // PAIR, steps),
            in_specs=[
                row_spec(query_at, first),
                key_spec(key_at, first),
                key_spec(value_at, first),
                row_spec(0, first),
                row_spec(0, first),
            ]
            + [pl.BlockSpec(memory_space=pl.ANY)] * len(begun),
            out_specs=(row_spec(0, first), key_spec(0, first), key_spec(0, first)),
            scratch_shapes=[pltpu.VMEM((keys, PAIR), jnp.float32)] * 2,
        ),
        input_output_aliases={6 + item: item for item in range(len(begun))},
        compiler_params=pltpu.CompilerParams(vmem_limit_bytes=40 * 2**20),
        cost_estimate=pl.CostEstimate(flops=10*seqs*rows*keys*D, bytes_accessed=seqs*(rows+keys)*D*16, transcendentals=seqs*HEADS*rows*keys),
    )(valid_len, query_in, keys_in, keys_in, stats, grad_out, *begun)


def norm_backward(stream, gain_row, grad_normed):
    _, pull_back = jax.vjp(rms_norm, stream, gain_row)
    return pull_back(grad_normed)


def self_forward(stream, gain_row, weight, valid_len, causal):
    normed = rms_norm(stream, gain_row).astype(jnp.bfloat16)
    joint_qkv = linear(normed, weight[:, : 3 * D]).astype(jnp.bfloat16)
    pairs = D // PAIR
    mixed_out, stats_kept = attend_forward(
        joint_qkv, 0, joint_qkv, pairs, 2 * pairs, valid_len, causal
    )
    return (
        stream + linear(mixed_out, weight[:, 3 * D :]),
        (stream, normed, joint_qkv, mixed_out, stats_kept),
    )


def self_backward(grad_stream, kept_block, gain_row, weight, valid_len, causal, between=None):
    stream, normed, joint_qkv, mixed_out, stats_kept = kept_block
    grad_low = grad_stream.astype(jnp.bfloat16)
    grad_out_w = outer_sum(mixed_out, grad_low)
    grad_mixed = linear_tr(grad_low, weight[:, 3 * D :]).astype(jnp.bfloat16)
    pairs = D // PAIR
    stages = 1 if between is None else MICRO
    grads = ()
    for stage in range(stages):
        if stage > 0:
            grad_mixed = between(grad_mixed)
        grads = attend_backward(
            joint_qkv,
            0,
            joint_qkv,
            pairs,
            2 * pairs,
            valid_len,
            causal,
            stats_kept,
            grad_mixed,
            stage * MICRO // stages,
            MICRO // stages,
            tuple(grads),
        )
    grad_joint = jnp.concatenate(grads, 1)
    if between is not None:
        grad_joint = between(grad_joint)
    grad_x, grad_gain = norm_backward(stream, gain_row, linear_tr(grad_joint, weight[:, : 3 * D]))
    return (
        grad_stream + grad_x,
        grad_gain,
        jnp.concatenate([outer_sum(normed, grad_joint), grad_out_w], 1).astype(jnp.bfloat16),
    )


def cross_forward(stream, gain_row, weight, memory, valid_len):
    normed = rms_norm(stream, gain_row).astype(jnp.bfloat16)
    query_in = linear(normed, weight[:, :D]).astype(jnp.bfloat16)
    pair_kv = linear(memory, weight[:, D : 3 * D]).astype(jnp.bfloat16)
    mixed_out, stats_kept = attend_forward(
        query_in, 0, pair_kv, 0, D // PAIR, valid_len, False
    )
    return (
        stream + linear(mixed_out, weight[:, 3 * D :]),
        (stream, normed, query_in, pair_kv, mixed_out, stats_kept),
    )


def cross_backward(grad_stream, kept_block, gain_row, weight, memory, valid_len):
    stream, normed, query_in, pair_kv, mixed_out, stats_kept = kept_block
    grad_low = grad_stream.astype(jnp.bfloat16)
    grad_out_w = outer_sum(mixed_out, grad_low)
    grad_mixed = linear_tr(grad_low, weight[:, 3 * D :]).astype(jnp.bfloat16)
    grad_query, grad_k, grad_v = attend_backward(
        query_in, 0, pair_kv, 0, D // PAIR, valid_len, False, stats_kept, grad_mixed
    )
    grad_pair = jnp.concatenate([grad_k, grad_v], 1)
    grad_weight = jnp.concatenate(
        [outer_sum(normed, grad_query), outer_sum(memory, grad_pair), grad_out_w], 1
    ).astype(jnp.bfloat16)
    grad_x, grad_gain = norm_backward(stream, gain_row, linear_tr(grad_query, weight[:, :D]))
    return (
        grad_stream + grad_x,
        grad_gain,
        grad_weight,
        linear_tr(grad_pair, weight[:, D : 3 * D]),
    )


def gelu_tanh(hidden):
    return jax.nn.gelu(hidden, approximate=True)


def ffn_forward(stream, gain_row, w_in, w_out):
    normed = rms_norm(stream, gain_row).astype(jnp.bfloat16)
    hidden = linear(normed, w_in)
    active = gelu_tanh(hidden).astype(jnp.bfloat16)
    return (stream + linear_tr(active, w_out), (stream, normed, hidden, active))


def ffn_backward(grad_stream, kept_block, gain_row, w_in, w_out):
    stream, normed, hidden, active = kept_block
    grad_low = grad_stream.astype(jnp.bfloat16)
    grad_out_w = outer_sum(grad_low, active).astype(jnp.bfloat16)
    _, pull_back = jax.vjp(gelu_tanh, hidden)
    grad_hidden = pull_back(linear(grad_low, w_out))[0].astype(jnp.bfloat16)
    grad_x, grad_gain = norm_backward(stream, gain_row, linear_tr(grad_hidden, w_in))
    return (
        grad_stream + grad_x,
        grad_gain,
        outer_sum(normed, grad_hidden).astype(jnp.bfloat16),
        grad_out_w,
    )


def forward_all(
    weights,
    gain_set,
    source_rows,
    source_len,
    target_len,
    place_rows,
    lay_decoder,
):
    stream = source_rows
    enc_kept = []
    for layer_no in range(ENC):
        stream, kept_self = self_forward(
            stream, gain_set[2 * layer_no], weights[layer_no], source_len, False
        )
        stream, kept_ffn = ffn_forward(
            stream,
            gain_set[2 * layer_no + 1],
            weights[ENC + 2 * DEC + layer_no],
            weights[2 * ENC + 3 * DEC + layer_no],
        )
        enc_kept.append((kept_self, kept_ffn))
    memory, decoded = lay_decoder(rms_norm(stream, gain_set[2 * ENC]).astype(jnp.bfloat16))
    dec_kept, exit_in, exit_rows = ([], [], [])
    for layer_no in range(DEC):
        base_at = 2 * ENC + 1 + 3 * layer_no
        decoded, kept_self = self_forward(
            decoded, gain_set[base_at], weights[ENC + layer_no], target_len, True
        )
        decoded, kept_cross = cross_forward(
            decoded, gain_set[base_at + 1], weights[ENC + DEC + layer_no], memory, source_len
        )
        decoded, kept_ffn = ffn_forward(
            decoded,
            gain_set[base_at + 2],
            weights[2 * ENC + 2 * DEC + layer_no],
            weights[3 * ENC + 3 * DEC + layer_no],
        )
        dec_kept.append((kept_self, kept_cross, kept_ffn))
        picked_rows = decoded[place_rows]
        exit_in.append(picked_rows)
        exit_rows.append(
            rms_norm(picked_rows, gain_set[2 * ENC + 1 + 3 * DEC + layer_no]).astype(jnp.bfloat16)
        )
    kept = (source_len, target_len, place_rows, enc_kept, stream, memory, dec_kept, exit_in)
    return (kept, jnp.concatenate(exit_rows, 0))


def backward_all(
    weights, gain_set, kept, exit_grads, matrix_store, gain_store, before_last, between_last
):
    source_len, target_len, place_rows, enc_kept, stream, memory, dec_kept, exit_in = kept
    exit_each = jnp.split(exit_grads, DEC, axis=0)
    grad_decoded = jnp.zeros(dec_kept[0][0][0].shape, jnp.float32)
    grad_memory = jnp.zeros(memory.shape, jnp.float32)
    for layer_no in reversed(range(DEC)):
        base_at = 2 * ENC + 1 + 3 * layer_no
        exit_at = 2 * ENC + 1 + 3 * DEC + layer_no
        grad_rows, gain_store[exit_at] = norm_backward(
            exit_in[layer_no], gain_set[exit_at], exit_each[layer_no]
        )
        grad_decoded = grad_decoded.at[place_rows].add(grad_rows)
        kept_self, kept_cross, kept_ffn = dec_kept[layer_no]
        in_at, out_at = (2 * ENC + 2 * DEC + layer_no, 3 * ENC + 3 * DEC + layer_no)
        grad_decoded, gain_store[base_at + 2], matrix_store[in_at], matrix_store[out_at] = (
            ffn_backward(
                grad_decoded, kept_ffn, gain_set[base_at + 2], weights[in_at], weights[out_at]
            )
        )
        cross_at = ENC + DEC + layer_no
        grad_decoded, gain_store[base_at + 1], matrix_store[cross_at], grad_mem = cross_backward(
            grad_decoded, kept_cross, gain_set[base_at + 1], weights[cross_at], memory, source_len
        )
        grad_memory = grad_memory + grad_mem
        grad_decoded, gain_store[base_at], matrix_store[ENC + layer_no] = self_backward(
            grad_decoded, kept_self, gain_set[base_at], weights[ENC + layer_no], target_len, True
        )
    grad_stream, gain_store[2 * ENC] = norm_backward(stream, gain_set[2 * ENC], grad_memory)
    for layer_no in reversed(range(ENC)):
        kept_self, kept_ffn = enc_kept[layer_no]
        in_at, out_at = (ENC + 2 * DEC + layer_no, 2 * ENC + 3 * DEC + layer_no)
        grad_stream, gain_store[2 * layer_no + 1], matrix_store[in_at], matrix_store[out_at] = (
            ffn_backward(
                grad_stream, kept_ffn, gain_set[2 * layer_no + 1], weights[in_at], weights[out_at]
            )
        )
        if layer_no == 0:
            grad_stream = before_last(grad_stream)
        grad_stream, gain_store[2 * layer_no], matrix_store[layer_no] = self_backward(
            grad_stream,
            kept_self,
            gain_set[2 * layer_no],
            weights[layer_no],
            source_len,
            False,
            between_last if layer_no == 0 else None,
        )
    return (grad_stream, grad_decoded)


def fold_ranked(tiles, rank_of):
    count, half = (tiles.shape[0], PB // 2)

    def kernel(rank_ref, tile_ref, out_ref):
        def one_block(tile_no, carry):
            value = tile_ref[tile_no]
            folded = jnp.concatenate([value[:half], value[half:]], axis=1)
            out_ref[rank_ref[tile_no]] = folded.astype(jnp.bfloat16)
            return carry

        lax.fori_loop(0, count, one_block, 0)

    return pl.pallas_call(
        kernel,
        out_shape=jax.ShapeDtypeStruct((count, half, 2 * PB), jnp.bfloat16),
        grid_spec=pltpu.PrefetchScalarGridSpec(
            num_scalar_prefetch=1,
            grid=(1,),
            in_specs=[pl.BlockSpec(memory_space=pltpu.VMEM)],
            out_specs=pl.BlockSpec(memory_space=pltpu.VMEM),
        ),
        compiler_params=pltpu.CompilerParams(vmem_limit_bytes=40 * 2**20),
    )(rank_of, tiles)


def unfold_ranked(folded, rank_of):
    count, half = (folded.shape[0], PB // 2)

    def kernel(rank_ref, folded_ref, out_ref):
        def one_block(tile_no, carry):
            value = folded_ref[rank_ref[tile_no]]
            out_ref[tile_no, :half] = value[:, :PB]
            out_ref[tile_no, half:] = value[:, PB:]
            return carry

        lax.fori_loop(0, count, one_block, 0)

    return pl.pallas_call(
        kernel,
        out_shape=jax.ShapeDtypeStruct((count, PB, PB), jnp.float32),
        grid_spec=pltpu.PrefetchScalarGridSpec(
            num_scalar_prefetch=1,
            grid=(1,),
            in_specs=[pl.BlockSpec(memory_space=pltpu.VMEM)],
            out_specs=pl.BlockSpec(memory_space=pltpu.VMEM),
        ),
        compiler_params=pltpu.CompilerParams(vmem_limit_bytes=40 * 2**20),
    )(rank_of, folded)


def is_encoder(mat_no):
    return (
        mat_no < ENC
        or ENC + 2 * DEC <= mat_no < 2 * ENC + 2 * DEC
        or 2 * ENC + 3 * DEC <= mat_no < 3 * ENC + 3 * DEC
    )


def is_last(mat_no):
    return mat_no == 0


def rank_blocks(slot_list, devices, is_first):
    blocks_each = D // PB * (FF // PB)
    mats = slot_list // blocks_each
    early = jnp.zeros(mats.shape, jnp.bool_)
    for mat_no in range(MATS):
        if is_first(mat_no):
            early = early | (mats == mat_no)
    early = early.reshape(devices, -1).astype(jnp.int32)
    early_count = jnp.sum(early, axis=1)
    ahead = jnp.cumsum(early, axis=1) - early
    later = early_count[:, None] + jnp.arange(early.shape[1])[None, :] - ahead
    return (jnp.where(early == 1, ahead, later), early_count)


def room_for(per_device, chosen):
    share = sum(chosen(mat_no) for mat_no in range(MATS)) / MATS
    mean = per_device * share
    return min(per_device - 1, -(-int(mean + 4.2 * math.sqrt(mean * (1 - share))) // 4) * 4)


def by_block(slot_list, values):
    width, base = (64, 128)
    height = -(-slot_list.shape[0] // width)
    rows = (slot_list[:, None] // width == jnp.arange(height)[None, :]).astype(jnp.bfloat16)
    lanes = (slot_list[:, None] % width == jnp.arange(width)[None, :]).astype(jnp.bfloat16)
    found = []
    for value in values:
        high, low = (
            outer_sum(rows * (part.astype(jnp.bfloat16))[:, None], lanes)
            for part in (value // base, value % base)
        )
        found.append((high * base + low).astype(jnp.int32).reshape(-1)[: slot_list.shape[0]])
    return found


def lay_matrices(buffers, place_of, mats):
    half = PB // 2
    row_blocks, pairs = (D // PB, FF // (2 * PB))
    sizes = [buffer.shape[0] for buffer in buffers]
    starts = [sum(sizes[:item]) for item in range(len(sizes))]
    count = len(mats)

    def kernel(place_ref, *refs):
        sources, outs = (refs[: len(sizes)], refs[len(sizes) : len(sizes) + count])
        folded_ref, made, arrived, left = refs[len(sizes) + count :]
        left_half = lax.broadcasted_iota(jnp.int32, (half, 2 * PB), 1) < PB
        fetches = [
            pltpu.make_async_copy(
                source, folded_ref.at[pl.ds(start, size)], arrived.at[item]
            )
            for item, (source, start, size) in enumerate(zip(sources, starts, sizes))
        ]
        for fetch in fetches:
            fetch.start()
        for fetch in fetches:
            fetch.wait()

        def send(item):
            return pltpu.make_async_copy(made.at[item % 2], outs[item], left.at[item % 2])

        for item, mat_no in enumerate(mats):
            if item >= 2:
                send(item - 2).wait()

            def one_row(row_no, carry, item=item, mat_no=mat_no):
                first = (mat_no * row_blocks + row_no) * 2 * pairs
                row_at = pl.multiple_of(row_no * PB, PB)
                for pair_no in range(pairs):
                    even = folded_ref[place_ref[first + 2 * pair_no]].astype(jnp.float32)
                    odd = folded_ref[place_ref[first + 2 * pair_no + 1]].astype(jnp.float32)
                    columns = slice(2 * PB * pair_no, 2 * PB * (pair_no + 1))
                    upper = jnp.where(left_half, even, pltpu.roll(odd, PB, 1))
                    lower = jnp.where(left_half, pltpu.roll(even, PB, 1), odd)
                    made[item % 2, pl.ds(row_at, half), columns] = upper.astype(jnp.bfloat16)
                    made[item % 2, pl.ds(row_at + half, half), columns] = lower.astype(jnp.bfloat16)
                return carry

            lax.fori_loop(0, row_blocks, one_row, 0)
            send(item).start()
        for item in range(max(count - 2, 0), count):
            send(item).wait()

    return pl.pallas_call(
        kernel,
        out_shape=[jax.ShapeDtypeStruct((D, FF), jnp.bfloat16)] * count,
        grid_spec=pltpu.PrefetchScalarGridSpec(
            num_scalar_prefetch=1,
            grid=(1,),
            in_specs=[pl.BlockSpec(memory_space=pl.ANY)] * len(sizes),
            out_specs=[pl.BlockSpec(memory_space=pl.ANY)] * count,
            scratch_shapes=[
                pltpu.VMEM((sum(sizes), half, 2 * PB), jnp.bfloat16),
                pltpu.VMEM((2, D, FF), jnp.bfloat16),
                pltpu.SemaphoreType.DMA((len(sizes),)),
                pltpu.SemaphoreType.DMA((2,)),
            ],
        ),
        compiler_params=pltpu.CompilerParams(vmem_limit_bytes=40 * 2**20),
    )(place_of, *buffers)


def fold_gradients(matrices, mats, place_of, sizes, begun=None):
    half = PB // 2
    row_blocks, pairs = (D // PB, FF // (2 * PB))
    count = len(mats)
    whole = sum(sizes)
    given = 0 if begun is None else 1
    skipped = 0 if begun is None else whole - begun.shape[0]
    kept = whole - skipped

    def kernel(place_ref, *refs):
        sources, old = (refs[:count], refs[count : count + given])
        outs = refs[count + given : -5]
        folded_ref, held, arrived, left, old_sem = refs[-5:]
        left_half = lax.broadcasted_iota(jnp.int32, (half, 2 * PB), 1) < PB

        def fetch(item):
            return pltpu.make_async_copy(sources[item], held.at[item % 2], arrived.at[item % 2])

        fetch(0).start()
        if given:
            before = pltpu.make_async_copy(
                old[0], folded_ref.at[pl.ds(0, kept)], old_sem.at[0]
            )
            before.start()
            before.wait()
        for item, mat_no in enumerate(mats):
            if item + 1 < count:
                fetch(item + 1).start()
            fetch(item).wait()

            def place(block, carry=None):
                spot = place_ref[block] - skipped
                return jnp.where(spot < 0, kept, spot) if given else spot

            def one_row(row_no, carry, item=item, mat_no=mat_no):
                first = (mat_no * row_blocks + row_no) * 2 * pairs
                row_at = pl.multiple_of(row_no * PB, PB)
                for pair_no in range(pairs):
                    columns = slice(2 * PB * pair_no, 2 * PB * (pair_no + 1))
                    upper = held[item % 2, pl.ds(row_at, half), columns].astype(jnp.float32)
                    lower = held[item % 2, pl.ds(row_at + half, half), columns].astype(jnp.float32)
                    even = jnp.where(left_half, upper, pltpu.roll(lower, PB, 1))
                    odd = jnp.where(left_half, pltpu.roll(upper, PB, 1), lower)
                    folded_ref[place(first + 2 * pair_no)] = even.astype(jnp.bfloat16)
                    folded_ref[place(first + 2 * pair_no + 1)] = odd.astype(jnp.bfloat16)
                return carry

            lax.fori_loop(0, row_blocks, one_row, 0)
        begin = 0
        sends = []
        for item, out in enumerate(outs):
            size = out.shape[0]
            sends.append(
                pltpu.make_async_copy(folded_ref.at[pl.ds(begin, size)], out, left.at[item])
            )
            begin += size
        for send in sends:
            send.start()
        for send in sends:
            send.wait()

    shapes = [kept] if given else list(sizes)
    return pl.pallas_call(
        kernel,
        out_shape=[jax.ShapeDtypeStruct((size, half, 2 * PB), jnp.bfloat16) for size in shapes],
        grid_spec=pltpu.PrefetchScalarGridSpec(
            num_scalar_prefetch=1,
            grid=(1,),
            in_specs=[pl.BlockSpec(memory_space=pl.ANY)] * (count + given),
            out_specs=[pl.BlockSpec(memory_space=pl.ANY)] * len(shapes),
            scratch_shapes=[
                pltpu.VMEM((kept + given, half, 2 * PB), jnp.bfloat16),
                pltpu.VMEM((2, D, FF), jnp.bfloat16),
                pltpu.SemaphoreType.DMA((2,)),
                pltpu.SemaphoreType.DMA((2,)),
                pltpu.SemaphoreType.DMA((1,)),
            ],
        ),
        compiler_params=pltpu.CompilerParams(vmem_limit_bytes=40 * 2**20),
    )(place_of, *[matrices[mat_no] for mat_no in mats], *([begun] if given else []))


def exchange_plan(dp_size, along, per_device):
    low, high = (along.bit_length() - 1, dp_size.bit_length() - 1)
    base = [low + bit for bit in range(high)] + list(range(1, low))
    third = per_device // 3
    sizes = [per_device - 2 * third, third, third]
    return [(size, base[turn:] + base[:turn]) for turn, size in enumerate(sizes)]


def places_for(ranks, plan, devices):
    per_device = sum(size for size, _ in plan)
    owner = jnp.arange(devices)[:, None]
    place = jnp.zeros_like(ranks)
    begin = 0
    for size, order in plan:
        spot = jnp.zeros_like(owner)
        for bit in order:
            spot = spot * 2 + owner // 2**bit % 2
        here = begin * (devices // 2) + spot * size + ranks - begin
        place = jnp.where((ranks >= begin) & (ranks < begin + size), here, place)
        begin += size
    return place + owner % 2 * (devices // 2 * per_device)


def halve(value, bit, devices):
    me = lax.axis_index("dp") * lax.axis_size("vocab") + lax.axis_index("vocab")

    mine = me // 2**bit % 2
    value = value.reshape(2, value.shape[0] // 2, *value.shape[1:])
    sent = lax.dynamic_index_in_dim(value, 1 - mine, 0, keepdims=False)
    kept = lax.dynamic_index_in_dim(value, mine, 0, keepdims=False)
    pairs = [(index, index ^ 2**bit) for index in range(devices)]
    arrived = lax.ppermute(sent, ("dp", "vocab"), pairs)
    return kept.astype(jnp.float32) + arrived.astype(jnp.float32)


def first_exchange(folded, devices):
    return halve(folded, 0, devices).astype(jnp.bfloat16)


def split_parts(total, plan, devices):
    parts, begin = ([], 0)
    for size, _ in plan:
        count = size * (devices // 2)
        parts.append(total[begin : begin + count])
        begin += count
    return parts


def one_exchange(parts, plan, round_no, devices):
    return [
        halve(part.astype(jnp.bfloat16), order[round_no], devices)
        for part, (_, order) in zip(parts, plan)
    ]


def other_exchanges(parts, plan, devices, done=0):
    for round_no in range(done, len(plan[0][1])):
        parts = one_exchange(parts, plan, round_no, devices)
    return jnp.concatenate(parts, 0)


def take_rows(source, index_at, kind):
    count, width, block = (index_at.shape[0], source.shape[1], 128)
    whole = -(-count // block) * block
    index_at = jnp.pad(index_at, (0, whole - count))

    def kernel(index_ref, source_ref, out_ref, held_ref):
        first = pl.program_id(0) * block

        def copy_eight(group, carry):
            base = pl.multiple_of(group * 8, 8)
            for row_no in range(8):
                held_ref[pl.ds(base + row_no, 1), :] = source_ref[
                    pl.ds(index_ref[first + base + row_no], 1), :
                ]
            return carry

        lax.fori_loop(0, block // 8, copy_eight, 0)
        out_ref[...] = held_ref[...].astype(kind)

    taken = pl.pallas_call(
        kernel,
        out_shape=jax.ShapeDtypeStruct((whole, width), kind),
        grid_spec=pltpu.PrefetchScalarGridSpec(
            num_scalar_prefetch=1,
            grid=(whole // block,),
            in_specs=[pl.BlockSpec(memory_space=pltpu.VMEM)],
            out_specs=pl.BlockSpec((block, width), lambda step, index: (step, 0)),
            scratch_shapes=[pltpu.VMEM((block, width), jnp.float32)],
        ),
        compiler_params=pltpu.CompilerParams(vmem_limit_bytes=40 * 2**20),
    )(index_at, source)
    return taken[:count]


def add_rows(rows, index_at, total):
    count, width, block = (rows.shape[0], rows.shape[1], 512)
    whole = -(-count // block) * block
    index_at = jnp.pad(index_at, (0, whole - count), constant_values=-1)[None, :]
    rows = jnp.pad(rows, ((0, whole - count), (0, 0)))
    height = total.shape[0]

    def kernel(index_ref, rows_ref, total_ref, out_ref):
        @pl.when(pl.program_id(0) == 0)
        def _():
            out_ref[...] = total_ref[...]

        hits = lax.broadcasted_iota(jnp.int32, (height, block), 0) == index_ref[...]
        out_ref[...] += jnp.dot(
            hits.astype(jnp.float32).astype(jnp.bfloat16),
            rows_ref[...],
            preferred_element_type=jnp.float32,
        )

    return pl.pallas_call(
        kernel,
        out_shape=jax.ShapeDtypeStruct(total.shape, jnp.float32),
        grid=(whole // block,),
        in_specs=[
            pl.BlockSpec((1, block), lambda step: (0, step)),
            pl.BlockSpec((block, width), lambda step: (step, 0)),
            pl.BlockSpec((height, width), lambda step: (0, 0)),
        ],
        out_specs=pl.BlockSpec((height, width), lambda step: (0, 0)),
        compiler_params=pltpu.CompilerParams(vmem_limit_bytes=40 * 2**20),
    )(index_at, rows, total)


def spread(value, axes, peers):
    return lax.all_to_all(
        jnp.broadcast_to(value[None], (peers, *value.shape)), axes, 0, 0, tiled=True
    )


def count_before(mask):
    size, width = (mask.shape[-1], 128)
    parts = mask.reshape(*mask.shape[:-1], size // width, width).astype(jnp.bfloat16)
    earlier = (jnp.arange(width)[:, None] < jnp.arange(width)[None, :]).astype(jnp.bfloat16)
    inside = jnp.einsum("...pw,wk->...pk", parts, earlier, preferred_element_type=jnp.float32)
    totals = jnp.sum(parts.astype(jnp.float32), axis=-1)
    ahead = jnp.cumsum(totals, axis=-1) - totals
    return (inside + ahead[..., None]).reshape(mask.shape).astype(jnp.int32)


def room(count, peers):
    mean = count / peers
    return min(count, -(-int(mean + 5.0 * math.sqrt(mean)) // 16) * 16)


def listed(mask, rank, values, size):
    width, base = (16, 128)
    rows = mask[..., None] & (rank[..., None] // width == jnp.arange(size // width))
    lanes = (rank[..., None] % width == jnp.arange(width)).astype(jnp.bfloat16)
    values = values + 1
    high, low = (
        jnp.einsum(
            "...th,...tl->...hl",
            jnp.where(rows, part[..., None].astype(jnp.bfloat16), 0),
            lanes,
            preferred_element_type=jnp.float32,
        )
        for part in (values // base, values % base)
    )
    return (high * base + low).astype(jnp.int32).reshape(*mask.shape[:-1], size) - 1


def rounds_needed(owner_all, peers, size):
    held = jnp.sum((owner_all[:, None, :] == jnp.arange(peers)[:, None]).astype(jnp.int32), axis=2)
    return (jnp.max(held) + size - 1) // size


def fetch_plan(table_part, tokens_all, peers_here, peer_me):
    peers, rows_each = (peers_here.shape[0], table_part.shape[0])
    count = tokens_all.shape[1]
    size = room(count, peers)
    asked = peers_here // rows_each == peer_me
    asked_rank = count_before(asked)
    own_tokens = lax.dynamic_index_in_dim(peers_here, peer_me, 0, keepdims=False)
    own_owner = own_tokens // rows_each
    own_mask = own_owner[None, :] == jnp.arange(peers)[:, None]
    own_rank = jnp.sum(jnp.where(own_mask, count_before(own_mask), 0), axis=0)

    def to_send(round_no):
        wanted = listed(
            asked, asked_rank - round_no * size, peers_here % rows_each, size
        )
        return take_rows(table_part, jnp.maximum(wanted.reshape(-1), 0), jnp.bfloat16)

    def found_in(arrived, round_no):
        rank_now = own_rank - round_no * size
        now = (rank_now >= 0) & (rank_now < size)
        found = take_rows(
            arrived.astype(jnp.float32), jnp.where(now, own_owner * size + rank_now, 0), jnp.float32
        )
        return (now, found)

    def again(round_no, rows):
        now, found = found_in(swap_rows(to_send(round_no)), round_no)
        return jnp.where(now[:, None], found, rows)

    rounds = rounds_needed(tokens_all // rows_each, peers, size)

    def finish(arrived):
        return lax.fori_loop(1, rounds, again, found_in(arrived, 0)[1])

    return (to_send(0), finish)


def swap_rows(rows):
    return lax.all_to_all(rows, "vocab", 0, 0, tiled=True)


def return_plan(tokens_all, rows_each, dp_size):
    peers, count = tokens_all.shape
    along = peers // dp_size
    quarter = rows_each // dp_size
    me = lax.axis_index("dp") * along + lax.axis_index("vocab")
    size = room(count, peers)
    owner_all = (tokens_all % rows_each) // quarter * along + tokens_all // rows_each
    arriving = owner_all == me
    arriving_rank = count_before(arriving)
    own_owner = lax.dynamic_index_in_dim(owner_all, me, 0, keepdims=False)
    leaving = own_owner[None, :] == jnp.arange(peers)[:, None]
    leaving_rank = count_before(leaving)
    place = jnp.broadcast_to(jnp.arange(count)[None, :], leaving.shape)

    def lists(round_no):
        return (
            jnp.maximum(
                listed(leaving, leaving_rank - round_no * size, place, size).reshape(-1), 0
            ),
            listed(
                arriving, arriving_rank - round_no * size, tokens_all % quarter, size
            ).reshape(-1),
        )

    return (lists, rounds_needed(owner_all, peers, size))


def return_rows(grad_rows, lists, first_lists, rounds, total, ready, landed):
    def swap_all(rows):
        return lax.all_to_all(rows, ("dp", "vocab"), 0, 0, tiled=True)

    def again(round_no, so_far):
        chosen, where = lists(round_no)
        return add_rows(swap_all(take_rows(grad_rows, chosen, jnp.bfloat16)), where, so_far)

    arrived = landed(swap_all(ready(take_rows(grad_rows, first_lists[0], jnp.bfloat16))))
    return lax.fori_loop(1, rounds, again, add_rows(arrived, first_lists[1], total))


def turn_in(left_basis, tiles, right_basis):
    half = jnp.einsum("tki,tkl->til", left_basis, tiles, precision=HIGH)
    return jnp.einsum("til,tlj->tij", half, right_basis, precision=HIGH)


def turn_out(left_basis, tiles, right_basis):
    half = jnp.einsum("tik,tkl->til", left_basis, tiles, precision=HIGH)
    return jnp.einsum("til,tjl->tij", half, right_basis, precision=HIGH)


def orthonormal(columns):
    lanes, group = (128, 4)

    def kernel(in_ref, out_ref):
        out_ref[...] = in_ref[...]

        def four_columns(group_at, carry):
            first = group_at * group
            pivots = []
            for item in range(group):
                pivot = out_ref[first + item]
                for before in pivots:
                    pivot = pivot - jnp.sum(before * pivot, axis=0, keepdims=True) * before
                pivot = pivot / jnp.sqrt(jnp.sum(pivot * pivot, axis=0, keepdims=True))
                out_ref[first + item] = pivot
                pivots.append(pivot)

            def one_group(group_no, inner):
                held = [out_ref[group_no * group + item] for item in range(group)]
                for item in range(group):
                    value = held[item]
                    shares = [
                        jnp.sum(pivot * value, axis=0, keepdims=True) for pivot in pivots
                    ]
                    for pivot, share in zip(pivots, shares):
                        value = value - share * pivot
                    held[item] = value
                for item in range(group):
                    out_ref[group_no * group + item] = held[item]
                return inner

            return lax.fori_loop(group_at + 1, PB // group, one_group, carry)

        lax.fori_loop(0, PB // group, four_columns, 0)

    spec = pl.BlockSpec((PB, PB, lanes), lambda step: (0, 0, step))
    return pl.pallas_call(
        kernel,
        out_shape=jax.ShapeDtypeStruct(columns.shape, jnp.float32),
        grid=(columns.shape[2] // lanes,),
        in_specs=[spec],
        out_specs=spec,
        compiler_params=pltpu.CompilerParams(vmem_limit_bytes=40 * 2**20),
    )(columns)


def renew_bases(left_moved, right_moved):
    moved = jnp.concatenate([left_moved, right_moved], 0)
    count = moved.shape[0]
    whole = -(-count // 128) * 128
    columns = jnp.pad(jnp.transpose(moved, (2, 1, 0)), ((0, 0), (0, 0), (0, whole - count)))
    renewed = jnp.transpose(orthonormal(columns)[:, :, :count], (2, 1, 0))
    return (renewed[: count // 2], renewed[count // 2 :])


def turned_by(stat, basis):
    return jnp.einsum("tij,tjk->tik", stat, basis, precision=HIGH)


def soap_update(
    master,
    grad_tiles,
    grad_turned,
    left_outer,
    right_outer,
    left_moves,
    right_moves,
    first_mom,
    first_turned,
    second_mom,
    left_stat,
    right_stat,
    left_basis,
    right_basis,
    factor,
):
    first_new = BETA_FIRST * first_mom + (1 - BETA_FIRST) * (factor * grad_tiles)
    grad_turned = factor * grad_turned
    first_turned = BETA_FIRST * first_turned + (1 - BETA_FIRST) * grad_turned
    second_new = BETA_SECOND * second_mom + (1 - BETA_SECOND) * grad_turned * grad_turned
    direction = (
        first_turned
        / (1 - BETA_FIRST**STEP)
        / (jnp.sqrt(second_new / (1 - BETA_SECOND**STEP)) + ADAM_EPS)
    )
    master_new = master - RATE_MATRIX * (
        turn_out(left_basis, direction, right_basis) + DECAY * master
    )
    left_new = BETA_STAT * left_stat + (1 - BETA_STAT) * (factor * (factor * left_outer))
    right_new = BETA_STAT * right_stat + (1 - BETA_STAT) * (factor * (factor * right_outer))
    return (
        master_new,
        first_new,
        second_new,
        left_new,
        right_new,
        *renew_bases(
            *(
                BETA_STAT * before + (1 - BETA_STAT) * (factor * (factor * change))
                for before, change in (left_moves, right_moves)
            )
        ),
    )


def adamw_update(master, grad_now, first_mom, second_mom, rate, decay_by):
    first_new = BETA_FIRST * first_mom + (1 - BETA_FIRST) * grad_now
    second_new = BETA_SECOND * second_mom + (1 - BETA_SECOND) * grad_now * grad_now
    direction = (
        first_new
        / (1 - BETA_FIRST**STEP)
        / (jnp.sqrt(second_new / (1 - BETA_SECOND**STEP)) + ADAM_EPS)
    )
    return (master - rate * (direction + decay_by * master), first_new, second_new)


def per_device(
    master_tiles,
    mom1_tiles,
    mom2_tiles,
    stat_left,
    stat_right,
    basis_left,
    basis_right,
    table_master,
    table_mom1,
    table_mom2,
    gains,
    gain_mom1,
    gain_mom2,
    source_ids,
    target_ids,
    source_len,
    target_len,
    loss_place,
    exit_layer,
    slot_list,
):
    dp_size, along = (lax.axis_size("dp"), lax.axis_size("vocab"))
    dp_me, peer_me = (lax.axis_index("dp"), lax.axis_index("vocab"))
    devices = dp_size * along
    rows_each = table_master.shape[0]
    quarter = rows_each // dp_size
    source_len, target_len = (source_len[:, 0], target_len[:, 0])

    shifted = jnp.pad(target_ids[:, 0, :-1], ((0, 0), (1, 0)))
    tokens = jnp.concatenate([source_ids.reshape(-1), shifted.reshape(-1)])
    places = loss_place[:, 0]
    counted = places < target_len[:, None]
    reach = [
        jnp.sum((counted & (exit_layer[:, 0] >= layer_no)).astype(jnp.int32))
        for layer_no in range(DEC)
    ]
    labels = jnp.take_along_axis(target_ids[:, 0], places, axis=1).reshape(-1)
    row_count = MICRO * LOSS_POS
    own_facts = jnp.concatenate(
        [tokens, labels, counted.reshape(-1).astype(jnp.int32), jnp.stack(reach)]
    )
    fact_count = own_facts.shape[0]
    own_facts = jnp.pad(own_facts, (0, -fact_count % 128))
    facts = spread(own_facts, ("dp", "vocab"), devices)
    slots_later, facts, mom1_later, left_later, right_later = lax.optimization_barrier(
        (slot_list, facts, mom1_tiles, basis_left, basis_right)
    )
    tokens_all = facts[:, : tokens.shape[0]]
    after = facts[:, tokens.shape[0] :]
    labels_all = after[:, :row_count]
    counted_all = after[:, row_count : 2 * row_count].astype(jnp.float32)
    reach_all = jnp.sum(after[:, 2 * row_count : 2 * row_count + DEC].astype(jnp.float32), axis=0)
    count_all = jnp.sum(counted_all)
    fraction = reach_all / jnp.sum(reach_all)

    per_device = master_tiles.shape[0]
    me = dp_me * along + peer_me
    ranks, early_count = rank_blocks(slot_list, devices, is_encoder)
    first_size = room_for(per_device, is_encoder)
    second_size = per_device - first_size
    place_at = jnp.where(
        ranks < first_size,
        jnp.arange(devices)[:, None] * first_size + ranks,
        devices * first_size
        + jnp.arange(devices)[:, None] * second_size
        + ranks
        - first_size,
    )
    late_size = room_for(per_device, is_last)
    soon_size = per_device - late_size
    back_ranks, soon_count = rank_blocks(slots_later, devices, lambda mat_no: not is_last(mat_no))
    soon_plan = exchange_plan(dp_size, along, soon_size)
    late_plan = exchange_plan(dp_size, along, late_size)
    back_at = jnp.where(
        back_ranks < soon_size,
        places_for(back_ranks, soon_plan, devices),
        devices * soon_size + places_for(back_ranks - soon_size, late_plan, devices),
    )
    place_of, back_of = by_block(slots_later, [place_at.reshape(-1), back_at.reshape(-1)])
    own_folded = fold_ranked(
        master_tiles, lax.dynamic_index_in_dim(ranks, me, 0, keepdims=False)
    )
    src_count, tgt_count = (source_ids.shape[2], target_ids.shape[2])

    def planned(first, length):
        ids_all = tokens_all[:, first : first + MICRO * length]
        peers_here = lax.dynamic_slice_in_dim(ids_all, dp_me * along, along, 0)
        return fetch_plan(table_master, ids_all, peers_here, peer_me)

    source_sent, source_finish = planned(0, src_count)
    target_sent, target_finish = planned(MICRO * src_count, tgt_count)
    first_tiles = lax.all_gather(own_folded[:first_size], ("dp", "vocab"), axis=0, tiled=True)
    lists, rounds = return_plan(tokens_all, rows_each, dp_size)
    (
        own_second,
        first_tiles,
        source_arrived,
        first_lists,
        first_turned,
        target_sent,
        place_of,
    ) = lax.optimization_barrier(
        (
            own_folded[first_size:],
            first_tiles,
            swap_rows(source_sent),
            lists(0),
            turn_in(left_later, mom1_later, right_later),
            target_sent,
            place_of,
        )
    )
    second_tiles = lax.all_gather(own_second, ("dp", "vocab"), axis=0, tiled=True)
    encoder_mats = [mat_no for mat_no in range(MATS) if is_encoder(mat_no)]
    decoder_mats = [mat_no for mat_no in range(MATS) if not is_encoder(mat_no)]

    def lay_with_all():
        others = lax.all_gather(own_second, ("dp", "vocab"), axis=0, tiled=True)
        return lay_matrices([first_tiles, others], place_of, encoder_mats)

    def lay_with_first():
        return lay_matrices([first_tiles], place_of, encoder_mats)

    encoder_set = lax.cond(
        jnp.max(early_count) > first_size, lay_with_all, lay_with_first
    )
    weights = [None] * MATS
    for mat_no, matrix in zip(encoder_mats, encoder_set):
        weights[mat_no] = matrix

    def lay_decoder(memory):
        held, tiles, arrived = lax.optimization_barrier((memory, second_tiles, target_arrived))
        decoder_set = lay_matrices([first_tiles, tiles], place_of, decoder_mats)
        for mat_no, matrix in zip(decoder_mats, decoder_set):
            weights[mat_no] = matrix
        return (held, with_waves(target_finish(arrived), tgt_count))

    wave_set = waves(src_count, D)

    def with_waves(rows, length):
        return rows * math.sqrt(D) + jnp.tile(wave_set[:length], (MICRO, 1))

    source_rows = with_waves(source_finish(source_arrived), src_count)
    source_rows, target_sent = lax.optimization_barrier((source_rows, target_sent))
    target_arrived = swap_rows(target_sent)

    place_rows = (places + jnp.arange(MICRO)[:, None] * tgt_count).reshape(-1)
    kept, exit_rows = forward_all(
        weights,
        gains,
        source_rows,
        source_len,
        target_len,
        place_rows,
        lay_decoder,
    )

    table_low_part = table_master.astype(jnp.bfloat16)
    exit_count = DEC * row_count
    exit_all = lax.all_gather(exit_rows, ("dp", "vocab"), axis=0, tiled=True)
    exit_here = spread(exit_rows, "vocab", along).reshape(-1, D)
    label_rows = jnp.tile(labels_all, (1, DEC)).reshape(-1)
    weight_rows = (
        jnp.repeat(fraction, row_count)[None, :] * jnp.tile(counted_all, (1, DEC))
    ).reshape(-1)
    group_rows = along * exit_count
    group_at = dp_me * group_rows
    label_here = lax.dynamic_slice_in_dim(label_rows, group_at, group_rows, 0)
    weight_here = lax.dynamic_slice_in_dim(weight_rows, group_at, group_rows, 0)
    logits = linear_tr(exit_here, table_low_part)
    hit_here = label_here[:, None] - peer_me * rows_each == jnp.arange(rows_each)[None, :]
    summit = jnp.max(logits, axis=1)
    spread_part = jnp.sum(jnp.exp(logits - summit[:, None]), axis=1)
    picked_part = jnp.sum(jnp.where(hit_here, logits, 0.0), axis=1)
    stats = spread(
        jnp.stack([summit, spread_part, picked_part]), ("dp", "vocab"), devices
    ).reshape(dp_size, along, 3, group_rows)
    summit_all = jnp.max(stats[:, :, 0], axis=1)
    total_all = jnp.sum(stats[:, :, 1] * jnp.exp(stats[:, :, 0] - summit_all[:, None]), axis=1)
    spread_all = summit_all + jnp.log(total_all)
    picked_all = jnp.sum(stats[:, :, 2], axis=1)
    loss_sum = jnp.sum(weight_rows * (spread_all - picked_all).reshape(-1))
    spread_here = lax.dynamic_index_in_dim(spread_all, dp_me, 0, keepdims=False)

    def logit_grads(logit_set, spread, weight_set, hits):
        return (
            (weight_set / count_all)[:, None]
            * (jnp.exp(logit_set - spread[:, None]) - hits.astype(jnp.float32))
        ).astype(jnp.bfloat16)

    grads_here = logit_grads(logits, spread_here, weight_here, hit_here)
    grad_parts = linear(grads_here, table_low_part).astype(jnp.bfloat16)
    grad_parts = lax.all_to_all(grad_parts, "vocab", 0, 0, tiled=True)
    exit_grads = jnp.sum(
        grad_parts.reshape(along, exit_count, D).astype(jnp.float32), axis=0
    )

    matrix_store = [None] * MATS
    gain_store = [None] * GAINS
    first_row = peer_me * rows_each + dp_me * quarter
    table_quarter = lax.dynamic_slice_in_dim(table_low_part, dp_me * quarter, quarter, 0)
    hit_quarter = label_rows[:, None] - first_row == jnp.arange(quarter)[None, :]
    grads_quarter = logit_grads(
        linear_tr(exit_all, table_quarter), spread_all.reshape(-1), weight_rows, hit_quarter
    )
    grad_quarter = outer_sum(grads_quarter, exit_all)
    soon_mats = [mat_no for mat_no in range(MATS) if not is_last(mat_no)]
    late_mats = [mat_no for mat_no in range(MATS) if is_last(mat_no)]
    both = [devices * soon_size, devices * late_size]
    held = {}

    def before_last(grad_stream):
        blocks, held["begun"] = fold_gradients(matrix_store, soon_mats, back_of, both)
        grad_stream, blocks, held["quarter"] = lax.optimization_barrier(
            (grad_stream, blocks, grad_quarter)
        )
        held["total"] = first_exchange(blocks, devices)
        return grad_stream

    def between_last(value):
        if "parts" not in held:
            value, total = lax.optimization_barrier((value, held["total"]))
            held["parts"], held["done"] = (split_parts(total, soon_plan, devices), 0)
        elif held["done"] < len(soon_plan[0][1]):
            parts = one_exchange(held["parts"], soon_plan, held["done"], devices)
            value, held["parts"] = lax.optimization_barrier((value, parts))
            held["done"] += 1
        return value

    grad_source, grad_target = backward_all(
        weights,
        gains,
        kept,
        exit_grads,
        matrix_store,
        gain_store,
        before_last,
        between_last,
    )

    grad_source = between_last(grad_source)
    grad_rows = jnp.concatenate([grad_source, grad_target], 0) * math.sqrt(D)
    grad_rows = between_last(grad_rows)
    [late_blocks] = fold_gradients(matrix_store, late_mats, back_of, both, held["begun"])
    late_parts = split_parts(first_exchange(late_blocks, devices), late_plan, devices)
    late_parts = one_exchange(late_parts, late_plan, 0, devices)

    late_sum = other_exchanges(late_parts, late_plan, devices, 1)

    def exchange_again():
        blocks, _ = fold_gradients(matrix_store, list(range(MATS)), back_of, both)
        parts = split_parts(first_exchange(blocks, devices), soon_plan, devices)
        return other_exchanges(parts, soon_plan, devices)

    share = -(-GAINS * D // (devices * 128)) * 128
    gain_flat = jnp.stack(gain_store).reshape(-1)
    gain_flat = jnp.pad(gain_flat, (0, devices * share - GAINS * D)).reshape(devices, share)

    def ready(rows):
        sums = other_exchanges(held["parts"], soon_plan, devices, held["done"])
        rows, sums, late, held["gains"] = lax.optimization_barrier(
            (rows, sums, late_sum, gain_flat)
        )
        sums = lax.cond(jnp.min(soon_count) < soon_size, exchange_again, lambda: sums)
        owned_grad = unfold_ranked(
            jnp.concatenate([sums, late], 0),
            lax.dynamic_index_in_dim(back_ranks, me, 0, keepdims=False),
        )
        left_outer = jnp.einsum("tik,tjk->tij", owned_grad, owned_grad, precision=HIGH)
        right_outer = jnp.einsum("tki,tkj->tij", owned_grad, owned_grad, precision=HIGH)
        gain_part = jnp.sum(
            lax.all_to_all(held["gains"], ("dp", "vocab"), 0, 0, tiled=True), axis=0
        )
        gain_total = spread(gain_part[None], ("dp", "vocab"), devices)
        held["owned"] = (
            owned_grad,
            turn_in(basis_left, owned_grad, basis_right),
            left_outer,
            right_outer,
            (turned_by(stat_left, basis_left), turned_by(left_outer, basis_left)),
            (turned_by(stat_right, basis_right), turned_by(right_outer, basis_right)),
            jnp.sum(owned_grad * owned_grad),
            gain_total.reshape(-1)[: GAINS * D].reshape(GAINS, D),
        )
        return rows

    def landed(arrived):
        arrived, held["owned"] = lax.optimization_barrier((arrived, held["owned"]))
        return arrived

    grad_quarter = return_rows(
        grad_rows, lists, first_lists, rounds, held["quarter"], ready, landed
    )

    (
        owned_grad,
        owned_turned,
        left_outer,
        right_outer,
        left_moves,
        right_moves,
        owned_squares,
        gain_total,
    ) = held["owned"]
    squares = owned_squares + jnp.sum(grad_quarter * grad_quarter)
    square_total = jnp.sum(
        spread(jnp.full((1, 128), squares), ("dp", "vocab"), devices)[:, 0, 0]
    )
    grad_norm = jnp.sqrt(square_total + jnp.sum(gain_total * gain_total))
    factor = jnp.minimum(1.0, CLIP_AT / grad_norm)
    table_grad = lax.all_gather(
        grad_quarter.astype(jnp.bfloat16), "dp", axis=0, tiled=True
    ).astype(jnp.float32)
    master_new, mom1_new, mom2_new, left_new, right_new, bleft_new, bright_new = soap_update(
        master_tiles,
        owned_grad,
        owned_turned,
        left_outer,
        right_outer,
        left_moves,
        right_moves,
        mom1_tiles,
        first_turned,
        mom2_tiles,
        stat_left,
        stat_right,
        basis_left,
        basis_right,
        factor,
    )
    table_new, table_m, table_v = adamw_update(
        table_master, table_grad * factor, table_mom1, table_mom2, RATE_MATRIX, DECAY
    )
    gains_new, gains_m, gains_v = adamw_update(
        gains, gain_total * factor, gain_mom1, gain_mom2, RATE_VECTOR, 0.0
    )
    return (
        loss_sum,
        count_all,
        grad_norm,
        master_new,
        master_new.astype(jnp.bfloat16),
        mom1_new,
        mom2_new,
        left_new,
        right_new,
        bleft_new,
        bright_new,
        table_new,
        table_new.astype(jnp.bfloat16),
        table_m,
        table_v,
        gains_new,
        gains_m,
        gains_v,
    )


def solution(mesh):
    placed = (
        P(("dp", "vocab"), None, None),
        P(("dp", "vocab"), None, None),
        P(("dp", "vocab"), None, None),
        P(("dp", "vocab"), None, None),
        P(("dp", "vocab"), None, None),
        P(("dp", "vocab"), None, None),
        P(("dp", "vocab"), None, None),
        P("vocab", None),
        P("vocab", None),
        P("vocab", None),
        P(),
        P(),
        P(),
        P(None, ("dp", "vocab"), None),
        P(None, ("dp", "vocab"), None),
        P(None, ("dp", "vocab")),
        P(None, ("dp", "vocab")),
        P(None, ("dp", "vocab"), None),
        P(None, ("dp", "vocab"), None),
        P(),
    )
    return jax.shard_map(
        per_device,
        mesh=mesh,
        in_specs=placed,
        out_specs=(
            P(),
            P(),
            P(),
            P(("dp", "vocab"), None, None),
            P(("dp", "vocab"), None, None),
            P(("dp", "vocab"), None, None),
            P(("dp", "vocab"), None, None),
            P(("dp", "vocab"), None, None),
            P(("dp", "vocab"), None, None),
            P(("dp", "vocab"), None, None),
            P(("dp", "vocab"), None, None),
            P("vocab", None),
            P("vocab", None),
            P("vocab", None),
            P("vocab", None),
            P(),
            P(),
            P(),
        ),
        check_vma=False,
    )
```

```python
import math

import jax
import jax.numpy as jnp
from jax import lax
from jax.experimental import pallas as pl
from jax.experimental.pallas import tpu as pltpu
from jax.sharding import PartitionSpec as P

D = 512
HEADS = 8
HEAD_DIM = 64
FF = 2048
ENC = 1
DEC = 2
MICRO = 2
LOSS_POS = 16
PB = 64
STEP = 10
MATS = 11
GAINS = 11


HIGH = lax.Precision.HIGH
NORM_EPS = 1e-06
CLIP_AT = 0.02
RATE_MATRIX = 0.1
RATE_VECTOR = 0.8
BETA_FIRST = 0.9
BETA_SECOND = 0.95
BETA_STAT = 0.95
ADAM_EPS = 1e-08
DECAY = 0.01


def rms_norm(stream, gain_row):
    return (
        stream * lax.rsqrt(jnp.mean(stream * stream, axis=-1, keepdims=True) + NORM_EPS) * gain_row
    )


def waves(length, columns):
    place_at = jnp.arange(length).astype(jnp.float32)[:, None]
    rate_at = jnp.exp(
        jnp.arange(columns // 2).astype(jnp.float32) * (-2.0 * math.log(10000.0) / columns)
    )
    angle = place_at * rate_at[None, :]
    return jnp.concatenate([jnp.sin(angle), jnp.cos(angle)], axis=1)


def linear(left_op, right_op):
    return jnp.dot(left_op, right_op, preferred_element_type=jnp.float32)


def linear_tr(left_op, right_op):
    return lax.dot_general(
        left_op, right_op, (((1,), (1,)), ((), ())), preferred_element_type=jnp.float32
    )


def outer_sum(left_op, right_op):
    return lax.dot_general(
        left_op, right_op, (((0,), (0,)), ((), ())), preferred_element_type=jnp.float32
    )


def split_heads(matrix):
    return matrix.reshape(matrix.shape[0], HEADS, HEAD_DIM)


NEVER=-1000000000.0
PAIR=2*HEAD_DIM
def kept_scores(query, keys, valid_len, causal, start_at):
    scores = lax.dot_general(query, keys, (((1,), (1,)), ((), ())), preferred_element_type=jnp.float32)
    key_at = lax.broadcasted_iota(jnp.int32, scores.shape if causal else (1, scores.shape[1]), 1)
    allowed = key_at < valid_len
    if causal:
        allowed = allowed & (key_at <= start_at + lax.broadcasted_iota(jnp.int32, scores.shape, 0))
    return jnp.where(allowed, scores, NEVER)

def head_masks(value):
    first = lax.broadcasted_iota(jnp.int32, value.shape, 1) < HEAD_DIM
    zero = jnp.zeros_like(value)
    return (jnp.where(first, value, zero), jnp.where(first, zero, value))

def attend_forward(query_in, query_at, keys_in, key_at, value_at, valid_len, causal):
    rows, keys = (query_in.shape[0] // MICRO, keys_in.shape[0] // MICRO)
    block = min(256, rows)
    steps = rows // block
    scale = HEAD_DIM ** (-0.5)

    def kernel(len_ref, query_ref, key_ref, value_ref, out_ref, stat_ref):
        start_at = pl.program_id(2) * block
        length = len_ref[pl.program_id(0)]
        queries = head_masks((query_ref[...].astype(jnp.float32) * scale).astype(jnp.bfloat16))
        values = head_masks(value_ref[...])
        total = jnp.zeros((block, PAIR), jnp.float32)
        stats = []
        for head in range(2):
            scores = kept_scores(queries[head], key_ref[...], length, causal, start_at)
            summit = jnp.max(scores, axis=1, keepdims=True)
            expo = jnp.exp(scores - summit)
            sums = jnp.sum(expo, axis=1, keepdims=True)
            probs = (expo * (1.0 / sums)).astype(jnp.bfloat16)
            total += jnp.dot(probs, values[head], preferred_element_type=jnp.float32)
            stats.append(summit + jnp.log(sums))
        out_ref[...] = total.astype(jnp.bfloat16)
        first = lax.broadcasted_iota(jnp.int32, (block, PAIR), 1) < HEAD_DIM
        stat_ref[...] = jnp.where(first, stats[0], stats[1])

    out_spec = pl.BlockSpec((block, PAIR), lambda seq, pair, step, lens: (seq * steps + step, pair))
    return pl.pallas_call(
        kernel,
        out_shape=(
            jax.ShapeDtypeStruct((MICRO * rows, D), jnp.bfloat16),
            jax.ShapeDtypeStruct((MICRO * rows, D), jnp.float32),
        ),
        grid_spec=pltpu.PrefetchScalarGridSpec(
            num_scalar_prefetch=1,
            grid=(MICRO, D // PAIR, steps),
            in_specs=[
                pl.BlockSpec((block, PAIR), lambda seq, pair, step, lens: (seq * steps + step, query_at + pair)),
                pl.BlockSpec((keys, PAIR), lambda seq, pair, step, lens: (seq, key_at + pair)),
                pl.BlockSpec((keys, PAIR), lambda seq, pair, step, lens: (seq, value_at + pair)),
            ],
            out_specs=(out_spec, out_spec),
        ),
        compiler_params=pltpu.CompilerParams(vmem_limit_bytes=40 * 2**20),
        cost_estimate=pl.CostEstimate(flops=4*MICRO*rows*keys*D, bytes_accessed=MICRO*(rows+keys)*D*8, transcendentals=MICRO*HEADS*rows*keys),
    )(valid_len, query_in, keys_in, keys_in)

def attend_backward(query_in, query_at, keys_in, key_at, value_at, valid_len, causal, stats, grad_out, first=0, seqs=MICRO, begun=()):
    rows, keys = (query_in.shape[0] // MICRO, keys_in.shape[0] // MICRO)
    block = min(512, rows)
    steps = rows // block
    scale = HEAD_DIM ** (-0.5)

    def kernel(len_ref, query_ref, key_ref, value_ref, stat_ref, up_ref, *refs):
        dq_ref, dk_ref, dv_ref, key_sum, value_sum = refs[len(begun) :]
        step = pl.program_id(2)
        start_at = step * block
        length = len_ref[first + pl.program_id(0)]
        queries = head_masks((query_ref[...].astype(jnp.float32) * scale).astype(jnp.bfloat16))
        upstream = head_masks(up_ref[...])
        keys_each = head_masks(key_ref[...])
        grad_query = jnp.zeros((block, PAIR), jnp.float32)
        grad_key = jnp.zeros((keys, PAIR), jnp.float32)
        grad_value = jnp.zeros((keys, PAIR), jnp.float32)
        over_rows = (((0,), (0,)), ((), ()))
        for head in range(2):
            scores = kept_scores(queries[head], key_ref[...], length, causal, start_at)
            probs = jnp.exp(scores - stat_ref[:, head * HEAD_DIM : head * HEAD_DIM + 1])
            grad_probs = lax.dot_general(upstream[head], value_ref[...], (((1,), (1,)), ((), ())), preferred_element_type=jnp.float32)
            inner = jnp.sum(probs * grad_probs, axis=1, keepdims=True)
            grad_scores = (probs * (grad_probs - inner)).astype(jnp.bfloat16)
            grad_query += jnp.dot(grad_scores, keys_each[head], preferred_element_type=jnp.float32)
            grad_key += lax.dot_general(grad_scores, queries[head], over_rows, preferred_element_type=jnp.float32)
            grad_value += lax.dot_general(probs.astype(jnp.bfloat16), upstream[head], over_rows, preferred_element_type=jnp.float32)
        dq_ref[...] = (grad_query * scale).astype(jnp.bfloat16)
        if steps == 1:
            dk_ref[...] = grad_key.astype(jnp.bfloat16)
            dv_ref[...] = grad_value.astype(jnp.bfloat16)
        else:
            @pl.when(step == 0)
            def _():
                key_sum[...] = grad_key
                value_sum[...] = grad_value

            @pl.when(step > 0)
            def _():
                key_sum[...] += grad_key
                value_sum[...] += grad_value

            @pl.when(step == steps - 1)
            def _():
                dk_ref[...] = key_sum[...].astype(jnp.bfloat16)
                dv_ref[...] = value_sum[...].astype(jnp.bfloat16)

    def row_spec(at, begin):
        return pl.BlockSpec(
            (block, PAIR),
            lambda seq, pair, step, lens: ((begin + seq) * steps + step, at + pair),
        )

    def key_spec(at, begin):
        return pl.BlockSpec((keys, PAIR), lambda seq, pair, step, lens: (begin + seq, at + pair))

    return pl.pallas_call(
        kernel,
        out_shape=(
            jax.ShapeDtypeStruct((MICRO * rows, D), jnp.bfloat16),
            jax.ShapeDtypeStruct((MICRO * keys, D), jnp.bfloat16),
            jax.ShapeDtypeStruct((MICRO * keys, D), jnp.bfloat16),
        ),
        grid_spec=pltpu.PrefetchScalarGridSpec(
            num_scalar_prefetch=1,
            grid=(seqs, D // PAIR, steps),
            in_specs=[
                row_spec(query_at, first),
                key_spec(key_at, first),
                key_spec(value_at, first),
                row_spec(0, first),
                row_spec(0, first),
            ]
            + [pl.BlockSpec(memory_space=pl.ANY)] * len(begun),
            out_specs=(row_spec(0, first), key_spec(0, first), key_spec(0, first)),
            scratch_shapes=[pltpu.VMEM((keys, PAIR), jnp.float32)] * 2,
        ),
        input_output_aliases={6 + item: item for item in range(len(begun))},
        compiler_params=pltpu.CompilerParams(vmem_limit_bytes=40 * 2**20),
        cost_estimate=pl.CostEstimate(flops=10*seqs*rows*keys*D, bytes_accessed=seqs*(rows+keys)*D*16, transcendentals=seqs*HEADS*rows*keys),
    )(valid_len, query_in, keys_in, keys_in, stats, grad_out, *begun)


def norm_backward(stream, gain_row, grad_normed):
    _, pull_back = jax.vjp(rms_norm, stream, gain_row)
    return pull_back(grad_normed)


def self_forward(stream, gain_row, weight, valid_len, causal):
    normed = rms_norm(stream, gain_row).astype(jnp.bfloat16)
    joint_qkv = linear(normed, weight[:, : 3 * D]).astype(jnp.bfloat16)
    pairs = D // PAIR
    mixed_out, stats_kept = attend_forward(
        joint_qkv, 0, joint_qkv, pairs, 2 * pairs, valid_len, causal
    )
    return (
        stream + linear(mixed_out, weight[:, 3 * D :]),
        (stream, normed, joint_qkv, mixed_out, stats_kept),
    )


def self_backward(grad_stream, kept_block, gain_row, weight, valid_len, causal, between=None):
    stream, normed, joint_qkv, mixed_out, stats_kept = kept_block
    grad_low = grad_stream.astype(jnp.bfloat16)
    grad_out_w = outer_sum(mixed_out, grad_low)
    grad_mixed = linear_tr(grad_low, weight[:, 3 * D :]).astype(jnp.bfloat16)
    pairs = D // PAIR
    stages = 1 if between is None else MICRO
    grads = ()
    for stage in range(stages):
        if stage > 0:
            grad_mixed = between(grad_mixed)
        grads = attend_backward(
            joint_qkv,
            0,
            joint_qkv,
            pairs,
            2 * pairs,
            valid_len,
            causal,
            stats_kept,
            grad_mixed,
            stage * MICRO // stages,
            MICRO // stages,
            tuple(grads),
        )
    grad_joint = jnp.concatenate(grads, 1)
    if between is not None:
        grad_joint = between(grad_joint)
    grad_x, grad_gain = norm_backward(stream, gain_row, linear_tr(grad_joint, weight[:, : 3 * D]))
    return (
        grad_stream + grad_x,
        grad_gain,
        jnp.concatenate([outer_sum(normed, grad_joint), grad_out_w], 1).astype(jnp.bfloat16),
    )


def cross_forward(stream, gain_row, weight, memory, valid_len):
    normed = rms_norm(stream, gain_row).astype(jnp.bfloat16)
    query_in = linear(normed, weight[:, :D]).astype(jnp.bfloat16)
    pair_kv = linear(memory, weight[:, D : 3 * D]).astype(jnp.bfloat16)
    mixed_out, stats_kept = attend_forward(
        query_in, 0, pair_kv, 0, D // PAIR, valid_len, False
    )
    return (
        stream + linear(mixed_out, weight[:, 3 * D :]),
        (stream, normed, query_in, pair_kv, mixed_out, stats_kept),
    )


def cross_backward(grad_stream, kept_block, gain_row, weight, memory, valid_len):
    stream, normed, query_in, pair_kv, mixed_out, stats_kept = kept_block
    grad_low = grad_stream.astype(jnp.bfloat16)
    grad_out_w = outer_sum(mixed_out, grad_low)
    grad_mixed = linear_tr(grad_low, weight[:, 3 * D :]).astype(jnp.bfloat16)
    grad_query, grad_k, grad_v = attend_backward(
        query_in, 0, pair_kv, 0, D // PAIR, valid_len, False, stats_kept, grad_mixed
    )
    grad_pair = jnp.concatenate([grad_k, grad_v], 1)
    grad_weight = jnp.concatenate(
        [outer_sum(normed, grad_query), outer_sum(memory, grad_pair), grad_out_w], 1
    ).astype(jnp.bfloat16)
    grad_x, grad_gain = norm_backward(stream, gain_row, linear_tr(grad_query, weight[:, :D]))
    return (
        grad_stream + grad_x,
        grad_gain,
        grad_weight,
        linear_tr(grad_pair, weight[:, D : 3 * D]),
    )


def gelu_tanh(hidden):
    return jax.nn.gelu(hidden, approximate=True)


def ffn_forward(stream, gain_row, w_in, w_out):
    normed = rms_norm(stream, gain_row).astype(jnp.bfloat16)
    hidden = linear(normed, w_in)
    active = gelu_tanh(hidden).astype(jnp.bfloat16)
    return (stream + linear_tr(active, w_out), (stream, normed, hidden, active))


def ffn_backward(grad_stream, kept_block, gain_row, w_in, w_out):
    stream, normed, hidden, active = kept_block
    grad_low = grad_stream.astype(jnp.bfloat16)
    grad_out_w = outer_sum(grad_low, active).astype(jnp.bfloat16)
    _, pull_back = jax.vjp(gelu_tanh, hidden)
    grad_hidden = pull_back(linear(grad_low, w_out))[0].astype(jnp.bfloat16)
    grad_x, grad_gain = norm_backward(stream, gain_row, linear_tr(grad_hidden, w_in))
    return (
        grad_stream + grad_x,
        grad_gain,
        outer_sum(normed, grad_hidden).astype(jnp.bfloat16),
        grad_out_w,
    )


def forward_all(
    weights,
    gain_set,
    source_rows,
    source_len,
    target_len,
    place_rows,
    lay_decoder,
):
    stream = source_rows
    enc_kept = []
    for layer_no in range(ENC):
        stream, kept_self = self_forward(
            stream, gain_set[2 * layer_no], weights[layer_no], source_len, False
        )
        stream, kept_ffn = ffn_forward(
            stream,
            gain_set[2 * layer_no + 1],
            weights[ENC + 2 * DEC + layer_no],
            weights[2 * ENC + 3 * DEC + layer_no],
        )
        enc_kept.append((kept_self, kept_ffn))
    memory, decoded = lay_decoder(rms_norm(stream, gain_set[2 * ENC]).astype(jnp.bfloat16))
    dec_kept, exit_in, exit_rows = ([], [], [])
    for layer_no in range(DEC):
        base_at = 2 * ENC + 1 + 3 * layer_no
        decoded, kept_self = self_forward(
            decoded, gain_set[base_at], weights[ENC + layer_no], target_len, True
        )
        decoded, kept_cross = cross_forward(
            decoded, gain_set[base_at + 1], weights[ENC + DEC + layer_no], memory, source_len
        )
        decoded, kept_ffn = ffn_forward(
            decoded,
            gain_set[base_at + 2],
            weights[2 * ENC + 2 * DEC + layer_no],
            weights[3 * ENC + 3 * DEC + layer_no],
        )
        dec_kept.append((kept_self, kept_cross, kept_ffn))
        picked_rows = decoded[place_rows]
        exit_in.append(picked_rows)
        exit_rows.append(
            rms_norm(picked_rows, gain_set[2 * ENC + 1 + 3 * DEC + layer_no]).astype(jnp.bfloat16)
        )
    kept = (source_len, target_len, place_rows, enc_kept, stream, memory, dec_kept, exit_in)
    return (kept, jnp.concatenate(exit_rows, 0))


def backward_all(
    weights, gain_set, kept, exit_grads, matrix_store, gain_store, before_last, between_last
):
    source_len, target_len, place_rows, enc_kept, stream, memory, dec_kept, exit_in = kept
    exit_each = jnp.split(exit_grads, DEC, axis=0)
    grad_decoded = jnp.zeros(dec_kept[0][0][0].shape, jnp.float32)
    grad_memory = jnp.zeros(memory.shape, jnp.float32)
    for layer_no in reversed(range(DEC)):
        base_at = 2 * ENC + 1 + 3 * layer_no
        exit_at = 2 * ENC + 1 + 3 * DEC + layer_no
        grad_rows, gain_store[exit_at] = norm_backward(
            exit_in[layer_no], gain_set[exit_at], exit_each[layer_no]
        )
        grad_decoded = grad_decoded.at[place_rows].add(grad_rows)
        kept_self, kept_cross, kept_ffn = dec_kept[layer_no]
        in_at, out_at = (2 * ENC + 2 * DEC + layer_no, 3 * ENC + 3 * DEC + layer_no)
        grad_decoded, gain_store[base_at + 2], matrix_store[in_at], matrix_store[out_at] = (
            ffn_backward(
                grad_decoded, kept_ffn, gain_set[base_at + 2], weights[in_at], weights[out_at]
            )
        )
        cross_at = ENC + DEC + layer_no
        grad_decoded, gain_store[base_at + 1], matrix_store[cross_at], grad_mem = cross_backward(
            grad_decoded, kept_cross, gain_set[base_at + 1], weights[cross_at], memory, source_len
        )
        grad_memory = grad_memory + grad_mem
        grad_decoded, gain_store[base_at], matrix_store[ENC + layer_no] = self_backward(
            grad_decoded, kept_self, gain_set[base_at], weights[ENC + layer_no], target_len, True
        )
    grad_stream, gain_store[2 * ENC] = norm_backward(stream, gain_set[2 * ENC], grad_memory)
    for layer_no in reversed(range(ENC)):
        kept_self, kept_ffn = enc_kept[layer_no]
        in_at, out_at = (ENC + 2 * DEC + layer_no, 2 * ENC + 3 * DEC + layer_no)
        grad_stream, gain_store[2 * layer_no + 1], matrix_store[in_at], matrix_store[out_at] = (
            ffn_backward(
                grad_stream, kept_ffn, gain_set[2 * layer_no + 1], weights[in_at], weights[out_at]
            )
        )
        if layer_no == 0:
            grad_stream = before_last(grad_stream)
        grad_stream, gain_store[2 * layer_no], matrix_store[layer_no] = self_backward(
            grad_stream,
            kept_self,
            gain_set[2 * layer_no],
            weights[layer_no],
            source_len,
            False,
            between_last if layer_no == 0 else None,
        )
    return (grad_stream, grad_decoded)


def fold_ranked(tiles, rank_of):
    count, half = (tiles.shape[0], PB // 2)

    def kernel(rank_ref, tile_ref, out_ref):
        def one_block(tile_no, carry):
            value = tile_ref[tile_no]
            folded = jnp.concatenate([value[:half], value[half:]], axis=1)
            out_ref[rank_ref[tile_no]] = folded.astype(jnp.bfloat16)
            return carry

        lax.fori_loop(0, count, one_block, 0)

    return pl.pallas_call(
        kernel,
        out_shape=jax.ShapeDtypeStruct((count, half, 2 * PB), jnp.bfloat16),
        grid_spec=pltpu.PrefetchScalarGridSpec(
            num_scalar_prefetch=1,
            grid=(1,),
            in_specs=[pl.BlockSpec(memory_space=pltpu.VMEM)],
            out_specs=pl.BlockSpec(memory_space=pltpu.VMEM),
        ),
        compiler_params=pltpu.CompilerParams(vmem_limit_bytes=40 * 2**20),
    )(rank_of, tiles)


def unfold_ranked(folded, rank_of):
    count, half = (folded.shape[0], PB // 2)

    def kernel(rank_ref, folded_ref, out_ref):
        def one_block(tile_no, carry):
            value = folded_ref[rank_ref[tile_no]]
            out_ref[tile_no, :half] = value[:, :PB]
            out_ref[tile_no, half:] = value[:, PB:]
            return carry

        lax.fori_loop(0, count, one_block, 0)

    return pl.pallas_call(
        kernel,
        out_shape=jax.ShapeDtypeStruct((count, PB, PB), jnp.float32),
        grid_spec=pltpu.PrefetchScalarGridSpec(
            num_scalar_prefetch=1,
            grid=(1,),
            in_specs=[pl.BlockSpec(memory_space=pltpu.VMEM)],
            out_specs=pl.BlockSpec(memory_space=pltpu.VMEM),
        ),
        compiler_params=pltpu.CompilerParams(vmem_limit_bytes=40 * 2**20),
    )(rank_of, folded)


def is_encoder(mat_no):
    return (
        mat_no < ENC
        or ENC + 2 * DEC <= mat_no < 2 * ENC + 2 * DEC
        or 2 * ENC + 3 * DEC <= mat_no < 3 * ENC + 3 * DEC
    )


def is_last(mat_no):
    return mat_no == 0


def rank_blocks(slot_list, devices, is_first):
    blocks_each = D // PB * (FF // PB)
    mats = slot_list // blocks_each
    early = jnp.zeros(mats.shape, jnp.bool_)
    for mat_no in range(MATS):
        if is_first(mat_no):
            early = early | (mats == mat_no)
    early = early.reshape(devices, -1).astype(jnp.int32)
    early_count = jnp.sum(early, axis=1)
    ahead = jnp.cumsum(early, axis=1) - early
    later = early_count[:, None] + jnp.arange(early.shape[1])[None, :] - ahead
    return (jnp.where(early == 1, ahead, later), early_count)


def room_for(per_device, chosen):
    share = sum(chosen(mat_no) for mat_no in range(MATS)) / MATS
    mean = per_device * share
    return min(per_device - 1, -(-int(mean + 4.2 * math.sqrt(mean * (1 - share))) // 4) * 4)


def by_block(slot_list, values):
    width, base = (64, 128)
    height = -(-slot_list.shape[0] // width)
    rows = (slot_list[:, None] // width == jnp.arange(height)[None, :]).astype(jnp.bfloat16)
    lanes = (slot_list[:, None] % width == jnp.arange(width)[None, :]).astype(jnp.bfloat16)
    found = []
    for value in values:
        high, low = (
            outer_sum(rows * (part.astype(jnp.bfloat16))[:, None], lanes)
            for part in (value // base, value % base)
        )
        found.append((high * base + low).astype(jnp.int32).reshape(-1)[: slot_list.shape[0]])
    return found


def lay_matrices(buffers, place_of, mats):
    half = PB // 2
    row_blocks, pairs = (D // PB, FF // (2 * PB))
    sizes = [buffer.shape[0] for buffer in buffers]
    starts = [sum(sizes[:item]) for item in range(len(sizes))]
    count = len(mats)

    def kernel(place_ref, *refs):
        sources, outs = (refs[: len(sizes)], refs[len(sizes) : len(sizes) + count])
        folded_ref, made, arrived, left = refs[len(sizes) + count :]
        left_half = lax.broadcasted_iota(jnp.int32, (half, 2 * PB), 1) < PB
        fetches = [
            pltpu.make_async_copy(
                source, folded_ref.at[pl.ds(start, size)], arrived.at[item]
            )
            for item, (source, start, size) in enumerate(zip(sources, starts, sizes))
        ]
        for fetch in fetches:
            fetch.start()
        for fetch in fetches:
            fetch.wait()

        def send(item):
            return pltpu.make_async_copy(made.at[item % 2], outs[item], left.at[item % 2])

        for item, mat_no in enumerate(mats):
            if item >= 2:
                send(item - 2).wait()

            def one_row(row_no, carry, item=item, mat_no=mat_no):
                first = (mat_no * row_blocks + row_no) * 2 * pairs
                row_at = pl.multiple_of(row_no * PB, PB)
                for pair_no in range(pairs):
                    even = folded_ref[place_ref[first + 2 * pair_no]].astype(jnp.float32)
                    odd = folded_ref[place_ref[first + 2 * pair_no + 1]].astype(jnp.float32)
                    columns = slice(2 * PB * pair_no, 2 * PB * (pair_no + 1))
                    upper = jnp.where(left_half, even, pltpu.roll(odd, PB, 1))
                    lower = jnp.where(left_half, pltpu.roll(even, PB, 1), odd)
                    made[item % 2, pl.ds(row_at, half), columns] = upper.astype(jnp.bfloat16)
                    made[item % 2, pl.ds(row_at + half, half), columns] = lower.astype(jnp.bfloat16)
                return carry

            lax.fori_loop(0, row_blocks, one_row, 0)
            send(item).start()
        for item in range(max(count - 2, 0), count):
            send(item).wait()

    return pl.pallas_call(
        kernel,
        out_shape=[jax.ShapeDtypeStruct((D, FF), jnp.bfloat16)] * count,
        grid_spec=pltpu.PrefetchScalarGridSpec(
            num_scalar_prefetch=1,
            grid=(1,),
            in_specs=[pl.BlockSpec(memory_space=pl.ANY)] * len(sizes),
            out_specs=[pl.BlockSpec(memory_space=pl.ANY)] * count,
            scratch_shapes=[
                pltpu.VMEM((sum(sizes), half, 2 * PB), jnp.bfloat16),
                pltpu.VMEM((2, D, FF), jnp.bfloat16),
                pltpu.SemaphoreType.DMA((len(sizes),)),
                pltpu.SemaphoreType.DMA((2,)),
            ],
        ),
        compiler_params=pltpu.CompilerParams(vmem_limit_bytes=40 * 2**20),
    )(place_of, *buffers)


def fold_gradients(matrices, mats, place_of, sizes, begun=None):
    half = PB // 2
    row_blocks, pairs = (D // PB, FF // (2 * PB))
    count = len(mats)
    whole = sum(sizes)
    given = 0 if begun is None else 1
    skipped = 0 if begun is None else whole - begun.shape[0]
    kept = whole - skipped

    def kernel(place_ref, *refs):
        sources, old = (refs[:count], refs[count : count + given])
        outs = refs[count + given : -5]
        folded_ref, held, arrived, left, old_sem = refs[-5:]
        left_half = lax.broadcasted_iota(jnp.int32, (half, 2 * PB), 1) < PB

        def fetch(item):
            return pltpu.make_async_copy(sources[item], held.at[item % 2], arrived.at[item % 2])

        fetch(0).start()
        if given:
            before = pltpu.make_async_copy(
                old[0], folded_ref.at[pl.ds(0, kept)], old_sem.at[0]
            )
            before.start()
            before.wait()
        for item, mat_no in enumerate(mats):
            if item + 1 < count:
                fetch(item + 1).start()
            fetch(item).wait()

            def place(block, carry=None):
                spot = place_ref[block] - skipped
                return jnp.where(spot < 0, kept, spot) if given else spot

            def one_row(row_no, carry, item=item, mat_no=mat_no):
                first = (mat_no * row_blocks + row_no) * 2 * pairs
                row_at = pl.multiple_of(row_no * PB, PB)
                for pair_no in range(pairs):
                    columns = slice(2 * PB * pair_no, 2 * PB * (pair_no + 1))
                    upper = held[item % 2, pl.ds(row_at, half), columns].astype(jnp.float32)
                    lower = held[item % 2, pl.ds(row_at + half, half), columns].astype(jnp.float32)
                    even = jnp.where(left_half, upper, pltpu.roll(lower, PB, 1))
                    odd = jnp.where(left_half, pltpu.roll(upper, PB, 1), lower)
                    folded_ref[place(first + 2 * pair_no)] = even.astype(jnp.bfloat16)
                    folded_ref[place(first + 2 * pair_no + 1)] = odd.astype(jnp.bfloat16)
                return carry

            lax.fori_loop(0, row_blocks, one_row, 0)
        begin = 0
        sends = []
        for item, out in enumerate(outs):
            size = out.shape[0]
            sends.append(
                pltpu.make_async_copy(folded_ref.at[pl.ds(begin, size)], out, left.at[item])
            )
            begin += size
        for send in sends:
            send.start()
        for send in sends:
            send.wait()

    shapes = [kept] if given else list(sizes)
    return pl.pallas_call(
        kernel,
        out_shape=[jax.ShapeDtypeStruct((size, half, 2 * PB), jnp.bfloat16) for size in shapes],
        grid_spec=pltpu.PrefetchScalarGridSpec(
            num_scalar_prefetch=1,
            grid=(1,),
            in_specs=[pl.BlockSpec(memory_space=pl.ANY)] * (count + given),
            out_specs=[pl.BlockSpec(memory_space=pl.ANY)] * len(shapes),
            scratch_shapes=[
                pltpu.VMEM((kept + given, half, 2 * PB), jnp.bfloat16),
                pltpu.VMEM((2, D, FF), jnp.bfloat16),
                pltpu.SemaphoreType.DMA((2,)),
                pltpu.SemaphoreType.DMA((2,)),
                pltpu.SemaphoreType.DMA((1,)),
            ],
        ),
        compiler_params=pltpu.CompilerParams(vmem_limit_bytes=40 * 2**20),
    )(place_of, *[matrices[mat_no] for mat_no in mats], *([begun] if given else []))


def exchange_plan(dp_size, along, per_device):
    low, high = (along.bit_length() - 1, dp_size.bit_length() - 1)
    base = [low + bit for bit in range(high)] + list(range(1, low))
    third = per_device // 3
    sizes = [per_device - 2 * third, third, third]
    return [(size, base[turn:] + base[:turn]) for turn, size in enumerate(sizes)]


def places_for(ranks, plan, devices):
    per_device = sum(size for size, _ in plan)
    owner = jnp.arange(devices)[:, None]
    place = jnp.zeros_like(ranks)
    begin = 0
    for size, order in plan:
        spot = jnp.zeros_like(owner)
        for bit in order:
            spot = spot * 2 + owner // 2**bit % 2
        here = begin * (devices // 2) + spot * size + ranks - begin
        place = jnp.where((ranks >= begin) & (ranks < begin + size), here, place)
        begin += size
    return place + owner % 2 * (devices // 2 * per_device)


def halve(value, bit, devices):
    me = lax.axis_index("dp") * lax.axis_size("vocab") + lax.axis_index("vocab")

    mine = me // 2**bit % 2
    value = value.reshape(2, value.shape[0] // 2, *value.shape[1:])
    sent = lax.dynamic_index_in_dim(value, 1 - mine, 0, keepdims=False)
    kept = lax.dynamic_index_in_dim(value, mine, 0, keepdims=False)
    pairs = [(index, index ^ 2**bit) for index in range(devices)]
    arrived = lax.ppermute(sent, ("dp", "vocab"), pairs)
    return kept.astype(jnp.float32) + arrived.astype(jnp.float32)


def first_exchange(folded, devices):
    return halve(folded, 0, devices).astype(jnp.bfloat16)


def split_parts(total, plan, devices):
    parts, begin = ([], 0)
    for size, _ in plan:
        count = size * (devices // 2)
        parts.append(total[begin : begin + count])
        begin += count
    return parts


def one_exchange(parts, plan, round_no, devices):
    return [
        halve(part.astype(jnp.bfloat16), order[round_no], devices)
        for part, (_, order) in zip(parts, plan)
    ]


def other_exchanges(parts, plan, devices, done=0):
    for round_no in range(done, len(plan[0][1])):
        parts = one_exchange(parts, plan, round_no, devices)
    return jnp.concatenate(parts, 0)


def take_rows(source, index_at, kind):
    count, width, block = (index_at.shape[0], source.shape[1], 128)
    whole = -(-count // block) * block
    index_at = jnp.pad(index_at, (0, whole - count))

    def kernel(index_ref, source_ref, out_ref, held_ref):
        first = pl.program_id(0) * block

        def copy_eight(group, carry):
            base = pl.multiple_of(group * 8, 8)
            for row_no in range(8):
                held_ref[pl.ds(base + row_no, 1), :] = source_ref[
                    pl.ds(index_ref[first + base + row_no], 1), :
                ]
            return carry

        lax.fori_loop(0, block // 8, copy_eight, 0)
        out_ref[...] = held_ref[...].astype(kind)

    taken = pl.pallas_call(
        kernel,
        out_shape=jax.ShapeDtypeStruct((whole, width), kind),
        grid_spec=pltpu.PrefetchScalarGridSpec(
            num_scalar_prefetch=1,
            grid=(whole // block,),
            in_specs=[pl.BlockSpec(memory_space=pltpu.VMEM)],
            out_specs=pl.BlockSpec((block, width), lambda step, index: (step, 0)),
            scratch_shapes=[pltpu.VMEM((block, width), jnp.float32)],
        ),
        compiler_params=pltpu.CompilerParams(vmem_limit_bytes=40 * 2**20),
    )(index_at, source)
    return taken[:count]


def add_rows(rows, index_at, total):
    count, width, block = (rows.shape[0], rows.shape[1], 512)
    whole = -(-count // block) * block
    index_at = jnp.pad(index_at, (0, whole - count), constant_values=-1)[None, :]
    rows = jnp.pad(rows, ((0, whole - count), (0, 0)))
    height = total.shape[0]

    def kernel(index_ref, rows_ref, total_ref, out_ref):
        @pl.when(pl.program_id(0) == 0)
        def _():
            out_ref[...] = total_ref[...]

        hits = lax.broadcasted_iota(jnp.int32, (height, block), 0) == index_ref[...]
        out_ref[...] += jnp.dot(
            hits.astype(jnp.float32).astype(jnp.bfloat16),
            rows_ref[...],
            preferred_element_type=jnp.float32,
        )

    return pl.pallas_call(
        kernel,
        out_shape=jax.ShapeDtypeStruct(total.shape, jnp.float32),
        grid=(whole // block,),
        in_specs=[
            pl.BlockSpec((1, block), lambda step: (0, step)),
            pl.BlockSpec((block, width), lambda step: (step, 0)),
            pl.BlockSpec((height, width), lambda step: (0, 0)),
        ],
        out_specs=pl.BlockSpec((height, width), lambda step: (0, 0)),
        compiler_params=pltpu.CompilerParams(vmem_limit_bytes=40 * 2**20),
    )(index_at, rows, total)


def spread(value, axes, peers):
    return lax.all_to_all(
        jnp.broadcast_to(value[None], (peers, *value.shape)), axes, 0, 0, tiled=True
    )


def count_before(mask):
    size, width = (mask.shape[-1], 128)
    parts = mask.reshape(*mask.shape[:-1], size // width, width).astype(jnp.bfloat16)
    earlier = (jnp.arange(width)[:, None] < jnp.arange(width)[None, :]).astype(jnp.bfloat16)
    inside = jnp.einsum("...pw,wk->...pk", parts, earlier, preferred_element_type=jnp.float32)
    totals = jnp.sum(parts.astype(jnp.float32), axis=-1)
    ahead = jnp.cumsum(totals, axis=-1) - totals
    return (inside + ahead[..., None]).reshape(mask.shape).astype(jnp.int32)


def room(count, peers):
    mean = count / peers
    return min(count, -(-int(mean + 5.0 * math.sqrt(mean)) // 16) * 16)


def listed(mask, rank, values, size):
    width, base = (16, 128)
    rows = mask[..., None] & (rank[..., None] // width == jnp.arange(size // width))
    lanes = (rank[..., None] % width == jnp.arange(width)).astype(jnp.bfloat16)
    values = values + 1
    high, low = (
        jnp.einsum(
            "...th,...tl->...hl",
            jnp.where(rows, part[..., None].astype(jnp.bfloat16), 0),
            lanes,
            preferred_element_type=jnp.float32,
        )
        for part in (values // base, values % base)
    )
    return (high * base + low).astype(jnp.int32).reshape(*mask.shape[:-1], size) - 1


def rounds_needed(owner_all, peers, size):
    held = jnp.sum((owner_all[:, None, :] == jnp.arange(peers)[:, None]).astype(jnp.int32), axis=2)
    return (jnp.max(held) + size - 1) // size


def fetch_plan(table_part, tokens_all, peers_here, peer_me):
    peers, rows_each = (peers_here.shape[0], table_part.shape[0])
    count = tokens_all.shape[1]
    size = room(count, peers)
    asked = peers_here // rows_each == peer_me
    asked_rank = count_before(asked)
    own_tokens = lax.dynamic_index_in_dim(peers_here, peer_me, 0, keepdims=False)
    own_owner = own_tokens // rows_each
    own_mask = own_owner[None, :] == jnp.arange(peers)[:, None]
    own_rank = jnp.sum(jnp.where(own_mask, count_before(own_mask), 0), axis=0)

    def to_send(round_no):
        wanted = listed(
            asked, asked_rank - round_no * size, peers_here % rows_each, size
        )
        return take_rows(table_part, jnp.maximum(wanted.reshape(-1), 0), jnp.bfloat16)

    def found_in(arrived, round_no):
        rank_now = own_rank - round_no * size
        now = (rank_now >= 0) & (rank_now < size)
        found = take_rows(
            arrived.astype(jnp.float32), jnp.where(now, own_owner * size + rank_now, 0), jnp.float32
        )
        return (now, found)

    def again(round_no, rows):
        now, found = found_in(swap_rows(to_send(round_no)), round_no)
        return jnp.where(now[:, None], found, rows)

    rounds = rounds_needed(tokens_all // rows_each, peers, size)

    def finish(arrived):
        return lax.fori_loop(1, rounds, again, found_in(arrived, 0)[1])

    return (to_send(0), finish)


def swap_rows(rows):
    return lax.all_to_all(rows, "vocab", 0, 0, tiled=True)


def return_plan(tokens_all, rows_each, dp_size):
    peers, count = tokens_all.shape
    along = peers // dp_size
    quarter = rows_each // dp_size
    me = lax.axis_index("dp") * along + lax.axis_index("vocab")
    size = room(count, peers)
    owner_all = (tokens_all % rows_each) // quarter * along + tokens_all // rows_each
    arriving = owner_all == me
    arriving_rank = count_before(arriving)
    own_owner = lax.dynamic_index_in_dim(owner_all, me, 0, keepdims=False)
    leaving = own_owner[None, :] == jnp.arange(peers)[:, None]
    leaving_rank = count_before(leaving)
    place = jnp.broadcast_to(jnp.arange(count)[None, :], leaving.shape)

    def lists(round_no):
        return (
            jnp.maximum(
                listed(leaving, leaving_rank - round_no * size, place, size).reshape(-1), 0
            ),
            listed(
                arriving, arriving_rank - round_no * size, tokens_all % quarter, size
            ).reshape(-1),
        )

    return (lists, rounds_needed(owner_all, peers, size))


def return_rows(grad_rows, lists, first_lists, rounds, total, ready, landed):
    def swap_all(rows):
        return lax.all_to_all(rows, ("dp", "vocab"), 0, 0, tiled=True)

    def again(round_no, so_far):
        chosen, where = lists(round_no)
        return add_rows(swap_all(take_rows(grad_rows, chosen, jnp.bfloat16)), where, so_far)

    arrived = landed(swap_all(ready(take_rows(grad_rows, first_lists[0], jnp.bfloat16))))
    return lax.fori_loop(1, rounds, again, add_rows(arrived, first_lists[1], total))


def turn_in(left_basis, tiles, right_basis):
    half = jnp.einsum("tki,tkl->til", left_basis, tiles, precision=HIGH)
    return jnp.einsum("til,tlj->tij", half, right_basis, precision=HIGH)


def turn_out(left_basis, tiles, right_basis):
    half = jnp.einsum("tik,tkl->til", left_basis, tiles, precision=HIGH)
    return jnp.einsum("til,tjl->tij", half, right_basis, precision=HIGH)


def orthonormal(columns):
    lanes, group = (128, 4)

    def kernel(in_ref, out_ref):
        out_ref[...] = in_ref[...]

        def four_columns(group_at, carry):
            first = group_at * group
            pivots = []
            for item in range(group):
                pivot = out_ref[first + item]
                for before in pivots:
                    pivot = pivot - jnp.sum(before * pivot, axis=0, keepdims=True) * before
                pivot = pivot / jnp.sqrt(jnp.sum(pivot * pivot, axis=0, keepdims=True))
                out_ref[first + item] = pivot
                pivots.append(pivot)

            def one_group(group_no, inner):
                held = [out_ref[group_no * group + item] for item in range(group)]
                for item in range(group):
                    value = held[item]
                    shares = [
                        jnp.sum(pivot * value, axis=0, keepdims=True) for pivot in pivots
                    ]
                    for pivot, share in zip(pivots, shares):
                        value = value - share * pivot
                    held[item] = value
                for item in range(group):
                    out_ref[group_no * group + item] = held[item]
                return inner

            return lax.fori_loop(group_at + 1, PB // group, one_group, carry)

        lax.fori_loop(0, PB // group, four_columns, 0)

    spec = pl.BlockSpec((PB, PB, lanes), lambda step: (0, 0, step))
    return pl.pallas_call(
        kernel,
        out_shape=jax.ShapeDtypeStruct(columns.shape, jnp.float32),
        grid=(columns.shape[2] // lanes,),
        in_specs=[spec],
        out_specs=spec,
        compiler_params=pltpu.CompilerParams(vmem_limit_bytes=40 * 2**20),
    )(columns)


def renew_bases(left_moved, right_moved):
    moved = jnp.concatenate([left_moved, right_moved], 0)
    count = moved.shape[0]
    whole = -(-count // 128) * 128
    columns = jnp.pad(jnp.transpose(moved, (2, 1, 0)), ((0, 0), (0, 0), (0, whole - count)))
    renewed = jnp.transpose(orthonormal(columns)[:, :, :count], (2, 1, 0))
    return (renewed[: count // 2], renewed[count // 2 :])


def turned_by(stat, basis):
    return jnp.einsum("tij,tjk->tik", stat, basis, precision=HIGH)


def soap_update(
    master,
    grad_tiles,
    grad_turned,
    left_outer,
    right_outer,
    left_moves,
    right_moves,
    first_mom,
    first_turned,
    second_mom,
    left_stat,
    right_stat,
    left_basis,
    right_basis,
    factor,
):
    first_new = BETA_FIRST * first_mom + (1 - BETA_FIRST) * (factor * grad_tiles)
    grad_turned = factor * grad_turned
    first_turned = BETA_FIRST * first_turned + (1 - BETA_FIRST) * grad_turned
    second_new = BETA_SECOND * second_mom + (1 - BETA_SECOND) * grad_turned * grad_turned
    direction = (
        first_turned
        / (1 - BETA_FIRST**STEP)
        / (jnp.sqrt(second_new / (1 - BETA_SECOND**STEP)) + ADAM_EPS)
    )
    master_new = master - RATE_MATRIX * (
        turn_out(left_basis, direction, right_basis) + DECAY * master
    )
    left_new = BETA_STAT * left_stat + (1 - BETA_STAT) * (factor * (factor * left_outer))
    right_new = BETA_STAT * right_stat + (1 - BETA_STAT) * (factor * (factor * right_outer))
    return (
        master_new,
        first_new,
        second_new,
        left_new,
        right_new,
        *renew_bases(
            *(
                BETA_STAT * before + (1 - BETA_STAT) * (factor * (factor * change))
                for before, change in (left_moves, right_moves)
            )
        ),
    )


def adamw_update(master, grad_now, first_mom, second_mom, rate, decay_by):
    first_new = BETA_FIRST * first_mom + (1 - BETA_FIRST) * grad_now
    second_new = BETA_SECOND * second_mom + (1 - BETA_SECOND) * grad_now * grad_now
    direction = (
        first_new
        / (1 - BETA_FIRST**STEP)
        / (jnp.sqrt(second_new / (1 - BETA_SECOND**STEP)) + ADAM_EPS)
    )
    return (master - rate * (direction + decay_by * master), first_new, second_new)


def per_device(
    master_tiles,
    mom1_tiles,
    mom2_tiles,
    stat_left,
    stat_right,
    basis_left,
    basis_right,
    table_master,
    table_mom1,
    table_mom2,
    gains,
    gain_mom1,
    gain_mom2,
    source_ids,
    target_ids,
    source_len,
    target_len,
    loss_place,
    exit_layer,
    slot_list,
):
    dp_size, along = (lax.axis_size("dp"), lax.axis_size("vocab"))
    dp_me, peer_me = (lax.axis_index("dp"), lax.axis_index("vocab"))
    devices = dp_size * along
    rows_each = table_master.shape[0]
    quarter = rows_each // dp_size
    source_len, target_len = (source_len[:, 0], target_len[:, 0])

    shifted = jnp.pad(target_ids[:, 0, :-1], ((0, 0), (1, 0)))
    tokens = jnp.concatenate([source_ids.reshape(-1), shifted.reshape(-1)])
    places = loss_place[:, 0]
    counted = places < target_len[:, None]
    reach = [
        jnp.sum((counted & (exit_layer[:, 0] >= layer_no)).astype(jnp.int32))
        for layer_no in range(DEC)
    ]
    labels = jnp.take_along_axis(target_ids[:, 0], places, axis=1).reshape(-1)
    row_count = MICRO * LOSS_POS
    own_facts = jnp.concatenate(
        [tokens, labels, counted.reshape(-1).astype(jnp.int32), jnp.stack(reach)]
    )
    fact_count = own_facts.shape[0]
    own_facts = jnp.pad(own_facts, (0, -fact_count % 128))
    facts = spread(own_facts, ("dp", "vocab"), devices)
    slots_later, facts, mom1_later, left_later, right_later = lax.optimization_barrier(
        (slot_list, facts, mom1_tiles, basis_left, basis_right)
    )
    tokens_all = facts[:, : tokens.shape[0]]
    after = facts[:, tokens.shape[0] :]
    labels_all = after[:, :row_count]
    counted_all = after[:, row_count : 2 * row_count].astype(jnp.float32)
    reach_all = jnp.sum(after[:, 2 * row_count : 2 * row_count + DEC].astype(jnp.float32), axis=0)
    count_all = jnp.sum(counted_all)
    fraction = reach_all / jnp.sum(reach_all)

    per_device = master_tiles.shape[0]
    me = dp_me * along + peer_me
    ranks, early_count = rank_blocks(slot_list, devices, is_encoder)
    first_size = room_for(per_device, is_encoder)
    second_size = per_device - first_size
    place_at = jnp.where(
        ranks < first_size,
        jnp.arange(devices)[:, None] * first_size + ranks,
        devices * first_size
        + jnp.arange(devices)[:, None] * second_size
        + ranks
        - first_size,
    )
    late_size = room_for(per_device, is_last)
    soon_size = per_device - late_size
    back_ranks, soon_count = rank_blocks(slots_later, devices, lambda mat_no: not is_last(mat_no))
    soon_plan = exchange_plan(dp_size, along, soon_size)
    late_plan = exchange_plan(dp_size, along, late_size)
    back_at = jnp.where(
        back_ranks < soon_size,
        places_for(back_ranks, soon_plan, devices),
        devices * soon_size + places_for(back_ranks - soon_size, late_plan, devices),
    )
    place_of, back_of = by_block(slots_later, [place_at.reshape(-1), back_at.reshape(-1)])
    own_folded = fold_ranked(
        master_tiles, lax.dynamic_index_in_dim(ranks, me, 0, keepdims=False)
    )
    src_count, tgt_count = (source_ids.shape[2], target_ids.shape[2])

    def planned(first, length):
        ids_all = tokens_all[:, first : first + MICRO * length]
        peers_here = lax.dynamic_slice_in_dim(ids_all, dp_me * along, along, 0)
        return fetch_plan(table_master, ids_all, peers_here, peer_me)

    source_sent, source_finish = planned(0, src_count)
    target_sent, target_finish = planned(MICRO * src_count, tgt_count)
    first_tiles = lax.all_gather(own_folded[:first_size], ("dp", "vocab"), axis=0, tiled=True)
    lists, rounds = return_plan(tokens_all, rows_each, dp_size)
    (
        own_second,
        first_tiles,
        source_arrived,
        first_lists,
        first_turned,
        target_sent,
        place_of,
        wave_set,
    ) = lax.optimization_barrier(
        (
            own_folded[first_size:],
            first_tiles,
            swap_rows(source_sent),
            lists(0),
            turn_in(left_later, mom1_later, right_later),
            target_sent,
            place_of,
            waves(src_count, D),
        )
    )
    second_tiles = lax.all_gather(own_second, ("dp", "vocab"), axis=0, tiled=True)
    encoder_mats = [mat_no for mat_no in range(MATS) if is_encoder(mat_no)]
    decoder_mats = [mat_no for mat_no in range(MATS) if not is_encoder(mat_no)]

    def lay_with_all():
        others = lax.all_gather(own_second, ("dp", "vocab"), axis=0, tiled=True)
        return lay_matrices([first_tiles, others], place_of, encoder_mats)

    def lay_with_first():
        return lay_matrices([first_tiles], place_of, encoder_mats)

    encoder_set = lax.cond(
        jnp.max(early_count) > first_size, lay_with_all, lay_with_first
    )
    weights = [None] * MATS
    for mat_no, matrix in zip(encoder_mats, encoder_set):
        weights[mat_no] = matrix

    def lay_decoder(memory):
        held, tiles, arrived = lax.optimization_barrier((memory, second_tiles, target_arrived))
        decoder_set = lay_matrices([first_tiles, tiles], place_of, decoder_mats)
        for mat_no, matrix in zip(decoder_mats, decoder_set):
            weights[mat_no] = matrix
        return (held, with_waves(target_finish(arrived), tgt_count))

    def with_waves(rows, length):
        return rows * math.sqrt(D) + jnp.tile(wave_set[:length], (MICRO, 1))

    source_rows = with_waves(source_finish(source_arrived), src_count)
    source_rows, target_sent = lax.optimization_barrier((source_rows, target_sent))
    target_arrived = swap_rows(target_sent)

    place_rows = (places + jnp.arange(MICRO)[:, None] * tgt_count).reshape(-1)
    kept, exit_rows = forward_all(
        weights,
        gains,
        source_rows,
        source_len,
        target_len,
        place_rows,
        lay_decoder,
    )

    table_low_part = table_master.astype(jnp.bfloat16)
    exit_count = DEC * row_count
    exit_all = lax.all_gather(exit_rows, ("dp", "vocab"), axis=0, tiled=True)
    exit_here = spread(exit_rows, "vocab", along).reshape(-1, D)
    label_rows = jnp.tile(labels_all, (1, DEC)).reshape(-1)
    weight_rows = (
        jnp.repeat(fraction, row_count)[None, :] * jnp.tile(counted_all, (1, DEC))
    ).reshape(-1)
    group_rows = along * exit_count
    group_at = dp_me * group_rows
    label_here = lax.dynamic_slice_in_dim(label_rows, group_at, group_rows, 0)
    weight_here = lax.dynamic_slice_in_dim(weight_rows, group_at, group_rows, 0)
    logits = linear_tr(exit_here, table_low_part)
    hit_here = label_here[:, None] - peer_me * rows_each == jnp.arange(rows_each)[None, :]
    summit = jnp.max(logits, axis=1)
    spread_part = jnp.sum(jnp.exp(logits - summit[:, None]), axis=1)
    picked_part = jnp.sum(jnp.where(hit_here, logits, 0.0), axis=1)
    stats = spread(
        jnp.stack([summit, spread_part, picked_part]), ("dp", "vocab"), devices
    ).reshape(dp_size, along, 3, group_rows)
    summit_all = jnp.max(stats[:, :, 0], axis=1)
    total_all = jnp.sum(stats[:, :, 1] * jnp.exp(stats[:, :, 0] - summit_all[:, None]), axis=1)
    spread_all = summit_all + jnp.log(total_all)
    picked_all = jnp.sum(stats[:, :, 2], axis=1)
    loss_sum = jnp.sum(weight_rows * (spread_all - picked_all).reshape(-1))
    spread_here = lax.dynamic_index_in_dim(spread_all, dp_me, 0, keepdims=False)

    def logit_grads(logit_set, spread, weight_set, hits):
        return (
            (weight_set / count_all)[:, None]
            * (jnp.exp(logit_set - spread[:, None]) - hits.astype(jnp.float32))
        ).astype(jnp.bfloat16)

    grads_here = logit_grads(logits, spread_here, weight_here, hit_here)
    grad_parts = linear(grads_here, table_low_part).astype(jnp.bfloat16)
    grad_parts = lax.all_to_all(grad_parts, "vocab", 0, 0, tiled=True)
    exit_grads = jnp.sum(
        grad_parts.reshape(along, exit_count, D).astype(jnp.float32), axis=0
    )

    matrix_store = [None] * MATS
    gain_store = [None] * GAINS
    first_row = peer_me * rows_each + dp_me * quarter
    table_quarter = lax.dynamic_slice_in_dim(table_low_part, dp_me * quarter, quarter, 0)
    hit_quarter = label_rows[:, None] - first_row == jnp.arange(quarter)[None, :]
    grads_quarter = logit_grads(
        linear_tr(exit_all, table_quarter), spread_all.reshape(-1), weight_rows, hit_quarter
    )
    grad_quarter = outer_sum(grads_quarter, exit_all)
    soon_mats = [mat_no for mat_no in range(MATS) if not is_last(mat_no)]
    late_mats = [mat_no for mat_no in range(MATS) if is_last(mat_no)]
    both = [devices * soon_size, devices * late_size]
    held = {}

    def gain_sums(gain_rows):
        count = gain_rows.shape[0] * D
        share = -(-count // (devices * 128)) * 128
        flat = jnp.pad(gain_rows.reshape(-1), (0, devices * share - count))
        parts = lax.all_to_all(
            flat.reshape(devices, share), ("dp", "vocab"), 0, 0, tiled=True
        )
        summed = spread(jnp.sum(parts, axis=0)[None], ("dp", "vocab"), devices)
        return summed.reshape(-1)[:count].reshape(gain_rows.shape)

    def before_last(grad_stream):
        held["gains"] = gain_sums(jnp.stack(gain_store[1:]))
        blocks, held["begun"] = fold_gradients(matrix_store, soon_mats, back_of, both)
        grad_stream, blocks, held["quarter"] = lax.optimization_barrier(
            (grad_stream, blocks, grad_quarter)
        )
        held["total"] = first_exchange(blocks, devices)
        return grad_stream

    def between_last(value):
        if "parts" not in held:
            value, total, held["gains"] = lax.optimization_barrier(
                (value, held["total"], held["gains"])
            )
            held["parts"], held["done"] = (split_parts(total, soon_plan, devices), 0)
        elif held["done"] < len(soon_plan[0][1]):
            parts = one_exchange(held["parts"], soon_plan, held["done"], devices)
            value, held["parts"] = lax.optimization_barrier((value, parts))
            held["done"] += 1
        return value

    grad_source, grad_target = backward_all(
        weights,
        gains,
        kept,
        exit_grads,
        matrix_store,
        gain_store,
        before_last,
        between_last,
    )

    grad_source = between_last(grad_source)
    grad_rows = jnp.concatenate([grad_source, grad_target], 0) * math.sqrt(D)
    grad_rows = between_last(grad_rows)
    [late_blocks] = fold_gradients(matrix_store, late_mats, back_of, both, held["begun"])
    late_total = first_exchange(late_blocks, devices)
    grad_rows, late_total = lax.optimization_barrier((grad_rows, late_total))
    late_parts = split_parts(late_total, late_plan, devices)
    late_parts = one_exchange(late_parts, late_plan, 0, devices)

    late_sum = other_exchanges(late_parts, late_plan, devices, 1)

    def exchange_again():
        blocks, _ = fold_gradients(matrix_store, list(range(MATS)), back_of, both)
        parts = split_parts(first_exchange(blocks, devices), soon_plan, devices)
        return other_exchanges(parts, soon_plan, devices)

    def ready(rows):
        sums = other_exchanges(held["parts"], soon_plan, devices, held["done"])
        rows, sums, late = lax.optimization_barrier((rows, sums, late_sum))
        sums = lax.cond(jnp.min(soon_count) < soon_size, exchange_again, lambda: sums)
        owned_grad = unfold_ranked(
            jnp.concatenate([sums, late], 0),
            lax.dynamic_index_in_dim(back_ranks, me, 0, keepdims=False),
        )
        left_outer = jnp.einsum("tik,tjk->tij", owned_grad, owned_grad, precision=HIGH)
        right_outer = jnp.einsum("tki,tkj->tij", owned_grad, owned_grad, precision=HIGH)
        held["owned"] = (
            owned_grad,
            turn_in(basis_left, owned_grad, basis_right),
            left_outer,
            right_outer,
            (turned_by(stat_left, basis_left), turned_by(left_outer, basis_left)),
            (turned_by(stat_right, basis_right), turned_by(right_outer, basis_right)),
            jnp.sum(owned_grad * owned_grad),
        )
        return rows

    def landed(arrived):
        arrived, held["owned"] = lax.optimization_barrier((arrived, held["owned"]))
        return arrived

    grad_quarter = return_rows(
        grad_rows, lists, first_lists, rounds, held["quarter"], ready, landed
    )

    (
        owned_grad,
        owned_turned,
        left_outer,
        right_outer,
        left_moves,
        right_moves,
        owned_squares,
    ) = held["owned"]
    squares = owned_squares + jnp.sum(grad_quarter * grad_quarter)
    last_facts = jnp.concatenate([gain_store[0].reshape(-1, 128), jnp.full((1, 128), squares)], 0)
    last_facts = spread(last_facts, ("dp", "vocab"), devices)
    last_facts = jnp.sum(last_facts.reshape(devices, -1, 128), axis=0)
    square_total = last_facts[-1, 0]
    gain_total = jnp.concatenate([last_facts[:-1].reshape(1, D), held["gains"]], 0)
    grad_norm = jnp.sqrt(square_total + jnp.sum(gain_total * gain_total))
    factor = jnp.minimum(1.0, CLIP_AT / grad_norm)
    table_grad = lax.all_gather(
        grad_quarter.astype(jnp.bfloat16), "dp", axis=0, tiled=True
    ).astype(jnp.float32)
    master_new, mom1_new, mom2_new, left_new, right_new, bleft_new, bright_new = soap_update(
        master_tiles,
        owned_grad,
        owned_turned,
        left_outer,
        right_outer,
        left_moves,
        right_moves,
        mom1_tiles,
        first_turned,
        mom2_tiles,
        stat_left,
        stat_right,
        basis_left,
        basis_right,
        factor,
    )
    table_new, table_m, table_v = adamw_update(
        table_master, table_grad * factor, table_mom1, table_mom2, RATE_MATRIX, DECAY
    )
    gains_new, gains_m, gains_v = adamw_update(
        gains, gain_total * factor, gain_mom1, gain_mom2, RATE_VECTOR, 0.0
    )
    return (
        loss_sum,
        count_all,
        grad_norm,
        master_new,
        master_new.astype(jnp.bfloat16),
        mom1_new,
        mom2_new,
        left_new,
        right_new,
        bleft_new,
        bright_new,
        table_new,
        table_new.astype(jnp.bfloat16),
        table_m,
        table_v,
        gains_new,
        gains_m,
        gains_v,
    )


def solution(mesh):
    placed = (
        P(("dp", "vocab"), None, None),
        P(("dp", "vocab"), None, None),
        P(("dp", "vocab"), None, None),
        P(("dp", "vocab"), None, None),
        P(("dp", "vocab"), None, None),
        P(("dp", "vocab"), None, None),
        P(("dp", "vocab"), None, None),
        P("vocab", None),
        P("vocab", None),
        P("vocab", None),
        P(),
        P(),
        P(),
        P(None, ("dp", "vocab"), None),
        P(None, ("dp", "vocab"), None),
        P(None, ("dp", "vocab")),
        P(None, ("dp", "vocab")),
        P(None, ("dp", "vocab"), None),
        P(None, ("dp", "vocab"), None),
        P(),
    )
    return jax.shard_map(
        per_device,
        mesh=mesh,
        in_specs=placed,
        out_specs=(
            P(),
            P(),
            P(),
            P(("dp", "vocab"), None, None),
            P(("dp", "vocab"), None, None),
            P(("dp", "vocab"), None, None),
            P(("dp", "vocab"), None, None),
            P(("dp", "vocab"), None, None),
            P(("dp", "vocab"), None, None),
            P(("dp", "vocab"), None, None),
            P(("dp", "vocab"), None, None),
            P("vocab", None),
            P("vocab", None),
            P("vocab", None),
            P("vocab", None),
            P(),
            P(),
            P(),
        ),
        check_vma=False,
    )
```

```python
import math

import jax
import jax.numpy as jnp
from jax import lax
from jax.experimental import pallas as pl
from jax.experimental.pallas import tpu as pltpu
from jax.sharding import PartitionSpec as P

D = 512
HEADS = 8
HEAD_DIM = 64
FF = 2048
ENC = 1
DEC = 2
MICRO = 2
LOSS_POS = 16
PB = 64
STEP = 10
MATS = 11
GAINS = 11


HIGH = lax.Precision.HIGH
NORM_EPS = 1e-06
CLIP_AT = 0.02
RATE_MATRIX = 0.1
RATE_VECTOR = 0.8
BETA_FIRST = 0.9
BETA_SECOND = 0.95
BETA_STAT = 0.95
ADAM_EPS = 1e-08
DECAY = 0.01


def rms_norm(stream, gain_row):
    return (
        stream * lax.rsqrt(jnp.mean(stream * stream, axis=-1, keepdims=True) + NORM_EPS) * gain_row
    )


def waves(length, columns):
    place_at = jnp.arange(length).astype(jnp.float32)[:, None]
    rate_at = jnp.exp(
        jnp.arange(columns // 2).astype(jnp.float32) * (-2.0 * math.log(10000.0) / columns)
    )
    angle = place_at * rate_at[None, :]
    return jnp.concatenate([jnp.sin(angle), jnp.cos(angle)], axis=1)


def linear(left_op, right_op):
    return jnp.dot(left_op, right_op, preferred_element_type=jnp.float32)


def linear_tr(left_op, right_op):
    return lax.dot_general(
        left_op, right_op, (((1,), (1,)), ((), ())), preferred_element_type=jnp.float32
    )


def outer_sum(left_op, right_op):
    return lax.dot_general(
        left_op, right_op, (((0,), (0,)), ((), ())), preferred_element_type=jnp.float32
    )


def split_heads(matrix):
    return matrix.reshape(matrix.shape[0], HEADS, HEAD_DIM)


NEVER=-1000000000.0
PAIR=2*HEAD_DIM
def kept_scores(query, keys, valid_len, causal, start_at):
    scores = lax.dot_general(query, keys, (((1,), (1,)), ((), ())), preferred_element_type=jnp.float32)
    key_at = lax.broadcasted_iota(jnp.int32, scores.shape if causal else (1, scores.shape[1]), 1)
    allowed = key_at < valid_len
    if causal:
        allowed = allowed & (key_at <= start_at + lax.broadcasted_iota(jnp.int32, scores.shape, 0))
    return jnp.where(allowed, scores, NEVER)

def head_masks(value):
    first = lax.broadcasted_iota(jnp.int32, value.shape, 1) < HEAD_DIM
    zero = jnp.zeros_like(value)
    return (jnp.where(first, value, zero), jnp.where(first, zero, value))

def attend_forward(query_in, query_at, keys_in, key_at, value_at, valid_len, causal):
    rows, keys = (query_in.shape[0] // MICRO, keys_in.shape[0] // MICRO)
    block = min(256, rows)
    steps = rows // block
    scale = HEAD_DIM ** (-0.5)

    def kernel(len_ref, query_ref, key_ref, value_ref, out_ref, stat_ref):
        start_at = pl.program_id(2) * block
        length = len_ref[pl.program_id(0)]
        queries = head_masks((query_ref[...].astype(jnp.float32) * scale).astype(jnp.bfloat16))
        values = head_masks(value_ref[...])
        total = jnp.zeros((block, PAIR), jnp.float32)
        stats = []
        for head in range(2):
            scores = kept_scores(queries[head], key_ref[...], length, causal, start_at)
            summit = jnp.max(scores, axis=1, keepdims=True)
            expo = jnp.exp(scores - summit)
            sums = jnp.sum(expo, axis=1, keepdims=True)
            probs = (expo * (1.0 / sums)).astype(jnp.bfloat16)
            total += jnp.dot(probs, values[head], preferred_element_type=jnp.float32)
            stats.append(summit + jnp.log(sums))
        out_ref[...] = total.astype(jnp.bfloat16)
        first = lax.broadcasted_iota(jnp.int32, (block, PAIR), 1) < HEAD_DIM
        stat_ref[...] = jnp.where(first, stats[0], stats[1])

    out_spec = pl.BlockSpec((block, PAIR), lambda seq, pair, step, lens: (seq * steps + step, pair))
    return pl.pallas_call(
        kernel,
        out_shape=(
            jax.ShapeDtypeStruct((MICRO * rows, D), jnp.bfloat16),
            jax.ShapeDtypeStruct((MICRO * rows, D), jnp.float32),
        ),
        grid_spec=pltpu.PrefetchScalarGridSpec(
            num_scalar_prefetch=1,
            grid=(MICRO, D // PAIR, steps),
            in_specs=[
                pl.BlockSpec((block, PAIR), lambda seq, pair, step, lens: (seq * steps + step, query_at + pair)),
                pl.BlockSpec((keys, PAIR), lambda seq, pair, step, lens: (seq, key_at + pair)),
                pl.BlockSpec((keys, PAIR), lambda seq, pair, step, lens: (seq, value_at + pair)),
            ],
            out_specs=(out_spec, out_spec),
        ),
        compiler_params=pltpu.CompilerParams(vmem_limit_bytes=40 * 2**20),
        cost_estimate=pl.CostEstimate(flops=4*MICRO*rows*keys*D, bytes_accessed=MICRO*(rows+keys)*D*8, transcendentals=MICRO*HEADS*rows*keys),
    )(valid_len, query_in, keys_in, keys_in)

def attend_backward(query_in, query_at, keys_in, key_at, value_at, valid_len, causal, stats, grad_out, first=0, seqs=MICRO, begun=()):
    rows, keys = (query_in.shape[0] // MICRO, keys_in.shape[0] // MICRO)
    block = min(512, rows)
    steps = rows // block
    scale = HEAD_DIM ** (-0.5)

    def kernel(len_ref, query_ref, key_ref, value_ref, stat_ref, up_ref, *refs):
        dq_ref, dk_ref, dv_ref, key_sum, value_sum = refs[len(begun) :]
        step = pl.program_id(2)
        start_at = step * block
        length = len_ref[first + pl.program_id(0)]
        queries = head_masks((query_ref[...].astype(jnp.float32) * scale).astype(jnp.bfloat16))
        upstream = head_masks(up_ref[...])
        keys_each = head_masks(key_ref[...])
        grad_query = jnp.zeros((block, PAIR), jnp.float32)
        grad_key = jnp.zeros((keys, PAIR), jnp.float32)
        grad_value = jnp.zeros((keys, PAIR), jnp.float32)
        over_rows = (((0,), (0,)), ((), ()))
        for head in range(2):
            scores = kept_scores(queries[head], key_ref[...], length, causal, start_at)
            probs = jnp.exp(scores - stat_ref[:, head * HEAD_DIM : head * HEAD_DIM + 1])
            grad_probs = lax.dot_general(upstream[head], value_ref[...], (((1,), (1,)), ((), ())), preferred_element_type=jnp.float32)
            inner = jnp.sum(probs * grad_probs, axis=1, keepdims=True)
            grad_scores = (probs * (grad_probs - inner)).astype(jnp.bfloat16)
            grad_query += jnp.dot(grad_scores, keys_each[head], preferred_element_type=jnp.float32)
            grad_key += lax.dot_general(grad_scores, queries[head], over_rows, preferred_element_type=jnp.float32)
            grad_value += lax.dot_general(probs.astype(jnp.bfloat16), upstream[head], over_rows, preferred_element_type=jnp.float32)
        dq_ref[...] = (grad_query * scale).astype(jnp.bfloat16)
        if steps == 1:
            dk_ref[...] = grad_key.astype(jnp.bfloat16)
            dv_ref[...] = grad_value.astype(jnp.bfloat16)
        else:
            @pl.when(step == 0)
            def _():
                key_sum[...] = grad_key
                value_sum[...] = grad_value

            @pl.when(step > 0)
            def _():
                key_sum[...] += grad_key
                value_sum[...] += grad_value

            @pl.when(step == steps - 1)
            def _():
                dk_ref[...] = key_sum[...].astype(jnp.bfloat16)
                dv_ref[...] = value_sum[...].astype(jnp.bfloat16)

    def row_spec(at, begin):
        return pl.BlockSpec(
            (block, PAIR),
            lambda seq, pair, step, lens: ((begin + seq) * steps + step, at + pair),
        )

    def key_spec(at, begin):
        return pl.BlockSpec((keys, PAIR), lambda seq, pair, step, lens: (begin + seq, at + pair))

    return pl.pallas_call(
        kernel,
        out_shape=(
            jax.ShapeDtypeStruct((MICRO * rows, D), jnp.bfloat16),
            jax.ShapeDtypeStruct((MICRO * keys, D), jnp.bfloat16),
            jax.ShapeDtypeStruct((MICRO * keys, D), jnp.bfloat16),
        ),
        grid_spec=pltpu.PrefetchScalarGridSpec(
            num_scalar_prefetch=1,
            grid=(seqs, D // PAIR, steps),
            in_specs=[
                row_spec(query_at, first),
                key_spec(key_at, first),
                key_spec(value_at, first),
                row_spec(0, first),
                row_spec(0, first),
            ]
            + [pl.BlockSpec(memory_space=pl.ANY)] * len(begun),
            out_specs=(row_spec(0, first), key_spec(0, first), key_spec(0, first)),
            scratch_shapes=[pltpu.VMEM((keys, PAIR), jnp.float32)] * 2,
        ),
        input_output_aliases={6 + item: item for item in range(len(begun))},
        compiler_params=pltpu.CompilerParams(vmem_limit_bytes=40 * 2**20),
        cost_estimate=pl.CostEstimate(flops=10*seqs*rows*keys*D, bytes_accessed=seqs*(rows+keys)*D*16, transcendentals=seqs*HEADS*rows*keys),
    )(valid_len, query_in, keys_in, keys_in, stats, grad_out, *begun)


def norm_backward(stream, gain_row, grad_normed):
    _, pull_back = jax.vjp(rms_norm, stream, gain_row)
    return pull_back(grad_normed)


def self_forward(stream, gain_row, weight, valid_len, causal):
    normed = rms_norm(stream, gain_row).astype(jnp.bfloat16)
    joint_qkv = linear(normed, weight[:, : 3 * D]).astype(jnp.bfloat16)
    pairs = D // PAIR
    mixed_out, stats_kept = attend_forward(
        joint_qkv, 0, joint_qkv, pairs, 2 * pairs, valid_len, causal
    )
    return (
        stream + linear(mixed_out, weight[:, 3 * D :]),
        (stream, normed, joint_qkv, mixed_out, stats_kept),
    )


def self_backward(grad_stream, kept_block, gain_row, weight, valid_len, causal, between=None):
    stream, normed, joint_qkv, mixed_out, stats_kept = kept_block
    grad_low = grad_stream.astype(jnp.bfloat16)
    grad_out_w = outer_sum(mixed_out, grad_low)
    grad_mixed = linear_tr(grad_low, weight[:, 3 * D :]).astype(jnp.bfloat16)
    pairs = D // PAIR
    stages = 1 if between is None else MICRO
    grads = ()
    for stage in range(stages):
        if stage > 0:
            grad_mixed = between(grad_mixed)
        grads = attend_backward(
            joint_qkv,
            0,
            joint_qkv,
            pairs,
            2 * pairs,
            valid_len,
            causal,
            stats_kept,
            grad_mixed,
            stage * MICRO // stages,
            MICRO // stages,
            tuple(grads),
        )
    grad_joint = jnp.concatenate(grads, 1)
    if between is not None:
        grad_joint = between(grad_joint)
    grad_x, grad_gain = norm_backward(stream, gain_row, linear_tr(grad_joint, weight[:, : 3 * D]))
    return (
        grad_stream + grad_x,
        grad_gain,
        jnp.concatenate([outer_sum(normed, grad_joint), grad_out_w], 1).astype(jnp.bfloat16),
    )


def cross_forward(stream, gain_row, weight, memory, valid_len):
    normed = rms_norm(stream, gain_row).astype(jnp.bfloat16)
    query_in = linear(normed, weight[:, :D]).astype(jnp.bfloat16)
    pair_kv = linear(memory, weight[:, D : 3 * D]).astype(jnp.bfloat16)
    mixed_out, stats_kept = attend_forward(
        query_in, 0, pair_kv, 0, D // PAIR, valid_len, False
    )
    return (
        stream + linear(mixed_out, weight[:, 3 * D :]),
        (stream, normed, query_in, pair_kv, mixed_out, stats_kept),
    )


def cross_backward(grad_stream, kept_block, gain_row, weight, memory, valid_len):
    stream, normed, query_in, pair_kv, mixed_out, stats_kept = kept_block
    grad_low = grad_stream.astype(jnp.bfloat16)
    grad_out_w = outer_sum(mixed_out, grad_low)
    grad_mixed = linear_tr(grad_low, weight[:, 3 * D :]).astype(jnp.bfloat16)
    grad_query, grad_k, grad_v = attend_backward(
        query_in, 0, pair_kv, 0, D // PAIR, valid_len, False, stats_kept, grad_mixed
    )
    grad_pair = jnp.concatenate([grad_k, grad_v], 1)
    grad_weight = jnp.concatenate(
        [outer_sum(normed, grad_query), outer_sum(memory, grad_pair), grad_out_w], 1
    ).astype(jnp.bfloat16)
    grad_x, grad_gain = norm_backward(stream, gain_row, linear_tr(grad_query, weight[:, :D]))
    return (
        grad_stream + grad_x,
        grad_gain,
        grad_weight,
        linear_tr(grad_pair, weight[:, D : 3 * D]),
    )


def gelu_tanh(hidden):
    return jax.nn.gelu(hidden, approximate=True)


def ffn_forward(stream, gain_row, w_in, w_out):
    normed = rms_norm(stream, gain_row).astype(jnp.bfloat16)
    hidden = linear(normed, w_in)
    active = gelu_tanh(hidden).astype(jnp.bfloat16)
    return (stream + linear_tr(active, w_out), (stream, normed, hidden, active))


def ffn_backward(grad_stream, kept_block, gain_row, w_in, w_out):
    stream, normed, hidden, active = kept_block
    grad_low = grad_stream.astype(jnp.bfloat16)
    grad_out_w = outer_sum(grad_low, active).astype(jnp.bfloat16)
    _, pull_back = jax.vjp(gelu_tanh, hidden)
    grad_hidden = pull_back(linear(grad_low, w_out))[0].astype(jnp.bfloat16)
    grad_x, grad_gain = norm_backward(stream, gain_row, linear_tr(grad_hidden, w_in))
    return (
        grad_stream + grad_x,
        grad_gain,
        outer_sum(normed, grad_hidden).astype(jnp.bfloat16),
        grad_out_w,
    )


def forward_all(
    weights,
    gain_set,
    source_rows,
    source_len,
    target_len,
    place_rows,
    lay_decoder,
):
    stream = source_rows
    enc_kept = []
    for layer_no in range(ENC):
        stream, kept_self = self_forward(
            stream, gain_set[2 * layer_no], weights[layer_no], source_len, False
        )
        stream, kept_ffn = ffn_forward(
            stream,
            gain_set[2 * layer_no + 1],
            weights[ENC + 2 * DEC + layer_no],
            weights[2 * ENC + 3 * DEC + layer_no],
        )
        enc_kept.append((kept_self, kept_ffn))
    memory, decoded = lay_decoder(rms_norm(stream, gain_set[2 * ENC]).astype(jnp.bfloat16))
    dec_kept, exit_in, exit_rows = ([], [], [])
    for layer_no in range(DEC):
        base_at = 2 * ENC + 1 + 3 * layer_no
        decoded, kept_self = self_forward(
            decoded, gain_set[base_at], weights[ENC + layer_no], target_len, True
        )
        decoded, kept_cross = cross_forward(
            decoded, gain_set[base_at + 1], weights[ENC + DEC + layer_no], memory, source_len
        )
        decoded, kept_ffn = ffn_forward(
            decoded,
            gain_set[base_at + 2],
            weights[2 * ENC + 2 * DEC + layer_no],
            weights[3 * ENC + 3 * DEC + layer_no],
        )
        dec_kept.append((kept_self, kept_cross, kept_ffn))
        picked_rows = decoded[place_rows]
        exit_in.append(picked_rows)
        exit_rows.append(
            rms_norm(picked_rows, gain_set[2 * ENC + 1 + 3 * DEC + layer_no]).astype(jnp.bfloat16)
        )
    kept = (source_len, target_len, place_rows, enc_kept, stream, memory, dec_kept, exit_in)
    return (kept, jnp.concatenate(exit_rows, 0))


def backward_all(
    weights, gain_set, kept, exit_grads, matrix_store, gain_store, before_last, between_last
):
    source_len, target_len, place_rows, enc_kept, stream, memory, dec_kept, exit_in = kept
    exit_each = jnp.split(exit_grads, DEC, axis=0)
    grad_decoded = jnp.zeros(dec_kept[0][0][0].shape, jnp.float32)
    grad_memory = jnp.zeros(memory.shape, jnp.float32)
    for layer_no in reversed(range(DEC)):
        base_at = 2 * ENC + 1 + 3 * layer_no
        exit_at = 2 * ENC + 1 + 3 * DEC + layer_no
        grad_rows, gain_store[exit_at] = norm_backward(
            exit_in[layer_no], gain_set[exit_at], exit_each[layer_no]
        )
        grad_decoded = grad_decoded.at[place_rows].add(grad_rows)
        kept_self, kept_cross, kept_ffn = dec_kept[layer_no]
        in_at, out_at = (2 * ENC + 2 * DEC + layer_no, 3 * ENC + 3 * DEC + layer_no)
        grad_decoded, gain_store[base_at + 2], matrix_store[in_at], matrix_store[out_at] = (
            ffn_backward(
                grad_decoded, kept_ffn, gain_set[base_at + 2], weights[in_at], weights[out_at]
            )
        )
        cross_at = ENC + DEC + layer_no
        grad_decoded, gain_store[base_at + 1], matrix_store[cross_at], grad_mem = cross_backward(
            grad_decoded, kept_cross, gain_set[base_at + 1], weights[cross_at], memory, source_len
        )
        grad_memory = grad_memory + grad_mem
        grad_decoded, gain_store[base_at], matrix_store[ENC + layer_no] = self_backward(
            grad_decoded, kept_self, gain_set[base_at], weights[ENC + layer_no], target_len, True
        )
    grad_stream, gain_store[2 * ENC] = norm_backward(stream, gain_set[2 * ENC], grad_memory)
    for layer_no in reversed(range(ENC)):
        kept_self, kept_ffn = enc_kept[layer_no]
        in_at, out_at = (ENC + 2 * DEC + layer_no, 2 * ENC + 3 * DEC + layer_no)
        grad_stream, gain_store[2 * layer_no + 1], matrix_store[in_at], matrix_store[out_at] = (
            ffn_backward(
                grad_stream, kept_ffn, gain_set[2 * layer_no + 1], weights[in_at], weights[out_at]
            )
        )
        if layer_no == 0:
            grad_stream = before_last(grad_stream)
        grad_stream, gain_store[2 * layer_no], matrix_store[layer_no] = self_backward(
            grad_stream,
            kept_self,
            gain_set[2 * layer_no],
            weights[layer_no],
            source_len,
            False,
            between_last if layer_no == 0 else None,
        )
    return (grad_stream, grad_decoded)


def fold_ranked(tiles, rank_of):
    count, half = (tiles.shape[0], PB // 2)

    def kernel(rank_ref, tile_ref, out_ref):
        def one_block(tile_no, carry):
            value = tile_ref[tile_no]
            folded = jnp.concatenate([value[:half], value[half:]], axis=1)
            out_ref[rank_ref[tile_no]] = folded.astype(jnp.bfloat16)
            return carry

        lax.fori_loop(0, count, one_block, 0)

    return pl.pallas_call(
        kernel,
        out_shape=jax.ShapeDtypeStruct((count, half, 2 * PB), jnp.bfloat16),
        grid_spec=pltpu.PrefetchScalarGridSpec(
            num_scalar_prefetch=1,
            grid=(1,),
            in_specs=[pl.BlockSpec(memory_space=pltpu.VMEM)],
            out_specs=pl.BlockSpec(memory_space=pltpu.VMEM),
        ),
        compiler_params=pltpu.CompilerParams(vmem_limit_bytes=40 * 2**20),
    )(rank_of, tiles)


def unfold_ranked(folded, rank_of):
    count, half = (folded.shape[0], PB // 2)

    def kernel(rank_ref, folded_ref, out_ref):
        def one_block(tile_no, carry):
            value = folded_ref[rank_ref[tile_no]]
            out_ref[tile_no, :half] = value[:, :PB]
            out_ref[tile_no, half:] = value[:, PB:]
            return carry

        lax.fori_loop(0, count, one_block, 0)

    return pl.pallas_call(
        kernel,
        out_shape=jax.ShapeDtypeStruct((count, PB, PB), jnp.float32),
        grid_spec=pltpu.PrefetchScalarGridSpec(
            num_scalar_prefetch=1,
            grid=(1,),
            in_specs=[pl.BlockSpec(memory_space=pltpu.VMEM)],
            out_specs=pl.BlockSpec(memory_space=pltpu.VMEM),
        ),
        compiler_params=pltpu.CompilerParams(vmem_limit_bytes=40 * 2**20),
    )(rank_of, folded)


def is_encoder(mat_no):
    return (
        mat_no < ENC
        or ENC + 2 * DEC <= mat_no < 2 * ENC + 2 * DEC
        or 2 * ENC + 3 * DEC <= mat_no < 3 * ENC + 3 * DEC
    )


def is_last(mat_no):
    return mat_no == 0


def rank_blocks(slot_list, devices, is_first):
    blocks_each = D // PB * (FF // PB)
    mats = slot_list // blocks_each
    early = jnp.zeros(mats.shape, jnp.bool_)
    for mat_no in range(MATS):
        if is_first(mat_no):
            early = early | (mats == mat_no)
    early = early.reshape(devices, -1).astype(jnp.int32)
    early_count = jnp.sum(early, axis=1)
    ahead = jnp.cumsum(early, axis=1) - early
    later = early_count[:, None] + jnp.arange(early.shape[1])[None, :] - ahead
    return (jnp.where(early == 1, ahead, later), early_count)


def room_for(per_device, chosen):
    share = sum(chosen(mat_no) for mat_no in range(MATS)) / MATS
    mean = per_device * share
    return min(per_device - 1, -(-int(mean + 4.2 * math.sqrt(mean * (1 - share))) // 4) * 4)


def by_block(slot_list, values):
    width, base = (64, 128)
    height = -(-slot_list.shape[0] // width)
    rows = (slot_list[:, None] // width == jnp.arange(height)[None, :]).astype(jnp.bfloat16)
    lanes = (slot_list[:, None] % width == jnp.arange(width)[None, :]).astype(jnp.bfloat16)
    found = []
    for value in values:
        high, low = (
            outer_sum(rows * (part.astype(jnp.bfloat16))[:, None], lanes)
            for part in (value // base, value % base)
        )
        found.append((high * base + low).astype(jnp.int32).reshape(-1)[: slot_list.shape[0]])
    return found


def lay_matrices(buffers, place_of, mats):
    half = PB // 2
    row_blocks, pairs = (D // PB, FF // (2 * PB))
    sizes = [buffer.shape[0] for buffer in buffers]
    starts = [sum(sizes[:item]) for item in range(len(sizes))]
    count = len(mats)

    def kernel(place_ref, *refs):
        sources, outs = (refs[: len(sizes)], refs[len(sizes) : len(sizes) + count])
        folded_ref, made, arrived, left = refs[len(sizes) + count :]
        left_half = lax.broadcasted_iota(jnp.int32, (half, 2 * PB), 1) < PB
        fetches = [
            pltpu.make_async_copy(
                source, folded_ref.at[pl.ds(start, size)], arrived.at[item]
            )
            for item, (source, start, size) in enumerate(zip(sources, starts, sizes))
        ]
        for fetch in fetches:
            fetch.start()
        for fetch in fetches:
            fetch.wait()

        def send(item):
            return pltpu.make_async_copy(made.at[item % 2], outs[item], left.at[item % 2])

        for item, mat_no in enumerate(mats):
            if item >= 2:
                send(item - 2).wait()

            def one_row(row_no, carry, item=item, mat_no=mat_no):
                first = (mat_no * row_blocks + row_no) * 2 * pairs
                row_at = pl.multiple_of(row_no * PB, PB)
                for pair_no in range(pairs):
                    even = folded_ref[place_ref[first + 2 * pair_no]].astype(jnp.float32)
                    odd = folded_ref[place_ref[first + 2 * pair_no + 1]].astype(jnp.float32)
                    columns = slice(2 * PB * pair_no, 2 * PB * (pair_no + 1))
                    upper = jnp.where(left_half, even, pltpu.roll(odd, PB, 1))
                    lower = jnp.where(left_half, pltpu.roll(even, PB, 1), odd)
                    made[item % 2, pl.ds(row_at, half), columns] = upper.astype(jnp.bfloat16)
                    made[item % 2, pl.ds(row_at + half, half), columns] = lower.astype(jnp.bfloat16)
                return carry

            lax.fori_loop(0, row_blocks, one_row, 0)
            send(item).start()
        for item in range(max(count - 2, 0), count):
            send(item).wait()

    return pl.pallas_call(
        kernel,
        out_shape=[jax.ShapeDtypeStruct((D, FF), jnp.bfloat16)] * count,
        grid_spec=pltpu.PrefetchScalarGridSpec(
            num_scalar_prefetch=1,
            grid=(1,),
            in_specs=[pl.BlockSpec(memory_space=pl.ANY)] * len(sizes),
            out_specs=[pl.BlockSpec(memory_space=pl.ANY)] * count,
            scratch_shapes=[
                pltpu.VMEM((sum(sizes), half, 2 * PB), jnp.bfloat16),
                pltpu.VMEM((2, D, FF), jnp.bfloat16),
                pltpu.SemaphoreType.DMA((len(sizes),)),
                pltpu.SemaphoreType.DMA((2,)),
            ],
        ),
        compiler_params=pltpu.CompilerParams(vmem_limit_bytes=40 * 2**20),
    )(place_of, *buffers)


def fold_gradients(matrices, mats, place_of, sizes, begun=None):
    half = PB // 2
    row_blocks, pairs = (D // PB, FF // (2 * PB))
    count = len(mats)
    whole = sum(sizes)
    given = 0 if begun is None else 1
    skipped = 0 if begun is None else whole - begun.shape[0]
    kept = whole - skipped

    def kernel(place_ref, *refs):
        sources, old = (refs[:count], refs[count : count + given])
        outs = refs[count + given : -5]
        folded_ref, held, arrived, left, old_sem = refs[-5:]
        left_half = lax.broadcasted_iota(jnp.int32, (half, 2 * PB), 1) < PB

        def fetch(item):
            return pltpu.make_async_copy(sources[item], held.at[item % 2], arrived.at[item % 2])

        fetch(0).start()
        if given:
            before = pltpu.make_async_copy(
                old[0], folded_ref.at[pl.ds(0, kept)], old_sem.at[0]
            )
            before.start()
            before.wait()
        for item, mat_no in enumerate(mats):
            if item + 1 < count:
                fetch(item + 1).start()
            fetch(item).wait()

            def place(block, carry=None):
                spot = place_ref[block] - skipped
                return jnp.where(spot < 0, kept, spot) if given else spot

            def one_row(row_no, carry, item=item, mat_no=mat_no):
                first = (mat_no * row_blocks + row_no) * 2 * pairs
                row_at = pl.multiple_of(row_no * PB, PB)
                for pair_no in range(pairs):
                    columns = slice(2 * PB * pair_no, 2 * PB * (pair_no + 1))
                    upper = held[item % 2, pl.ds(row_at, half), columns].astype(jnp.float32)
                    lower = held[item % 2, pl.ds(row_at + half, half), columns].astype(jnp.float32)
                    even = jnp.where(left_half, upper, pltpu.roll(lower, PB, 1))
                    odd = jnp.where(left_half, pltpu.roll(upper, PB, 1), lower)
                    folded_ref[place(first + 2 * pair_no)] = even.astype(jnp.bfloat16)
                    folded_ref[place(first + 2 * pair_no + 1)] = odd.astype(jnp.bfloat16)
                return carry

            lax.fori_loop(0, row_blocks, one_row, 0)
        begin = 0
        sends = []
        for item, out in enumerate(outs):
            size = out.shape[0]
            sends.append(
                pltpu.make_async_copy(folded_ref.at[pl.ds(begin, size)], out, left.at[item])
            )
            begin += size
        for send in sends:
            send.start()
        for send in sends:
            send.wait()

    shapes = [kept] if given else list(sizes)
    return pl.pallas_call(
        kernel,
        out_shape=[jax.ShapeDtypeStruct((size, half, 2 * PB), jnp.bfloat16) for size in shapes],
        grid_spec=pltpu.PrefetchScalarGridSpec(
            num_scalar_prefetch=1,
            grid=(1,),
            in_specs=[pl.BlockSpec(memory_space=pl.ANY)] * (count + given),
            out_specs=[pl.BlockSpec(memory_space=pl.ANY)] * len(shapes),
            scratch_shapes=[
                pltpu.VMEM((kept + given, half, 2 * PB), jnp.bfloat16),
                pltpu.VMEM((2, D, FF), jnp.bfloat16),
                pltpu.SemaphoreType.DMA((2,)),
                pltpu.SemaphoreType.DMA((2,)),
                pltpu.SemaphoreType.DMA((1,)),
            ],
        ),
        compiler_params=pltpu.CompilerParams(vmem_limit_bytes=40 * 2**20),
    )(place_of, *[matrices[mat_no] for mat_no in mats], *([begun] if given else []))


def exchange_plan(dp_size, along, per_device):
    low, high = (along.bit_length() - 1, dp_size.bit_length() - 1)
    base = [low + bit for bit in range(high)] + list(range(1, low))
    third = per_device // 3
    sizes = [per_device - 2 * third, third, third]
    return [(size, base[turn:] + base[:turn]) for turn, size in enumerate(sizes)]


def places_for(ranks, plan, devices):
    per_device = sum(size for size, _ in plan)
    owner = jnp.arange(devices)[:, None]
    place = jnp.zeros_like(ranks)
    begin = 0
    for size, order in plan:
        spot = jnp.zeros_like(owner)
        for bit in order:
            spot = spot * 2 + owner // 2**bit % 2
        here = begin * (devices // 2) + spot * size + ranks - begin
        place = jnp.where((ranks >= begin) & (ranks < begin + size), here, place)
        begin += size
    return place + owner % 2 * (devices // 2 * per_device)


def halve(value, bit, devices):
    me = lax.axis_index("dp") * lax.axis_size("vocab") + lax.axis_index("vocab")

    mine = me // 2**bit % 2
    value = value.reshape(2, value.shape[0] // 2, *value.shape[1:])
    sent = lax.dynamic_index_in_dim(value, 1 - mine, 0, keepdims=False)
    kept = lax.dynamic_index_in_dim(value, mine, 0, keepdims=False)
    pairs = [(index, index ^ 2**bit) for index in range(devices)]
    arrived = lax.ppermute(sent, ("dp", "vocab"), pairs)
    return kept.astype(jnp.float32) + arrived.astype(jnp.float32)


def first_exchange(folded, devices):
    return halve(folded, 0, devices).astype(jnp.bfloat16)


def split_parts(total, plan, devices):
    parts, begin = ([], 0)
    for size, _ in plan:
        count = size * (devices // 2)
        parts.append(total[begin : begin + count])
        begin += count
    return parts


def one_exchange(parts, plan, round_no, devices):
    return [
        halve(part.astype(jnp.bfloat16), order[round_no], devices)
        for part, (_, order) in zip(parts, plan)
    ]


def other_exchanges(parts, plan, devices, done=0):
    for round_no in range(done, len(plan[0][1])):
        parts = one_exchange(parts, plan, round_no, devices)
    return jnp.concatenate(parts, 0)


def take_rows(source, index_at, kind):
    count, width, block = (index_at.shape[0], source.shape[1], 128)
    whole = -(-count // block) * block
    index_at = jnp.pad(index_at, (0, whole - count))

    def kernel(index_ref, source_ref, out_ref, held_ref):
        first = pl.program_id(0) * block

        def copy_eight(group, carry):
            base = pl.multiple_of(group * 8, 8)
            for row_no in range(8):
                held_ref[pl.ds(base + row_no, 1), :] = source_ref[
                    pl.ds(index_ref[first + base + row_no], 1), :
                ]
            return carry

        lax.fori_loop(0, block // 8, copy_eight, 0)
        out_ref[...] = held_ref[...].astype(kind)

    taken = pl.pallas_call(
        kernel,
        out_shape=jax.ShapeDtypeStruct((whole, width), kind),
        grid_spec=pltpu.PrefetchScalarGridSpec(
            num_scalar_prefetch=1,
            grid=(whole // block,),
            in_specs=[pl.BlockSpec(memory_space=pltpu.VMEM)],
            out_specs=pl.BlockSpec((block, width), lambda step, index: (step, 0)),
            scratch_shapes=[pltpu.VMEM((block, width), jnp.float32)],
        ),
        compiler_params=pltpu.CompilerParams(vmem_limit_bytes=40 * 2**20),
    )(index_at, source)
    return taken[:count]


def add_rows(rows, index_at, total):
    count, width, block = (rows.shape[0], rows.shape[1], 512)
    whole = -(-count // block) * block
    index_at = jnp.pad(index_at, (0, whole - count), constant_values=-1)[None, :]
    rows = jnp.pad(rows, ((0, whole - count), (0, 0)))
    height = total.shape[0]

    def kernel(index_ref, rows_ref, total_ref, out_ref):
        @pl.when(pl.program_id(0) == 0)
        def _():
            out_ref[...] = total_ref[...]

        hits = lax.broadcasted_iota(jnp.int32, (height, block), 0) == index_ref[...]
        out_ref[...] += jnp.dot(
            hits.astype(jnp.float32).astype(jnp.bfloat16),
            rows_ref[...],
            preferred_element_type=jnp.float32,
        )

    return pl.pallas_call(
        kernel,
        out_shape=jax.ShapeDtypeStruct(total.shape, jnp.float32),
        grid=(whole // block,),
        in_specs=[
            pl.BlockSpec((1, block), lambda step: (0, step)),
            pl.BlockSpec((block, width), lambda step: (step, 0)),
            pl.BlockSpec((height, width), lambda step: (0, 0)),
        ],
        out_specs=pl.BlockSpec((height, width), lambda step: (0, 0)),
        compiler_params=pltpu.CompilerParams(vmem_limit_bytes=40 * 2**20),
    )(index_at, rows, total)


def spread(value, axes, peers):
    return lax.all_to_all(
        jnp.broadcast_to(value[None], (peers, *value.shape)), axes, 0, 0, tiled=True
    )


def count_before(mask):
    size, width = (mask.shape[-1], 128)
    parts = mask.reshape(*mask.shape[:-1], size // width, width).astype(jnp.bfloat16)
    earlier = (jnp.arange(width)[:, None] < jnp.arange(width)[None, :]).astype(jnp.bfloat16)
    inside = jnp.einsum("...pw,wk->...pk", parts, earlier, preferred_element_type=jnp.float32)
    totals = jnp.sum(parts.astype(jnp.float32), axis=-1)
    ahead = jnp.cumsum(totals, axis=-1) - totals
    return (inside + ahead[..., None]).reshape(mask.shape).astype(jnp.int32)


def room(count, peers):
    mean = count / peers
    return min(count, -(-int(mean + 5.0 * math.sqrt(mean)) // 16) * 16)


def listed(mask, rank, values, size):
    width, base = (16, 128)
    rows = mask[..., None] & (rank[..., None] // width == jnp.arange(size // width))
    lanes = (rank[..., None] % width == jnp.arange(width)).astype(jnp.bfloat16)
    values = values + 1
    high, low = (
        jnp.einsum(
            "...th,...tl->...hl",
            jnp.where(rows, part[..., None].astype(jnp.bfloat16), 0),
            lanes,
            preferred_element_type=jnp.float32,
        )
        for part in (values // base, values % base)
    )
    return (high * base + low).astype(jnp.int32).reshape(*mask.shape[:-1], size) - 1


def rounds_needed(owner_all, peers, size):
    held = jnp.sum((owner_all[:, None, :] == jnp.arange(peers)[:, None]).astype(jnp.int32), axis=2)
    return (jnp.max(held) + size - 1) // size


def fetch_plan(table_part, tokens_all, peers_here, peer_me):
    peers, rows_each = (peers_here.shape[0], table_part.shape[0])
    count = tokens_all.shape[1]
    size = room(count, peers)
    asked = peers_here // rows_each == peer_me
    asked_rank = count_before(asked)
    own_tokens = lax.dynamic_index_in_dim(peers_here, peer_me, 0, keepdims=False)
    own_owner = own_tokens // rows_each
    own_mask = own_owner[None, :] == jnp.arange(peers)[:, None]
    own_rank = jnp.sum(jnp.where(own_mask, count_before(own_mask), 0), axis=0)

    def to_send(round_no):
        wanted = listed(
            asked, asked_rank - round_no * size, peers_here % rows_each, size
        )
        return take_rows(table_part, jnp.maximum(wanted.reshape(-1), 0), jnp.bfloat16)

    def found_in(arrived, round_no):
        rank_now = own_rank - round_no * size
        now = (rank_now >= 0) & (rank_now < size)
        found = take_rows(
            arrived.astype(jnp.float32), jnp.where(now, own_owner * size + rank_now, 0), jnp.float32
        )
        return (now, found)

    def again(round_no, rows):
        now, found = found_in(swap_rows(to_send(round_no)), round_no)
        return jnp.where(now[:, None], found, rows)

    rounds = rounds_needed(tokens_all // rows_each, peers, size)

    def finish(arrived):
        return lax.fori_loop(1, rounds, again, found_in(arrived, 0)[1])

    return (to_send(0), finish)


def swap_rows(rows):
    return lax.all_to_all(rows, "vocab", 0, 0, tiled=True)


def return_plan(tokens_all, rows_each, dp_size):
    peers, count = tokens_all.shape
    along = peers // dp_size
    quarter = rows_each // dp_size
    me = lax.axis_index("dp") * along + lax.axis_index("vocab")
    size = room(count, peers)
    owner_all = (tokens_all % rows_each) // quarter * along + tokens_all // rows_each
    arriving = owner_all == me
    arriving_rank = count_before(arriving)
    own_owner = lax.dynamic_index_in_dim(owner_all, me, 0, keepdims=False)
    leaving = own_owner[None, :] == jnp.arange(peers)[:, None]
    leaving_rank = count_before(leaving)
    place = jnp.broadcast_to(jnp.arange(count)[None, :], leaving.shape)

    def lists(round_no):
        return (
            jnp.maximum(
                listed(leaving, leaving_rank - round_no * size, place, size).reshape(-1), 0
            ),
            listed(
                arriving, arriving_rank - round_no * size, tokens_all % quarter, size
            ).reshape(-1),
        )

    return (lists, rounds_needed(owner_all, peers, size))


def return_rows(grad_rows, lists, first_lists, rounds, total, ready, landed):
    def swap_all(rows):
        return lax.all_to_all(rows, ("dp", "vocab"), 0, 0, tiled=True)

    def again(round_no, so_far):
        chosen, where = lists(round_no)
        return add_rows(swap_all(take_rows(grad_rows, chosen, jnp.bfloat16)), where, so_far)

    arrived = landed(swap_all(ready(take_rows(grad_rows, first_lists[0], jnp.bfloat16))))
    return lax.fori_loop(1, rounds, again, add_rows(arrived, first_lists[1], total))


def turn_in(left_basis, tiles, right_basis):
    half = jnp.einsum("tki,tkl->til", left_basis, tiles, precision=HIGH)
    return jnp.einsum("til,tlj->tij", half, right_basis, precision=HIGH)


def turn_out(left_basis, tiles, right_basis):
    half = jnp.einsum("tik,tkl->til", left_basis, tiles, precision=HIGH)
    return jnp.einsum("til,tjl->tij", half, right_basis, precision=HIGH)


def orthonormal(columns):
    lanes, group = (128, 4)

    def kernel(in_ref, out_ref):
        out_ref[...] = in_ref[...]

        def four_columns(group_at, carry):
            first = group_at * group
            pivots = []
            for item in range(group):
                pivot = out_ref[first + item]
                for before in pivots:
                    pivot = pivot - jnp.sum(before * pivot, axis=0, keepdims=True) * before
                pivot = pivot / jnp.sqrt(jnp.sum(pivot * pivot, axis=0, keepdims=True))
                out_ref[first + item] = pivot
                pivots.append(pivot)

            def one_group(group_no, inner):
                held = [out_ref[group_no * group + item] for item in range(group)]
                for item in range(group):
                    value = held[item]
                    shares = [
                        jnp.sum(pivot * value, axis=0, keepdims=True) for pivot in pivots
                    ]
                    for pivot, share in zip(pivots, shares):
                        value = value - share * pivot
                    held[item] = value
                for item in range(group):
                    out_ref[group_no * group + item] = held[item]
                return inner

            return lax.fori_loop(group_at + 1, PB // group, one_group, carry)

        lax.fori_loop(0, PB // group, four_columns, 0)

    spec = pl.BlockSpec((PB, PB, lanes), lambda step: (0, 0, step))
    return pl.pallas_call(
        kernel,
        out_shape=jax.ShapeDtypeStruct(columns.shape, jnp.float32),
        grid=(columns.shape[2] // lanes,),
        in_specs=[spec],
        out_specs=spec,
        compiler_params=pltpu.CompilerParams(vmem_limit_bytes=40 * 2**20),
    )(columns)


def as_columns(left, right):
    both = jnp.transpose(jnp.concatenate([left, right], 0), (2, 1, 0))
    return jnp.pad(both, ((0, 0), (0, 0), (0, -both.shape[2] % 128)))


def renew_bases(columns, count):
    renewed = jnp.transpose(orthonormal(columns)[:, :, : 2 * count], (2, 1, 0))
    return (renewed[:count], renewed[count:])


def turned_by(stat, basis):
    return jnp.einsum("tij,tjk->tik", stat, basis, precision=HIGH)


def soap_update(
    master,
    grad_tiles,
    grad_turned,
    left_outer,
    right_outer,
    columns_before,
    columns_change,
    first_mom,
    first_turned,
    second_mom,
    left_stat,
    right_stat,
    left_basis,
    right_basis,
    factor,
):
    first_new = BETA_FIRST * first_mom + (1 - BETA_FIRST) * (factor * grad_tiles)
    grad_turned = factor * grad_turned
    first_turned = BETA_FIRST * first_turned + (1 - BETA_FIRST) * grad_turned
    second_new = BETA_SECOND * second_mom + (1 - BETA_SECOND) * grad_turned * grad_turned
    direction = (
        first_turned
        / (1 - BETA_FIRST**STEP)
        / (jnp.sqrt(second_new / (1 - BETA_SECOND**STEP)) + ADAM_EPS)
    )
    master_new = master - RATE_MATRIX * (
        turn_out(left_basis, direction, right_basis) + DECAY * master
    )
    left_new = BETA_STAT * left_stat + (1 - BETA_STAT) * (factor * (factor * left_outer))
    right_new = BETA_STAT * right_stat + (1 - BETA_STAT) * (factor * (factor * right_outer))
    return (
        master_new,
        first_new,
        second_new,
        left_new,
        right_new,
        *renew_bases(
            BETA_STAT * columns_before + (1 - BETA_STAT) * (factor * (factor * columns_change)),
            master.shape[0],
        ),
    )


def adamw_update(master, grad_now, first_mom, second_mom, rate, decay_by):
    first_new = BETA_FIRST * first_mom + (1 - BETA_FIRST) * grad_now
    second_new = BETA_SECOND * second_mom + (1 - BETA_SECOND) * grad_now * grad_now
    direction = (
        first_new
        / (1 - BETA_FIRST**STEP)
        / (jnp.sqrt(second_new / (1 - BETA_SECOND**STEP)) + ADAM_EPS)
    )
    return (master - rate * (direction + decay_by * master), first_new, second_new)


def per_device(
    master_tiles,
    mom1_tiles,
    mom2_tiles,
    stat_left,
    stat_right,
    basis_left,
    basis_right,
    table_master,
    table_mom1,
    table_mom2,
    gains,
    gain_mom1,
    gain_mom2,
    source_ids,
    target_ids,
    source_len,
    target_len,
    loss_place,
    exit_layer,
    slot_list,
):
    dp_size, along = (lax.axis_size("dp"), lax.axis_size("vocab"))
    dp_me, peer_me = (lax.axis_index("dp"), lax.axis_index("vocab"))
    devices = dp_size * along
    rows_each = table_master.shape[0]
    quarter = rows_each // dp_size
    source_len, target_len = (source_len[:, 0], target_len[:, 0])

    shifted = jnp.pad(target_ids[:, 0, :-1], ((0, 0), (1, 0)))
    tokens = jnp.concatenate([source_ids.reshape(-1), shifted.reshape(-1)])
    places = loss_place[:, 0]
    counted = places < target_len[:, None]
    reach = [
        jnp.sum((counted & (exit_layer[:, 0] >= layer_no)).astype(jnp.int32))
        for layer_no in range(DEC)
    ]
    labels = jnp.take_along_axis(target_ids[:, 0], places, axis=1).reshape(-1)
    row_count = MICRO * LOSS_POS
    own_facts = jnp.concatenate(
        [tokens, labels, counted.reshape(-1).astype(jnp.int32), jnp.stack(reach)]
    )
    fact_count = own_facts.shape[0]
    own_facts = jnp.pad(own_facts, (0, -fact_count % 128))
    facts = spread(own_facts, ("dp", "vocab"), devices)
    slots_later, facts, mom1_later, left_later, right_later = lax.optimization_barrier(
        (slot_list, facts, mom1_tiles, basis_left, basis_right)
    )
    tokens_all = facts[:, : tokens.shape[0]]
    after = facts[:, tokens.shape[0] :]
    labels_all = after[:, :row_count]
    counted_all = after[:, row_count : 2 * row_count].astype(jnp.float32)
    reach_all = jnp.sum(after[:, 2 * row_count : 2 * row_count + DEC].astype(jnp.float32), axis=0)
    count_all = jnp.sum(counted_all)
    fraction = reach_all / jnp.sum(reach_all)

    per_device = master_tiles.shape[0]
    me = dp_me * along + peer_me
    ranks, early_count = rank_blocks(slot_list, devices, is_encoder)
    first_size = room_for(per_device, is_encoder)
    second_size = per_device - first_size
    place_at = jnp.where(
        ranks < first_size,
        jnp.arange(devices)[:, None] * first_size + ranks,
        devices * first_size
        + jnp.arange(devices)[:, None] * second_size
        + ranks
        - first_size,
    )
    late_size = room_for(per_device, is_last)
    soon_size = per_device - late_size
    back_ranks, soon_count = rank_blocks(slots_later, devices, lambda mat_no: not is_last(mat_no))
    soon_plan = exchange_plan(dp_size, along, soon_size)
    late_plan = exchange_plan(dp_size, along, late_size)
    back_at = jnp.where(
        back_ranks < soon_size,
        places_for(back_ranks, soon_plan, devices),
        devices * soon_size + places_for(back_ranks - soon_size, late_plan, devices),
    )
    place_of, back_of = by_block(slots_later, [place_at.reshape(-1), back_at.reshape(-1)])
    own_folded = fold_ranked(
        master_tiles, lax.dynamic_index_in_dim(ranks, me, 0, keepdims=False)
    )
    src_count, tgt_count = (source_ids.shape[2], target_ids.shape[2])

    def planned(first, length):
        ids_all = tokens_all[:, first : first + MICRO * length]
        peers_here = lax.dynamic_slice_in_dim(ids_all, dp_me * along, along, 0)
        return fetch_plan(table_master, ids_all, peers_here, peer_me)

    source_sent, source_finish = planned(0, src_count)
    target_sent, target_finish = planned(MICRO * src_count, tgt_count)
    first_tiles = lax.all_gather(own_folded[:first_size], ("dp", "vocab"), axis=0, tiled=True)
    lists, rounds = return_plan(tokens_all, rows_each, dp_size)
    (
        own_second,
        first_tiles,
        source_arrived,
        first_lists,
        first_turned,
        target_sent,
        place_of,
        wave_set,
    ) = lax.optimization_barrier(
        (
            own_folded[first_size:],
            first_tiles,
            swap_rows(source_sent),
            lists(0),
            turn_in(left_later, mom1_later, right_later),
            target_sent,
            place_of,
            waves(src_count, D),
        )
    )
    second_tiles = lax.all_gather(own_second, ("dp", "vocab"), axis=0, tiled=True)
    encoder_mats = [mat_no for mat_no in range(MATS) if is_encoder(mat_no)]
    decoder_mats = [mat_no for mat_no in range(MATS) if not is_encoder(mat_no)]

    def lay_with_all():
        others = lax.all_gather(own_second, ("dp", "vocab"), axis=0, tiled=True)
        return lay_matrices([first_tiles, others], place_of, encoder_mats)

    def lay_with_first():
        return lay_matrices([first_tiles], place_of, encoder_mats)

    encoder_set = lax.cond(
        jnp.max(early_count) > first_size, lay_with_all, lay_with_first
    )
    weights = [None] * MATS
    for mat_no, matrix in zip(encoder_mats, encoder_set):
        weights[mat_no] = matrix

    def lay_decoder(memory):
        held, tiles, arrived = lax.optimization_barrier((memory, second_tiles, target_arrived))
        decoder_set = lay_matrices([first_tiles, tiles], place_of, decoder_mats)
        for mat_no, matrix in zip(decoder_mats, decoder_set):
            weights[mat_no] = matrix
        return (held, with_waves(target_finish(arrived), tgt_count))

    def with_waves(rows, length):
        return rows * math.sqrt(D) + jnp.tile(wave_set[:length], (MICRO, 1))

    source_rows = with_waves(source_finish(source_arrived), src_count)
    source_rows, target_sent = lax.optimization_barrier((source_rows, target_sent))
    target_arrived = swap_rows(target_sent)

    place_rows = (places + jnp.arange(MICRO)[:, None] * tgt_count).reshape(-1)
    kept, exit_rows = forward_all(
        weights,
        gains,
        source_rows,
        source_len,
        target_len,
        place_rows,
        lay_decoder,
    )

    table_low_part = table_master.astype(jnp.bfloat16)
    exit_count = DEC * row_count
    exit_all = lax.all_gather(exit_rows, ("dp", "vocab"), axis=0, tiled=True)
    exit_here = spread(exit_rows, "vocab", along).reshape(-1, D)
    label_rows = jnp.tile(labels_all, (1, DEC)).reshape(-1)
    weight_rows = (
        jnp.repeat(fraction, row_count)[None, :] * jnp.tile(counted_all, (1, DEC))
    ).reshape(-1)
    group_rows = along * exit_count
    group_at = dp_me * group_rows
    label_here = lax.dynamic_slice_in_dim(label_rows, group_at, group_rows, 0)
    weight_here = lax.dynamic_slice_in_dim(weight_rows, group_at, group_rows, 0)
    logits = linear_tr(exit_here, table_low_part)
    hit_here = label_here[:, None] - peer_me * rows_each == jnp.arange(rows_each)[None, :]
    summit = jnp.max(logits, axis=1)
    spread_part = jnp.sum(jnp.exp(logits - summit[:, None]), axis=1)
    picked_part = jnp.sum(jnp.where(hit_here, logits, 0.0), axis=1)
    stats = spread(
        jnp.stack([summit, spread_part, picked_part]), ("dp", "vocab"), devices
    ).reshape(dp_size, along, 3, group_rows)
    summit_all = jnp.max(stats[:, :, 0], axis=1)
    total_all = jnp.sum(stats[:, :, 1] * jnp.exp(stats[:, :, 0] - summit_all[:, None]), axis=1)
    spread_all = summit_all + jnp.log(total_all)
    picked_all = jnp.sum(stats[:, :, 2], axis=1)
    loss_sum = jnp.sum(weight_rows * (spread_all - picked_all).reshape(-1))
    spread_here = lax.dynamic_index_in_dim(spread_all, dp_me, 0, keepdims=False)

    def logit_grads(logit_set, spread, weight_set, hits):
        return (
            (weight_set / count_all)[:, None]
            * (jnp.exp(logit_set - spread[:, None]) - hits.astype(jnp.float32))
        ).astype(jnp.bfloat16)

    grads_here = logit_grads(logits, spread_here, weight_here, hit_here)
    grad_parts = linear(grads_here, table_low_part).astype(jnp.bfloat16)
    grad_parts = lax.all_to_all(grad_parts, "vocab", 0, 0, tiled=True)
    exit_grads = jnp.sum(
        grad_parts.reshape(along, exit_count, D).astype(jnp.float32), axis=0
    )

    matrix_store = [None] * MATS
    gain_store = [None] * GAINS
    first_row = peer_me * rows_each + dp_me * quarter
    table_quarter = lax.dynamic_slice_in_dim(table_low_part, dp_me * quarter, quarter, 0)
    hit_quarter = label_rows[:, None] - first_row == jnp.arange(quarter)[None, :]
    grads_quarter = logit_grads(
        linear_tr(exit_all, table_quarter), spread_all.reshape(-1), weight_rows, hit_quarter
    )
    grad_quarter = outer_sum(grads_quarter, exit_all)
    soon_mats = [mat_no for mat_no in range(MATS) if not is_last(mat_no)]
    late_mats = [mat_no for mat_no in range(MATS) if is_last(mat_no)]
    both = [devices * soon_size, devices * late_size]
    held = {}

    def before_last(grad_stream):
        blocks, held["begun"] = fold_gradients(matrix_store, soon_mats, back_of, both)
        grad_stream, blocks, held["quarter"] = lax.optimization_barrier(
            (grad_stream, blocks, grad_quarter)
        )
        held["total"] = first_exchange(blocks, devices)
        return grad_stream

    def between_last(value):
        if "parts" not in held:
            value, total = lax.optimization_barrier((value, held["total"]))
            held["parts"], held["done"] = (split_parts(total, soon_plan, devices), 0)
        elif held["done"] < len(soon_plan[0][1]):
            parts = one_exchange(held["parts"], soon_plan, held["done"], devices)
            value, held["parts"] = lax.optimization_barrier((value, parts))
            held["done"] += 1
        return value

    grad_source, grad_target = backward_all(
        weights,
        gains,
        kept,
        exit_grads,
        matrix_store,
        gain_store,
        before_last,
        between_last,
    )

    grad_source = between_last(grad_source)
    grad_rows = jnp.concatenate([grad_source, grad_target], 0) * math.sqrt(D)
    grad_rows = between_last(grad_rows)
    [late_blocks] = fold_gradients(matrix_store, late_mats, back_of, both, held["begun"])
    late_parts = split_parts(first_exchange(late_blocks, devices), late_plan, devices)
    late_parts = one_exchange(late_parts, late_plan, 0, devices)

    late_sum = other_exchanges(late_parts, late_plan, devices, 1)

    def exchange_again():
        blocks, _ = fold_gradients(matrix_store, list(range(MATS)), back_of, both)
        parts = split_parts(first_exchange(blocks, devices), soon_plan, devices)
        return other_exchanges(parts, soon_plan, devices)

    share = -(-GAINS * D // (devices * 128)) * 128
    gain_flat = jnp.stack(gain_store).reshape(-1)
    gain_flat = jnp.pad(gain_flat, (0, devices * share - GAINS * D)).reshape(devices, share)

    def ready(rows):
        sums = other_exchanges(held["parts"], soon_plan, devices, held["done"])
        rows, sums, late = lax.optimization_barrier((rows, sums, late_sum))
        sums = lax.cond(jnp.min(soon_count) < soon_size, exchange_again, lambda: sums)
        owned_grad = unfold_ranked(
            jnp.concatenate([sums, late], 0),
            lax.dynamic_index_in_dim(back_ranks, me, 0, keepdims=False),
        )
        left_outer = jnp.einsum("tik,tjk->tij", owned_grad, owned_grad, precision=HIGH)
        right_outer = jnp.einsum("tki,tkj->tij", owned_grad, owned_grad, precision=HIGH)
        held["owned"] = (
            owned_grad,
            turn_in(basis_left, owned_grad, basis_right),
            left_outer,
            right_outer,
            as_columns(turned_by(stat_left, basis_left), turned_by(stat_right, basis_right)),
            as_columns(turned_by(left_outer, basis_left), turned_by(right_outer, basis_right)),
            jnp.sum(owned_grad * owned_grad),
        )
        return rows

    def landed(arrived):
        arrived, held["owned"], held["gains"] = lax.optimization_barrier(
            (arrived, held["owned"], gain_flat)
        )
        return arrived

    grad_quarter = return_rows(
        grad_rows, lists, first_lists, rounds, held["quarter"], ready, landed
    )

    (
        owned_grad,
        owned_turned,
        left_outer,
        right_outer,
        columns_before,
        columns_change,
        owned_squares,
    ) = held["owned"]
    squares = owned_squares + jnp.sum(grad_quarter * grad_quarter)
    gain_part = jnp.sum(
        lax.all_to_all(held["gains"], ("dp", "vocab"), 0, 0, tiled=True), axis=0
    )
    last_facts = jnp.concatenate([gain_part.reshape(-1, 128), jnp.full((1, 128), squares)], 0)
    last_facts = spread(last_facts, ("dp", "vocab"), devices).reshape(devices, -1, 128)
    square_total = jnp.sum(last_facts[:, -1, 0])
    gain_total = last_facts[:, :-1].reshape(-1)[: GAINS * D].reshape(GAINS, D)
    grad_norm = jnp.sqrt(square_total + jnp.sum(gain_total * gain_total))
    factor = jnp.minimum(1.0, CLIP_AT / grad_norm)
    table_grad = lax.all_gather(
        grad_quarter.astype(jnp.bfloat16), "dp", axis=0, tiled=True
    ).astype(jnp.float32)
    master_new, mom1_new, mom2_new, left_new, right_new, bleft_new, bright_new = soap_update(
        master_tiles,
        owned_grad,
        owned_turned,
        left_outer,
        right_outer,
        columns_before,
        columns_change,
        mom1_tiles,
        first_turned,
        mom2_tiles,
        stat_left,
        stat_right,
        basis_left,
        basis_right,
        factor,
    )
    table_new, table_m, table_v = adamw_update(
        table_master, table_grad * factor, table_mom1, table_mom2, RATE_MATRIX, DECAY
    )
    gains_new, gains_m, gains_v = adamw_update(
        gains, gain_total * factor, gain_mom1, gain_mom2, RATE_VECTOR, 0.0
    )
    return (
        loss_sum,
        count_all,
        grad_norm,
        master_new,
        master_new.astype(jnp.bfloat16),
        mom1_new,
        mom2_new,
        left_new,
        right_new,
        bleft_new,
        bright_new,
        table_new,
        table_new.astype(jnp.bfloat16),
        table_m,
        table_v,
        gains_new,
        gains_m,
        gains_v,
    )


def solution(mesh):
    placed = (
        P(("dp", "vocab"), None, None),
        P(("dp", "vocab"), None, None),
        P(("dp", "vocab"), None, None),
        P(("dp", "vocab"), None, None),
        P(("dp", "vocab"), None, None),
        P(("dp", "vocab"), None, None),
        P(("dp", "vocab"), None, None),
        P("vocab", None),
        P("vocab", None),
        P("vocab", None),
        P(),
        P(),
        P(),
        P(None, ("dp", "vocab"), None),
        P(None, ("dp", "vocab"), None),
        P(None, ("dp", "vocab")),
        P(None, ("dp", "vocab")),
        P(None, ("dp", "vocab"), None),
        P(None, ("dp", "vocab"), None),
        P(),
    )
    return jax.shard_map(
        per_device,
        mesh=mesh,
        in_specs=placed,
        out_specs=(
            P(),
            P(),
            P(),
            P(("dp", "vocab"), None, None),
            P(("dp", "vocab"), None, None),
            P(("dp", "vocab"), None, None),
            P(("dp", "vocab"), None, None),
            P(("dp", "vocab"), None, None),
            P(("dp", "vocab"), None, None),
            P(("dp", "vocab"), None, None),
            P(("dp", "vocab"), None, None),
            P("vocab", None),
            P("vocab", None),
            P("vocab", None),
            P("vocab", None),
            P(),
            P(),
            P(),
        ),
        check_vma=False,
    )
```

```python
import math

import jax
import jax.numpy as jnp
from jax import lax
from jax.experimental import pallas as pl
from jax.experimental.pallas import tpu as pltpu
from jax.sharding import PartitionSpec as P

D = 512
HEADS = 8
HEAD_DIM = 64
FF = 2048
ENC = 1
DEC = 2
MICRO = 2
LOSS_POS = 16
PB = 64
STEP = 10
MATS = 11
GAINS = 11


HIGH = lax.Precision.HIGH
NORM_EPS = 1e-06
CLIP_AT = 0.02
RATE_MATRIX = 0.1
RATE_VECTOR = 0.8
BETA_FIRST = 0.9
BETA_SECOND = 0.95
BETA_STAT = 0.95
ADAM_EPS = 1e-08
DECAY = 0.01


def rms_norm(stream, gain_row):
    return (
        stream * lax.rsqrt(jnp.mean(stream * stream, axis=-1, keepdims=True) + NORM_EPS) * gain_row
    )


def waves(length, columns):
    place_at = jnp.arange(length).astype(jnp.float32)[:, None]
    rate_at = jnp.exp(
        jnp.arange(columns // 2).astype(jnp.float32) * (-2.0 * math.log(10000.0) / columns)
    )
    angle = place_at * rate_at[None, :]
    return jnp.concatenate([jnp.sin(angle), jnp.cos(angle)], axis=1)


def linear(left_op, right_op):
    return jnp.dot(left_op, right_op, preferred_element_type=jnp.float32)


def linear_tr(left_op, right_op):
    return lax.dot_general(
        left_op, right_op, (((1,), (1,)), ((), ())), preferred_element_type=jnp.float32
    )


def outer_sum(left_op, right_op):
    return lax.dot_general(
        left_op, right_op, (((0,), (0,)), ((), ())), preferred_element_type=jnp.float32
    )


def split_heads(matrix):
    return matrix.reshape(matrix.shape[0], HEADS, HEAD_DIM)


NEVER=-1000000000.0
PAIR=2*HEAD_DIM
def kept_scores(query, keys, valid_len, causal, start_at):
    scores = lax.dot_general(query, keys, (((1,), (1,)), ((), ())), preferred_element_type=jnp.float32)
    key_at = lax.broadcasted_iota(jnp.int32, scores.shape if causal else (1, scores.shape[1]), 1)
    allowed = key_at < valid_len
    if causal:
        allowed = allowed & (key_at <= start_at + lax.broadcasted_iota(jnp.int32, scores.shape, 0))
    return jnp.where(allowed, scores, NEVER)

def head_masks(value):
    first = lax.broadcasted_iota(jnp.int32, value.shape, 1) < HEAD_DIM
    zero = jnp.zeros_like(value)
    return (jnp.where(first, value, zero), jnp.where(first, zero, value))

def attend_forward(query_in, query_at, keys_in, key_at, value_at, valid_len, causal):
    rows, keys = (query_in.shape[0] // MICRO, keys_in.shape[0] // MICRO)
    block = min(256, rows)
    steps = rows // block
    scale = HEAD_DIM ** (-0.5)

    def kernel(len_ref, query_ref, key_ref, value_ref, out_ref, stat_ref):
        start_at = pl.program_id(2) * block
        length = len_ref[pl.program_id(0)]
        queries = head_masks((query_ref[...].astype(jnp.float32) * scale).astype(jnp.bfloat16))
        values = head_masks(value_ref[...])
        total = jnp.zeros((block, PAIR), jnp.float32)
        stats = []
        for head in range(2):
            scores = kept_scores(queries[head], key_ref[...], length, causal, start_at)
            summit = jnp.max(scores, axis=1, keepdims=True)
            expo = jnp.exp(scores - summit)
            sums = jnp.sum(expo, axis=1, keepdims=True)
            total += jnp.dot(
                expo.astype(jnp.bfloat16), values[head], preferred_element_type=jnp.float32
            ) * (1.0 / sums)
            stats.append(summit + jnp.log(sums))
        out_ref[...] = total.astype(jnp.bfloat16)
        first = lax.broadcasted_iota(jnp.int32, (block, PAIR), 1) < HEAD_DIM
        stat_ref[...] = jnp.where(first, stats[0], stats[1])

    out_spec = pl.BlockSpec((block, PAIR), lambda seq, pair, step, lens: (seq * steps + step, pair))
    return pl.pallas_call(
        kernel,
        out_shape=(
            jax.ShapeDtypeStruct((MICRO * rows, D), jnp.bfloat16),
            jax.ShapeDtypeStruct((MICRO * rows, D), jnp.float32),
        ),
        grid_spec=pltpu.PrefetchScalarGridSpec(
            num_scalar_prefetch=1,
            grid=(MICRO, D // PAIR, steps),
            in_specs=[
                pl.BlockSpec((block, PAIR), lambda seq, pair, step, lens: (seq * steps + step, query_at + pair)),
                pl.BlockSpec((keys, PAIR), lambda seq, pair, step, lens: (seq, key_at + pair)),
                pl.BlockSpec((keys, PAIR), lambda seq, pair, step, lens: (seq, value_at + pair)),
            ],
            out_specs=(out_spec, out_spec),
        ),
        compiler_params=pltpu.CompilerParams(vmem_limit_bytes=40 * 2**20),
        cost_estimate=pl.CostEstimate(flops=4*MICRO*rows*keys*D, bytes_accessed=MICRO*(rows+keys)*D*8, transcendentals=MICRO*HEADS*rows*keys),
    )(valid_len, query_in, keys_in, keys_in)

def attend_backward(query_in, query_at, keys_in, key_at, value_at, valid_len, causal, stats, grad_out, first=0, seqs=MICRO, begun=()):
    rows, keys = (query_in.shape[0] // MICRO, keys_in.shape[0] // MICRO)
    block = min(512, rows)
    steps = rows // block
    scale = HEAD_DIM ** (-0.5)

    def kernel(len_ref, query_ref, key_ref, value_ref, stat_ref, up_ref, *refs):
        dq_ref, dk_ref, dv_ref, key_sum, value_sum = refs[len(begun) :]
        step = pl.program_id(2)
        start_at = step * block
        length = len_ref[first + pl.program_id(0)]
        queries = head_masks((query_ref[...].astype(jnp.float32) * scale).astype(jnp.bfloat16))
        upstream = head_masks(up_ref[...])
        keys_each = head_masks(key_ref[...])
        grad_query = jnp.zeros((block, PAIR), jnp.float32)
        grad_key = jnp.zeros((keys, PAIR), jnp.float32)
        grad_value = jnp.zeros((keys, PAIR), jnp.float32)
        over_rows = (((0,), (0,)), ((), ()))
        for head in range(2):
            scores = kept_scores(queries[head], key_ref[...], length, causal, start_at)
            probs = jnp.exp(scores - stat_ref[:, head * HEAD_DIM : head * HEAD_DIM + 1])
            grad_probs = lax.dot_general(upstream[head], value_ref[...], (((1,), (1,)), ((), ())), preferred_element_type=jnp.float32)
            inner = jnp.sum(probs * grad_probs, axis=1, keepdims=True)
            grad_scores = (probs * (grad_probs - inner)).astype(jnp.bfloat16)
            grad_query += jnp.dot(grad_scores, keys_each[head], preferred_element_type=jnp.float32)
            grad_key += lax.dot_general(grad_scores, queries[head], over_rows, preferred_element_type=jnp.float32)
            grad_value += lax.dot_general(probs.astype(jnp.bfloat16), upstream[head], over_rows, preferred_element_type=jnp.float32)
        dq_ref[...] = (grad_query * scale).astype(jnp.bfloat16)
        if steps == 1:
            dk_ref[...] = grad_key.astype(jnp.bfloat16)
            dv_ref[...] = grad_value.astype(jnp.bfloat16)
        else:
            @pl.when(step == 0)
            def _():
                key_sum[...] = grad_key
                value_sum[...] = grad_value

            @pl.when(step > 0)
            def _():
                key_sum[...] += grad_key
                value_sum[...] += grad_value

            @pl.when(step == steps - 1)
            def _():
                dk_ref[...] = key_sum[...].astype(jnp.bfloat16)
                dv_ref[...] = value_sum[...].astype(jnp.bfloat16)

    def row_spec(at, begin):
        return pl.BlockSpec(
            (block, PAIR),
            lambda seq, pair, step, lens: ((begin + seq) * steps + step, at + pair),
        )

    def key_spec(at, begin):
        return pl.BlockSpec((keys, PAIR), lambda seq, pair, step, lens: (begin + seq, at + pair))

    return pl.pallas_call(
        kernel,
        out_shape=(
            jax.ShapeDtypeStruct((MICRO * rows, D), jnp.bfloat16),
            jax.ShapeDtypeStruct((MICRO * keys, D), jnp.bfloat16),
            jax.ShapeDtypeStruct((MICRO * keys, D), jnp.bfloat16),
        ),
        grid_spec=pltpu.PrefetchScalarGridSpec(
            num_scalar_prefetch=1,
            grid=(seqs, D // PAIR, steps),
            in_specs=[
                row_spec(query_at, first),
                key_spec(key_at, first),
                key_spec(value_at, first),
                row_spec(0, first),
                row_spec(0, first),
            ]
            + [pl.BlockSpec(memory_space=pl.ANY)] * len(begun),
            out_specs=(row_spec(0, first), key_spec(0, first), key_spec(0, first)),
            scratch_shapes=[pltpu.VMEM((keys, PAIR), jnp.float32)] * 2,
        ),
        input_output_aliases={6 + item: item for item in range(len(begun))},
        compiler_params=pltpu.CompilerParams(vmem_limit_bytes=40 * 2**20),
        cost_estimate=pl.CostEstimate(flops=10*seqs*rows*keys*D, bytes_accessed=seqs*(rows+keys)*D*16, transcendentals=seqs*HEADS*rows*keys),
    )(valid_len, query_in, keys_in, keys_in, stats, grad_out, *begun)


def norm_backward(stream, gain_row, grad_normed):
    _, pull_back = jax.vjp(rms_norm, stream, gain_row)
    return pull_back(grad_normed)


def self_forward(stream, gain_row, weight, valid_len, causal):
    normed = rms_norm(stream, gain_row).astype(jnp.bfloat16)
    joint_qkv = linear(normed, weight[:, : 3 * D]).astype(jnp.bfloat16)
    pairs = D // PAIR
    mixed_out, stats_kept = attend_forward(
        joint_qkv, 0, joint_qkv, pairs, 2 * pairs, valid_len, causal
    )
    return (
        stream + linear(mixed_out, weight[:, 3 * D :]),
        (stream, normed, joint_qkv, mixed_out, stats_kept),
    )


def self_backward(grad_stream, kept_block, gain_row, weight, valid_len, causal, between=None):
    stream, normed, joint_qkv, mixed_out, stats_kept = kept_block
    grad_low = grad_stream.astype(jnp.bfloat16)
    grad_out_w = outer_sum(mixed_out, grad_low)
    grad_mixed = linear_tr(grad_low, weight[:, 3 * D :]).astype(jnp.bfloat16)
    pairs = D // PAIR
    stages = 1 if between is None else MICRO
    grads = ()
    for stage in range(stages):
        if stage > 0:
            grad_mixed = between(grad_mixed)
        grads = attend_backward(
            joint_qkv,
            0,
            joint_qkv,
            pairs,
            2 * pairs,
            valid_len,
            causal,
            stats_kept,
            grad_mixed,
            stage * MICRO // stages,
            MICRO // stages,
            tuple(grads),
        )
    grad_joint = jnp.concatenate(grads, 1)
    if between is not None:
        grad_joint = between(grad_joint)
    grad_x, grad_gain = norm_backward(stream, gain_row, linear_tr(grad_joint, weight[:, : 3 * D]))
    return (
        grad_stream + grad_x,
        grad_gain,
        jnp.concatenate([outer_sum(normed, grad_joint), grad_out_w], 1).astype(jnp.bfloat16),
    )


def cross_forward(stream, gain_row, weight, memory, valid_len):
    normed = rms_norm(stream, gain_row).astype(jnp.bfloat16)
    query_in = linear(normed, weight[:, :D]).astype(jnp.bfloat16)
    pair_kv = linear(memory, weight[:, D : 3 * D]).astype(jnp.bfloat16)
    mixed_out, stats_kept = attend_forward(
        query_in, 0, pair_kv, 0, D // PAIR, valid_len, False
    )
    return (
        stream + linear(mixed_out, weight[:, 3 * D :]),
        (stream, normed, query_in, pair_kv, mixed_out, stats_kept),
    )


def cross_backward(grad_stream, kept_block, gain_row, weight, memory, valid_len):
    stream, normed, query_in, pair_kv, mixed_out, stats_kept = kept_block
    grad_low = grad_stream.astype(jnp.bfloat16)
    grad_out_w = outer_sum(mixed_out, grad_low)
    grad_mixed = linear_tr(grad_low, weight[:, 3 * D :]).astype(jnp.bfloat16)
    grad_query, grad_k, grad_v = attend_backward(
        query_in, 0, pair_kv, 0, D // PAIR, valid_len, False, stats_kept, grad_mixed
    )
    grad_pair = jnp.concatenate([grad_k, grad_v], 1)
    grad_weight = jnp.concatenate(
        [outer_sum(normed, grad_query), outer_sum(memory, grad_pair), grad_out_w], 1
    ).astype(jnp.bfloat16)
    grad_x, grad_gain = norm_backward(stream, gain_row, linear_tr(grad_query, weight[:, :D]))
    return (
        grad_stream + grad_x,
        grad_gain,
        grad_weight,
        linear_tr(grad_pair, weight[:, D : 3 * D]),
    )


def gelu_tanh(hidden):
    return jax.nn.gelu(hidden, approximate=True)


def ffn_forward(stream, gain_row, w_in, w_out):
    normed = rms_norm(stream, gain_row).astype(jnp.bfloat16)
    hidden = linear(normed, w_in)
    active = gelu_tanh(hidden).astype(jnp.bfloat16)
    return (stream + linear_tr(active, w_out), (stream, normed, hidden, active))


def ffn_backward(grad_stream, kept_block, gain_row, w_in, w_out):
    stream, normed, hidden, active = kept_block
    grad_low = grad_stream.astype(jnp.bfloat16)
    grad_out_w = outer_sum(grad_low, active).astype(jnp.bfloat16)
    _, pull_back = jax.vjp(gelu_tanh, hidden)
    grad_hidden = pull_back(linear(grad_low, w_out))[0].astype(jnp.bfloat16)
    grad_x, grad_gain = norm_backward(stream, gain_row, linear_tr(grad_hidden, w_in))
    return (
        grad_stream + grad_x,
        grad_gain,
        outer_sum(normed, grad_hidden).astype(jnp.bfloat16),
        grad_out_w,
    )


def forward_all(
    weights,
    gain_set,
    source_rows,
    source_len,
    target_len,
    place_rows,
    lay_decoder,
):
    stream = source_rows
    enc_kept = []
    for layer_no in range(ENC):
        stream, kept_self = self_forward(
            stream, gain_set[2 * layer_no], weights[layer_no], source_len, False
        )
        stream, kept_ffn = ffn_forward(
            stream,
            gain_set[2 * layer_no + 1],
            weights[ENC + 2 * DEC + layer_no],
            weights[2 * ENC + 3 * DEC + layer_no],
        )
        enc_kept.append((kept_self, kept_ffn))
    memory, decoded = lay_decoder(rms_norm(stream, gain_set[2 * ENC]).astype(jnp.bfloat16))
    dec_kept, exit_in, exit_rows = ([], [], [])
    for layer_no in range(DEC):
        base_at = 2 * ENC + 1 + 3 * layer_no
        decoded, kept_self = self_forward(
            decoded, gain_set[base_at], weights[ENC + layer_no], target_len, True
        )
        decoded, kept_cross = cross_forward(
            decoded, gain_set[base_at + 1], weights[ENC + DEC + layer_no], memory, source_len
        )
        decoded, kept_ffn = ffn_forward(
            decoded,
            gain_set[base_at + 2],
            weights[2 * ENC + 2 * DEC + layer_no],
            weights[3 * ENC + 3 * DEC + layer_no],
        )
        dec_kept.append((kept_self, kept_cross, kept_ffn))
        picked_rows = decoded[place_rows]
        exit_in.append(picked_rows)
        exit_rows.append(
            rms_norm(picked_rows, gain_set[2 * ENC + 1 + 3 * DEC + layer_no]).astype(jnp.bfloat16)
        )
    kept = (source_len, target_len, place_rows, enc_kept, stream, memory, dec_kept, exit_in)
    return (kept, jnp.concatenate(exit_rows, 0))


def backward_all(
    weights, gain_set, kept, exit_grads, matrix_store, gain_store, before_last, between_last
):
    source_len, target_len, place_rows, enc_kept, stream, memory, dec_kept, exit_in = kept
    exit_each = jnp.split(exit_grads, DEC, axis=0)
    grad_decoded = jnp.zeros(dec_kept[0][0][0].shape, jnp.float32)
    grad_memory = jnp.zeros(memory.shape, jnp.float32)
    for layer_no in reversed(range(DEC)):
        base_at = 2 * ENC + 1 + 3 * layer_no
        exit_at = 2 * ENC + 1 + 3 * DEC + layer_no
        grad_rows, gain_store[exit_at] = norm_backward(
            exit_in[layer_no], gain_set[exit_at], exit_each[layer_no]
        )
        grad_decoded = grad_decoded.at[place_rows].add(grad_rows)
        kept_self, kept_cross, kept_ffn = dec_kept[layer_no]
        in_at, out_at = (2 * ENC + 2 * DEC + layer_no, 3 * ENC + 3 * DEC + layer_no)
        grad_decoded, gain_store[base_at + 2], matrix_store[in_at], matrix_store[out_at] = (
            ffn_backward(
                grad_decoded, kept_ffn, gain_set[base_at + 2], weights[in_at], weights[out_at]
            )
        )
        cross_at = ENC + DEC + layer_no
        grad_decoded, gain_store[base_at + 1], matrix_store[cross_at], grad_mem = cross_backward(
            grad_decoded, kept_cross, gain_set[base_at + 1], weights[cross_at], memory, source_len
        )
        grad_memory = grad_memory + grad_mem
        grad_decoded, gain_store[base_at], matrix_store[ENC + layer_no] = self_backward(
            grad_decoded, kept_self, gain_set[base_at], weights[ENC + layer_no], target_len, True
        )
    grad_stream, gain_store[2 * ENC] = norm_backward(stream, gain_set[2 * ENC], grad_memory)
    for layer_no in reversed(range(ENC)):
        kept_self, kept_ffn = enc_kept[layer_no]
        in_at, out_at = (ENC + 2 * DEC + layer_no, 2 * ENC + 3 * DEC + layer_no)
        grad_stream, gain_store[2 * layer_no + 1], matrix_store[in_at], matrix_store[out_at] = (
            ffn_backward(
                grad_stream, kept_ffn, gain_set[2 * layer_no + 1], weights[in_at], weights[out_at]
            )
        )
        if layer_no == 0:
            grad_stream = before_last(grad_stream)
        grad_stream, gain_store[2 * layer_no], matrix_store[layer_no] = self_backward(
            grad_stream,
            kept_self,
            gain_set[2 * layer_no],
            weights[layer_no],
            source_len,
            False,
            between_last if layer_no == 0 else None,
        )
    return (grad_stream, grad_decoded)


def fold_ranked(tiles, rank_of):
    count, half = (tiles.shape[0], PB // 2)

    def kernel(rank_ref, tile_ref, out_ref):
        def one_block(tile_no, carry):
            value = tile_ref[tile_no]
            folded = jnp.concatenate([value[:half], value[half:]], axis=1)
            out_ref[rank_ref[tile_no]] = folded.astype(jnp.bfloat16)
            return carry

        lax.fori_loop(0, count, one_block, 0)

    return pl.pallas_call(
        kernel,
        out_shape=jax.ShapeDtypeStruct((count, half, 2 * PB), jnp.bfloat16),
        grid_spec=pltpu.PrefetchScalarGridSpec(
            num_scalar_prefetch=1,
            grid=(1,),
            in_specs=[pl.BlockSpec(memory_space=pltpu.VMEM)],
            out_specs=pl.BlockSpec(memory_space=pltpu.VMEM),
        ),
        compiler_params=pltpu.CompilerParams(vmem_limit_bytes=40 * 2**20),
    )(rank_of, tiles)


def unfold_ranked(folded, rank_of):
    count, half = (folded.shape[0], PB // 2)

    def kernel(rank_ref, folded_ref, out_ref):
        def one_block(tile_no, carry):
            value = folded_ref[rank_ref[tile_no]]
            out_ref[tile_no, :half] = value[:, :PB]
            out_ref[tile_no, half:] = value[:, PB:]
            return carry

        lax.fori_loop(0, count, one_block, 0)

    return pl.pallas_call(
        kernel,
        out_shape=jax.ShapeDtypeStruct((count, PB, PB), jnp.float32),
        grid_spec=pltpu.PrefetchScalarGridSpec(
            num_scalar_prefetch=1,
            grid=(1,),
            in_specs=[pl.BlockSpec(memory_space=pltpu.VMEM)],
            out_specs=pl.BlockSpec(memory_space=pltpu.VMEM),
        ),
        compiler_params=pltpu.CompilerParams(vmem_limit_bytes=40 * 2**20),
    )(rank_of, folded)


def is_encoder(mat_no):
    return (
        mat_no < ENC
        or ENC + 2 * DEC <= mat_no < 2 * ENC + 2 * DEC
        or 2 * ENC + 3 * DEC <= mat_no < 3 * ENC + 3 * DEC
    )


def is_last(mat_no):
    return mat_no == 0


def rank_blocks(slot_list, devices, is_first):
    blocks_each = D // PB * (FF // PB)
    mats = slot_list // blocks_each
    early = jnp.zeros(mats.shape, jnp.bool_)
    for mat_no in range(MATS):
        if is_first(mat_no):
            early = early | (mats == mat_no)
    early = early.reshape(devices, -1).astype(jnp.int32)
    early_count = jnp.sum(early, axis=1)
    ahead = jnp.cumsum(early, axis=1) - early
    later = early_count[:, None] + jnp.arange(early.shape[1])[None, :] - ahead
    return (jnp.where(early == 1, ahead, later), early_count)


def room_for(per_device, chosen):
    share = sum(chosen(mat_no) for mat_no in range(MATS)) / MATS
    mean = per_device * share
    return min(per_device - 1, -(-int(mean + 4.2 * math.sqrt(mean * (1 - share))) // 4) * 4)


def by_block(slot_list, values):
    width, base = (64, 128)
    height = -(-slot_list.shape[0] // width)
    rows = (slot_list[:, None] // width == jnp.arange(height)[None, :]).astype(jnp.bfloat16)
    lanes = (slot_list[:, None] % width == jnp.arange(width)[None, :]).astype(jnp.bfloat16)
    found = []
    for value in values:
        high, low = (
            outer_sum(rows * (part.astype(jnp.bfloat16))[:, None], lanes)
            for part in (value // base, value % base)
        )
        found.append((high * base + low).astype(jnp.int32).reshape(-1)[: slot_list.shape[0]])
    return found


def lay_matrices(buffers, place_of, mats):
    half = PB // 2
    row_blocks, pairs = (D // PB, FF // (2 * PB))
    sizes = [buffer.shape[0] for buffer in buffers]
    starts = [sum(sizes[:item]) for item in range(len(sizes))]
    count = len(mats)

    def kernel(place_ref, *refs):
        sources, outs = (refs[: len(sizes)], refs[len(sizes) : len(sizes) + count])
        folded_ref, made, arrived, left = refs[len(sizes) + count :]
        left_half = lax.broadcasted_iota(jnp.int32, (half, 2 * PB), 1) < PB
        fetches = [
            pltpu.make_async_copy(
                source, folded_ref.at[pl.ds(start, size)], arrived.at[item]
            )
            for item, (source, start, size) in enumerate(zip(sources, starts, sizes))
        ]
        for fetch in fetches:
            fetch.start()
        for fetch in fetches:
            fetch.wait()

        def send(item):
            return pltpu.make_async_copy(made.at[item % 2], outs[item], left.at[item % 2])

        for item, mat_no in enumerate(mats):
            if item >= 2:
                send(item - 2).wait()

            def one_row(row_no, carry, item=item, mat_no=mat_no):
                first = (mat_no * row_blocks + row_no) * 2 * pairs
                row_at = pl.multiple_of(row_no * PB, PB)
                for pair_no in range(pairs):
                    even = folded_ref[place_ref[first + 2 * pair_no]].astype(jnp.float32)
                    odd = folded_ref[place_ref[first + 2 * pair_no + 1]].astype(jnp.float32)
                    columns = slice(2 * PB * pair_no, 2 * PB * (pair_no + 1))
                    upper = jnp.where(left_half, even, pltpu.roll(odd, PB, 1))
                    lower = jnp.where(left_half, pltpu.roll(even, PB, 1), odd)
                    made[item % 2, pl.ds(row_at, half), columns] = upper.astype(jnp.bfloat16)
                    made[item % 2, pl.ds(row_at + half, half), columns] = lower.astype(jnp.bfloat16)
                return carry

            lax.fori_loop(0, row_blocks, one_row, 0)
            send(item).start()
        for item in range(max(count - 2, 0), count):
            send(item).wait()

    return pl.pallas_call(
        kernel,
        out_shape=[jax.ShapeDtypeStruct((D, FF), jnp.bfloat16)] * count,
        grid_spec=pltpu.PrefetchScalarGridSpec(
            num_scalar_prefetch=1,
            grid=(1,),
            in_specs=[pl.BlockSpec(memory_space=pl.ANY)] * len(sizes),
            out_specs=[pl.BlockSpec(memory_space=pl.ANY)] * count,
            scratch_shapes=[
                pltpu.VMEM((sum(sizes), half, 2 * PB), jnp.bfloat16),
                pltpu.VMEM((2, D, FF), jnp.bfloat16),
                pltpu.SemaphoreType.DMA((len(sizes),)),
                pltpu.SemaphoreType.DMA((2,)),
            ],
        ),
        compiler_params=pltpu.CompilerParams(vmem_limit_bytes=40 * 2**20),
    )(place_of, *buffers)


def fold_gradients(matrices, mats, place_of, sizes, begun=None):
    half = PB // 2
    row_blocks, pairs = (D // PB, FF // (2 * PB))
    count = len(mats)
    whole = sum(sizes)
    given = 0 if begun is None else 1
    skipped = 0 if begun is None else whole - begun.shape[0]
    kept = whole - skipped

    def kernel(place_ref, *refs):
        sources, old = (refs[:count], refs[count : count + given])
        outs = refs[count + given : -5]
        folded_ref, held, arrived, left, old_sem = refs[-5:]
        left_half = lax.broadcasted_iota(jnp.int32, (half, 2 * PB), 1) < PB

        def fetch(item):
            return pltpu.make_async_copy(sources[item], held.at[item % 2], arrived.at[item % 2])

        fetch(0).start()
        if given:
            before = pltpu.make_async_copy(
                old[0], folded_ref.at[pl.ds(0, kept)], old_sem.at[0]
            )
            before.start()
            before.wait()
        for item, mat_no in enumerate(mats):
            if item + 1 < count:
                fetch(item + 1).start()
            fetch(item).wait()

            def place(block, carry=None):
                spot = place_ref[block] - skipped
                return jnp.where(spot < 0, kept, spot) if given else spot

            def one_row(row_no, carry, item=item, mat_no=mat_no):
                first = (mat_no * row_blocks + row_no) * 2 * pairs
                row_at = pl.multiple_of(row_no * PB, PB)
                for pair_no in range(pairs):
                    columns = slice(2 * PB * pair_no, 2 * PB * (pair_no + 1))
                    upper = held[item % 2, pl.ds(row_at, half), columns].astype(jnp.float32)
                    lower = held[item % 2, pl.ds(row_at + half, half), columns].astype(jnp.float32)
                    even = jnp.where(left_half, upper, pltpu.roll(lower, PB, 1))
                    odd = jnp.where(left_half, pltpu.roll(upper, PB, 1), lower)
                    folded_ref[place(first + 2 * pair_no)] = even.astype(jnp.bfloat16)
                    folded_ref[place(first + 2 * pair_no + 1)] = odd.astype(jnp.bfloat16)
                return carry

            lax.fori_loop(0, row_blocks, one_row, 0)
        begin = 0
        sends = []
        for item, out in enumerate(outs):
            size = out.shape[0]
            sends.append(
                pltpu.make_async_copy(folded_ref.at[pl.ds(begin, size)], out, left.at[item])
            )
            begin += size
        for send in sends:
            send.start()
        for send in sends:
            send.wait()

    shapes = [kept] if given else list(sizes)
    return pl.pallas_call(
        kernel,
        out_shape=[jax.ShapeDtypeStruct((size, half, 2 * PB), jnp.bfloat16) for size in shapes],
        grid_spec=pltpu.PrefetchScalarGridSpec(
            num_scalar_prefetch=1,
            grid=(1,),
            in_specs=[pl.BlockSpec(memory_space=pl.ANY)] * (count + given),
            out_specs=[pl.BlockSpec(memory_space=pl.ANY)] * len(shapes),
            scratch_shapes=[
                pltpu.VMEM((kept + given, half, 2 * PB), jnp.bfloat16),
                pltpu.VMEM((2, D, FF), jnp.bfloat16),
                pltpu.SemaphoreType.DMA((2,)),
                pltpu.SemaphoreType.DMA((2,)),
                pltpu.SemaphoreType.DMA((1,)),
            ],
        ),
        compiler_params=pltpu.CompilerParams(vmem_limit_bytes=40 * 2**20),
    )(place_of, *[matrices[mat_no] for mat_no in mats], *([begun] if given else []))


def exchange_plan(dp_size, along, per_device):
    low, high = (along.bit_length() - 1, dp_size.bit_length() - 1)
    base = [low + bit for bit in range(high)] + list(range(1, low))
    third = per_device // 3
    sizes = [per_device - 2 * third, third, third]
    return [(size, base[turn:] + base[:turn]) for turn, size in enumerate(sizes)]


def places_for(ranks, plan, devices):
    per_device = sum(size for size, _ in plan)
    owner = jnp.arange(devices)[:, None]
    place = jnp.zeros_like(ranks)
    begin = 0
    for size, order in plan:
        spot = jnp.zeros_like(owner)
        for bit in order:
            spot = spot * 2 + owner // 2**bit % 2
        here = begin * (devices // 2) + spot * size + ranks - begin
        place = jnp.where((ranks >= begin) & (ranks < begin + size), here, place)
        begin += size
    return place + owner % 2 * (devices // 2 * per_device)


def halve(value, bit, devices):
    me = lax.axis_index("dp") * lax.axis_size("vocab") + lax.axis_index("vocab")

    mine = me // 2**bit % 2
    value = value.reshape(2, value.shape[0] // 2, *value.shape[1:])
    sent = lax.dynamic_index_in_dim(value, 1 - mine, 0, keepdims=False)
    kept = lax.dynamic_index_in_dim(value, mine, 0, keepdims=False)
    pairs = [(index, index ^ 2**bit) for index in range(devices)]
    arrived = lax.ppermute(sent, ("dp", "vocab"), pairs)
    return kept.astype(jnp.float32) + arrived.astype(jnp.float32)


def first_exchange(folded, devices):
    return halve(folded, 0, devices).astype(jnp.bfloat16)


def split_parts(total, plan, devices):
    parts, begin = ([], 0)
    for size, _ in plan:
        count = size * (devices // 2)
        parts.append(total[begin : begin + count])
        begin += count
    return parts


def one_exchange(parts, plan, round_no, devices):
    return [
        halve(part.astype(jnp.bfloat16), order[round_no], devices)
        for part, (_, order) in zip(parts, plan)
    ]


def other_exchanges(parts, plan, devices, done=0):
    for round_no in range(done, len(plan[0][1])):
        parts = one_exchange(parts, plan, round_no, devices)
    return jnp.concatenate(parts, 0)


def take_rows(source, index_at, kind):
    count, width, unroll = (index_at.shape[0], source.shape[1], 32)
    whole = -(-count // 128) * 128
    block = max(size for size in range(128, 1025, 128) if whole % size == 0)
    index_at = jnp.pad(index_at, (0, whole - count))

    def kernel(index_ref, source_ref, out_ref, held_ref):
        first = pl.program_id(0) * block

        def copy_some(group, carry):
            base = pl.multiple_of(group * unroll, unroll)
            for row_no in range(unroll):
                held_ref[pl.ds(base + row_no, 1), :] = source_ref[
                    pl.ds(index_ref[first + base + row_no], 1), :
                ]
            return carry

        lax.fori_loop(0, block // unroll, copy_some, 0)
        out_ref[...] = held_ref[...].astype(kind)

    taken = pl.pallas_call(
        kernel,
        out_shape=jax.ShapeDtypeStruct((whole, width), kind),
        grid_spec=pltpu.PrefetchScalarGridSpec(
            num_scalar_prefetch=1,
            grid=(whole // block,),
            in_specs=[pl.BlockSpec(memory_space=pltpu.VMEM)],
            out_specs=pl.BlockSpec((block, width), lambda step, index: (step, 0)),
            scratch_shapes=[pltpu.VMEM((block, width), jnp.float32)],
        ),
        compiler_params=pltpu.CompilerParams(vmem_limit_bytes=40 * 2**20),
    )(index_at, source)
    return taken[:count]


def add_rows(rows, index_at, total):
    count, width, block = (rows.shape[0], rows.shape[1], 512)
    whole = -(-count // block) * block
    index_at = jnp.pad(index_at, (0, whole - count), constant_values=-1)[None, :]
    rows = jnp.pad(rows, ((0, whole - count), (0, 0)))
    height = total.shape[0]

    def kernel(index_ref, rows_ref, total_ref, out_ref):
        @pl.when(pl.program_id(0) == 0)
        def _():
            out_ref[...] = total_ref[...]

        hits = lax.broadcasted_iota(jnp.int32, (height, block), 0) == index_ref[...]
        out_ref[...] += jnp.dot(
            hits.astype(jnp.float32).astype(jnp.bfloat16),
            rows_ref[...],
            preferred_element_type=jnp.float32,
        )

    return pl.pallas_call(
        kernel,
        out_shape=jax.ShapeDtypeStruct(total.shape, jnp.float32),
        grid=(whole // block,),
        in_specs=[
            pl.BlockSpec((1, block), lambda step: (0, step)),
            pl.BlockSpec((block, width), lambda step: (step, 0)),
            pl.BlockSpec((height, width), lambda step: (0, 0)),
        ],
        out_specs=pl.BlockSpec((height, width), lambda step: (0, 0)),
        compiler_params=pltpu.CompilerParams(vmem_limit_bytes=40 * 2**20),
    )(index_at, rows, total)


def spread(value, axes, peers):
    return lax.all_to_all(
        jnp.broadcast_to(value[None], (peers, *value.shape)), axes, 0, 0, tiled=True
    )


def count_before(mask):
    size, width = (mask.shape[-1], 128)
    parts = mask.reshape(*mask.shape[:-1], size // width, width).astype(jnp.bfloat16)
    earlier = (jnp.arange(width)[:, None] < jnp.arange(width)[None, :]).astype(jnp.bfloat16)
    inside = jnp.einsum("...pw,wk->...pk", parts, earlier, preferred_element_type=jnp.float32)
    totals = jnp.sum(parts.astype(jnp.float32), axis=-1)
    ahead = jnp.cumsum(totals, axis=-1) - totals
    return (inside + ahead[..., None]).reshape(mask.shape).astype(jnp.int32)


def room(count, peers):
    mean = count / peers
    return min(count, -(-int(mean + 5.0 * math.sqrt(mean)) // 16) * 16)


def listed(mask, rank, values, size):
    width, base = (16, 128)
    rows = mask[..., None] & (rank[..., None] // width == jnp.arange(size // width))
    lanes = (rank[..., None] % width == jnp.arange(width)).astype(jnp.bfloat16)
    values = values + 1
    high, low = (
        jnp.einsum(
            "...th,...tl->...hl",
            jnp.where(rows, part[..., None].astype(jnp.bfloat16), 0),
            lanes,
            preferred_element_type=jnp.float32,
        )
        for part in (values // base, values % base)
    )
    return (high * base + low).astype(jnp.int32).reshape(*mask.shape[:-1], size) - 1


def rounds_needed(owner_all, peers, size):
    held = jnp.sum((owner_all[:, None, :] == jnp.arange(peers)[:, None]).astype(jnp.int32), axis=2)
    return (jnp.max(held) + size - 1) // size


def fetch_plan(table_part, tokens_all, peers_here, peer_me):
    peers, rows_each = (peers_here.shape[0], table_part.shape[0])
    count = tokens_all.shape[1]
    size = room(count, peers)
    asked = peers_here // rows_each == peer_me
    asked_rank = count_before(asked)
    own_tokens = lax.dynamic_index_in_dim(peers_here, peer_me, 0, keepdims=False)
    own_owner = own_tokens // rows_each
    own_mask = own_owner[None, :] == jnp.arange(peers)[:, None]
    own_rank = jnp.sum(jnp.where(own_mask, count_before(own_mask), 0), axis=0)

    def to_send(round_no):
        wanted = listed(
            asked, asked_rank - round_no * size, peers_here % rows_each, size
        )
        return take_rows(table_part, jnp.maximum(wanted.reshape(-1), 0), jnp.bfloat16)

    def found_in(arrived, round_no):
        rank_now = own_rank - round_no * size
        now = (rank_now >= 0) & (rank_now < size)
        found = take_rows(
            arrived.astype(jnp.float32), jnp.where(now, own_owner * size + rank_now, 0), jnp.float32
        )
        return (now, found)

    def again(round_no, rows):
        now, found = found_in(swap_rows(to_send(round_no)), round_no)
        return jnp.where(now[:, None], found, rows)

    rounds = rounds_needed(tokens_all // rows_each, peers, size)

    def finish(arrived):
        return lax.fori_loop(1, rounds, again, found_in(arrived, 0)[1])

    return (to_send(0), finish)


def swap_rows(rows):
    return lax.all_to_all(rows, "vocab", 0, 0, tiled=True)


def return_plan(tokens_all, rows_each, dp_size):
    peers, count = tokens_all.shape
    along = peers // dp_size
    quarter = rows_each // dp_size
    me = lax.axis_index("dp") * along + lax.axis_index("vocab")
    size = room(count, peers)
    owner_all = (tokens_all % rows_each) // quarter * along + tokens_all // rows_each
    arriving = owner_all == me
    arriving_rank = count_before(arriving)
    own_owner = lax.dynamic_index_in_dim(owner_all, me, 0, keepdims=False)
    leaving = own_owner[None, :] == jnp.arange(peers)[:, None]
    leaving_rank = count_before(leaving)
    place = jnp.broadcast_to(jnp.arange(count)[None, :], leaving.shape)

    def lists(round_no):
        return (
            jnp.maximum(
                listed(leaving, leaving_rank - round_no * size, place, size).reshape(-1), 0
            ),
            listed(
                arriving, arriving_rank - round_no * size, tokens_all % quarter, size
            ).reshape(-1),
        )

    return (lists, rounds_needed(owner_all, peers, size))


def return_rows(grad_rows, lists, first_lists, rounds, total, ready, landed):
    def swap_all(rows):
        return lax.all_to_all(rows, ("dp", "vocab"), 0, 0, tiled=True)

    def again(round_no, so_far):
        chosen, where = lists(round_no)
        return add_rows(swap_all(take_rows(grad_rows, chosen, jnp.bfloat16)), where, so_far)

    arrived = landed(swap_all(ready(take_rows(grad_rows, first_lists[0], jnp.bfloat16))))
    return lax.fori_loop(1, rounds, again, add_rows(arrived, first_lists[1], total))


def turn_in(left_basis, tiles, right_basis):
    half = jnp.einsum("tki,tkl->til", left_basis, tiles, precision=HIGH)
    return jnp.einsum("til,tlj->tij", half, right_basis, precision=HIGH)


def turn_out(left_basis, tiles, right_basis):
    half = jnp.einsum("tik,tkl->til", left_basis, tiles, precision=HIGH)
    return jnp.einsum("til,tjl->tij", half, right_basis, precision=HIGH)


def orthonormal(columns):
    lanes, group = (128, 4)

    def kernel(in_ref, out_ref):
        out_ref[...] = in_ref[...]

        def four_columns(group_at, carry):
            first = group_at * group
            pivots = []
            for item in range(group):
                pivot = out_ref[first + item]
                for before in pivots:
                    pivot = pivot - jnp.sum(before * pivot, axis=0, keepdims=True) * before
                pivot = pivot / jnp.sqrt(jnp.sum(pivot * pivot, axis=0, keepdims=True))
                out_ref[first + item] = pivot
                pivots.append(pivot)

            def one_group(group_no, inner):
                held = [out_ref[group_no * group + item] for item in range(group)]
                for item in range(group):
                    value = held[item]
                    shares = [
                        jnp.sum(pivot * value, axis=0, keepdims=True) for pivot in pivots
                    ]
                    for pivot, share in zip(pivots, shares):
                        value = value - share * pivot
                    held[item] = value
                for item in range(group):
                    out_ref[group_no * group + item] = held[item]
                return inner

            return lax.fori_loop(group_at + 1, PB // group, one_group, carry)

        lax.fori_loop(0, PB // group, four_columns, 0)

    spec = pl.BlockSpec((PB, PB, lanes), lambda step: (0, 0, step))
    return pl.pallas_call(
        kernel,
        out_shape=jax.ShapeDtypeStruct(columns.shape, jnp.float32),
        grid=(columns.shape[2] // lanes,),
        in_specs=[spec],
        out_specs=spec,
        compiler_params=pltpu.CompilerParams(vmem_limit_bytes=40 * 2**20),
    )(columns)


def as_columns(left, right):
    both = jnp.transpose(jnp.concatenate([left, right], 0), (2, 1, 0))
    return jnp.pad(both, ((0, 0), (0, 0), (0, -both.shape[2] % 128)))


def renew_bases(columns, count):
    renewed = jnp.transpose(orthonormal(columns)[:, :, : 2 * count], (2, 1, 0))
    return (renewed[:count], renewed[count:])


def turned_by(stat, basis):
    return jnp.einsum("tij,tjk->tik", stat, basis, precision=HIGH)


def soap_update(
    master,
    grad_tiles,
    grad_turned,
    left_outer,
    right_outer,
    columns_before,
    columns_change,
    first_mom,
    first_turned,
    second_mom,
    left_stat,
    right_stat,
    left_basis,
    right_basis,
    factor,
):
    first_new = BETA_FIRST * first_mom + (1 - BETA_FIRST) * (factor * grad_tiles)
    grad_turned = factor * grad_turned
    first_turned = BETA_FIRST * first_turned + (1 - BETA_FIRST) * grad_turned
    second_new = BETA_SECOND * second_mom + (1 - BETA_SECOND) * grad_turned * grad_turned
    direction = (
        first_turned
        / (1 - BETA_FIRST**STEP)
        / (jnp.sqrt(second_new / (1 - BETA_SECOND**STEP)) + ADAM_EPS)
    )
    master_new = master - RATE_MATRIX * (
        turn_out(left_basis, direction, right_basis) + DECAY * master
    )
    left_new = BETA_STAT * left_stat + (1 - BETA_STAT) * (factor * (factor * left_outer))
    right_new = BETA_STAT * right_stat + (1 - BETA_STAT) * (factor * (factor * right_outer))
    return (
        master_new,
        first_new,
        second_new,
        left_new,
        right_new,
        *renew_bases(
            BETA_STAT * columns_before + (1 - BETA_STAT) * (factor * (factor * columns_change)),
            master.shape[0],
        ),
    )


def adamw_update(master, grad_now, first_mom, second_mom, rate, decay_by):
    first_new = BETA_FIRST * first_mom + (1 - BETA_FIRST) * grad_now
    second_new = BETA_SECOND * second_mom + (1 - BETA_SECOND) * grad_now * grad_now
    direction = (
        first_new
        / (1 - BETA_FIRST**STEP)
        / (jnp.sqrt(second_new / (1 - BETA_SECOND**STEP)) + ADAM_EPS)
    )
    return (master - rate * (direction + decay_by * master), first_new, second_new)


def per_device(
    master_tiles,
    mom1_tiles,
    mom2_tiles,
    stat_left,
    stat_right,
    basis_left,
    basis_right,
    table_master,
    table_mom1,
    table_mom2,
    gains,
    gain_mom1,
    gain_mom2,
    source_ids,
    target_ids,
    source_len,
    target_len,
    loss_place,
    exit_layer,
    slot_list,
):
    dp_size, along = (lax.axis_size("dp"), lax.axis_size("vocab"))
    dp_me, peer_me = (lax.axis_index("dp"), lax.axis_index("vocab"))
    devices = dp_size * along
    rows_each = table_master.shape[0]
    quarter = rows_each // dp_size
    source_len, target_len = (source_len[:, 0], target_len[:, 0])

    shifted = jnp.pad(target_ids[:, 0, :-1], ((0, 0), (1, 0)))
    tokens = jnp.concatenate([source_ids.reshape(-1), shifted.reshape(-1)])
    places = loss_place[:, 0]
    counted = places < target_len[:, None]
    reach = [
        jnp.sum((counted & (exit_layer[:, 0] >= layer_no)).astype(jnp.int32))
        for layer_no in range(DEC)
    ]
    labels = jnp.take_along_axis(target_ids[:, 0], places, axis=1).reshape(-1)
    row_count = MICRO * LOSS_POS
    own_facts = jnp.concatenate(
        [tokens, labels, counted.reshape(-1).astype(jnp.int32), jnp.stack(reach)]
    )
    fact_count = own_facts.shape[0]
    own_facts = jnp.pad(own_facts, (0, -fact_count % 128))
    facts = spread(own_facts, ("dp", "vocab"), devices)
    slots_later, facts, mom1_later, left_later, right_later = lax.optimization_barrier(
        (slot_list, facts, mom1_tiles, basis_left, basis_right)
    )
    tokens_all = facts[:, : tokens.shape[0]]
    after = facts[:, tokens.shape[0] :]
    labels_all = after[:, :row_count]
    counted_all = after[:, row_count : 2 * row_count].astype(jnp.float32)
    reach_all = jnp.sum(after[:, 2 * row_count : 2 * row_count + DEC].astype(jnp.float32), axis=0)
    count_all = jnp.sum(counted_all)
    fraction = reach_all / jnp.sum(reach_all)

    per_device = master_tiles.shape[0]
    me = dp_me * along + peer_me
    ranks, early_count = rank_blocks(slot_list, devices, is_encoder)
    first_size = room_for(per_device, is_encoder)
    second_size = per_device - first_size
    place_at = jnp.where(
        ranks < first_size,
        jnp.arange(devices)[:, None] * first_size + ranks,
        devices * first_size
        + jnp.arange(devices)[:, None] * second_size
        + ranks
        - first_size,
    )
    late_size = room_for(per_device, is_last)
    soon_size = per_device - late_size
    back_ranks, soon_count = rank_blocks(slots_later, devices, lambda mat_no: not is_last(mat_no))
    soon_plan = exchange_plan(dp_size, along, soon_size)
    late_plan = exchange_plan(dp_size, along, late_size)
    back_at = jnp.where(
        back_ranks < soon_size,
        places_for(back_ranks, soon_plan, devices),
        devices * soon_size + places_for(back_ranks - soon_size, late_plan, devices),
    )
    place_of, back_of = by_block(slots_later, [place_at.reshape(-1), back_at.reshape(-1)])
    own_folded = fold_ranked(
        master_tiles, lax.dynamic_index_in_dim(ranks, me, 0, keepdims=False)
    )
    src_count, tgt_count = (source_ids.shape[2], target_ids.shape[2])

    def planned(first, length):
        ids_all = tokens_all[:, first : first + MICRO * length]
        peers_here = lax.dynamic_slice_in_dim(ids_all, dp_me * along, along, 0)
        return fetch_plan(table_master, ids_all, peers_here, peer_me)

    source_sent, source_finish = planned(0, src_count)
    target_sent, target_finish = planned(MICRO * src_count, tgt_count)
    first_tiles = lax.all_gather(own_folded[:first_size], ("dp", "vocab"), axis=0, tiled=True)
    lists, rounds = return_plan(tokens_all, rows_each, dp_size)
    (
        own_second,
        first_tiles,
        source_arrived,
        first_lists,
        first_turned,
        target_sent,
        place_of,
        wave_set,
    ) = lax.optimization_barrier(
        (
            own_folded[first_size:],
            first_tiles,
            swap_rows(source_sent),
            lists(0),
            turn_in(left_later, mom1_later, right_later),
            target_sent,
            place_of,
            waves(src_count, D),
        )
    )
    second_tiles = lax.all_gather(own_second, ("dp", "vocab"), axis=0, tiled=True)
    encoder_mats = [mat_no for mat_no in range(MATS) if is_encoder(mat_no)]
    decoder_mats = [mat_no for mat_no in range(MATS) if not is_encoder(mat_no)]

    def lay_with_all():
        others = lax.all_gather(own_second, ("dp", "vocab"), axis=0, tiled=True)
        return lay_matrices([first_tiles, others], place_of, encoder_mats)

    def lay_with_first():
        return lay_matrices([first_tiles], place_of, encoder_mats)

    encoder_set = lax.cond(
        jnp.max(early_count) > first_size, lay_with_all, lay_with_first
    )
    weights = [None] * MATS
    for mat_no, matrix in zip(encoder_mats, encoder_set):
        weights[mat_no] = matrix

    def lay_decoder(memory):
        held, tiles, arrived = lax.optimization_barrier((memory, second_tiles, target_arrived))
        decoder_set = lay_matrices([first_tiles, tiles], place_of, decoder_mats)
        for mat_no, matrix in zip(decoder_mats, decoder_set):
            weights[mat_no] = matrix
        return (held, with_waves(target_finish(arrived), tgt_count))

    def with_waves(rows, length):
        return rows * math.sqrt(D) + jnp.tile(wave_set[:length], (MICRO, 1))

    source_rows = with_waves(source_finish(source_arrived), src_count)
    source_rows, target_sent = lax.optimization_barrier((source_rows, target_sent))
    target_arrived = swap_rows(target_sent)

    place_rows = (places + jnp.arange(MICRO)[:, None] * tgt_count).reshape(-1)
    kept, exit_rows = forward_all(
        weights,
        gains,
        source_rows,
        source_len,
        target_len,
        place_rows,
        lay_decoder,
    )

    table_low_part = table_master.astype(jnp.bfloat16)
    exit_count = DEC * row_count
    exit_all = lax.all_gather(exit_rows, ("dp", "vocab"), axis=0, tiled=True)
    exit_here = spread(exit_rows, "vocab", along).reshape(-1, D)
    label_rows = jnp.tile(labels_all, (1, DEC)).reshape(-1)
    weight_rows = (
        jnp.repeat(fraction, row_count)[None, :] * jnp.tile(counted_all, (1, DEC))
    ).reshape(-1)
    group_rows = along * exit_count
    group_at = dp_me * group_rows
    label_here = lax.dynamic_slice_in_dim(label_rows, group_at, group_rows, 0)
    weight_here = lax.dynamic_slice_in_dim(weight_rows, group_at, group_rows, 0)
    logits = linear_tr(exit_here, table_low_part)
    hit_here = label_here[:, None] - peer_me * rows_each == jnp.arange(rows_each)[None, :]
    summit = jnp.max(logits, axis=1)
    spread_part = jnp.sum(jnp.exp(logits - summit[:, None]), axis=1)
    picked_part = jnp.sum(jnp.where(hit_here, logits, 0.0), axis=1)
    stats = spread(
        jnp.stack([summit, spread_part, picked_part]), ("dp", "vocab"), devices
    ).reshape(dp_size, along, 3, group_rows)
    summit_all = jnp.max(stats[:, :, 0], axis=1)
    total_all = jnp.sum(stats[:, :, 1] * jnp.exp(stats[:, :, 0] - summit_all[:, None]), axis=1)
    spread_all = summit_all + jnp.log(total_all)
    picked_all = jnp.sum(stats[:, :, 2], axis=1)
    loss_sum = jnp.sum(weight_rows * (spread_all - picked_all).reshape(-1))
    spread_here = lax.dynamic_index_in_dim(spread_all, dp_me, 0, keepdims=False)

    def logit_grads(logit_set, spread, weight_set, hits):
        return (
            (weight_set / count_all)[:, None]
            * (jnp.exp(logit_set - spread[:, None]) - hits.astype(jnp.float32))
        ).astype(jnp.bfloat16)

    grads_here = logit_grads(logits, spread_here, weight_here, hit_here)
    grad_parts = linear(grads_here, table_low_part).astype(jnp.bfloat16)
    grad_parts = lax.all_to_all(grad_parts, "vocab", 0, 0, tiled=True)
    exit_grads = jnp.sum(
        grad_parts.reshape(along, exit_count, D).astype(jnp.float32), axis=0
    )

    matrix_store = [None] * MATS
    gain_store = [None] * GAINS
    first_row = peer_me * rows_each + dp_me * quarter
    table_quarter = lax.dynamic_slice_in_dim(table_low_part, dp_me * quarter, quarter, 0)
    hit_quarter = label_rows[:, None] - first_row == jnp.arange(quarter)[None, :]
    grads_quarter = logit_grads(
        linear_tr(exit_all, table_quarter), spread_all.reshape(-1), weight_rows, hit_quarter
    )
    grad_quarter = outer_sum(grads_quarter, exit_all)
    soon_mats = [mat_no for mat_no in range(MATS) if not is_last(mat_no)]
    late_mats = [mat_no for mat_no in range(MATS) if is_last(mat_no)]
    both = [devices * soon_size, devices * late_size]
    held = {}

    def before_last(grad_stream):
        blocks, held["begun"] = fold_gradients(matrix_store, soon_mats, back_of, both)
        grad_stream, blocks, held["quarter"] = lax.optimization_barrier(
            (grad_stream, blocks, grad_quarter)
        )
        held["total"] = first_exchange(blocks, devices)
        return grad_stream

    def between_last(value):
        if "parts" not in held:
            value, total = lax.optimization_barrier((value, held["total"]))
            held["parts"], held["done"] = (split_parts(total, soon_plan, devices), 0)
        elif held["done"] < len(soon_plan[0][1]):
            parts = one_exchange(held["parts"], soon_plan, held["done"], devices)
            value, held["parts"] = lax.optimization_barrier((value, parts))
            held["done"] += 1
        return value

    grad_source, grad_target = backward_all(
        weights,
        gains,
        kept,
        exit_grads,
        matrix_store,
        gain_store,
        before_last,
        between_last,
    )

    grad_source = between_last(grad_source)
    grad_rows = jnp.concatenate([grad_source, grad_target], 0) * math.sqrt(D)
    grad_rows = between_last(grad_rows)
    [late_blocks] = fold_gradients(matrix_store, late_mats, back_of, both, held["begun"])
    late_parts = split_parts(first_exchange(late_blocks, devices), late_plan, devices)
    late_parts = one_exchange(late_parts, late_plan, 0, devices)

    late_sum = other_exchanges(late_parts, late_plan, devices, 1)

    def exchange_again():
        blocks, _ = fold_gradients(matrix_store, list(range(MATS)), back_of, both)
        parts = split_parts(first_exchange(blocks, devices), soon_plan, devices)
        return other_exchanges(parts, soon_plan, devices)

    share = -(-GAINS * D // (devices * 128)) * 128
    gain_flat = jnp.stack(gain_store).reshape(-1)
    gain_flat = jnp.pad(gain_flat, (0, devices * share - GAINS * D)).reshape(devices, share)

    def ready(rows):
        sums = other_exchanges(held["parts"], soon_plan, devices, held["done"])
        rows, sums, late = lax.optimization_barrier((rows, sums, late_sum))
        sums = lax.cond(jnp.min(soon_count) < soon_size, exchange_again, lambda: sums)
        owned_grad = unfold_ranked(
            jnp.concatenate([sums, late], 0),
            lax.dynamic_index_in_dim(back_ranks, me, 0, keepdims=False),
        )
        left_outer = jnp.einsum("tik,tjk->tij", owned_grad, owned_grad, precision=HIGH)
        right_outer = jnp.einsum("tki,tkj->tij", owned_grad, owned_grad, precision=HIGH)
        held["owned"] = (
            owned_grad,
            turn_in(basis_left, owned_grad, basis_right),
            left_outer,
            right_outer,
            as_columns(turned_by(stat_left, basis_left), turned_by(stat_right, basis_right)),
            as_columns(turned_by(left_outer, basis_left), turned_by(right_outer, basis_right)),
            jnp.sum(owned_grad * owned_grad),
        )
        return rows

    def landed(arrived):
        arrived, held["owned"], held["gains"] = lax.optimization_barrier(
            (arrived, held["owned"], gain_flat)
        )
        return arrived

    grad_quarter = return_rows(
        grad_rows, lists, first_lists, rounds, held["quarter"], ready, landed
    )

    (
        owned_grad,
        owned_turned,
        left_outer,
        right_outer,
        columns_before,
        columns_change,
        owned_squares,
    ) = held["owned"]
    squares = owned_squares + jnp.sum(grad_quarter * grad_quarter)
    gain_part = jnp.sum(
        lax.all_to_all(held["gains"], ("dp", "vocab"), 0, 0, tiled=True), axis=0
    )
    last_facts = jnp.concatenate([gain_part.reshape(-1, 128), jnp.full((1, 128), squares)], 0)
    last_facts = spread(last_facts, ("dp", "vocab"), devices).reshape(devices, -1, 128)
    square_total = jnp.sum(last_facts[:, -1, 0])
    gain_total = last_facts[:, :-1].reshape(-1)[: GAINS * D].reshape(GAINS, D)
    grad_norm = jnp.sqrt(square_total + jnp.sum(gain_total * gain_total))
    factor = jnp.minimum(1.0, CLIP_AT / grad_norm)
    table_grad = lax.all_gather(
        grad_quarter.astype(jnp.bfloat16), "dp", axis=0, tiled=True
    ).astype(jnp.float32)
    master_new, mom1_new, mom2_new, left_new, right_new, bleft_new, bright_new = soap_update(
        master_tiles,
        owned_grad,
        owned_turned,
        left_outer,
        right_outer,
        columns_before,
        columns_change,
        mom1_tiles,
        first_turned,
        mom2_tiles,
        stat_left,
        stat_right,
        basis_left,
        basis_right,
        factor,
    )
    table_new, table_m, table_v = adamw_update(
        table_master, table_grad * factor, table_mom1, table_mom2, RATE_MATRIX, DECAY
    )
    gains_new, gains_m, gains_v = adamw_update(
        gains, gain_total * factor, gain_mom1, gain_mom2, RATE_VECTOR, 0.0
    )
    return (
        loss_sum,
        count_all,
        grad_norm,
        master_new,
        master_new.astype(jnp.bfloat16),
        mom1_new,
        mom2_new,
        left_new,
        right_new,
        bleft_new,
        bright_new,
        table_new,
        table_new.astype(jnp.bfloat16),
        table_m,
        table_v,
        gains_new,
        gains_m,
        gains_v,
    )


def solution(mesh):
    placed = (
        P(("dp", "vocab"), None, None),
        P(("dp", "vocab"), None, None),
        P(("dp", "vocab"), None, None),
        P(("dp", "vocab"), None, None),
        P(("dp", "vocab"), None, None),
        P(("dp", "vocab"), None, None),
        P(("dp", "vocab"), None, None),
        P("vocab", None),
        P("vocab", None),
        P("vocab", None),
        P(),
        P(),
        P(),
        P(None, ("dp", "vocab"), None),
        P(None, ("dp", "vocab"), None),
        P(None, ("dp", "vocab")),
        P(None, ("dp", "vocab")),
        P(None, ("dp", "vocab"), None),
        P(None, ("dp", "vocab"), None),
        P(),
    )
    return jax.shard_map(
        per_device,
        mesh=mesh,
        in_specs=placed,
        out_specs=(
            P(),
            P(),
            P(),
            P(("dp", "vocab"), None, None),
            P(("dp", "vocab"), None, None),
            P(("dp", "vocab"), None, None),
            P(("dp", "vocab"), None, None),
            P(("dp", "vocab"), None, None),
            P(("dp", "vocab"), None, None),
            P(("dp", "vocab"), None, None),
            P(("dp", "vocab"), None, None),
            P("vocab", None),
            P("vocab", None),
            P("vocab", None),
            P("vocab", None),
            P(),
            P(),
            P(),
        ),
        check_vma=False,
    )
```
